32 devices in a mesh: grp: 2 (over y), lon: 4 (over z), lat: 4 (over x, core).
Axes of the slice: x: 2, y: 2, z: 4, core: 2. Of those that a mesh axis runs over, the one named last changes fastest.
Arguments:
- state_old: float32 [8, 256, 512], P('grp', 'lat', 'lon'), parts along dimension 0, may hold values from -6 to 6
- state_now: float32 [8, 256, 512], P('grp', 'lat', 'lon'), parts along dimension 0, may hold values from -6 to 6
- drift: float32 [8, 256, 512], P('grp', 'lat', 'lon'), parts along dimension 0, may hold values from -1 to 1
- ocean: int32 [512, 512], P(('grp', 'lat'), 'lon'), parts along dimension 0, may hold values from 0 to 1, as said below
- w_in: bfloat16 [12, 256], replicated, may hold values from -1.75 to 1.75
- w_mid: bfloat16 [256, 256], replicated, may hold values from -0.375 to 0.375
- w_out: bfloat16 [256, 4], replicated, may hold values from -0.375 to 0.375
- cot_mid: float32 [8, 256, 512], P('grp', 'lat', 'lon'), parts along dimension 0, may hold values from -6 to 6
- cot_new: float32 [8, 256, 512], P('grp', 'lat', 'lon'), parts along dimension 0, may hold values from -6 to 6
Outputs:
- state_mid: float32 [8, 256, 512], P('grp', 'lat', 'lon'), parts along dimension 0
- state_new: float32 [8, 256, 512], P('grp', 'lat', 'lon'), parts along dimension 0
- grad_old: float32 [8, 256, 512], P('grp', 'lat', 'lon'), parts along dimension 0
- grad_now: float32 [8, 256, 512], P('grp', 'lat', 'lon'), parts along dimension 0
- grad_in: float32 [24, 256], P('grp'), parts along dimension 0
- grad_mid: float32 [512, 256], P('grp'), parts along dimension 0
- grad_out: float32 [512, 4], P('grp'), parts along dimension 0
The draws below stay inside these ranges and needn't reach their ends.
There are 2 independent parts, one for each index of `grp`. The reference program is written for one: setup_inputs(seed, part) draws one part's arguments, and reference() takes and returns one part's arrays. A program takes and returns all parts, laid end to end along the dimension named above; an argument that names none is the same for every part. Nothing has to cross between parts.
Inputs may be any that keep to these rules, and one draw needn't show every extreme that they name: 1 marks an ocean column, 0 land; land covers whole latitude rows of some blocks.
All inputs are finite; a program needn't handle non-finite values.
Results may differ from the reference program's by a relative error of at most 0.00055.
The reference program's roundings to bfloat16 on the way count: a program that leaves them out, or rounds other values in their place, can miss the bound.
Values may be sent and summed in bfloat16 or wider, within the bound.
No kernel may reach another device: no remote copies, remote signals or barrier semaphores. Data moves between devices by JAX's collectives and lax.ppermute only.
A program may use at most 64 MiB of HBM per device.

```python
import jax
import jax.numpy as jnp
from jax import lax

LEV = 4
H = 256
F_IN = 12
CLAT = 64
CLON = 128
NLAT = 256
NLON = 512


def draw_ocean(key, part):
    key = jax.random.fold_in(key, 7)
    deep_key, lake_key = jax.random.split(key)
    depth = jax.random.randint(deep_key, (NLAT // CLAT, NLON // CLON), 0, CLAT + 1)
    depth = jnp.repeat(jnp.repeat(depth, CLAT, axis=0), CLON, axis=1)
    row_index = (jnp.arange(NLAT) % CLAT)[:, None]
    lakes = jax.random.randint(lake_key, (NLAT, NLON), 0, 8)
    return jnp.where((row_index >= depth) & (lakes > 0), 1, 0).astype(jnp.int32)


def block_levels(rng, shape, cuts, smallest, largest):
    level, own = 1.0, jax.random.fold_in(rng, 6)
    for axis_at, shards_of in cuts:
        steps = jnp.exp(jax.random.uniform(jax.random.fold_in(own, axis_at), (shards_of,), jnp.float32, smallest / len(cuts), largest / len(cuts)))
        level = level * jnp.repeat(steps, shape[axis_at] // shards_of).reshape([-1 if axis == axis_at else 1 for axis in range(len(shape))])
    return level


def centred(key, dims, width, bound, cuts=(), dtype=jnp.bfloat16):
    gain = block_levels(key, dims, cuts, -0.22, 0.18) if cuts else 1.0
    array = jax.random.normal(key, dims, jnp.float32) * width * gain
    return jnp.minimum(jnp.maximum(array, -bound), bound).astype(dtype)


def setup_inputs(seed: int = 0, part: int = 0) -> dict:
    key_list = jax.random.split(jax.random.key(seed), 10)
    part_keys = jax.random.split(jax.random.fold_in(key_list[9], part), 10)
    state_old = centred(part_keys[0], (LEV, NLAT, NLON), 1.0, 6.0, ((1, 4), (2, 4)), jnp.float32)
    state_now = centred(part_keys[1], (LEV, NLAT, NLON), 1.0, 6.0, ((1, 4), (2, 4)), jnp.float32)
    drift = jnp.clip(jax.random.uniform(part_keys[2], (LEV, NLAT, NLON), jnp.float32, -1.0, 1.0) * block_levels(part_keys[2], (LEV, NLAT, NLON), ((1, 4), (2, 4)), -0.4, 0.0), -1.0, 1.0)
    ocean = draw_ocean(jax.random.fold_in(jax.random.fold_in(key_list[9], part), 71), part)
    w_in = centred(key_list[4], (F_IN, H), F_IN ** -0.5, 1.75)
    w_mid = centred(key_list[5], (H, H), H ** -0.5, 0.375)
    w_out = centred(key_list[6], (H, LEV), H ** -0.5, 0.375)
    cot_mid = centred(part_keys[7], (LEV, NLAT, NLON), 1.0, 6.0, ((1, 4), (2, 4)), jnp.float32)
    cot_new = centred(part_keys[8], (LEV, NLAT, NLON), 1.0, 6.0, ((1, 4), (2, 4)), jnp.float32)
    return {"state_old": state_old, "state_now": state_now, "drift": drift, "ocean": ocean, "w_in": w_in, "w_mid": w_mid, "w_out": w_out, "cot_mid": cot_mid, "cot_new": cot_new}


KAPPA = 0.2
DT = 0.1
GAIN_GRAD = 10.0
HIGHEST = lax.Precision.HIGHEST

def lowered(value):
    return lax.optimization_barrier(value.astype(jnp.bfloat16))

def product(form, left, right):
    return jnp.einsum(form, left.astype(jnp.float32), right.astype(jnp.float32), precision=HIGHEST)

def shifted(field):
    eastward = jnp.roll(field, -1, axis=2)
    westward = jnp.roll(field, 1, axis=2)
    zero_row = jnp.zeros_like(field[:, :1])
    northward = jnp.concatenate([field[:, 1:], zero_row], 1)
    southward = jnp.concatenate([zero_row, field[:, :-1]], 1)
    return (eastward, westward, northward, southward)

def layer_rows(w_in, w_mid, w_out, features):
    first = jnp.tanh(product('fh,fc->hc', w_in, features))
    second = jnp.tanh(product('gh,gc->hc', w_mid, lowered(first)))
    result = product('hl,hc->lc', w_out, lowered(second)).astype(jnp.bfloat16)
    return (result, first, second)

def closure_all(w_in, w_mid, w_out, features):

    def one_row(row_feats):
        return layer_rows(w_in, w_mid, w_out, row_feats)[0]
    result = lax.map(one_row, jnp.moveaxis(features, 1, 0))
    return jnp.moveaxis(result, 0, 1)

def closure_back_all(w_in, w_mid, w_out, features, cotangent):

    def one_row(totals, pair):
        row_feats, row_cot = pair
        result, first, second = layer_rows(w_in, w_mid, w_out, row_feats)
        dz_two = lowered(product('hl,lc->hc', w_out, row_cot) * (1.0 - second * second))
        dz_one = lowered(product('gh,hc->gc', w_mid, dz_two) * (1.0 - first * first))
        dfeat = lowered(product('fh,hc->fc', w_in, dz_one))
        term_in = product('fc,hc->fh', row_feats, dz_one)
        term_mid = product('gc,hc->gh', lowered(first), dz_two)
        term_out = product('hc,lc->hl', lowered(second), row_cot)
        return ((totals[0] + term_in, totals[1] + term_mid, totals[2] + term_out), dfeat)
    start = (jnp.zeros((F_IN, H), jnp.float32), jnp.zeros((H, H), jnp.float32), jnp.zeros((H, LEV), jnp.float32))
    totals, dfeats = lax.scan(one_row, start, (jnp.moveaxis(features, 1, 0), jnp.moveaxis(cotangent, 1, 0)))
    return (jnp.moveaxis(dfeats, 0, 1), totals)

def tendency(field, drift, wet, weights):
    eastward, westward, northward, southward = shifted(field)
    slope_x = 0.5 * (eastward - westward)
    slope_y = 0.5 * (northward - southward)
    features = lowered(jnp.concatenate([field, slope_x, slope_y], 0))
    closed = closure_all(weights[0], weights[1], weights[2], features)
    laplace = eastward + westward + northward + southward - 4.0 * field
    return (wet * (KAPPA * laplace - drift * slope_x + closed.astype(jnp.float32)), features)

def adjoint(weighted, features, drift, wet, weights):
    masked = wet * weighted
    dfeat, totals = closure_back_all(weights[0], weights[1], weights[2], features, lowered(masked))
    dfeat = dfeat.astype(jnp.float32)
    east_m, west_m, north_m, south_m = shifted(masked)
    east_p, west_p, unused_n, unused_s = shifted(drift * masked)
    east_a, west_a, other_n, other_s = shifted(dfeat[LEV:2 * LEV])
    other_e, other_w, north_b, south_b = shifted(dfeat[2 * LEV:])
    result = KAPPA * (east_m + west_m + north_m + south_m - 4.0 * masked)
    result = result + 0.5 * (east_p - west_p) + dfeat[:LEV]
    result = result - 0.5 * (east_a - west_a) - 0.5 * (north_b - south_b)
    return (result, totals)

def reference(state_old, state_now, drift, ocean, w_in, w_mid, w_out, cot_mid, cot_new):
    weights = (w_in, w_mid, w_out)
    wet = ocean.astype(jnp.float32)[None]
    force, feats_one = tendency(state_now, drift, wet, weights)
    state_mid = state_old + 2.0 * DT * force
    force, feats_two = tendency(state_mid, drift, wet, weights)
    state_new = state_now + 2.0 * DT * force
    result, totals_two = adjoint(2.0 * DT * cot_new, feats_two, drift, wet, weights)
    grad_old = cot_mid + result
    result, totals_one = adjoint(2.0 * DT * grad_old, feats_one, drift, wet, weights)
    grad_now = cot_new + result
    factor = GAIN_GRAD / jnp.sqrt(jnp.float32(NLAT * NLON))
    grad_in = (totals_one[0] + totals_two[0]) * factor
    grad_mid = (totals_one[1] + totals_two[1]) * factor
    grad_out = (totals_one[2] + totals_two[2]) * factor
    return (state_mid, state_new, grad_old, grad_now, grad_in, grad_mid, grad_out)
```

```python
import functools

import jax
import jax.numpy as jnp
from jax import lax
from jax.experimental import pallas as pl
from jax.experimental.pallas import tpu as pltpu
from jax.sharding import PartitionSpec as P

KAPPA = 0.2
DT = 0.1
GAIN_GRAD = 10.0

WIDE = 4
LANES = 128
TILES = 8

F32 = jnp.float32
BF16 = jnp.bfloat16


def dot(left, right):
    return lax.dot_general(left, right, (((1,), (0,)), ((), ())), preferred_element_type=F32)


def dot_nt(left, right):
    return lax.dot_general(left, right, (((1,), (1,)), ((), ())), preferred_element_type=F32)


def planes_of(refs, ocean):
    out = []
    for ref in refs:
        for level in range(ref.shape[0]):
            out.append(ref[level])
    out.append(ocean[...].astype(F32))
    return out


def pack_kernel(now, old, drift, cnew, cmid, ocean, west, east, top, bottom):
    rows = ocean.shape[0]
    lane = lax.broadcasted_iota(jnp.int32, (rows, LANES), 1)
    to_west = jnp.zeros((rows, LANES), F32)
    to_east = jnp.zeros((rows, LANES), F32)
    for p, plane in enumerate(planes_of((now, old, drift, cnew, cmid), ocean)):
        here = (lane >= WIDE * p) & (lane < WIDE * (p + 1))
        to_west = jnp.where(here, pltpu.roll(plane, WIDE * p, 1) if p else plane, to_west)
        to_east = jnp.where(here, pltpu.roll(plane, WIDE * (p + 1), 1), to_east)
        top[pl.ds(WIDE * p, WIDE), :] = plane[:WIDE]
        bottom[pl.ds(WIDE * p, WIDE), :] = plane[rows - WIDE :]
    west[...] = to_west
    east[...] = to_east


def east_of(v):
    return pltpu.roll(v, v.shape[1] - 1, 1)


def west_of(v):
    return pltpu.roll(v, 1, 1)


def north_of(v):
    return pltpu.roll(v, v.shape[0] - 1, 0)


def south_of(v):
    return pltpu.roll(v, 1, 0)


def main_kernel(
    now, old, drift, cnew, cmid, ocean, left, right, low, high,
    w_in, w_in_t, w_mid, w_mid_t, w_out, w_out_t,
    o_mid, o_new, o_old, o_now, o_grad,
    planes, ft, fth, ftx, cl, clh, clx, dc, dch, dcx, df, dfh, dfx,
    keep1, keep2, halo1, halo2, acc_mid, acc_in, acc_out,
):
    rows = ocean.shape[0]
    ext = rows + 2 * WIDE
    levels = now.shape[0]
    count = 5 * levels + 1
    chunks = rows // TILES
    span = TILES * LANES
    packs = rows // 16
    near = [rows, ext - 1]
    corner = rows + 2
    first_pack = rows + 3
    far = [rows + 1, ext - 2, rows + 2, ext - 3]
    slots = {near[0]: rows, near[1]: rows + 1}
    for i, r in enumerate(far):
        slots[r] = first_pack + packs + i
    halo_one = 3 + packs
    halo_two = halo_one + 2
    halo_all = halo_one + 4

    lane = lax.broadcasted_iota(jnp.int32, (ext, LANES), 1)
    strips = planes_base = WIDE * count
    left_all = jnp.concatenate([left[...], high[pl.ds(strips, WIDE), :], low[pl.ds(strips, WIDE), :]], 0)
    right_all = jnp.concatenate([right[...], high[pl.ds(strips + WIDE, WIDE), :], low[pl.ds(strips + WIDE, WIDE), :]], 0)
    for p, plane in enumerate(planes_of((now, old, drift, cnew, cmid), ocean)):
        body = jnp.concatenate([plane, high[pl.ds(WIDE * p, WIDE), :], low[pl.ds(WIDE * p, WIDE), :]], 0)
        from_right = pltpu.roll(right_all, LANES - WIDE * p, 1) if p else right_all
        from_left = pltpu.roll(left_all, LANES - WIDE * (p + 1), 1)
        side = jnp.where(lane < WIDE, from_right, jnp.where(lane >= LANES - WIDE, from_left, 0.0))
        planes[p] = jnp.concatenate([body, side], 1)

    def field(which, level):
        return planes[which * levels + level]

    wet = planes[count - 1]

    ft[...] = jnp.zeros_like(ft)
    fth[...] = jnp.zeros_like(fth)
    ftx[...] = jnp.zeros_like(ftx)
    dc[...] = jnp.zeros_like(dc)
    dch[...] = jnp.zeros_like(dch)
    dcx[...] = jnp.zeros_like(dcx)
    acc_mid[...] = jnp.zeros_like(acc_mid)
    acc_in[...] = jnp.zeros_like(acc_in)
    acc_out[...] = jnp.zeros_like(acc_out)

    def spread(plane, index, deep, main, extra, side):
        main[pl.ds(index, rows, stride=deep), :] = plane[:rows, :LANES]
        extra[pl.ds(index, 2 * WIDE, stride=deep), :] = plane[rows:, :LANES]
        side[pl.ds(index, ext, stride=deep), :] = plane[:, LANES:]

    def gathered(index, deep, main, extra, side):
        body = jnp.concatenate(
            [main[pl.ds(index, rows, stride=deep), :], extra[pl.ds(index, 2 * WIDE, stride=deep), :]], 0
        )
        return jnp.concatenate([body, side[pl.ds(index, ext, stride=deep), :]], 1)

    def pack_halo(deep, main, extra, side):
        where = lax.broadcasted_iota(jnp.int32, (deep, LANES), 1)
        for r, slot in slots.items():
            main[pl.ds(slot * deep, deep), :] = extra[pl.ds((r - rows) * deep, deep), :]
        groups = [(first_pack + q, range(16 * q, 16 * q + 16)) for q in range(packs)]
        groups.append((corner, range(rows, ext)))
        for slot, members in groups:
            total = jnp.zeros((deep, LANES), F32)
            for j, r in enumerate(members):
                moved = pltpu.roll(side[pl.ds(r * deep, deep), :], (2 * WIDE * j + WIDE) % LANES, 1)
                total = jnp.where((where >= 2 * WIDE * j) & (where < 2 * WIDE * (j + 1)), moved, total)
            main[pl.ds(slot * deep, deep), :] = total

    def unpack_halo(deep, main, extra, side, live):
        for r, slot in slots.items():
            if slot < rows + live:
                extra[pl.ds((r - rows) * deep, deep), :] = main[pl.ds(slot * deep, deep), :]
        groups = [(first_pack + q, range(16 * q, 16 * q + 16)) for q in range(packs)]
        groups.append((corner, range(rows, ext)))
        for slot, members in groups:
            tile = main[pl.ds(slot * deep, deep), :]
            for j, r in enumerate(members):
                side[pl.ds(r * deep, deep), :] = pltpu.roll(tile, LANES - (2 * WIDE * j + WIDE) % LANES, 1)

    def lanes_of(ref, deep, base, tiles):
        block = ref[pl.ds(base * deep, tiles * deep), :]
        return jnp.concatenate([block[k * deep : (k + 1) * deep] for k in range(tiles)], 1)

    def put_lanes(ref, deep, base, tiles, value):
        for k in range(tiles):
            ref[pl.ds((base + k) * deep, deep), :] = value[:, k * LANES : (k + 1) * LANES]

    def inputs_at(base, tiles):
        return lanes_of(ft, 16, base, tiles).astype(BF16)

    def cotangents_at(base, tiles):
        part = lanes_of(dc, 8, base, tiles)
        return jnp.concatenate([part, jnp.zeros_like(part)], 0).astype(BF16)

    def forward(x):
        first = jnp.tanh(dot(w_in_t[...], x))
        second = jnp.tanh(dot(w_mid_t[...], first.astype(BF16)))
        return first, second

    def closure(second):
        return dot(w_out_t[...], second.astype(BF16)).astype(BF16).astype(F32)[:8]

    def backward(first, second, cot):
        dz_two = (dot(w_out[...], cot) * (1.0 - second * second)).astype(BF16)
        dz_one = (dot(w_mid[...], dz_two) * (1.0 - first * first)).astype(BF16)
        dfeat = dot(w_in[...], dz_one).astype(BF16).astype(F32)
        return dz_one, dz_two, dfeat

    def add_terms(x, first, second, cot, dz_one, dz_two):
        acc_mid[...] += dot_nt(first.astype(BF16), dz_two)
        acc_in[...] += dot_nt(x, dz_one)
        acc_out[...] += dot_nt(cot, second.astype(BF16))

    def features_from(values):
        for level, v in enumerate(values):
            slope_x = 0.5 * (east_of(v) - west_of(v))
            slope_y = 0.5 * (north_of(v) - south_of(v))
            spread(v, level, 16, ft, ftx, fth)
            spread(slope_x, levels + level, 16, ft, ftx, fth)
            spread(slope_y, 2 * levels + level, 16, ft, ftx, fth)
        pack_halo(16, ft, ftx, fth)

    def force(v, velocity, closed):
        eastward, westward, northward, southward = east_of(v), west_of(v), north_of(v), south_of(v)
        laplace = eastward + westward + northward + southward - 4.0 * v
        return wet_like(v) * (KAPPA * laplace - velocity * (0.5 * (eastward - westward)) + closed)

    def wet_like(v):
        return planes[count - 1]

    features_from([field(0, level) for level in range(levels)])

    def first_step(c, carry):
        base = pl.multiple_of(c * TILES, TILES)
        x = inputs_at(base, TILES)
        first, second = forward(x)
        keep1[c] = first
        keep2[c] = second
        put_lanes(cl, 8, base, TILES, closure(second))
        return carry

    lax.fori_loop(0, chunks, first_step, 0)
    first, second = forward(inputs_at(rows, halo_all))
    halo1[...] = first
    halo2[...] = second
    put_lanes(cl, 8, rows, halo_all, closure(second))
    unpack_halo(8, cl, clx, clh, halo_all)
    mids = []
    for level in range(levels):
        closed = gathered(level, 8, cl, clx, clh)
        mid = field(1, level) + 2.0 * DT * force(field(0, level), field(2, level), closed)
        o_mid[level] = mid[:rows, :LANES]
        mids.append(mid)

    features_from(mids)
    for level in range(levels):
        spread(wet * (2.0 * DT * field(3, level)), level, 8, dc, dcx, dch)
    pack_halo(8, dc, dcx, dch)

    def second_step(c, carry):
        base = pl.multiple_of(c * TILES, TILES)
        x = inputs_at(base, TILES)
        cot = cotangents_at(base, TILES)
        first, second = forward(x)
        put_lanes(cl, 8, base, TILES, closure(second))
        dz_one, dz_two, dfeat = backward(first, second, cot)
        put_lanes(df, 16, base, TILES, dfeat)
        add_terms(x, first, second, cot, dz_one, dz_two)
        return carry

    lax.fori_loop(0, chunks, second_step, 0)
    first, second = forward(inputs_at(rows, halo_two))
    unused_one, unused_two, dfeat = backward(first, second, cotangents_at(rows, halo_two))
    put_lanes(df, 16, rows, halo_two, dfeat)
    unpack_halo(16, df, dfx, dfh, halo_two)
    for level in range(levels):
        mid = mids[level]
        velocity = field(2, level)
        closed = cl[pl.ds(level, rows, stride=8), :]
        eastward, westward, northward, southward = east_of(mid), west_of(mid), north_of(mid), south_of(mid)
        laplace = (eastward + westward + northward + southward - 4.0 * mid)[:rows, :LANES]
        slope = (0.5 * (eastward - westward))[:rows, :LANES]
        total = wet[:rows, :LANES] * (KAPPA * laplace - velocity[:rows, :LANES] * slope + closed)
        o_new[level] = now[level] + 2.0 * DT * total

    def adjoint_planes(weighted, level):
        masked = wet * weighted
        carried = field(2, level) * masked
        a0 = gathered(level, 16, df, dfx, dfh)
        a1 = gathered(levels + level, 16, df, dfx, dfh)
        a2 = gathered(2 * levels + level, 16, df, dfx, dfh)
        result = KAPPA * (east_of(masked) + west_of(masked) + north_of(masked) + south_of(masked) - 4.0 * masked)
        result = result + 0.5 * (east_of(carried) - west_of(carried)) + a0
        return result - 0.5 * (east_of(a1) - west_of(a1)) - 0.5 * (north_of(a2) - south_of(a2))

    olds = []
    for level in range(levels):
        grad = field(4, level) + adjoint_planes(2.0 * DT * field(3, level), level)
        o_old[level] = grad[:rows, :LANES]
        olds.append(grad)
    for level in range(levels):
        spread(wet * (2.0 * DT * olds[level]), level, 8, dc, dcx, dch)
    pack_halo(8, dc, dcx, dch)
    features_again([field(0, level) for level in range(levels)], levels, spread, ft, ftx, fth)

    def third_step(c, carry):
        base = pl.multiple_of(c * TILES, TILES)
        x = inputs_at(base, TILES)
        cot = cotangents_at(base, TILES)
        first = keep1[c]
        second = keep2[c]
        dz_one, dz_two, dfeat = backward(first, second, cot)
        put_lanes(df, 16, base, TILES, dfeat)
        add_terms(x, first, second, cot, dz_one, dz_two)
        return carry

    lax.fori_loop(0, chunks, third_step, 0)
    near_lanes = halo_one * LANES
    unused_one, unused_two, dfeat = backward(
        halo1[:, :near_lanes], halo2[:, :near_lanes], cotangents_at(rows, halo_one)
    )
    put_lanes(df, 16, rows, halo_one, dfeat)
    unpack_halo(16, df, dfx, dfh, halo_one)
    for level in range(levels):
        grad = adjoint_planes(2.0 * DT * olds[level], level)
        o_now[level] = cnew[level] + grad[:rows, :LANES]

    hidden = acc_mid.shape[0]
    o_grad[...] = jnp.zeros_like(o_grad)
    start = 0
    for acc in (acc_mid, acc_in, acc_out):
        deep = acc.shape[0]
        for half in range(hidden // LANES):
            o_grad[pl.ds(start, deep), :] = acc[:, half * LANES : (half + 1) * LANES]
            start += deep


def features_again(values, levels, spread, ft, ftx, fth):
    for level, v in enumerate(values):
        spread(v, level, 16, ft, ftx, fth)
        spread(0.5 * (east_of(v) - west_of(v)), levels + level, 16, ft, ftx, fth)
        spread(0.5 * (north_of(v) - south_of(v)), 2 * levels + level, 16, ft, ftx, fth)


def along(value, axis, step, periodic):
    count = lax.axis_size(axis)
    pairs = [(i, (i + step) % count) for i in range(count) if periodic or 0 <= i + step < count]
    return lax.ppermute(value, axis, pairs)


def body(state_old, state_now, drift, ocean, w_in, w_mid, w_out, cot_mid, cot_new):
    levels, rows, cols = state_now.shape
    width_in, hidden = w_in.shape
    ext = rows + 2 * WIDE
    count = 5 * levels + 1
    fields = (state_now, state_old, drift, cot_new, cot_mid, ocean)
    vmem = pl.BlockSpec(memory_space=pltpu.VMEM)
    strip = jax.ShapeDtypeStruct((rows, LANES), F32)
    edge = jax.ShapeDtypeStruct((WIDE * count, LANES), F32)
    west, east, top, bottom = pl.pallas_call(
        pack_kernel,
        out_shape=(strip, strip, edge, edge),
        in_specs=[vmem] * 6,
        out_specs=(vmem,) * 4,
        compiler_params=pltpu.CompilerParams(vmem_limit_bytes=32 * 2**20),
    )(*fields)
    left = along(east, "lon", 1, True)
    right = along(west, "lon", -1, True)
    up = jnp.concatenate([bottom, left[rows - WIDE :], right[rows - WIDE :]], 0)
    down = jnp.concatenate([top, left[:WIDE], right[:WIDE]], 0)
    low = along(up, "lat", 1, False)
    high = along(down, "lat", -1, False)

    in_pad = jnp.pad(w_in, ((0, 16 - width_in), (0, 0)))
    out_pad = jnp.pad(w_out, ((0, 0), (0, 16 - levels)))
    weights = (in_pad, in_pad.T, w_mid, w_mid.T, out_pad, out_pad.T)

    members = lax.axis_size("lon") * lax.axis_size("lat")
    used = (hidden // LANES) * (hidden + 32)
    piece = -(-used // (8 * members)) * 8
    field = jax.ShapeDtypeStruct((levels, rows, cols), F32)
    packs = rows // 16
    slots = rows + 7 + packs
    chunks = rows // TILES
    span = TILES * LANES
    halo = (7 + packs) * LANES
    state_mid, state_new, grad_old, grad_now, terms = pl.pallas_call(
        main_kernel,
        out_shape=(field, field, field, field, jax.ShapeDtypeStruct((piece * members, LANES), F32)),
        in_specs=[vmem] * 16,
        out_specs=(vmem,) * 5,
        scratch_shapes=[
            pltpu.VMEM((count, ext, 2 * LANES), F32),
            pltpu.VMEM((slots * 16, LANES), F32),
            pltpu.VMEM((ext * 16, LANES), F32),
            pltpu.VMEM((2 * WIDE * 16, LANES), F32),
            pltpu.VMEM((slots * 8, LANES), F32),
            pltpu.VMEM((ext * 8, LANES), F32),
            pltpu.VMEM((2 * WIDE * 8, LANES), F32),
            pltpu.VMEM((slots * 8, LANES), F32),
            pltpu.VMEM((ext * 8, LANES), F32),
            pltpu.VMEM((2 * WIDE * 8, LANES), F32),
            pltpu.VMEM((slots * 16, LANES), F32),
            pltpu.VMEM((ext * 16, LANES), F32),
            pltpu.VMEM((2 * WIDE * 16, LANES), F32),
            pltpu.VMEM((chunks, hidden, span), F32),
            pltpu.VMEM((chunks, hidden, span), F32),
            pltpu.VMEM((hidden, halo), F32),
            pltpu.VMEM((hidden, halo), F32),
            pltpu.VMEM((hidden, hidden), F32),
            pltpu.VMEM((16, hidden), F32),
            pltpu.VMEM((16, hidden), F32),
        ],
        compiler_params=pltpu.CompilerParams(vmem_limit_bytes=56 * 2**20),
    )(*fields, left, right, low, high, *weights)

    pieces = lax.all_to_all(terms.reshape(members, piece, LANES), ("lon", "lat"), 0, 0)
    cells_all = rows * lax.axis_size("lat") * cols * lax.axis_size("lon")
    factor = GAIN_GRAD / jnp.sqrt(jnp.float32(cells_all))
    own = jnp.sum(pieces, 0) * factor
    spread = jnp.broadcast_to(own[None], (members, piece, LANES))
    summed = lax.all_to_all(spread, ("lon", "lat"), 0, 0).reshape(members * piece, LANES)
    halves = hidden // LANES
    parts = []
    start = 0
    for deep in (hidden, 16, 16):
        block = summed[start : start + halves * deep].reshape(halves, deep, LANES)
        parts.append(jnp.swapaxes(block, 0, 1).reshape(deep, hidden))
        start += halves * deep
    return (
        state_mid,
        state_new,
        grad_old,
        grad_now,
        parts[1][:width_in],
        parts[0],
        parts[2][:levels].T,
    )


def solution(mesh):
    field = P("grp", "lat", "lon")
    whole = P("grp", None)
    in_specs = (field, field, field, P(("grp", "lat"), "lon"), P(), P(), P(), field, field)
    out_specs = (field, field, field, field, whole, whole, whole)
    return jax.shard_map(body, mesh=mesh, in_specs=in_specs, out_specs=out_specs, check_vma=False)
```

```python
import functools

import jax
import jax.numpy as jnp
from jax import lax
from jax.experimental import pallas as pl
from jax.experimental.pallas import tpu as pltpu
from jax.sharding import PartitionSpec as P

KAPPA = 0.2
DT = 0.1
GAIN_GRAD = 10.0

WIDE = 4
LANES = 128
TILES = 8
DEEP = 16
SHALLOW = 8

F32 = jnp.float32
BF16 = jnp.bfloat16


def dot(left, right):
    return lax.dot_general(left, right, (((1,), (0,)), ((), ())), preferred_element_type=F32)


def dot_nt(left, right):
    return lax.dot_general(left, right, (((1,), (1,)), ((), ())), preferred_element_type=F32)


def pack_kernel(now, old, drift, cnew, cmid, ocean, west, east, top, bottom, fields, wet, sems):
    levels, rows, cols = now.shape
    copies = [
        pltpu.make_async_copy(ref, fields.at[pl.ds(levels * f, levels)], sems.at[f])
        for f, ref in enumerate((now, old, drift, cnew, cmid))
    ]
    copies.append(pltpu.make_async_copy(ocean, wet, sems.at[5]))
    for copy in copies:
        copy.start()
    for copy in copies:
        copy.wait()
    count = 5 * levels
    fields[count] = wet[...].astype(F32)
    lane = lax.broadcasted_iota(jnp.int32, (rows, LANES), 1)
    west[...] = jnp.zeros_like(west)
    east[...] = jnp.zeros_like(east)

    def one_plane(p, carry):
        plane = fields[p]
        here = (lane >= WIDE * p) & (lane < WIDE * (p + 1))
        west[...] = jnp.where(here, pltpu.roll(plane, WIDE * p, 1), west[...])
        east[...] = jnp.where(here, pltpu.roll(plane, WIDE * (p + 1), 1), east[...])
        top[p] = plane[:WIDE]
        bottom[p] = plane[rows - WIDE :]
        return carry

    lax.fori_loop(0, count + 1, one_plane, 0)


def east_of(v):
    return pltpu.roll(v, v.shape[1] - 1, 1)


def west_of(v):
    return pltpu.roll(v, 1, 1)


def north_of(v):
    return pltpu.roll(v, v.shape[0] - 1, 0)


def south_of(v):
    return pltpu.roll(v, 1, 0)


def main_kernel(
    fields, left, right, low, high, w_in, w_mid, w_out_t,
    o_mid, o_new, o_old, o_now, o_grad,
    planes, mids, olds, ft1, ft2, fth, ftx, cl, clh, clx, dc, dch, dcx, df, dfh, dfx,
    keep1, keep2, acc_mid, acc_in, acc_out, wi, wi_t, wm_t, wo, wo_t,
):
    levels, rows, cols = o_mid.shape
    width_in, hidden = w_in.shape
    count = 5 * levels + 1
    ext = rows + 2 * WIDE
    chunks = rows // TILES
    packs = -(-ext // 16)
    order = [rows, ext - 1] + [None] * packs + [rows + 1, ext - 2, rows + 2, ext - 3]
    first_pack = rows + 2
    halo_one = 2 + packs
    halo_two = halo_one + 2

    spare = jnp.zeros((DEEP - width_in, hidden), F32)
    wide_in = jnp.concatenate([w_in[...].astype(F32), spare], 0)
    wi[...] = wide_in.astype(BF16)
    wi_t[...] = wide_in.T.astype(BF16)
    wm_t[...] = w_mid[...].astype(F32).T.astype(BF16)
    spare = jnp.zeros((DEEP - levels, hidden), F32)
    wide_out = jnp.concatenate([w_out_t[...].astype(F32), spare], 0)
    wo_t[...] = wide_out.astype(BF16)
    wo[...] = wide_out.T.astype(BF16)

    lane = lax.broadcasted_iota(jnp.int32, (ext, LANES), 1)
    left_all = jnp.concatenate([left[...], high[count], low[count]], 0)
    right_all = jnp.concatenate([right[...], high[count + 1], low[count + 1]], 0)

    def one_plane(p, carry):
        from_right = pltpu.roll(right_all, LANES - WIDE * p, 1)
        from_left = pltpu.roll(left_all, LANES - WIDE * (p + 1), 1)
        side = jnp.where(lane < WIDE, from_right, jnp.where(lane >= LANES - WIDE, from_left, 0.0))
        planes[p, :, pl.ds(0, LANES)] = jnp.concatenate([fields[p], high[p], low[p]], 0)
        planes[p, :, pl.ds(LANES, LANES)] = side
        return carry

    lax.fori_loop(0, count, one_plane, 0)

    for ref in (ft1, ft2, fth, ftx, dc, dch, dcx, acc_mid, acc_in, acc_out):
        ref[...] = jnp.zeros_like(ref)

    def spread(plane, index, deep, main, extra, side):
        main[pl.ds(index, rows, stride=deep), :] = plane[:rows, :LANES]
        extra[pl.ds(index, 2 * WIDE, stride=deep), :] = plane[rows:, :LANES]
        side[pl.ds(index, ext, stride=deep), :] = plane[:, LANES:]

    def gathered(index, deep, main, extra, side):
        body = jnp.concatenate(
            [main[pl.ds(index, rows, stride=deep), :], extra[pl.ds(index, 2 * WIDE, stride=deep), :]], 0
        )
        return jnp.concatenate([body, side[pl.ds(index, ext, stride=deep), :]], 1)

    def pack_halo(deep, main, extra, side):
        where = lax.broadcasted_iota(jnp.int32, (deep, LANES), 1)
        for i, r in enumerate(order):
            if r is not None:
                main[pl.ds((rows + i) * deep, deep), :] = extra[pl.ds((r - rows) * deep, deep), :]

        def one_pack(q, carry):
            total = jnp.zeros((deep, LANES), F32)
            for j in range(16):
                moved = side[pl.ds(pl.multiple_of((16 * q + j) * deep, deep), deep), :]
                moved = pltpu.roll(moved, (2 * WIDE * j + WIDE) % LANES, 1)
                total = jnp.where((where >= 2 * WIDE * j) & (where < 2 * WIDE * (j + 1)), moved, total)
            main[pl.ds(pl.multiple_of((first_pack + q) * deep, deep), deep), :] = total
            return carry

        lax.fori_loop(0, packs, one_pack, 0)

    def unpack_halo(deep, main, extra, side, live):
        for i, r in enumerate(order[:live]):
            if r is not None:
                extra[pl.ds((r - rows) * deep, deep), :] = main[pl.ds((rows + i) * deep, deep), :]

        def one_pack(q, carry):
            tile = main[pl.ds(pl.multiple_of((first_pack + q) * deep, deep), deep), :]
            for j in range(16):
                moved = pltpu.roll(tile, LANES - (2 * WIDE * j + WIDE) % LANES, 1)
                side[pl.ds(pl.multiple_of((16 * q + j) * deep, deep), deep), :] = moved
            return carry

        lax.fori_loop(0, packs, one_pack, 0)

    def lanes_of(ref, deep, base, tiles):
        block = ref[pl.ds(base * deep, tiles * deep), :]
        return jnp.concatenate([block[k * deep : (k + 1) * deep] for k in range(tiles)], 1)

    def put_lanes(ref, deep, base, tiles, value):
        for k in range(tiles):
            ref[pl.ds((base + k) * deep, deep), :] = value[:, k * LANES : (k + 1) * LANES]

    def inputs_at(ref, base, tiles):
        return lanes_of(ref, DEEP, base, tiles).astype(BF16)

    def cotangents_at(base, tiles):
        part = lanes_of(dc, SHALLOW, base, tiles)
        return jnp.concatenate([part, jnp.zeros_like(part)], 0).astype(BF16)

    def forward(x):
        first = jnp.tanh(dot(wi_t[...], x))
        second = jnp.tanh(dot(wm_t[...], first.astype(BF16)))
        return first, second

    def closure(second):
        return dot(wo_t[...], second.astype(BF16)).astype(BF16).astype(F32)[:SHALLOW]

    def backward(first, second, cot):
        dz_two = (dot(wo[...], cot) * (1.0 - second * second)).astype(BF16)
        dz_one = (dot(w_mid[...], dz_two) * (1.0 - first * first)).astype(BF16)
        dfeat = dot(wi[...], dz_one).astype(BF16).astype(F32)
        return dz_one, dz_two, dfeat

    def add_terms(x, first, second, cot, dz_one, dz_two):
        acc_mid[...] += dot_nt(first.astype(BF16), dz_two)
        acc_in[...] += dot_nt(x, dz_one)
        acc_out[...] += dot_nt(cot, second.astype(BF16))

    def features_of(source, ft):
        def one_level(level, carry):
            v = source[level]
            spread(v, level, DEEP, ft, ftx, fth)
            spread(0.5 * (east_of(v) - west_of(v)), levels + level, DEEP, ft, ftx, fth)
            spread(0.5 * (north_of(v) - south_of(v)), 2 * levels + level, DEEP, ft, ftx, fth)
            return carry

        lax.fori_loop(0, levels, one_level, 0)
        pack_halo(DEEP, ft, ftx, fth)

    def cotangents_of(source, offset):
        def one_level(level, carry):
            spread(planes[count - 1] * (2.0 * DT * source[offset + level]), level, SHALLOW, dc, dcx, dch)
            return carry

        lax.fori_loop(0, levels, one_level, 0)
        pack_halo(SHALLOW, dc, dcx, dch)

    def force(v, level, closed):
        eastward, westward, northward, southward = east_of(v), west_of(v), north_of(v), south_of(v)
        laplace = eastward + westward + northward + southward - 4.0 * v
        slope = 0.5 * (eastward - westward)
        return planes[count - 1] * (KAPPA * laplace - planes[2 * levels + level] * slope + closed)

    features_of(planes, ft1)

    def first_step(c, carry):
        base = pl.multiple_of(c * TILES, TILES)
        first, second = forward(inputs_at(ft1, base, TILES))
        keep1[c] = first
        keep2[c] = second
        put_lanes(cl, SHALLOW, base, TILES, closure(second))
        return carry

    lax.fori_loop(0, keep1.shape[0], first_step, 0)
    unpack_halo(SHALLOW, cl, clx, clh, len(order))

    def first_state(level, carry):
        closed = gathered(level, SHALLOW, cl, clx, clh)
        mid = planes[levels + level] + 2.0 * DT * force(planes[level], level, closed)
        o_mid[level] = mid[:rows, :LANES]
        mids[level] = mid
        return carry

    lax.fori_loop(0, levels, first_state, 0)

    features_of(mids, ft2)
    cotangents_of(planes, 3 * levels)

    def second_step(c, carry):
        base = pl.multiple_of(c * TILES, TILES)
        x = inputs_at(ft2, base, TILES)
        cot = cotangents_at(base, TILES)
        first, second = forward(x)
        put_lanes(cl, SHALLOW, base, TILES, closure(second))
        dz_one, dz_two, dfeat = backward(first, second, cot)
        put_lanes(df, DEEP, base, TILES, dfeat)
        add_terms(x, first, second, cot, dz_one, dz_two)
        return carry

    lax.fori_loop(0, chunks, second_step, 0)
    first, second = forward(inputs_at(ft2, rows, halo_two))
    unused_one, unused_two, dfeat = backward(first, second, cotangents_at(rows, halo_two))
    put_lanes(df, DEEP, rows, halo_two, dfeat)
    unpack_halo(DEEP, df, dfx, dfh, halo_two)

    def adjoint_of(weighted, level):
        masked = planes[count - 1] * weighted
        carried = planes[2 * levels + level] * masked
        a0 = gathered(level, DEEP, df, dfx, dfh)
        a1 = gathered(levels + level, DEEP, df, dfx, dfh)
        a2 = gathered(2 * levels + level, DEEP, df, dfx, dfh)
        result = KAPPA * (east_of(masked) + west_of(masked) + north_of(masked) + south_of(masked) - 4.0 * masked)
        result = result + 0.5 * (east_of(carried) - west_of(carried)) + a0
        return result - 0.5 * (east_of(a1) - west_of(a1)) - 0.5 * (north_of(a2) - south_of(a2))

    def second_state(level, carry):
        closed = jnp.concatenate([cl[pl.ds(level, rows, stride=SHALLOW), :], jnp.zeros((2 * WIDE, LANES), F32)], 0)
        closed = jnp.concatenate([closed, jnp.zeros_like(closed)], 1)
        new = planes[level] + 2.0 * DT * force(mids[level], level, closed)
        o_new[level] = new[:rows, :LANES]
        grad = planes[4 * levels + level] + adjoint_of(2.0 * DT * planes[3 * levels + level], level)
        o_old[level] = grad[:rows, :LANES]
        olds[level] = grad
        return carry

    lax.fori_loop(0, levels, second_state, 0)

    cotangents_of(olds, 0)

    def third_step(c, carry):
        base = pl.multiple_of(c * TILES, TILES)
        x = inputs_at(ft1, base, TILES)
        cot = cotangents_at(base, TILES)
        first = keep1[c]
        second = keep2[c]
        dz_one, dz_two, dfeat = backward(first, second, cot)
        put_lanes(df, DEEP, base, TILES, dfeat)
        add_terms(x, first, second, cot, dz_one, dz_two)
        return carry

    lax.fori_loop(0, chunks, third_step, 0)
    near = halo_one * LANES
    unused_one, unused_two, dfeat = backward(
        keep1[chunks, :, pl.ds(0, near)], keep2[chunks, :, pl.ds(0, near)], cotangents_at(rows, halo_one)
    )
    put_lanes(df, DEEP, rows, halo_one, dfeat)
    unpack_halo(DEEP, df, dfx, dfh, halo_one)

    def third_state(level, carry):
        grad = adjoint_of(2.0 * DT * olds[level], level)
        o_now[level] = planes[3 * levels + level, pl.ds(0, rows), pl.ds(0, LANES)] + grad[:rows, :LANES]
        return carry

    lax.fori_loop(0, levels, third_state, 0)

    start = 0
    for acc in (acc_mid, acc_in, acc_out):
        deep = acc.shape[0]
        for half in range(hidden // LANES):
            o_grad[pl.ds(start, deep), :] = acc[:, half * LANES : (half + 1) * LANES]
            start += deep
    if start < o_grad.shape[0]:
        o_grad[pl.ds(start, o_grad.shape[0] - start), :] = jnp.zeros((o_grad.shape[0] - start, LANES), F32)


def scale_kernel(factor, terms, g_in, g_mid, g_out):
    hidden = g_mid.shape[0]
    start = 0
    for ref, deep in ((g_mid, hidden), (g_in, DEEP), (g_out, DEEP)):
        keep = ref.shape[0]
        for half in range(hidden // LANES):
            ref[:, half * LANES : (half + 1) * LANES] = terms[pl.ds(start, keep), :] * factor
            start += deep


def along(value, axis, step, periodic):
    count = lax.axis_size(axis)
    pairs = [(i, (i + step) % count) for i in range(count) if periodic or 0 <= i + step < count]
    return lax.ppermute(value, axis, pairs)


def swapped(value, axis, bit):
    return lax.ppermute(value, axis, [(i, i ^ bit) for i in range(lax.axis_size(axis))])


def summed_over(value, halving, doubling):
    bits = []
    bit = 1
    while bit < lax.axis_size(halving):
        upper = (lax.axis_index(halving) & bit) != 0
        half = value.shape[0] // 2
        lower_part, upper_part = value[:half], value[half:]
        sent = jnp.where(upper, lower_part, upper_part)
        value = jnp.where(upper, upper_part, lower_part) + swapped(sent, halving, bit)
        bits.append((bit, upper))
        bit *= 2
    bit = 1
    while bit < lax.axis_size(doubling):
        value = value + swapped(value, doubling, bit)
        bit *= 2
    for bit, upper in reversed(bits):
        other = swapped(value, halving, bit)
        value = jnp.concatenate([jnp.where(upper, other, value), jnp.where(upper, value, other)], 0)
    return value


def body(state_old, state_now, drift, ocean, w_in, w_mid, w_out, cot_mid, cot_new):
    levels, rows, cols = state_now.shape
    width_in, hidden = w_in.shape
    ext = rows + 2 * WIDE
    count = 5 * levels + 1
    packs = -(-ext // 16)
    steps = -(-(rows + 6 + packs) // TILES)
    slots = steps * TILES
    vmem = pl.BlockSpec(memory_space=pltpu.VMEM)
    hbm = pl.BlockSpec(memory_space=pltpu.HBM)
    strip = jax.ShapeDtypeStruct((rows, LANES), F32)
    edge = jax.ShapeDtypeStruct((count, WIDE, LANES), F32)
    west, east, top, bottom, fields = pl.pallas_call(
        pack_kernel,
        out_shape=(strip, strip, edge, edge, jax.ShapeDtypeStruct((count, rows, cols), F32)),
        in_specs=[hbm] * 6,
        out_specs=(vmem,) * 5,
        scratch_shapes=[pltpu.VMEM((rows, cols), jnp.int32), pltpu.SemaphoreType.DMA((6,))],
        compiler_params=pltpu.CompilerParams(vmem_limit_bytes=8 * 2**20),
    )(state_now, state_old, drift, cot_new, cot_mid, ocean)
    left = along(east, "lon", 1, True)
    right = along(west, "lon", -1, True)
    up = jnp.concatenate([bottom, left[None, rows - WIDE :], right[None, rows - WIDE :]], 0)
    down = jnp.concatenate([top, left[None, :WIDE], right[None, :WIDE]], 0)
    low = along(up, "lat", 1, False)
    high = along(down, "lat", -1, False)

    halves = hidden // LANES
    grain = 8 * lax.axis_size("lat")
    terms_rows = -(-halves * (hidden + 2 * DEEP) // grain) * grain
    field = jax.ShapeDtypeStruct((levels, rows, cols), F32)
    ext_planes = pltpu.VMEM((levels, ext, 2 * LANES), F32)
    side_rows = 16 * packs

    def tiles(deep):
        return [pltpu.VMEM((n * deep, LANES), F32) for n in (slots, side_rows, 2 * WIDE)]

    kept = pltpu.VMEM((steps, hidden, TILES * LANES), F32)
    state_mid, state_new, grad_old, grad_now, terms = pl.pallas_call(
        main_kernel,
        out_shape=(field, field, field, field, jax.ShapeDtypeStruct((terms_rows, LANES), F32)),
        in_specs=[vmem] * 8,
        out_specs=(vmem,) * 5,
        scratch_shapes=[
            pltpu.VMEM((count, ext, 2 * LANES), F32),
            ext_planes,
            ext_planes,
            tiles(DEEP)[0],
            *tiles(DEEP),
            *tiles(SHALLOW),
            *tiles(SHALLOW),
            *tiles(DEEP),
            kept,
            kept,
            pltpu.VMEM((hidden, hidden), F32),
            pltpu.VMEM((DEEP, hidden), F32),
            pltpu.VMEM((DEEP, hidden), F32),
            pltpu.VMEM((DEEP, hidden), BF16),
            pltpu.VMEM((hidden, DEEP), BF16),
            pltpu.VMEM((hidden, hidden), BF16),
            pltpu.VMEM((hidden, DEEP), BF16),
            pltpu.VMEM((DEEP, hidden), BF16),
        ],
        compiler_params=pltpu.CompilerParams(vmem_limit_bytes=44 * 2**20),
    )(fields, left, right, low, high, w_in, w_mid, w_out.T)

    summed = summed_over(terms, "lat", "lon")
    cells_all = rows * lax.axis_size("lat") * cols * lax.axis_size("lon")
    grad_in, grad_mid, grad_out = pl.pallas_call(
        functools.partial(scale_kernel, GAIN_GRAD / cells_all**0.5),
        out_shape=(
            jax.ShapeDtypeStruct((width_in, hidden), F32),
            jax.ShapeDtypeStruct((hidden, hidden), F32),
            jax.ShapeDtypeStruct((levels, hidden), F32),
        ),
        in_specs=[vmem],
        out_specs=(vmem,) * 3,
        compiler_params=pltpu.CompilerParams(vmem_limit_bytes=8 * 2**20),
    )(summed)
    return state_mid, state_new, grad_old, grad_now, grad_in, grad_mid, grad_out.T


def solution(mesh):
    field = P("grp", "lat", "lon")
    whole = P("grp", None)
    in_specs = (field, field, field, P(("grp", "lat"), "lon"), P(), P(), P(), field, field)
    out_specs = (field, field, field, field, whole, whole, whole)
    return jax.shard_map(body, mesh=mesh, in_specs=in_specs, out_specs=out_specs, check_vma=False)
```

```python
import functools

import jax
import jax.numpy as jnp
from jax import lax
from jax.experimental import pallas as pl
from jax.experimental.pallas import tpu as pltpu
from jax.sharding import PartitionSpec as P

KAPPA = 0.2
DT = 0.1
GAIN_GRAD = 10.0

WIDE = 4
LANES = 128
TILES = 8
DEEP = 16
SHALLOW = 8

F32 = jnp.float32
BF16 = jnp.bfloat16


def dot(left, right):
    return lax.dot_general(left, right, (((1,), (0,)), ((), ())), preferred_element_type=F32)


def dot_nt(left, right):
    return lax.dot_general(left, right, (((1,), (1,)), ((), ())), preferred_element_type=F32)


def pack_kernel(fields, west, east, top, bottom):
    count, rows, cols = fields.shape
    lane = lax.broadcasted_iota(jnp.int32, (rows, LANES), 1)
    to_west = jnp.zeros((rows, LANES), F32)
    to_east = jnp.zeros((rows, LANES), F32)
    for p in range(count):
        plane = fields[p]
        here = (lane >= WIDE * p) & (lane < WIDE * (p + 1))
        to_west = jnp.where(here, pltpu.roll(plane, WIDE * p, 1) if p else plane, to_west)
        to_east = jnp.where(here, pltpu.roll(plane, WIDE * (p + 1), 1), to_east)
        top[p] = plane[:WIDE]
        bottom[p] = plane[rows - WIDE :]
    west[...] = to_west
    east[...] = to_east


def east_of(v):
    return pltpu.roll(v, v.shape[1] - 1, 1)


def west_of(v):
    return pltpu.roll(v, 1, 1)


def north_of(v):
    return pltpu.roll(v, v.shape[0] - 1, 0)


def south_of(v):
    return pltpu.roll(v, 1, 0)


def main_kernel(
    fields, left, right, low, high, w_in, w_mid, w_out_t,
    o_mid, o_new, o_old, o_now, o_grad,
    planes, mids, olds, ft1, ft2, fth, ftx, cl, clh, clx, dc, dch, dcx, df, dfh, dfx,
    keep1, keep2, acc_mid, acc_in, acc_out, wi, wi_t, wm_t, wo, wo_t,
):
    levels, rows, cols = o_mid.shape
    width_in, hidden = w_in.shape
    count = 5 * levels + 1
    ext = rows + 2 * WIDE
    chunks = rows // TILES
    packs = -(-ext // 16)
    order = [rows, ext - 1] + [None] * packs + [rows + 1, ext - 2, rows + 2, ext - 3]
    first_pack = rows + 2
    halo_one = 2 + packs
    halo_two = halo_one + 2

    spare = jnp.zeros((DEEP - width_in, hidden), F32)
    wide_in = jnp.concatenate([w_in[...].astype(F32), spare], 0)
    wi[...] = wide_in.astype(BF16)
    wi_t[...] = wide_in.T.astype(BF16)
    wm_t[...] = w_mid[...].astype(F32).T.astype(BF16)
    spare = jnp.zeros((DEEP - levels, hidden), F32)
    wide_out = jnp.concatenate([w_out_t[...].astype(F32), spare], 0)
    wo_t[...] = wide_out.astype(BF16)
    wo[...] = wide_out.T.astype(BF16)

    lane = lax.broadcasted_iota(jnp.int32, (ext, LANES), 1)
    left_all = jnp.concatenate([left[...], high[count], low[count]], 0)
    right_all = jnp.concatenate([right[...], high[count + 1], low[count + 1]], 0)

    for p in range(count):
        from_right = pltpu.roll(right_all, LANES - WIDE * p, 1) if p else right_all
        from_left = pltpu.roll(left_all, LANES - WIDE * (p + 1), 1)
        side = jnp.where(lane < WIDE, from_right, jnp.where(lane >= LANES - WIDE, from_left, 0.0))
        planes[p, :, pl.ds(0, LANES)] = jnp.concatenate([fields[p], high[p], low[p]], 0)
        planes[p, :, pl.ds(LANES, LANES)] = side

    for ref in (ft1, ft2, fth, ftx, dc, dch, dcx, acc_mid, acc_in, acc_out):
        ref[...] = jnp.zeros_like(ref)

    def spread(plane, index, deep, main, extra, side):
        main[pl.ds(index, rows, stride=deep), :] = plane[:rows, :LANES]
        extra[pl.ds(index, 2 * WIDE, stride=deep), :] = plane[rows:, :LANES]
        side[pl.ds(index, ext, stride=deep), :] = plane[:, LANES:]

    def gathered(index, deep, main, extra, side):
        body = jnp.concatenate(
            [main[pl.ds(index, rows, stride=deep), :], extra[pl.ds(index, 2 * WIDE, stride=deep), :]], 0
        )
        return jnp.concatenate([body, side[pl.ds(index, ext, stride=deep), :]], 1)

    def pack_halo(deep, main, extra, side):
        where = lax.broadcasted_iota(jnp.int32, (deep, LANES), 1)
        for i, r in enumerate(order):
            if r is not None:
                main[pl.ds((rows + i) * deep, deep), :] = extra[pl.ds((r - rows) * deep, deep), :]

        for q in range(packs):
            total = jnp.zeros((deep, LANES), F32)
            for j in range(min(16, ext - 16 * q)):
                moved = pltpu.roll(side[pl.ds((16 * q + j) * deep, deep), :], (2 * WIDE * j + WIDE) % LANES, 1)
                total = jnp.where((where >= 2 * WIDE * j) & (where < 2 * WIDE * (j + 1)), moved, total)
            main[pl.ds((first_pack + q) * deep, deep), :] = total

    def unpack_halo(deep, main, extra, side, live):
        for i, r in enumerate(order[:live]):
            if r is not None:
                extra[pl.ds((r - rows) * deep, deep), :] = main[pl.ds((rows + i) * deep, deep), :]

        for q in range(packs):
            tile = main[pl.ds((first_pack + q) * deep, deep), :]
            for j in range(min(16, ext - 16 * q)):
                moved = pltpu.roll(tile, LANES - (2 * WIDE * j + WIDE) % LANES, 1)
                side[pl.ds((16 * q + j) * deep, deep), :] = moved

    def lanes_of(ref, deep, base, tiles):
        block = ref[pl.ds(base * deep, tiles * deep), :]
        return jnp.concatenate([block[k * deep : (k + 1) * deep] for k in range(tiles)], 1)

    def put_lanes(ref, deep, base, tiles, value):
        for k in range(tiles):
            ref[pl.ds((base + k) * deep, deep), :] = value[:, k * LANES : (k + 1) * LANES]

    def inputs_at(ref, base, tiles):
        return lanes_of(ref, DEEP, base, tiles).astype(BF16)

    def cotangents_at(base, tiles):
        part = lanes_of(dc, SHALLOW, base, tiles)
        return jnp.concatenate([part, jnp.zeros_like(part)], 0).astype(BF16)

    def forward(x):
        first = jnp.tanh(dot(wi_t[...], x))
        second = jnp.tanh(dot(wm_t[...], first.astype(BF16)))
        return first, second

    def closure(second):
        return dot(wo_t[...], second.astype(BF16)).astype(BF16).astype(F32)[:SHALLOW]

    def backward(first, second, cot):
        dz_two = (dot(wo[...], cot) * (1.0 - second * second)).astype(BF16)
        dz_one = (dot(w_mid[...], dz_two) * (1.0 - first * first)).astype(BF16)
        dfeat = dot(wi[...], dz_one).astype(BF16).astype(F32)
        return dz_one, dz_two, dfeat

    def add_terms(x, first, second, cot, dz_one, dz_two):
        acc_mid[...] += dot_nt(first.astype(BF16), dz_two)
        acc_in[...] += dot_nt(x, dz_one)
        acc_out[...] += dot_nt(cot, second.astype(BF16))

    def features_of(source, ft):
        for level in range(levels):
            v = source[level]
            spread(v, level, DEEP, ft, ftx, fth)
            spread(0.5 * (east_of(v) - west_of(v)), levels + level, DEEP, ft, ftx, fth)
            spread(0.5 * (north_of(v) - south_of(v)), 2 * levels + level, DEEP, ft, ftx, fth)

        pack_halo(DEEP, ft, ftx, fth)

    def cotangents_of(source, offset):
        for level in range(levels):
            spread(planes[count - 1] * (2.0 * DT * source[offset + level]), level, SHALLOW, dc, dcx, dch)

        pack_halo(SHALLOW, dc, dcx, dch)

    def force(v, level, closed):
        eastward, westward, northward, southward = east_of(v), west_of(v), north_of(v), south_of(v)
        laplace = eastward + westward + northward + southward - 4.0 * v
        slope = 0.5 * (eastward - westward)
        return planes[count - 1] * (KAPPA * laplace - planes[2 * levels + level] * slope + closed)

    features_of(planes, ft1)

    def first_step(c, carry):
        base = pl.multiple_of(c * TILES, TILES)
        first, second = forward(inputs_at(ft1, base, TILES))
        keep1[c] = first
        keep2[c] = second
        put_lanes(cl, SHALLOW, base, TILES, closure(second))
        return carry

    lax.fori_loop(0, keep1.shape[0], first_step, 0)
    unpack_halo(SHALLOW, cl, clx, clh, len(order))

    for level in range(levels):
        closed = gathered(level, SHALLOW, cl, clx, clh)
        mid = planes[levels + level] + 2.0 * DT * force(planes[level], level, closed)
        o_mid[level] = mid[:rows, :LANES]
        mids[level] = mid

    features_of(mids, ft2)
    cotangents_of(planes, 3 * levels)

    def second_step(c, carry):
        base = pl.multiple_of(c * TILES, TILES)
        x = inputs_at(ft2, base, TILES)
        cot = cotangents_at(base, TILES)
        first, second = forward(x)
        put_lanes(cl, SHALLOW, base, TILES, closure(second))
        dz_one, dz_two, dfeat = backward(first, second, cot)
        put_lanes(df, DEEP, base, TILES, dfeat)
        add_terms(x, first, second, cot, dz_one, dz_two)
        return carry

    lax.fori_loop(0, chunks, second_step, 0)
    first, second = forward(inputs_at(ft2, rows, halo_two))
    unused_one, unused_two, dfeat = backward(first, second, cotangents_at(rows, halo_two))
    put_lanes(df, DEEP, rows, halo_two, dfeat)
    unpack_halo(DEEP, df, dfx, dfh, halo_two)

    def adjoint_of(weighted, level):
        masked = planes[count - 1] * weighted
        carried = planes[2 * levels + level] * masked
        a0 = gathered(level, DEEP, df, dfx, dfh)
        a1 = gathered(levels + level, DEEP, df, dfx, dfh)
        a2 = gathered(2 * levels + level, DEEP, df, dfx, dfh)
        result = KAPPA * (east_of(masked) + west_of(masked) + north_of(masked) + south_of(masked) - 4.0 * masked)
        result = result + 0.5 * (east_of(carried) - west_of(carried)) + a0
        return result - 0.5 * (east_of(a1) - west_of(a1)) - 0.5 * (north_of(a2) - south_of(a2))

    for level in range(levels):
        closed = jnp.concatenate([cl[pl.ds(level, rows, stride=SHALLOW), :], jnp.zeros((2 * WIDE, LANES), F32)], 0)
        closed = jnp.concatenate([closed, jnp.zeros_like(closed)], 1)
        new = planes[level] + 2.0 * DT * force(mids[level], level, closed)
        o_new[level] = new[:rows, :LANES]
        grad = planes[4 * levels + level] + adjoint_of(2.0 * DT * planes[3 * levels + level], level)
        o_old[level] = grad[:rows, :LANES]
        olds[level] = grad

    cotangents_of(olds, 0)

    def third_step(c, carry):
        base = pl.multiple_of(c * TILES, TILES)
        x = inputs_at(ft1, base, TILES)
        cot = cotangents_at(base, TILES)
        first = keep1[c]
        second = keep2[c]
        dz_one, dz_two, dfeat = backward(first, second, cot)
        put_lanes(df, DEEP, base, TILES, dfeat)
        add_terms(x, first, second, cot, dz_one, dz_two)
        return carry

    lax.fori_loop(0, chunks, third_step, 0)
    near = halo_one * LANES
    unused_one, unused_two, dfeat = backward(
        keep1[chunks, :, pl.ds(0, near)], keep2[chunks, :, pl.ds(0, near)], cotangents_at(rows, halo_one)
    )
    put_lanes(df, DEEP, rows, halo_one, dfeat)
    unpack_halo(DEEP, df, dfx, dfh, halo_one)

    for level in range(levels):
        grad = adjoint_of(2.0 * DT * olds[level], level)
        o_now[level] = planes[3 * levels + level, pl.ds(0, rows), pl.ds(0, LANES)] + grad[:rows, :LANES]

    start = 0
    for acc in (acc_mid, acc_in, acc_out):
        deep = acc.shape[0]
        for half in range(hidden // LANES):
            o_grad[pl.ds(start, deep), :] = acc[:, half * LANES : (half + 1) * LANES]
            start += deep
    if start < o_grad.shape[0]:
        o_grad[pl.ds(start, o_grad.shape[0] - start), :] = jnp.zeros((o_grad.shape[0] - start, LANES), F32)


def scale_kernel(factor, terms, g_in, g_mid, g_out):
    hidden = g_mid.shape[0]
    start = 0
    for ref, deep in ((g_mid, hidden), (g_in, DEEP), (g_out, DEEP)):
        keep = ref.shape[0]
        for half in range(hidden // LANES):
            ref[:, half * LANES : (half + 1) * LANES] = terms[pl.ds(start, keep), :] * factor
            start += deep


def along(value, axis, step, periodic):
    count = lax.axis_size(axis)
    pairs = [(i, (i + step) % count) for i in range(count) if periodic or 0 <= i + step < count]
    return lax.ppermute(value, axis, pairs)


def swapped(value, axis, bit):
    return lax.ppermute(value, axis, [(i, i ^ bit) for i in range(lax.axis_size(axis))])


def summed_over(value, halving, doubling):
    bits = []
    bit = 1
    while bit < lax.axis_size(halving):
        upper = (lax.axis_index(halving) & bit) != 0
        half = value.shape[0] // 2
        lower_part, upper_part = value[:half], value[half:]
        sent = jnp.where(upper, lower_part, upper_part)
        value = jnp.where(upper, upper_part, lower_part) + swapped(sent, halving, bit)
        bits.append((bit, upper))
        bit *= 2
    bit = 1
    while bit < lax.axis_size(doubling):
        value = value + swapped(value, doubling, bit)
        bit *= 2
    for bit, upper in reversed(bits):
        other = swapped(value, halving, bit)
        value = jnp.concatenate([jnp.where(upper, other, value), jnp.where(upper, value, other)], 0)
    return value


def body(state_old, state_now, drift, ocean, w_in, w_mid, w_out, cot_mid, cot_new):
    levels, rows, cols = state_now.shape
    width_in, hidden = w_in.shape
    ext = rows + 2 * WIDE
    count = 5 * levels + 1
    packs = -(-ext // 16)
    steps = -(-(rows + 6 + packs) // TILES)
    slots = steps * TILES
    vmem = pl.BlockSpec(memory_space=pltpu.VMEM)
    strip = jax.ShapeDtypeStruct((rows, LANES), F32)
    edge = jax.ShapeDtypeStruct((count, WIDE, LANES), F32)
    wet = ocean.astype(F32)[None]
    fields = jnp.concatenate([state_now, state_old, drift, cot_new, cot_mid, wet], 0)
    west, east, top, bottom = pl.pallas_call(
        pack_kernel,
        out_shape=(strip, strip, edge, edge),
        in_specs=[vmem],
        out_specs=(vmem,) * 4,
        compiler_params=pltpu.CompilerParams(vmem_limit_bytes=8 * 2**20),
    )(fields)
    left = along(east, "lon", 1, True)
    right = along(west, "lon", -1, True)
    up = jnp.concatenate([bottom, left[None, rows - WIDE :], right[None, rows - WIDE :]], 0)
    down = jnp.concatenate([top, left[None, :WIDE], right[None, :WIDE]], 0)
    low = along(up, "lat", 1, False)
    high = along(down, "lat", -1, False)

    halves = hidden // LANES
    grain = 8 * lax.axis_size("lat")
    terms_rows = -(-halves * (hidden + 2 * DEEP) // grain) * grain
    field = jax.ShapeDtypeStruct((levels, rows, cols), F32)
    ext_planes = pltpu.VMEM((levels, ext, 2 * LANES), F32)
    side_rows = 16 * packs

    def tiles(deep):
        return [pltpu.VMEM((n * deep, LANES), F32) for n in (slots, side_rows, 2 * WIDE)]

    kept = pltpu.VMEM((steps, hidden, TILES * LANES), F32)
    state_mid, state_new, grad_old, grad_now, terms = pl.pallas_call(
        main_kernel,
        out_shape=(field, field, field, field, jax.ShapeDtypeStruct((terms_rows, LANES), F32)),
        in_specs=[vmem] * 8,
        out_specs=(vmem,) * 5,
        scratch_shapes=[
            pltpu.VMEM((count, ext, 2 * LANES), F32),
            ext_planes,
            ext_planes,
            tiles(DEEP)[0],
            *tiles(DEEP),
            *tiles(SHALLOW),
            *tiles(SHALLOW),
            *tiles(DEEP),
            kept,
            kept,
            pltpu.VMEM((hidden, hidden), F32),
            pltpu.VMEM((DEEP, hidden), F32),
            pltpu.VMEM((DEEP, hidden), F32),
            pltpu.VMEM((DEEP, hidden), BF16),
            pltpu.VMEM((hidden, DEEP), BF16),
            pltpu.VMEM((hidden, hidden), BF16),
            pltpu.VMEM((hidden, DEEP), BF16),
            pltpu.VMEM((DEEP, hidden), BF16),
        ],
        compiler_params=pltpu.CompilerParams(vmem_limit_bytes=44 * 2**20),
    )(fields, left, right, low, high, w_in, w_mid, w_out.T)

    summed = summed_over(terms, "lat", "lon")
    cells_all = rows * lax.axis_size("lat") * cols * lax.axis_size("lon")
    grad_in, grad_mid, grad_out = pl.pallas_call(
        functools.partial(scale_kernel, GAIN_GRAD / cells_all**0.5),
        out_shape=(
            jax.ShapeDtypeStruct((width_in, hidden), F32),
            jax.ShapeDtypeStruct((hidden, hidden), F32),
            jax.ShapeDtypeStruct((levels, hidden), F32),
        ),
        in_specs=[vmem],
        out_specs=(vmem,) * 3,
        compiler_params=pltpu.CompilerParams(vmem_limit_bytes=8 * 2**20),
    )(summed)
    return state_mid, state_new, grad_old, grad_now, grad_in, grad_mid, grad_out.T


def solution(mesh):
    field = P("grp", "lat", "lon")
    whole = P("grp", None)
    in_specs = (field, field, field, P(("grp", "lat"), "lon"), P(), P(), P(), field, field)
    out_specs = (field, field, field, field, whole, whole, whole)
    return jax.shard_map(body, mesh=mesh, in_specs=in_specs, out_specs=out_specs, check_vma=False)
```

```python
import functools

import jax
import jax.numpy as jnp
from jax import lax
from jax.experimental import pallas as pl
from jax.experimental.pallas import tpu as pltpu
from jax.sharding import PartitionSpec as P

KAPPA = 0.2
DT = 0.1
GAIN_GRAD = 10.0

WIDE = 4
LANES = 128
TILES = 8
PART = 2
DEEP = 16
SHALLOW = 8

F32 = jnp.float32
BF16 = jnp.bfloat16


def dot(left, right):
    return lax.dot_general(left, right, (((1,), (0,)), ((), ())), preferred_element_type=F32)


def dot_nt(left, right):
    return lax.dot_general(left, right, (((1,), (1,)), ((), ())), preferred_element_type=F32)


def pack_kernel(now, old, drift, cnew, cmid, ocean, west, east, top, bottom, fields, wet, sems):
    levels, rows, cols = now.shape
    copies = [
        pltpu.make_async_copy(ref, fields.at[pl.ds(levels * f, levels)], sems.at[f])
        for f, ref in enumerate((now, old, drift, cnew, cmid))
    ]
    copies.append(pltpu.make_async_copy(ocean, wet, sems.at[5]))
    for copy in copies:
        copy.start()
    lane = lax.broadcasted_iota(jnp.int32, (rows, LANES), 1)
    to_west = jnp.zeros((rows, LANES), F32)
    to_east = jnp.zeros((rows, LANES), F32)
    count = fields.shape[0]
    for p in range(count):
        if p % levels == 0:
            copies[p // levels].wait()
        if p == count - 1:
            fields[p] = wet[...].astype(F32)
        plane = fields[p]
        here = (lane >= WIDE * p) & (lane < WIDE * (p + 1))
        to_west = jnp.where(here, pltpu.roll(plane, WIDE * p, 1) if p else plane, to_west)
        to_east = jnp.where(here, pltpu.roll(plane, WIDE * (p + 1), 1), to_east)
        top[p] = plane[:WIDE]
        bottom[p] = plane[rows - WIDE :]
    west[...] = to_west
    east[...] = to_east


def east_of(v):
    return pltpu.roll(v, v.shape[1] - 1, 1)


def west_of(v):
    return pltpu.roll(v, 1, 1)


def north_of(v):
    return pltpu.roll(v, v.shape[0] - 1, 0)


def south_of(v):
    return pltpu.roll(v, 1, 0)


def main_kernel(
    fields, left, right, low, high, w_in, w_mid, w_out_t,
    o_mid, o_new, o_old, o_now, o_grad,
    planes, mids, olds, ft1, ft2, fth, ftx, cl, clh, clx, dc, dch, dcx, df, dfh, dfx,
    keep1, keep2, acc_mid, acc_in, acc_out, wi, wi_t, wm_t, wo, wo_t,
):
    levels, rows, cols = o_mid.shape
    width_in, hidden = w_in.shape
    count = 5 * levels + 1
    ext = rows + 2 * WIDE
    chunks = rows // TILES
    packs = -(-ext // 16)
    order = [rows, ext - 1] + [None] * packs + [rows + 1, ext - 2, rows + 2, ext - 3]
    first_pack = rows + 2
    halo_one = 2 + packs
    halo_two = halo_one + 2

    spare = jnp.zeros((DEEP - width_in, hidden), F32)
    wide_in = jnp.concatenate([w_in[...].astype(F32), spare], 0)
    wi[...] = wide_in.astype(BF16)
    wi_t[...] = wide_in.T.astype(BF16)
    wm_t[...] = w_mid[...].astype(F32).T.astype(BF16)
    spare = jnp.zeros((DEEP - levels, hidden), F32)
    wide_out = jnp.concatenate([w_out_t[...].astype(F32), spare], 0)
    wo_t[...] = wide_out.astype(BF16)
    wo[...] = wide_out.T.astype(BF16)

    lane = lax.broadcasted_iota(jnp.int32, (ext, LANES), 1)
    left_all = jnp.concatenate([left[...], high[count], low[count]], 0)
    right_all = jnp.concatenate([right[...], high[count + 1], low[count + 1]], 0)

    for p in range(count):
        from_right = pltpu.roll(right_all, LANES - WIDE * p, 1) if p else right_all
        from_left = pltpu.roll(left_all, LANES - WIDE * (p + 1), 1)
        side = jnp.where(lane < WIDE, from_right, jnp.where(lane >= LANES - WIDE, from_left, 0.0))
        planes[p, :, pl.ds(0, LANES)] = jnp.concatenate([fields[p], high[p], low[p]], 0)
        planes[p, :, pl.ds(LANES, LANES)] = side

    for ref in (ft1, ft2, fth, ftx, dc, dch, dcx, acc_mid, acc_in, acc_out):
        ref[...] = jnp.zeros_like(ref)

    def spread(plane, index, deep, main, extra, side):
        main[pl.ds(index, rows, stride=deep), :] = plane[:rows, :LANES]
        extra[pl.ds(index, 2 * WIDE, stride=deep), :] = plane[rows:, :LANES]
        side[pl.ds(index, ext, stride=deep), :] = plane[:, LANES:]

    def gathered(index, deep, main, extra, side):
        body = jnp.concatenate(
            [main[pl.ds(index, rows, stride=deep), :], extra[pl.ds(index, 2 * WIDE, stride=deep), :]], 0
        )
        return jnp.concatenate([body, side[pl.ds(index, ext, stride=deep), :]], 1)

    def pack_halo(deep, main, extra, side):
        where = lax.broadcasted_iota(jnp.int32, (deep, LANES), 1)
        for i, r in enumerate(order):
            if r is not None:
                main[pl.ds((rows + i) * deep, deep), :] = extra[pl.ds((r - rows) * deep, deep), :]

        for q in range(packs):
            total = jnp.zeros((deep, LANES), F32)
            for j in range(min(16, ext - 16 * q)):
                moved = pltpu.roll(side[pl.ds((16 * q + j) * deep, deep), :], (2 * WIDE * j + WIDE) % LANES, 1)
                total = jnp.where((where >= 2 * WIDE * j) & (where < 2 * WIDE * (j + 1)), moved, total)
            main[pl.ds((first_pack + q) * deep, deep), :] = total

    def unpack_halo(deep, main, extra, side, live):
        for i, r in enumerate(order[:live]):
            if r is not None:
                extra[pl.ds((r - rows) * deep, deep), :] = main[pl.ds((rows + i) * deep, deep), :]

        for q in range(packs):
            tile = main[pl.ds((first_pack + q) * deep, deep), :]
            for j in range(min(16, ext - 16 * q)):
                moved = pltpu.roll(tile, LANES - (2 * WIDE * j + WIDE) % LANES, 1)
                side[pl.ds((16 * q + j) * deep, deep), :] = moved

    def lanes_of(ref, deep, base, tiles):
        block = ref[pl.ds(base * deep, tiles * deep), :]
        return jnp.concatenate([block[k * deep : (k + 1) * deep] for k in range(tiles)], 1)

    def put_lanes(ref, deep, base, tiles, value):
        for k in range(tiles):
            ref[pl.ds((base + k) * deep, deep), :] = value[:, k * LANES : (k + 1) * LANES]

    def inputs_at(ref, base, tiles):
        return lanes_of(ref, DEEP, base, tiles).astype(BF16)

    def cotangents_at(base, tiles):
        part = lanes_of(dc, SHALLOW, base, tiles)
        return jnp.concatenate([part, jnp.zeros_like(part)], 0).astype(BF16)

    def forward(x):
        first = jnp.tanh(dot(wi_t[...], x))
        second = jnp.tanh(dot(wm_t[...], first.astype(BF16)))
        return first, second

    def closure(second):
        return dot(wo_t[...], second.astype(BF16)).astype(BF16).astype(F32)[:SHALLOW]

    def backward(first, second, cot):
        dz_two = (dot(wo[...], cot) * (1.0 - second * second)).astype(BF16)
        dz_one = (dot(w_mid[...], dz_two) * (1.0 - first * first)).astype(BF16)
        dfeat = dot(wi[...], dz_one).astype(BF16).astype(F32)
        return dz_one, dz_two, dfeat

    def add_terms(x, first, second, cot, dz_one, dz_two):
        acc_mid[...] += dot_nt(first, dz_two)
        acc_in[...] += dot_nt(x, dz_one)
        acc_out[...] += dot_nt(cot, second)

    def features_of(source, ft):
        for level in range(levels):
            v = source[level]
            spread(v, level, DEEP, ft, ftx, fth)
            spread(0.5 * (east_of(v) - west_of(v)), levels + level, DEEP, ft, ftx, fth)
            spread(0.5 * (north_of(v) - south_of(v)), 2 * levels + level, DEEP, ft, ftx, fth)

        pack_halo(DEEP, ft, ftx, fth)

    def cotangents_of(source, offset):
        for level in range(levels):
            spread(planes[count - 1] * (2.0 * DT * source[offset + level]), level, SHALLOW, dc, dcx, dch)

        pack_halo(SHALLOW, dc, dcx, dch)

    def force(v, level, closed):
        eastward, westward, northward, southward = east_of(v), west_of(v), north_of(v), south_of(v)
        laplace = eastward + westward + northward + southward - 4.0 * v
        slope = 0.5 * (eastward - westward)
        return planes[count - 1] * (KAPPA * laplace - planes[2 * levels + level] * slope + closed)

    features_of(planes, ft1)

    def first_step(c, carry):
        for k in range(0, TILES, PART):
            base = pl.multiple_of(c * TILES + k, PART)
            first, second = forward(inputs_at(ft1, base, PART))
            keep1[c, :, pl.ds(k * LANES, PART * LANES)] = first
            keep2[c, :, pl.ds(k * LANES, PART * LANES)] = second
            put_lanes(cl, SHALLOW, base, PART, closure(second))
        return carry

    lax.fori_loop(0, keep1.shape[0], first_step, 0)
    unpack_halo(SHALLOW, cl, clx, clh, len(order))

    for level in range(levels):
        closed = gathered(level, SHALLOW, cl, clx, clh)
        mid = planes[levels + level] + 2.0 * DT * force(planes[level], level, closed)
        o_mid[level] = mid[:rows, :LANES]
        mids[level] = mid

    features_of(mids, ft2)
    cotangents_of(planes, 3 * levels)

    def second_step(c, carry):
        parts = []
        for k in range(0, TILES, PART):
            base = pl.multiple_of(c * TILES + k, PART)
            x = inputs_at(ft2, base, PART)
            cot = cotangents_at(base, PART)
            first, second = forward(x)
            put_lanes(cl, SHALLOW, base, PART, closure(second))
            dz_one, dz_two, dfeat = backward(first, second, cot)
            put_lanes(df, DEEP, base, PART, dfeat)
            parts.append((x, first.astype(BF16), second.astype(BF16), cot, dz_one, dz_two))
        add_terms(*(jnp.concatenate(part, 1) for part in zip(*parts)))
        return carry

    lax.fori_loop(0, chunks, second_step, 0)
    first, second = forward(inputs_at(ft2, rows, halo_two))
    unused_one, unused_two, dfeat = backward(first, second, cotangents_at(rows, halo_two))
    put_lanes(df, DEEP, rows, halo_two, dfeat)
    unpack_halo(DEEP, df, dfx, dfh, halo_two)

    def adjoint_of(weighted, level):
        masked = planes[count - 1] * weighted
        carried = planes[2 * levels + level] * masked
        a0 = gathered(level, DEEP, df, dfx, dfh)
        a1 = gathered(levels + level, DEEP, df, dfx, dfh)
        a2 = gathered(2 * levels + level, DEEP, df, dfx, dfh)
        result = KAPPA * (east_of(masked) + west_of(masked) + north_of(masked) + south_of(masked) - 4.0 * masked)
        result = result + 0.5 * (east_of(carried) - west_of(carried)) + a0
        return result - 0.5 * (east_of(a1) - west_of(a1)) - 0.5 * (north_of(a2) - south_of(a2))

    for level in range(levels):
        closed = jnp.concatenate([cl[pl.ds(level, rows, stride=SHALLOW), :], jnp.zeros((2 * WIDE, LANES), F32)], 0)
        closed = jnp.concatenate([closed, jnp.zeros_like(closed)], 1)
        new = planes[level] + 2.0 * DT * force(mids[level], level, closed)
        o_new[level] = new[:rows, :LANES]
        grad = planes[4 * levels + level] + adjoint_of(2.0 * DT * planes[3 * levels + level], level)
        o_old[level] = grad[:rows, :LANES]
        olds[level] = grad

    cotangents_of(olds, 0)

    def third_step(c, carry):
        parts = []
        for k in range(0, TILES, PART):
            base = pl.multiple_of(c * TILES + k, PART)
            x = inputs_at(ft1, base, PART)
            cot = cotangents_at(base, PART)
            first = keep1[c, :, pl.ds(k * LANES, PART * LANES)]
            second = keep2[c, :, pl.ds(k * LANES, PART * LANES)]
            dz_one, dz_two, dfeat = backward(first, second, cot)
            put_lanes(df, DEEP, base, PART, dfeat)
            parts.append((x, first.astype(BF16), second.astype(BF16), cot, dz_one, dz_two))
        add_terms(*(jnp.concatenate(part, 1) for part in zip(*parts)))
        return carry

    lax.fori_loop(0, chunks, third_step, 0)
    near = halo_one * LANES
    unused_one, unused_two, dfeat = backward(
        keep1[chunks, :, pl.ds(0, near)], keep2[chunks, :, pl.ds(0, near)], cotangents_at(rows, halo_one)
    )
    put_lanes(df, DEEP, rows, halo_one, dfeat)
    unpack_halo(DEEP, df, dfx, dfh, halo_one)

    for level in range(levels):
        grad = adjoint_of(2.0 * DT * olds[level], level)
        o_now[level] = planes[3 * levels + level, pl.ds(0, rows), pl.ds(0, LANES)] + grad[:rows, :LANES]

    start = 0
    for acc in (acc_mid, acc_in, acc_out):
        deep = acc.shape[0]
        for half in range(hidden // LANES):
            o_grad[pl.ds(start, deep), :] = acc[:, half * LANES : (half + 1) * LANES]
            start += deep
    if start < o_grad.shape[0]:
        o_grad[pl.ds(start, o_grad.shape[0] - start), :] = jnp.zeros((o_grad.shape[0] - start, LANES), F32)


def scale_kernel(factor, terms, g_in, g_mid, g_out):
    hidden = g_mid.shape[0]
    start = 0
    for ref, deep in ((g_mid, hidden), (g_in, DEEP), (g_out, DEEP)):
        keep = ref.shape[0]
        for half in range(hidden // LANES):
            ref[:, half * LANES : (half + 1) * LANES] = terms[pl.ds(start, keep), :] * factor
            start += deep


def along(value, axis, step, periodic):
    count = lax.axis_size(axis)
    pairs = [(i, (i + step) % count) for i in range(count) if periodic or 0 <= i + step < count]
    return lax.ppermute(value, axis, pairs)


def swapped(value, axis, bit):
    return lax.ppermute(value, axis, [(i, i ^ bit) for i in range(lax.axis_size(axis))])


def summed_over(value, halving, doubling):
    members = lax.axis_size(halving)
    piece = value.shape[0] // members
    value = lax.all_to_all(value.reshape(members, piece, LANES), halving, 0, 0)
    value = jnp.sum(value, 0)
    bit = 1
    while bit < lax.axis_size(doubling):
        value = value + swapped(value, doubling, bit)
        bit *= 2
    value = jnp.broadcast_to(value[None], (members, piece, LANES))
    return lax.all_to_all(value, halving, 0, 0).reshape(members * piece, LANES)


def body(state_old, state_now, drift, ocean, w_in, w_mid, w_out, cot_mid, cot_new):
    levels, rows, cols = state_now.shape
    width_in, hidden = w_in.shape
    ext = rows + 2 * WIDE
    count = 5 * levels + 1
    packs = -(-ext // 16)
    steps = -(-(rows + 6 + packs) // TILES)
    slots = steps * TILES
    vmem = pl.BlockSpec(memory_space=pltpu.VMEM)
    strip = jax.ShapeDtypeStruct((rows, LANES), F32)
    edge = jax.ShapeDtypeStruct((count, WIDE, LANES), F32)
    place = pl.BlockSpec(memory_space=pltpu.HBM)
    arrays = (state_now, state_old, drift, cot_new, cot_mid, ocean)
    arrays = tuple(pltpu.with_memory_space_constraint(a, pltpu.HBM) for a in arrays)
    west, east, top, bottom, fields = pl.pallas_call(
        pack_kernel,
        out_shape=(strip, strip, edge, edge, jax.ShapeDtypeStruct((count, rows, cols), F32)),
        in_specs=[place] * 6,
        out_specs=(vmem,) * 5,
        scratch_shapes=[pltpu.VMEM((rows, cols), jnp.int32), pltpu.SemaphoreType.DMA((6,))],
        compiler_params=pltpu.CompilerParams(vmem_limit_bytes=8 * 2**20),
    )(*arrays)
    left = along(east, "lon", 1, True)
    right = along(west, "lon", -1, True)
    up = jnp.concatenate([bottom, left[None, rows - WIDE :], right[None, rows - WIDE :]], 0)
    down = jnp.concatenate([top, left[None, :WIDE], right[None, :WIDE]], 0)
    low = along(up, "lat", 1, False)
    high = along(down, "lat", -1, False)

    halves = hidden // LANES
    grain = 8 * lax.axis_size("lat")
    terms_rows = -(-halves * (hidden + 2 * DEEP) // grain) * grain
    field = jax.ShapeDtypeStruct((levels, rows, cols), F32)
    ext_planes = pltpu.VMEM((levels, ext, 2 * LANES), F32)
    side_rows = 16 * packs

    def tiles(deep):
        return [pltpu.VMEM((n * deep, LANES), F32) for n in (slots, side_rows, 2 * WIDE)]

    kept = pltpu.VMEM((steps, hidden, TILES * LANES), F32)
    state_mid, state_new, grad_old, grad_now, terms = pl.pallas_call(
        main_kernel,
        out_shape=(field, field, field, field, jax.ShapeDtypeStruct((terms_rows, LANES), F32)),
        in_specs=[vmem] * 8,
        out_specs=(vmem,) * 5,
        scratch_shapes=[
            pltpu.VMEM((count, ext, 2 * LANES), F32),
            ext_planes,
            ext_planes,
            tiles(DEEP)[0],
            *tiles(DEEP),
            *tiles(SHALLOW),
            *tiles(SHALLOW),
            *tiles(DEEP),
            kept,
            kept,
            pltpu.VMEM((hidden, hidden), F32),
            pltpu.VMEM((DEEP, hidden), F32),
            pltpu.VMEM((DEEP, hidden), F32),
            pltpu.VMEM((DEEP, hidden), BF16),
            pltpu.VMEM((hidden, DEEP), BF16),
            pltpu.VMEM((hidden, hidden), BF16),
            pltpu.VMEM((hidden, DEEP), BF16),
            pltpu.VMEM((DEEP, hidden), BF16),
        ],
        compiler_params=pltpu.CompilerParams(vmem_limit_bytes=44 * 2**20),
    )(fields, left, right, low, high, w_in, w_mid, w_out.T)

    summed = summed_over(terms, "lat", "lon")
    cells_all = rows * lax.axis_size("lat") * cols * lax.axis_size("lon")
    grad_in, grad_mid, grad_out = pl.pallas_call(
        functools.partial(scale_kernel, GAIN_GRAD / cells_all**0.5),
        out_shape=(
            jax.ShapeDtypeStruct((width_in, hidden), F32),
            jax.ShapeDtypeStruct((hidden, hidden), F32),
            jax.ShapeDtypeStruct((levels, hidden), F32),
        ),
        in_specs=[vmem],
        out_specs=(vmem,) * 3,
        compiler_params=pltpu.CompilerParams(vmem_limit_bytes=8 * 2**20),
    )(summed)
    return state_mid, state_new, grad_old, grad_now, grad_in, grad_mid, grad_out.T


def solution(mesh):
    field = P("grp", "lat", "lon")
    whole = P("grp", None)
    in_specs = (field, field, field, P(("grp", "lat"), "lon"), P(), P(), P(), field, field)
    out_specs = (field, field, field, field, whole, whole, whole)
    return jax.shard_map(body, mesh=mesh, in_specs=in_specs, out_specs=out_specs, check_vma=False)
```

```python
import functools

import jax
import jax.numpy as jnp
from jax import lax
from jax.experimental import pallas as pl
from jax.experimental.pallas import tpu as pltpu
from jax.sharding import PartitionSpec as P

KAPPA = 0.2
DT = 0.1
GAIN_GRAD = 10.0

WIDE = 4
LANES = 128
TILES = 16
PART = 16
DEEP = 16
SHALLOW = 8

F32 = jnp.float32
BF16 = jnp.bfloat16


def dot(left, right):
    return lax.dot_general(left, right, (((1,), (0,)), ((), ())), preferred_element_type=F32)


def dot_nt(left, right):
    return lax.dot_general(left, right, (((1,), (1,)), ((), ())), preferred_element_type=F32)


def pack_kernel(now, old, drift, cnew, cmid, ocean, west, east, top, bottom, fields, wet, sems):
    levels, rows, cols = now.shape
    copies = [
        pltpu.make_async_copy(ref, fields.at[pl.ds(levels * f, levels)], sems.at[f])
        for f, ref in enumerate((now, old, drift, cnew, cmid))
    ]
    copies.append(pltpu.make_async_copy(ocean, wet, sems.at[5]))
    for copy in copies:
        copy.start()
    lane = lax.broadcasted_iota(jnp.int32, (rows, LANES), 1)
    to_west = jnp.zeros((rows, LANES), F32)
    to_east = jnp.zeros((rows, LANES), F32)
    count = fields.shape[0]
    for p in range(count):
        if p % levels == 0:
            copies[p // levels].wait()
        if p == count - 1:
            fields[p] = wet[...].astype(F32)
        plane = fields[p]
        here = (lane >= WIDE * p) & (lane < WIDE * (p + 1))
        to_west = jnp.where(here, pltpu.roll(plane, WIDE * p, 1) if p else plane, to_west)
        to_east = jnp.where(here, pltpu.roll(plane, WIDE * (p + 1), 1), to_east)
        top[p] = plane[:WIDE]
        bottom[p] = plane[rows - WIDE :]
    west[...] = to_west
    east[...] = to_east


def east_of(v):
    return pltpu.roll(v, v.shape[1] - 1, 1)


def west_of(v):
    return pltpu.roll(v, 1, 1)


def north_of(v):
    return pltpu.roll(v, v.shape[0] - 1, 0)


def south_of(v):
    return pltpu.roll(v, 1, 0)


def main_kernel(
    fields, left, right, low, high, w_in, w_mid, w_out_t,
    o_mid, o_new, o_old, o_now, o_grad,
    planes, mids, olds, ft1, ft2, fth, ftx, cl, clh, clx, dc, dch, dcx, df, dfh, dfx,
    keep1, keep2, acc_mid, acc_in, acc_out, wi, wi_t, wm_t, wo, wo_t,
):
    levels, rows, cols = o_mid.shape
    width_in, hidden = w_in.shape
    count = 5 * levels + 1
    ext = rows + 2 * WIDE
    chunks = rows // TILES
    packs = -(-ext // 16)
    order = [rows, ext - 1] + [None] * packs + [rows + 1, ext - 2, rows + 2, ext - 3]
    first_pack = rows + 2
    halo_one = 2 + packs
    halo_two = halo_one + 2

    spare = jnp.zeros((DEEP - width_in, hidden), F32)
    wide_in = jnp.concatenate([w_in[...].astype(F32), spare], 0)
    wi[...] = wide_in.astype(BF16)
    wi_t[...] = wide_in.T.astype(BF16)
    wm_t[...] = w_mid[...].astype(F32).T.astype(BF16)
    spare = jnp.zeros((DEEP - levels, hidden), F32)
    wide_out = jnp.concatenate([w_out_t[...].astype(F32), spare], 0)
    wo_t[...] = wide_out.astype(BF16)
    wo[...] = wide_out.T.astype(BF16)

    lane = lax.broadcasted_iota(jnp.int32, (ext, LANES), 1)
    left_all = jnp.concatenate([left[...], high[count], low[count]], 0)
    right_all = jnp.concatenate([right[...], high[count + 1], low[count + 1]], 0)

    for p in range(count):
        from_right = pltpu.roll(right_all, LANES - WIDE * p, 1) if p else right_all
        from_left = pltpu.roll(left_all, LANES - WIDE * (p + 1), 1)
        side = jnp.where(lane < WIDE, from_right, jnp.where(lane >= LANES - WIDE, from_left, 0.0))
        planes[p, :, pl.ds(0, LANES)] = jnp.concatenate([fields[p], high[p], low[p]], 0)
        planes[p, :, pl.ds(LANES, LANES)] = side

    for ref in (ft1, ft2, fth, ftx, dc, dch, dcx, acc_mid, acc_in, acc_out):
        ref[...] = jnp.zeros_like(ref)

    def spread(plane, index, deep, main, extra, side):
        main[pl.ds(index, rows, stride=deep), :] = plane[:rows, :LANES]
        extra[pl.ds(index, 2 * WIDE, stride=deep), :] = plane[rows:, :LANES]
        side[pl.ds(index, ext, stride=deep), :] = plane[:, LANES:]

    def gathered(index, deep, main, extra, side):
        body = jnp.concatenate(
            [main[pl.ds(index, rows, stride=deep), :], extra[pl.ds(index, 2 * WIDE, stride=deep), :]], 0
        )
        return jnp.concatenate([body, side[pl.ds(index, ext, stride=deep), :]], 1)

    def pack_halo(deep, main, extra, side):
        where = lax.broadcasted_iota(jnp.int32, (deep, LANES), 1)
        for i, r in enumerate(order):
            if r is not None:
                main[pl.ds((rows + i) * deep, deep), :] = extra[pl.ds((r - rows) * deep, deep), :]

        for q in range(packs):
            total = jnp.zeros((deep, LANES), F32)
            for j in range(min(16, ext - 16 * q)):
                moved = pltpu.roll(side[pl.ds((16 * q + j) * deep, deep), :], (2 * WIDE * j + WIDE) % LANES, 1)
                total = jnp.where((where >= 2 * WIDE * j) & (where < 2 * WIDE * (j + 1)), moved, total)
            main[pl.ds((first_pack + q) * deep, deep), :] = total

    def unpack_halo(deep, main, extra, side, live):
        for i, r in enumerate(order[:live]):
            if r is not None:
                extra[pl.ds((r - rows) * deep, deep), :] = main[pl.ds((rows + i) * deep, deep), :]

        for q in range(packs):
            tile = main[pl.ds((first_pack + q) * deep, deep), :]
            for j in range(min(16, ext - 16 * q)):
                moved = pltpu.roll(tile, LANES - (2 * WIDE * j + WIDE) % LANES, 1)
                side[pl.ds((16 * q + j) * deep, deep), :] = moved

    def lanes_of(ref, deep, base, tiles):
        block = ref[pl.ds(base * deep, tiles * deep), :]
        return jnp.concatenate([block[k * deep : (k + 1) * deep] for k in range(tiles)], 1)

    def put_lanes(ref, deep, base, tiles, value):
        for k in range(tiles):
            ref[pl.ds((base + k) * deep, deep), :] = value[:, k * LANES : (k + 1) * LANES]

    def inputs_at(ref, base, tiles):
        return lanes_of(ref, DEEP, base, tiles).astype(BF16)

    def cotangents_at(base, tiles):
        part = lanes_of(dc, SHALLOW, base, tiles)
        return jnp.concatenate([part, jnp.zeros_like(part)], 0).astype(BF16)

    def forward(x):
        first = jnp.tanh(dot(wi_t[...], x))
        second = jnp.tanh(dot(wm_t[...], first.astype(BF16)))
        return first, second

    def closure(second):
        return dot(wo_t[...], second.astype(BF16)).astype(BF16).astype(F32)[:SHALLOW]

    def backward(first, second, cot):
        dz_two = (dot(wo[...], cot) * (1.0 - second * second)).astype(BF16)
        dz_one = (dot(w_mid[...], dz_two) * (1.0 - first * first)).astype(BF16)
        dfeat = dot(wi[...], dz_one).astype(BF16).astype(F32)
        return dz_one, dz_two, dfeat

    def add_terms(x, first, second, cot, dz_one, dz_two):
        acc_mid[...] += dot_nt(first, dz_two)
        acc_in[...] += dot_nt(x, dz_one)
        acc_out[...] += dot_nt(cot, second)

    def features_of(source, ft):
        for level in range(levels):
            v = source[level]
            spread(v, level, DEEP, ft, ftx, fth)
            spread(0.5 * (east_of(v) - west_of(v)), levels + level, DEEP, ft, ftx, fth)
            spread(0.5 * (north_of(v) - south_of(v)), 2 * levels + level, DEEP, ft, ftx, fth)

        pack_halo(DEEP, ft, ftx, fth)

    def cotangents_of(source, offset):
        for level in range(levels):
            spread(planes[count - 1] * (2.0 * DT * source[offset + level]), level, SHALLOW, dc, dcx, dch)

        pack_halo(SHALLOW, dc, dcx, dch)

    def force(v, level, closed):
        eastward, westward, northward, southward = east_of(v), west_of(v), north_of(v), south_of(v)
        laplace = eastward + westward + northward + southward - 4.0 * v
        slope = 0.5 * (eastward - westward)
        return planes[count - 1] * (KAPPA * laplace - planes[2 * levels + level] * slope + closed)

    features_of(planes, ft1)

    def first_step(c, carry):
        for k in range(0, TILES, PART):
            base = pl.multiple_of(c * TILES + k, PART)
            first, second = forward(inputs_at(ft1, base, PART))
            keep1[c, :, pl.ds(k * LANES, PART * LANES)] = first
            keep2[c, :, pl.ds(k * LANES, PART * LANES)] = second
            put_lanes(cl, SHALLOW, base, PART, closure(second))
        return carry

    lax.fori_loop(0, keep1.shape[0], first_step, 0)
    unpack_halo(SHALLOW, cl, clx, clh, len(order))

    for level in range(levels):
        closed = gathered(level, SHALLOW, cl, clx, clh)
        mid = planes[levels + level] + 2.0 * DT * force(planes[level], level, closed)
        o_mid[level] = mid[:rows, :LANES]
        mids[level] = mid

    features_of(mids, ft2)
    cotangents_of(planes, 3 * levels)

    def second_step(c, carry):
        parts = []
        for k in range(0, TILES, PART):
            base = pl.multiple_of(c * TILES + k, PART)
            x = inputs_at(ft2, base, PART)
            cot = cotangents_at(base, PART)
            first, second = forward(x)
            put_lanes(cl, SHALLOW, base, PART, closure(second))
            dz_one, dz_two, dfeat = backward(first, second, cot)
            put_lanes(df, DEEP, base, PART, dfeat)
            parts.append((x, first.astype(BF16), second.astype(BF16), cot, dz_one, dz_two))
        add_terms(*(jnp.concatenate(part, 1) for part in zip(*parts)))
        return carry

    lax.fori_loop(0, chunks, second_step, 0)
    first, second = forward(inputs_at(ft2, rows, halo_two))
    unused_one, unused_two, dfeat = backward(first, second, cotangents_at(rows, halo_two))
    put_lanes(df, DEEP, rows, halo_two, dfeat)
    unpack_halo(DEEP, df, dfx, dfh, halo_two)

    def adjoint_of(weighted, level):
        masked = planes[count - 1] * weighted
        carried = planes[2 * levels + level] * masked
        a0 = gathered(level, DEEP, df, dfx, dfh)
        a1 = gathered(levels + level, DEEP, df, dfx, dfh)
        a2 = gathered(2 * levels + level, DEEP, df, dfx, dfh)
        result = KAPPA * (east_of(masked) + west_of(masked) + north_of(masked) + south_of(masked) - 4.0 * masked)
        result = result + 0.5 * (east_of(carried) - west_of(carried)) + a0
        return result - 0.5 * (east_of(a1) - west_of(a1)) - 0.5 * (north_of(a2) - south_of(a2))

    for level in range(levels):
        closed = jnp.concatenate([cl[pl.ds(level, rows, stride=SHALLOW), :], jnp.zeros((2 * WIDE, LANES), F32)], 0)
        closed = jnp.concatenate([closed, jnp.zeros_like(closed)], 1)
        new = planes[level] + 2.0 * DT * force(mids[level], level, closed)
        o_new[level] = new[:rows, :LANES]
        grad = planes[4 * levels + level] + adjoint_of(2.0 * DT * planes[3 * levels + level], level)
        o_old[level] = grad[:rows, :LANES]
        olds[level] = grad

    cotangents_of(olds, 0)

    def third_step(c, carry):
        parts = []
        for k in range(0, TILES, PART):
            base = pl.multiple_of(c * TILES + k, PART)
            x = inputs_at(ft1, base, PART)
            cot = cotangents_at(base, PART)
            first = keep1[c, :, pl.ds(k * LANES, PART * LANES)]
            second = keep2[c, :, pl.ds(k * LANES, PART * LANES)]
            dz_one, dz_two, dfeat = backward(first, second, cot)
            put_lanes(df, DEEP, base, PART, dfeat)
            parts.append((x, first.astype(BF16), second.astype(BF16), cot, dz_one, dz_two))
        add_terms(*(jnp.concatenate(part, 1) for part in zip(*parts)))
        return carry

    lax.fori_loop(0, chunks, third_step, 0)
    near = halo_one * LANES
    unused_one, unused_two, dfeat = backward(
        keep1[chunks, :, pl.ds(0, near)], keep2[chunks, :, pl.ds(0, near)], cotangents_at(rows, halo_one)
    )
    put_lanes(df, DEEP, rows, halo_one, dfeat)
    unpack_halo(DEEP, df, dfx, dfh, halo_one)

    for level in range(levels):
        grad = adjoint_of(2.0 * DT * olds[level], level)
        o_now[level] = planes[3 * levels + level, pl.ds(0, rows), pl.ds(0, LANES)] + grad[:rows, :LANES]

    start = 0
    for acc in (acc_mid, acc_in, acc_out):
        deep = acc.shape[0]
        for half in range(hidden // LANES):
            o_grad[pl.ds(start, deep), :] = acc[:, half * LANES : (half + 1) * LANES]
            start += deep
    if start < o_grad.shape[0]:
        o_grad[pl.ds(start, o_grad.shape[0] - start), :] = jnp.zeros((o_grad.shape[0] - start, LANES), F32)


def scale_kernel(factor, terms, g_in, g_mid, g_out):
    hidden = g_mid.shape[0]
    start = 0
    for ref, deep in ((g_mid, hidden), (g_in, DEEP), (g_out, DEEP)):
        keep = ref.shape[0]
        for half in range(hidden // LANES):
            ref[:, half * LANES : (half + 1) * LANES] = terms[pl.ds(start, keep), :] * factor
            start += deep


def along(value, axis, step, periodic):
    count = lax.axis_size(axis)
    pairs = [(i, (i + step) % count) for i in range(count) if periodic or 0 <= i + step < count]
    return lax.ppermute(value, axis, pairs)


def swapped(value, axis, bit):
    return lax.ppermute(value, axis, [(i, i ^ bit) for i in range(lax.axis_size(axis))])


def summed_over(value, halving, doubling):
    bits = []
    bit = 1
    while bit < lax.axis_size(halving):
        upper = (lax.axis_index(halving) & bit) != 0
        half = value.shape[0] // 2
        lower_part, upper_part = value[:half], value[half:]
        sent = jnp.where(upper, lower_part, upper_part)
        value = jnp.where(upper, upper_part, lower_part) + swapped(sent, halving, bit)
        bits.append((bit, upper))
        bit *= 2
    bit = 1
    while bit < lax.axis_size(doubling):
        value = value + swapped(value, doubling, bit)
        bit *= 2
    for bit, upper in reversed(bits):
        other = swapped(value, halving, bit)
        value = jnp.concatenate([jnp.where(upper, other, value), jnp.where(upper, value, other)], 0)
    return value


def body(state_old, state_now, drift, ocean, w_in, w_mid, w_out, cot_mid, cot_new):
    levels, rows, cols = state_now.shape
    width_in, hidden = w_in.shape
    ext = rows + 2 * WIDE
    count = 5 * levels + 1
    packs = -(-ext // 16)
    steps = -(-(rows + 6 + packs) // TILES)
    slots = steps * TILES
    vmem = pl.BlockSpec(memory_space=pltpu.VMEM)
    strip = jax.ShapeDtypeStruct((rows, LANES), F32)
    edge = jax.ShapeDtypeStruct((count, WIDE, LANES), F32)
    place = pl.BlockSpec(memory_space=pltpu.HBM)
    arrays = (state_now, state_old, drift, cot_new, cot_mid, ocean)
    arrays = tuple(pltpu.with_memory_space_constraint(a, pltpu.HBM) for a in arrays)
    west, east, top, bottom, fields = pl.pallas_call(
        pack_kernel,
        out_shape=(strip, strip, edge, edge, jax.ShapeDtypeStruct((count, rows, cols), F32)),
        in_specs=[place] * 6,
        out_specs=(vmem,) * 5,
        scratch_shapes=[pltpu.VMEM((rows, cols), jnp.int32), pltpu.SemaphoreType.DMA((6,))],
        compiler_params=pltpu.CompilerParams(vmem_limit_bytes=8 * 2**20),
    )(*arrays)
    left = along(east, "lon", 1, True)
    right = along(west, "lon", -1, True)
    up = jnp.concatenate([bottom, left[None, rows - WIDE :], right[None, rows - WIDE :]], 0)
    down = jnp.concatenate([top, left[None, :WIDE], right[None, :WIDE]], 0)
    low = along(up, "lat", 1, False)
    high = along(down, "lat", -1, False)

    halves = hidden // LANES
    grain = 8 * lax.axis_size("lat")
    terms_rows = -(-halves * (hidden + 2 * DEEP) // grain) * grain
    field = jax.ShapeDtypeStruct((levels, rows, cols), F32)
    ext_planes = pltpu.VMEM((levels, ext, 2 * LANES), F32)
    side_rows = 16 * packs

    def tiles(deep):
        return [pltpu.VMEM((n * deep, LANES), F32) for n in (slots, side_rows, 2 * WIDE)]

    kept = pltpu.VMEM((steps, hidden, TILES * LANES), F32)
    state_mid, state_new, grad_old, grad_now, terms = pl.pallas_call(
        main_kernel,
        out_shape=(field, field, field, field, jax.ShapeDtypeStruct((terms_rows, LANES), F32)),
        in_specs=[vmem] * 8,
        out_specs=(vmem,) * 5,
        scratch_shapes=[
            pltpu.VMEM((count, ext, 2 * LANES), F32),
            ext_planes,
            ext_planes,
            tiles(DEEP)[0],
            *tiles(DEEP),
            *tiles(SHALLOW),
            *tiles(SHALLOW),
            *tiles(DEEP),
            kept,
            kept,
            pltpu.VMEM((hidden, hidden), F32),
            pltpu.VMEM((DEEP, hidden), F32),
            pltpu.VMEM((DEEP, hidden), F32),
            pltpu.VMEM((DEEP, hidden), BF16),
            pltpu.VMEM((hidden, DEEP), BF16),
            pltpu.VMEM((hidden, hidden), BF16),
            pltpu.VMEM((hidden, DEEP), BF16),
            pltpu.VMEM((DEEP, hidden), BF16),
        ],
        compiler_params=pltpu.CompilerParams(vmem_limit_bytes=44 * 2**20),
    )(fields, left, right, low, high, w_in, w_mid, w_out.T)

    summed = summed_over(terms, "lat", "lon")
    cells_all = rows * lax.axis_size("lat") * cols * lax.axis_size("lon")
    grad_in, grad_mid, grad_out = pl.pallas_call(
        functools.partial(scale_kernel, GAIN_GRAD / cells_all**0.5),
        out_shape=(
            jax.ShapeDtypeStruct((width_in, hidden), F32),
            jax.ShapeDtypeStruct((hidden, hidden), F32),
            jax.ShapeDtypeStruct((levels, hidden), F32),
        ),
        in_specs=[vmem],
        out_specs=(vmem,) * 3,
        compiler_params=pltpu.CompilerParams(vmem_limit_bytes=8 * 2**20),
    )(summed)
    return state_mid, state_new, grad_old, grad_now, grad_in, grad_mid, grad_out.T


def solution(mesh):
    field = P("grp", "lat", "lon")
    whole = P("grp", None)
    in_specs = (field, field, field, P(("grp", "lat"), "lon"), P(), P(), P(), field, field)
    out_specs = (field, field, field, field, whole, whole, whole)
    return jax.shard_map(body, mesh=mesh, in_specs=in_specs, out_specs=out_specs, check_vma=False)
```

```python
import functools

import jax
import jax.numpy as jnp
from jax import lax
from jax.experimental import pallas as pl
from jax.experimental.pallas import tpu as pltpu
from jax.sharding import PartitionSpec as P

KAPPA = 0.2
DT = 0.1
GAIN_GRAD = 10.0

WIDE = 4
LANES = 128
TILES = 32
PART = 8
DEEP = 16
SHALLOW = 8

F32 = jnp.float32
BF16 = jnp.bfloat16


def dot(left, right):
    return lax.dot_general(left, right, (((1,), (0,)), ((), ())), preferred_element_type=F32)


def dot_nt(left, right):
    return lax.dot_general(left, right, (((1,), (1,)), ((), ())), preferred_element_type=F32)


def pack_kernel(now, old, drift, cnew, cmid, ocean, west, east, top, bottom, fields, wet, sems):
    levels, rows, cols = now.shape
    copies = [
        pltpu.make_async_copy(ref, fields.at[pl.ds(levels * f, levels)], sems.at[f])
        for f, ref in enumerate((now, old, drift, cnew, cmid))
    ]
    copies.append(pltpu.make_async_copy(ocean, wet, sems.at[5]))
    for copy in copies:
        copy.start()
    lane = lax.broadcasted_iota(jnp.int32, (rows, LANES), 1)
    to_west = jnp.zeros((rows, LANES), F32)
    to_east = jnp.zeros((rows, LANES), F32)
    count = fields.shape[0]
    for p in range(count):
        if p % levels == 0:
            copies[p // levels].wait()
        if p == count - 1:
            fields[p] = wet[...].astype(F32)
        plane = fields[p]
        here = (lane >= WIDE * p) & (lane < WIDE * (p + 1))
        to_west = jnp.where(here, pltpu.roll(plane, WIDE * p, 1) if p else plane, to_west)
        to_east = jnp.where(here, pltpu.roll(plane, WIDE * (p + 1), 1), to_east)
        top[p] = plane[:WIDE]
        bottom[p] = plane[rows - WIDE :]
    west[...] = to_west
    east[...] = to_east


def east_of(v):
    return pltpu.roll(v, v.shape[1] - 1, 1)


def west_of(v):
    return pltpu.roll(v, 1, 1)


def north_of(v):
    return pltpu.roll(v, v.shape[0] - 1, 0)


def south_of(v):
    return pltpu.roll(v, 1, 0)


def main_kernel(
    fields, left, right, low, high, w_in, w_mid, w_out_t,
    o_mid, o_new, o_old, o_now, o_grad,
    planes, mids, olds, ft1, ft2, fth, ftx, cl, clh, clx, dc, dch, dcx, df, dfh, dfx,
    keep1, keep2, halo1, halo2, acc_mid, acc_in, acc_out, wi, wi_t, wm_t, wo, wo_t,
):
    levels, rows, cols = o_mid.shape
    width_in, hidden = w_in.shape
    count = 5 * levels + 1
    ext = rows + 2 * WIDE
    parts = min(TILES, rows) // PART
    packs = -(-ext // 16)
    order = [rows, ext - 1] + [None] * packs + [rows + 1, ext - 2, rows + 2, ext - 3]
    first_pack = rows + 2
    halo_one = 2 + packs
    halo_two = halo_one + 2

    spare = jnp.zeros((DEEP - width_in, hidden), F32)
    wide_in = jnp.concatenate([w_in[...].astype(F32), spare], 0)
    wi[...] = wide_in.astype(BF16)
    wi_t[...] = wide_in.T.astype(BF16)
    wm_t[...] = w_mid[...].astype(F32).T.astype(BF16)
    spare = jnp.zeros((DEEP - levels, hidden), F32)
    wide_out = jnp.concatenate([w_out_t[...].astype(F32), spare], 0)
    wo_t[...] = wide_out.astype(BF16)
    wo[...] = wide_out.T.astype(BF16)

    lane = lax.broadcasted_iota(jnp.int32, (ext, LANES), 1)
    left_all = jnp.concatenate([left[...], high[count], low[count]], 0)
    right_all = jnp.concatenate([right[...], high[count + 1], low[count + 1]], 0)

    for p in range(count):
        from_right = pltpu.roll(right_all, LANES - WIDE * p, 1) if p else right_all
        from_left = pltpu.roll(left_all, LANES - WIDE * (p + 1), 1)
        side = jnp.where(lane < WIDE, from_right, jnp.where(lane >= LANES - WIDE, from_left, 0.0))
        planes[p, :, pl.ds(0, LANES)] = jnp.concatenate([fields[p], high[p], low[p]], 0)
        planes[p, :, pl.ds(LANES, LANES)] = side

    for ref in (ft1, ft2, fth, ftx, dc, dch, dcx, acc_mid, acc_in, acc_out):
        ref[...] = jnp.zeros_like(ref)

    def spread(plane, index, deep, main, extra, side):
        main[pl.ds(index, rows, stride=deep), :] = plane[:rows, :LANES]
        extra[pl.ds(index, 2 * WIDE, stride=deep), :] = plane[rows:, :LANES]
        side[pl.ds(index, ext, stride=deep), :] = plane[:, LANES:]

    def gathered(index, deep, main, extra, side):
        body = jnp.concatenate(
            [main[pl.ds(index, rows, stride=deep), :], extra[pl.ds(index, 2 * WIDE, stride=deep), :]], 0
        )
        return jnp.concatenate([body, side[pl.ds(index, ext, stride=deep), :]], 1)

    def pack_halo(deep, main, extra, side):
        where = lax.broadcasted_iota(jnp.int32, (deep, LANES), 1)
        for i, r in enumerate(order):
            if r is not None:
                main[pl.ds((rows + i) * deep, deep), :] = extra[pl.ds((r - rows) * deep, deep), :]

        for q in range(packs):
            total = jnp.zeros((deep, LANES), F32)
            for j in range(min(16, ext - 16 * q)):
                moved = pltpu.roll(side[pl.ds((16 * q + j) * deep, deep), :], (2 * WIDE * j + WIDE) % LANES, 1)
                total = jnp.where((where >= 2 * WIDE * j) & (where < 2 * WIDE * (j + 1)), moved, total)
            main[pl.ds((first_pack + q) * deep, deep), :] = total

    def unpack_halo(deep, main, extra, side, live):
        for i, r in enumerate(order[:live]):
            if r is not None:
                extra[pl.ds((r - rows) * deep, deep), :] = main[pl.ds((rows + i) * deep, deep), :]

        for q in range(packs):
            tile = main[pl.ds((first_pack + q) * deep, deep), :]
            for j in range(min(16, ext - 16 * q)):
                moved = pltpu.roll(tile, LANES - (2 * WIDE * j + WIDE) % LANES, 1)
                side[pl.ds((16 * q + j) * deep, deep), :] = moved

    def lanes_of(ref, deep, base, tiles):
        block = ref[pl.ds(base * deep, tiles * deep), :]
        return jnp.concatenate([block[k * deep : (k + 1) * deep] for k in range(tiles)], 1)

    def put_lanes(ref, deep, base, tiles, value):
        for k in range(tiles):
            ref[pl.ds((base + k) * deep, deep), :] = value[:, k * LANES : (k + 1) * LANES]

    def inputs_at(ref, base, tiles):
        return lanes_of(ref, DEEP, base, tiles).astype(BF16)

    def cotangents_at(base, tiles):
        part = lanes_of(dc, SHALLOW, base, tiles)
        return jnp.concatenate([part, jnp.zeros_like(part)], 0).astype(BF16)

    def forward_stages(x):
        z_one = dot(wi_t[...], x)
        yield
        first = jnp.tanh(z_one)
        low_first = first.astype(BF16)
        yield
        z_two = dot(wm_t[...], low_first)
        yield
        second = jnp.tanh(z_two)
        return first, second, low_first, second.astype(BF16)

    def closure(low_second):
        return dot(wo_t[...], low_second).astype(BF16).astype(F32)[:SHALLOW]

    def backward_stages(first, second, cot):
        g_two = dot(wo[...], cot)
        yield
        dz_two = (g_two * (1.0 - second * second)).astype(BF16)
        yield
        g_one = dot(w_mid[...], dz_two)
        yield
        dz_one = (g_one * (1.0 - first * first)).astype(BF16)
        yield
        return dz_one, dz_two, dot(wi[...], dz_one).astype(BF16).astype(F32)

    def first_part(base, tiles, kept1, kept2):
        first, second, unused, low_second = yield from forward_stages(inputs_at(ft1, base, tiles))
        kept1[...] = first
        kept2[...] = second
        yield
        put_lanes(cl, SHALLOW, base, tiles, closure(low_second))

    def second_part(base, tiles, sums):
        x = inputs_at(ft2, base, tiles)
        cot = cotangents_at(base, tiles)
        first, second, low_first, low_second = yield from forward_stages(x)
        yield
        if sums is not None:
            put_lanes(cl, SHALLOW, base, tiles, closure(low_second))
        dz_one, dz_two, dfeat = yield from backward_stages(first, second, cot)
        if sums is not None:
            sums.append((dot_nt(low_first, dz_two), dot_nt(x, dz_one), dot_nt(cot, low_second)))
        yield
        put_lanes(df, DEEP, base, tiles, dfeat)

    def third_part(base, tiles, kept1, kept2, sums):
        cot = cotangents_at(base, tiles)
        first = kept1[...]
        second = kept2[...]
        dz_one, dz_two, dfeat = yield from backward_stages(first, second, cot)
        if sums is not None:
            x = inputs_at(ft1, base, tiles)
            sums.append((dot_nt(first.astype(BF16), dz_two), dot_nt(x, dz_one), dot_nt(cot, second.astype(BF16))))
        yield
        put_lanes(df, DEEP, base, tiles, dfeat)

    def staggered(generators):
        live = []
        waiting = list(generators)
        while live or waiting:
            if waiting:
                live.append(waiting.pop(0))
            for part in list(live):
                try:
                    next(part)
                except StopIteration:
                    live.remove(part)

    def add_terms(sums):
        for acc, terms in zip((acc_mid, acc_in, acc_out), zip(*sums)):
            acc[...] += functools.reduce(jnp.add, terms)

    def features_of(source, ft):
        for level in range(levels):
            v = source[level]
            spread(v, level, DEEP, ft, ftx, fth)
            spread(0.5 * (east_of(v) - west_of(v)), levels + level, DEEP, ft, ftx, fth)
            spread(0.5 * (north_of(v) - south_of(v)), 2 * levels + level, DEEP, ft, ftx, fth)

        pack_halo(DEEP, ft, ftx, fth)

    def cotangents_of(source, offset):
        for level in range(levels):
            spread(planes[count - 1] * (2.0 * DT * source[offset + level]), level, SHALLOW, dc, dcx, dch)

        pack_halo(SHALLOW, dc, dcx, dch)

    def force(v, level, closed):
        eastward, westward, northward, southward = east_of(v), west_of(v), north_of(v), south_of(v)
        laplace = eastward + westward + northward + southward - 4.0 * v
        slope = 0.5 * (eastward - westward)
        return planes[count - 1] * (KAPPA * laplace - planes[2 * levels + level] * slope + closed)

    features_of(planes, ft1)

    def first_step(c, carry):
        staggered(
            first_part(pl.multiple_of((c * parts + k) * PART, PART), PART, keep1.at[c * parts + k], keep2.at[c * parts + k])
            for k in range(parts)
        )
        return carry

    lax.fori_loop(0, rows // (parts * PART), first_step, 0)
    staggered([first_part(rows, len(order), halo1, halo2)])
    unpack_halo(SHALLOW, cl, clx, clh, len(order))

    for level in range(levels):
        closed = gathered(level, SHALLOW, cl, clx, clh)
        mid = planes[levels + level] + 2.0 * DT * force(planes[level], level, closed)
        o_mid[level] = mid[:rows, :LANES]
        mids[level] = mid

    features_of(mids, ft2)
    cotangents_of(planes, 3 * levels)

    def second_step(c, carry):
        sums = []
        staggered(second_part(pl.multiple_of((c * parts + k) * PART, PART), PART, sums) for k in range(parts))
        add_terms(sums)
        return carry

    lax.fori_loop(0, rows // (parts * PART), second_step, 0)
    staggered([second_part(rows, halo_two, None)])
    unpack_halo(DEEP, df, dfx, dfh, halo_two)

    def adjoint_of(weighted, level):
        masked = planes[count - 1] * weighted
        carried = planes[2 * levels + level] * masked
        a0 = gathered(level, DEEP, df, dfx, dfh)
        a1 = gathered(levels + level, DEEP, df, dfx, dfh)
        a2 = gathered(2 * levels + level, DEEP, df, dfx, dfh)
        result = KAPPA * (east_of(masked) + west_of(masked) + north_of(masked) + south_of(masked) - 4.0 * masked)
        result = result + 0.5 * (east_of(carried) - west_of(carried)) + a0
        return result - 0.5 * (east_of(a1) - west_of(a1)) - 0.5 * (north_of(a2) - south_of(a2))

    for level in range(levels):
        closed = jnp.concatenate([cl[pl.ds(level, rows, stride=SHALLOW), :], jnp.zeros((2 * WIDE, LANES), F32)], 0)
        closed = jnp.concatenate([closed, jnp.zeros_like(closed)], 1)
        new = planes[level] + 2.0 * DT * force(mids[level], level, closed)
        o_new[level] = new[:rows, :LANES]
        grad = planes[4 * levels + level] + adjoint_of(2.0 * DT * planes[3 * levels + level], level)
        o_old[level] = grad[:rows, :LANES]
        olds[level] = grad

    cotangents_of(olds, 0)

    def third_step(c, carry):
        sums = []
        staggered(
            third_part(
                pl.multiple_of((c * parts + k) * PART, PART), PART, keep1.at[c * parts + k], keep2.at[c * parts + k], sums
            )
            for k in range(parts)
        )
        add_terms(sums)
        return carry

    lax.fori_loop(0, rows // (parts * PART), third_step, 0)
    near = pl.ds(0, halo_one * LANES)
    staggered([third_part(rows, halo_one, halo1.at[:, near], halo2.at[:, near], None)])
    unpack_halo(DEEP, df, dfx, dfh, halo_one)

    for level in range(levels):
        grad = adjoint_of(2.0 * DT * olds[level], level)
        o_now[level] = planes[3 * levels + level, pl.ds(0, rows), pl.ds(0, LANES)] + grad[:rows, :LANES]

    start = 0
    for acc in (acc_mid, acc_in, acc_out):
        deep = acc.shape[0]
        for half in range(hidden // LANES):
            o_grad[pl.ds(start, deep), :] = acc[:, half * LANES : (half + 1) * LANES]
            start += deep
    if start < o_grad.shape[0]:
        o_grad[pl.ds(start, o_grad.shape[0] - start), :] = jnp.zeros((o_grad.shape[0] - start, LANES), F32)


def scale_kernel(factor, terms, g_in, g_mid, g_out):
    hidden = g_mid.shape[0]
    start = 0
    for ref, deep in ((g_mid, hidden), (g_in, DEEP), (g_out, DEEP)):
        keep = ref.shape[0]
        for half in range(hidden // LANES):
            ref[:, half * LANES : (half + 1) * LANES] = terms[pl.ds(start, keep), :] * factor
            start += deep


def along(value, axis, step, periodic):
    count = lax.axis_size(axis)
    pairs = [(i, (i + step) % count) for i in range(count) if periodic or 0 <= i + step < count]
    return lax.ppermute(value, axis, pairs)


def swapped(value, axis, bit):
    return lax.ppermute(value, axis, [(i, i ^ bit) for i in range(lax.axis_size(axis))])


def summed_over(value, halving, doubling):
    bits = []
    bit = 1
    while bit < lax.axis_size(halving):
        upper = (lax.axis_index(halving) & bit) != 0
        half = value.shape[0] // 2
        lower_part, upper_part = value[:half], value[half:]
        sent = jnp.where(upper, lower_part, upper_part)
        value = jnp.where(upper, upper_part, lower_part) + swapped(sent, halving, bit)
        bits.append((bit, upper))
        bit *= 2
    bit = 1
    while bit < lax.axis_size(doubling):
        value = value + swapped(value, doubling, bit)
        bit *= 2
    for bit, upper in reversed(bits):
        other = swapped(value, halving, bit)
        value = jnp.concatenate([jnp.where(upper, other, value), jnp.where(upper, value, other)], 0)
    return value


def body(state_old, state_now, drift, ocean, w_in, w_mid, w_out, cot_mid, cot_new):
    levels, rows, cols = state_now.shape
    width_in, hidden = w_in.shape
    ext = rows + 2 * WIDE
    count = 5 * levels + 1
    packs = -(-ext // 16)
    slots = rows + 6 + packs
    vmem = pl.BlockSpec(memory_space=pltpu.VMEM)
    strip = jax.ShapeDtypeStruct((rows, LANES), F32)
    edge = jax.ShapeDtypeStruct((count, WIDE, LANES), F32)
    place = pl.BlockSpec(memory_space=pltpu.HBM)
    arrays = (state_now, state_old, drift, cot_new, cot_mid, ocean)
    arrays = tuple(pltpu.with_memory_space_constraint(a, pltpu.HBM) for a in arrays)
    west, east, top, bottom, fields = pl.pallas_call(
        pack_kernel,
        out_shape=(strip, strip, edge, edge, jax.ShapeDtypeStruct((count, rows, cols), F32)),
        in_specs=[place] * 6,
        out_specs=(vmem,) * 5,
        scratch_shapes=[pltpu.VMEM((rows, cols), jnp.int32), pltpu.SemaphoreType.DMA((6,))],
        compiler_params=pltpu.CompilerParams(vmem_limit_bytes=8 * 2**20),
    )(*arrays)
    left = along(east, "lon", 1, True)
    right = along(west, "lon", -1, True)
    up = jnp.concatenate([bottom, left[None, rows - WIDE :], right[None, rows - WIDE :]], 0)
    down = jnp.concatenate([top, left[None, :WIDE], right[None, :WIDE]], 0)
    low = along(up, "lat", 1, False)
    high = along(down, "lat", -1, False)

    halves = hidden // LANES
    grain = 8 * lax.axis_size("lat")
    terms_rows = -(-halves * (hidden + 2 * DEEP) // grain) * grain
    field = jax.ShapeDtypeStruct((levels, rows, cols), F32)
    ext_planes = pltpu.VMEM((levels, ext, 2 * LANES), F32)
    side_rows = 16 * packs

    def tiles(deep):
        return [pltpu.VMEM((n * deep, LANES), F32) for n in (slots, side_rows, 2 * WIDE)]

    kept = pltpu.VMEM((rows // PART, hidden, PART * LANES), F32)
    kept_halo = pltpu.VMEM((hidden, (6 + packs) * LANES), F32)
    state_mid, state_new, grad_old, grad_now, terms = pl.pallas_call(
        main_kernel,
        out_shape=(field, field, field, field, jax.ShapeDtypeStruct((terms_rows, LANES), F32)),
        in_specs=[vmem] * 8,
        out_specs=(vmem,) * 5,
        scratch_shapes=[
            pltpu.VMEM((count, ext, 2 * LANES), F32),
            ext_planes,
            ext_planes,
            tiles(DEEP)[0],
            *tiles(DEEP),
            *tiles(SHALLOW),
            *tiles(SHALLOW),
            *tiles(DEEP),
            kept,
            kept,
            kept_halo,
            kept_halo,
            pltpu.VMEM((hidden, hidden), F32),
            pltpu.VMEM((DEEP, hidden), F32),
            pltpu.VMEM((DEEP, hidden), F32),
            pltpu.VMEM((DEEP, hidden), BF16),
            pltpu.VMEM((hidden, DEEP), BF16),
            pltpu.VMEM((hidden, hidden), BF16),
            pltpu.VMEM((hidden, DEEP), BF16),
            pltpu.VMEM((DEEP, hidden), BF16),
        ],
        compiler_params=pltpu.CompilerParams(vmem_limit_bytes=48 * 2**20),
    )(fields, left, right, low, high, w_in, w_mid, w_out.T)

    summed = summed_over(terms, "lat", "lon")
    cells_all = rows * lax.axis_size("lat") * cols * lax.axis_size("lon")
    grad_in, grad_mid, grad_out = pl.pallas_call(
        functools.partial(scale_kernel, GAIN_GRAD / cells_all**0.5),
        out_shape=(
            jax.ShapeDtypeStruct((width_in, hidden), F32),
            jax.ShapeDtypeStruct((hidden, hidden), F32),
            jax.ShapeDtypeStruct((levels, hidden), F32),
        ),
        in_specs=[vmem],
        out_specs=(vmem,) * 3,
        compiler_params=pltpu.CompilerParams(vmem_limit_bytes=8 * 2**20),
    )(summed)
    return state_mid, state_new, grad_old, grad_now, grad_in, grad_mid, grad_out.T


def solution(mesh):
    field = P("grp", "lat", "lon")
    whole = P("grp", None)
    in_specs = (field, field, field, P(("grp", "lat"), "lon"), P(), P(), P(), field, field)
    out_specs = (field, field, field, field, whole, whole, whole)
    return jax.shard_map(body, mesh=mesh, in_specs=in_specs, out_specs=out_specs, check_vma=False)
```

```python
import functools

import jax
import jax.numpy as jnp
from jax import lax
from jax.experimental import pallas as pl
from jax.experimental.pallas import tpu as pltpu
from jax.sharding import PartitionSpec as P

KAPPA = 0.2
DT = 0.1
GAIN_GRAD = 10.0

WIDE = 4
LANES = 128
PART = 8
EARLY = 2
DEEP = 16
SHALLOW = 8

F32 = jnp.float32
BF16 = jnp.bfloat16


def dot(left, right):
    return lax.dot_general(left, right, (((1,), (0,)), ((), ())), preferred_element_type=F32)


def dot_nt(left, right):
    return lax.dot_general(left, right, (((1,), (1,)), ((), ())), preferred_element_type=F32)


def pack_kernel(now, old, drift, cnew, cmid, ocean, west, east, top, bottom, fields, wet, sems):
    levels, rows, cols = now.shape
    copies = [
        pltpu.make_async_copy(ref, fields.at[pl.ds(levels * f, levels)], sems.at[f])
        for f, ref in enumerate((now, old, drift, cnew, cmid))
    ]
    copies.append(pltpu.make_async_copy(ocean, wet, sems.at[5]))
    for copy in copies:
        copy.start()
    lane = lax.broadcasted_iota(jnp.int32, (rows, LANES), 1)
    to_west = jnp.zeros((rows, LANES), F32)
    to_east = jnp.zeros((rows, LANES), F32)
    count = fields.shape[0]
    for p in range(count):
        if p % levels == 0:
            copies[p // levels].wait()
        if p == count - 1:
            fields[p] = wet[...].astype(F32)
        plane = fields[p]
        here = (lane >= WIDE * p) & (lane < WIDE * (p + 1))
        to_west = jnp.where(here, pltpu.roll(plane, WIDE * p, 1) if p else plane, to_west)
        to_east = jnp.where(here, pltpu.roll(plane, WIDE * (p + 1), 1), to_east)
        top[p] = plane[:WIDE]
        bottom[p] = plane[rows - WIDE :]
    west[...] = to_west
    east[...] = to_east


def east_of(v):
    return pltpu.roll(v, v.shape[1] - 1, 1)


def west_of(v):
    return pltpu.roll(v, 1, 1)


def north_of(v):
    return pltpu.roll(v, v.shape[0] - 1, 0)


def south_of(v):
    return pltpu.roll(v, 1, 0)


def forward_stages(x, w_first_t, w_second_t):
    z_one = dot(w_first_t[...], x)
    yield
    first = jnp.tanh(z_one)
    low_first = first.astype(BF16)
    yield
    z_two = dot(w_second_t[...], low_first)
    yield
    second = jnp.tanh(z_two)
    return first, second, low_first, second.astype(BF16)


def closure(low_second, w_last_t):
    return dot(w_last_t[...], low_second).astype(BF16).astype(F32)[:SHALLOW]


def staggered(generators):
    live = []
    waiting = list(generators)
    while live or waiting:
        if waiting:
            live.append(waiting.pop(0))
        for part in list(live):
            try:
                next(part)
            except StopIteration:
                live.remove(part)


def lanes_of(ref, deep, base, tiles):
    block = ref[pl.ds(base * deep, tiles * deep), :]
    return jnp.concatenate([block[k * deep : (k + 1) * deep] for k in range(tiles)], 1)


def put_lanes(ref, deep, base, tiles, value):
    for k in range(tiles):
        ref[pl.ds((base + k) * deep, deep), :] = value[:, k * LANES : (k + 1) * LANES]


def early_kernel(start, fields, *refs):
    if start == 0:
        w_in, w_mid, w_out_t, keep1, keep2, cl, wi, wi_t, wm_t, wo, wo_t, ft = refs
        width_in, hidden = w_in.shape
        levels = w_out_t.shape[0]
        spare = jnp.zeros((DEEP - width_in, hidden), F32)
        wide_in = jnp.concatenate([w_in[...].astype(F32), spare], 0)
        wi[...] = wide_in.astype(BF16)
        wi_t[...] = wide_in.T.astype(BF16)
        wm_t[...] = w_mid[...].astype(F32).T.astype(BF16)
        spare = jnp.zeros((DEEP - levels, hidden), F32)
        wide_out = jnp.concatenate([w_out_t[...].astype(F32), spare], 0)
        wo_t[...] = wide_out.astype(BF16)
        wo[...] = wide_out.T.astype(BF16)
    else:
        unused, wi_t, wm_t, wo_t, keep1, keep2, cl, ft = refs
        levels = (fields.shape[0] - 1) // 5
    tall = cl.shape[0] // SHALLOW
    ft[...] = jnp.zeros_like(ft)
    for level in range(levels):
        v = fields[level]
        slope_x = 0.5 * (east_of(v) - west_of(v))
        slope_y = 0.5 * (north_of(v) - south_of(v))
        for f, plane in enumerate((v, slope_x, slope_y)):
            ft[pl.ds(f * levels + level, tall, stride=DEEP), :] = plane[start : start + tall]

    def part(base, kept1, kept2):
        x = lanes_of(ft, DEEP, base, PART).astype(BF16)
        first, second, unused_low, low_second = yield from forward_stages(x, wi_t, wm_t)
        kept1[...] = first
        kept2[...] = second
        yield
        put_lanes(cl, SHALLOW, base, PART, closure(low_second, wo_t))

    staggered(part(k * PART, keep1.at[k], keep2.at[k]) for k in range(tall // PART))


def main_kernel(*refs):
    fields, left, right, low, high, wi, wi_t, wm_t, w_mid, wo, wo_t, *refs = refs
    early, refs = refs[: 3 * EARLY], refs[3 * EARLY :]
    o_mid, o_new, o_old, o_now, o_grad, planes, mids, olds, *refs = refs
    ft1, ft2, fth, ftx, cl, clh, clx, dc, dch, dcx, df, dfh, dfx, halo1, halo2, acc_mid, acc_in, acc_out = refs
    levels, rows, cols = o_mid.shape
    hidden = w_mid.shape[0]
    count = 5 * levels + 1
    ext = rows + 2 * WIDE
    packs = -(-ext // 16)
    kept1 = [ref.at[k] for ref in early[0::3] for k in range(ref.shape[0])]
    kept2 = [ref.at[k] for ref in early[1::3] for k in range(ref.shape[0])]
    packed = [None] * packs
    rim = [0, rows - 1, rows, ext - 1] + packed + [rows + 1, ext - 2, rows + 2, ext - 3]
    rim_near = 4 + packs
    outer = [rows, ext - 1] + packed + [rows + 1, ext - 2]

    lane = lax.broadcasted_iota(jnp.int32, (ext, LANES), 1)
    left_all = jnp.concatenate([left[...], high[count], low[count]], 0)
    right_all = jnp.concatenate([right[...], high[count + 1], low[count + 1]], 0)
    for p in range(count):
        from_right = pltpu.roll(right_all, LANES - WIDE * p, 1) if p else right_all
        from_left = pltpu.roll(left_all, LANES - WIDE * (p + 1), 1)
        side = jnp.where(lane < WIDE, from_right, jnp.where(lane >= LANES - WIDE, from_left, 0.0))
        planes[p, :, pl.ds(0, LANES)] = jnp.concatenate([fields[p], high[p], low[p]], 0)
        planes[p, :, pl.ds(LANES, LANES)] = side

    for ref in (ft1, ft2, fth, ftx, dc, dch, dcx):
        ref[...] = jnp.zeros_like(ref)

    def with_rim(plane):
        body, side = plane[:, :LANES], plane[:, LANES:]
        own = jnp.where(lane == LANES - WIDE, pltpu.roll(body, LANES - WIDE, 1), pltpu.roll(body, WIDE, 1))
        return jnp.where((lane == LANES - WIDE) | (lane == WIDE - 1), own, side)

    def from_rim(body, side):
        own = jnp.where(lane == 0, pltpu.roll(side, WIDE, 1), pltpu.roll(side, LANES - WIDE, 1))
        return jnp.where((lane == 0) | (lane == LANES - 1), own, body)

    def spread(plane, index, deep, main, extra, side, rimmed):
        main[pl.ds(index, rows, stride=deep), :] = plane[:rows, :LANES]
        extra[pl.ds(index, 2 * WIDE, stride=deep), :] = plane[rows:, :LANES]
        side[pl.ds(index, ext, stride=deep), :] = with_rim(plane) if rimmed else plane[:, LANES:]

    def gathered(index, deep, main, extra, side, rimmed):
        body = jnp.concatenate(
            [main[pl.ds(index, rows, stride=deep), :], extra[pl.ds(index, 2 * WIDE, stride=deep), :]], 0
        )
        beside = side[pl.ds(index, ext, stride=deep), :]
        return jnp.concatenate([from_rim(body, beside) if rimmed else body, beside], 1)

    def home(r, deep, main, extra):
        return main.at[pl.ds(r * deep, deep)] if r < rows else extra.at[pl.ds((r - rows) * deep, deep)]

    def pack_halo(order, deep, main, extra, side, rim_too=True):
        where = lax.broadcasted_iota(jnp.int32, (deep, LANES), 1)
        for i, r in enumerate(order):
            if r is not None and (rim_too or r >= rows):
                main[pl.ds((rows + i) * deep, deep), :] = home(r, deep, main, extra)[...]
        first_pack = rows + order.index(None)
        for q in range(packs):
            total = jnp.zeros((deep, LANES), F32)
            for j in range(min(16, ext - 16 * q)):
                moved = pltpu.roll(side[pl.ds((16 * q + j) * deep, deep), :], (2 * WIDE * j + WIDE) % LANES, 1)
                total = jnp.where((where >= 2 * WIDE * j) & (where < 2 * WIDE * (j + 1)), moved, total)
            main[pl.ds((first_pack + q) * deep, deep), :] = total

    def unpack_halo(order, deep, main, extra, side):
        for i, r in enumerate(order):
            if r is not None:
                home(r, deep, main, extra)[...] = main[pl.ds((rows + i) * deep, deep), :]
        first_pack = rows + order.index(None)
        for q in range(packs):
            tile = main[pl.ds((first_pack + q) * deep, deep), :]
            for j in range(min(16, ext - 16 * q)):
                moved = pltpu.roll(tile, LANES - (2 * WIDE * j + WIDE) % LANES, 1)
                side[pl.ds((16 * q + j) * deep, deep), :] = moved

    def inputs_at(ref, base, tiles):
        return lanes_of(ref, DEEP, base, tiles).astype(BF16)

    def cotangents_at(base, tiles):
        part = lanes_of(dc, SHALLOW, base, tiles)
        return jnp.concatenate([part, jnp.zeros_like(part)], 0).astype(BF16)

    def backward_stages(first, second, cot):
        g_two = dot(wo[...], cot)
        yield
        dz_two = (g_two * (1.0 - second * second)).astype(BF16)
        yield
        g_one = dot(w_mid[...], dz_two)
        yield
        dz_one = (g_one * (1.0 - first * first)).astype(BF16)
        yield
        return dz_one, dz_two, dot(wi[...], dz_one).astype(BF16).astype(F32)

    def second_part(base, tiles, sums):
        x = inputs_at(ft2, base, tiles)
        cot = cotangents_at(base, tiles)
        first, second, low_first, low_second = yield from forward_stages(x, wi_t, wm_t)
        yield
        if sums is not None:
            put_lanes(cl, SHALLOW, base, tiles, closure(low_second, wo_t))
        dz_one, dz_two, dfeat = yield from backward_stages(first, second, cot)
        if sums is not None:
            add_terms(sums, (low_first, dz_two), (x, dz_one), (cot, low_second))
        yield
        put_lanes(df, DEEP, base, tiles, dfeat)

    def third_part(base, tiles, held1, held2, counted, sums):
        cot = cotangents_at(base, tiles)
        first = held1[...]
        second = held2[...]
        dz_one, dz_two, dfeat = yield from backward_stages(first, second, cot)
        x = inputs_at(ft1, base, tiles)
        if counted is not None:
            dz_one, dz_two, cot = (jnp.where(counted, v.astype(F32), 0.0).astype(BF16) for v in (dz_one, dz_two, cot))
        add_terms(sums, (first.astype(BF16), dz_two), (x, dz_one), (cot, second.astype(BF16)))
        yield
        put_lanes(df, DEEP, base, tiles, dfeat)

    def add_terms(sums, *pairs):
        for k, pair in enumerate(pairs):
            sums[k] = dot_nt(*pair) if sums[k] is None else sums[k] + dot_nt(*pair)

    def keep_terms(sums, again):
        for acc, total in zip((acc_mid, acc_in, acc_out), sums):
            acc[...] = acc[...] + total if again else total

    def features_of(source, ft, order, rimmed):
        for level in range(levels):
            v = source[level]
            spread(v, level, DEEP, ft, ftx, fth, rimmed)
            spread(0.5 * (east_of(v) - west_of(v)), levels + level, DEEP, ft, ftx, fth, rimmed)
            spread(0.5 * (north_of(v) - south_of(v)), 2 * levels + level, DEEP, ft, ftx, fth, rimmed)
        pack_halo(order, DEEP, ft, ftx, fth)

    def force(v, level, closed):
        eastward, westward, northward, southward = east_of(v), west_of(v), north_of(v), south_of(v)
        laplace = eastward + westward + northward + southward - 4.0 * v
        slope = 0.5 * (eastward - westward)
        return planes[count - 1] * (KAPPA * laplace - planes[2 * levels + level] * slope + closed)

    features_of(planes, ft1, rim, True)
    for k, ref in enumerate(early[2::3]):
        cl[pl.ds(k * ref.shape[0], ref.shape[0]), :] = ref[...]

    def first_part(base, tiles):
        first, second, unused, low_second = yield from forward_stages(inputs_at(ft1, base, tiles), wi_t, wm_t)
        halo1[...] = first
        halo2[...] = second
        yield
        put_lanes(cl, SHALLOW, base, tiles, closure(low_second, wo_t))

    staggered([first_part(rows, len(rim))])
    unpack_halo(rim, SHALLOW, cl, clx, clh)
    for level in range(levels):
        closed = gathered(level, SHALLOW, cl, clx, clh, True)
        mid = planes[levels + level] + 2.0 * DT * force(planes[level], level, closed)
        o_mid[level] = mid[:rows, :LANES]
        mids[level] = mid

    features_of(mids, ft2, outer, False)
    for level in range(levels):
        masked = planes[count - 1] * (2.0 * DT * planes[3 * levels + level])
        spread(masked, level, SHALLOW, dc, dcx, dch, False)
    pack_halo(outer, SHALLOW, dc, dcx, dch)
    sums = [None] * 3
    staggered(
        [second_part(rows, len(outer), None)] + [second_part(k * PART, PART, sums) for k in range(rows // PART)]
    )
    keep_terms(sums, False)
    unpack_halo(outer, DEEP, df, dfx, dfh)

    def adjoint_of(weighted, level, rimmed):
        masked = planes[count - 1] * weighted
        carried = planes[2 * levels + level] * masked
        a0 = gathered(level, DEEP, df, dfx, dfh, rimmed)
        a1 = gathered(levels + level, DEEP, df, dfx, dfh, rimmed)
        a2 = gathered(2 * levels + level, DEEP, df, dfx, dfh, rimmed)
        result = KAPPA * (east_of(masked) + west_of(masked) + north_of(masked) + south_of(masked) - 4.0 * masked)
        result = result + 0.5 * (east_of(carried) - west_of(carried)) + a0
        return result - 0.5 * (east_of(a1) - west_of(a1)) - 0.5 * (north_of(a2) - south_of(a2))

    for level in range(levels):
        closed = jnp.concatenate([cl[pl.ds(level, rows, stride=SHALLOW), :], jnp.zeros((2 * WIDE, LANES), F32)], 0)
        closed = jnp.concatenate([closed, jnp.zeros_like(closed)], 1)
        new = planes[level] + 2.0 * DT * force(mids[level], level, closed)
        o_new[level] = new[:rows, :LANES]
        grad = planes[4 * levels + level] + adjoint_of(2.0 * DT * planes[3 * levels + level], level, False)
        o_old[level] = grad[:rows, :LANES]
        olds[level] = grad

    row = lax.broadcasted_iota(jnp.int32, (ext, LANES), 0)
    inside = (lane > 0) & (lane < LANES - 1) & (row > 0) & (row < rows - 1)
    for level in range(levels):
        masked = planes[count - 1] * (2.0 * DT * olds[level])
        body = masked[:, :LANES]
        dc[pl.ds(level, rows, stride=SHALLOW), :] = jnp.where(inside, body, 0.0)[:rows]
        dcx[pl.ds(level, 2 * WIDE, stride=SHALLOW), :] = body[rows:]
        dch[pl.ds(level, ext, stride=SHALLOW), :] = with_rim(masked)
        for k, r in enumerate(rim[:2]):
            dc[pl.ds((rows + k) * SHALLOW + level, 1), :] = body[r : r + 1]
    pack_halo(rim[:rim_near], SHALLOW, dc, dcx, dch, False)
    at = lax.broadcasted_iota(jnp.int32, (1, rim_near * LANES), 1)
    tile, place = at >> 7, at & (LANES - 1)
    side_row = (tile - 4) * 16 + (place >> 3)
    edge = ((place & 7) == 0) | ((place & 7) == 7)
    counted = (tile < 2) | ((tile >= 4) & edge & (side_row > 0) & (side_row < rows - 1))
    near = pl.ds(0, rim_near * LANES)
    sums = [None] * 3
    staggered(
        [third_part(rows, rim_near, halo1.at[:, near], halo2.at[:, near], counted, sums)]
        + [third_part(k * PART, PART, kept1[k], kept2[k], None, sums) for k in range(rows // PART)]
    )
    keep_terms(sums, True)
    unpack_halo(rim[:rim_near], DEEP, df, dfx, dfh)
    for level in range(levels):
        grad = adjoint_of(2.0 * DT * olds[level], level, True)
        o_now[level] = planes[3 * levels + level, pl.ds(0, rows), pl.ds(0, LANES)] + grad[:rows, :LANES]

    start = 0
    for acc in (acc_mid, acc_in, acc_out):
        deep = acc.shape[0]
        for half in range(hidden // LANES):
            o_grad[pl.ds(start, deep), :] = acc[:, half * LANES : (half + 1) * LANES]
            start += deep
    if start < o_grad.shape[0]:
        o_grad[pl.ds(start, o_grad.shape[0] - start), :] = jnp.zeros((o_grad.shape[0] - start, LANES), F32)


def scale_kernel(factor, terms, g_in, g_mid, g_out):
    hidden = g_mid.shape[0]
    start = 0
    for ref, deep in ((g_mid, hidden), (g_in, DEEP), (g_out, DEEP)):
        keep = ref.shape[0]
        for half in range(hidden // LANES):
            ref[:, half * LANES : (half + 1) * LANES] = terms[pl.ds(start, keep), :] * factor
            start += deep


def along(value, axis, step, periodic):
    count = lax.axis_size(axis)
    pairs = [(i, (i + step) % count) for i in range(count) if periodic or 0 <= i + step < count]
    return lax.ppermute(value, axis, pairs)


def swapped(value, axis, bit):
    return lax.ppermute(value, axis, [(i, i ^ bit) for i in range(lax.axis_size(axis))])


def summed_over(value, halving, doubling):
    bits = []
    bit = 1
    while bit < lax.axis_size(halving):
        upper = (lax.axis_index(halving) & bit) != 0
        half = value.shape[0] // 2
        lower_part, upper_part = value[:half], value[half:]
        sent = jnp.where(upper, lower_part, upper_part)
        value = jnp.where(upper, upper_part, lower_part) + swapped(sent, halving, bit)
        bits.append((bit, upper))
        bit *= 2
    bit = 1
    while bit < lax.axis_size(doubling):
        value = value + swapped(value, doubling, bit)
        bit *= 2
    for bit, upper in reversed(bits):
        other = swapped(value, halving, bit)
        value = jnp.concatenate([jnp.where(upper, other, value), jnp.where(upper, value, other)], 0)
    return value


def body(state_old, state_now, drift, ocean, w_in, w_mid, w_out, cot_mid, cot_new):
    levels, rows, cols = state_now.shape
    width_in, hidden = w_in.shape
    ext = rows + 2 * WIDE
    count = 5 * levels + 1
    packs = -(-ext // 16)
    slots = rows + 8 + packs
    tall = rows // EARLY
    vmem = pl.BlockSpec(memory_space=pltpu.VMEM)
    strip = jax.ShapeDtypeStruct((rows, LANES), F32)
    edge = jax.ShapeDtypeStruct((count, WIDE, LANES), F32)
    arrays = (state_now, state_old, drift, cot_new, cot_mid, ocean)
    west, east, top, bottom, fields = pl.pallas_call(
        pack_kernel,
        out_shape=(strip, strip, edge, edge, jax.ShapeDtypeStruct((count, rows, cols), F32)),
        in_specs=[pl.BlockSpec(memory_space=pltpu.HBM)] * 6,
        out_specs=(vmem,) * 5,
        scratch_shapes=[pltpu.VMEM((rows, cols), jnp.int32), pltpu.SemaphoreType.DMA((6,))],
        compiler_params=pltpu.CompilerParams(vmem_limit_bytes=8 * 2**20),
    )(*(pltpu.with_memory_space_constraint(a, pltpu.HBM) for a in arrays))

    kept = jax.ShapeDtypeStruct((tall // PART, hidden, PART * LANES), F32)
    closed = jax.ShapeDtypeStruct((tall * SHALLOW, LANES), F32)
    tall_weight = jax.ShapeDtypeStruct((hidden, DEEP), BF16)
    flat_weight = jax.ShapeDtypeStruct((DEEP, hidden), BF16)
    prepared = (flat_weight, tall_weight, jax.ShapeDtypeStruct((hidden, hidden), BF16), tall_weight, flat_weight)

    def early(k, extra, extra_out):
        return pl.pallas_call(
            functools.partial(early_kernel, k * tall),
            out_shape=(kept, kept, closed) + extra_out,
            in_specs=[vmem] * (1 + len(extra)),
            out_specs=(vmem,) * (3 + len(extra_out)),
            scratch_shapes=[pltpu.VMEM((tall * DEEP, LANES), F32)],
            compiler_params=pltpu.CompilerParams(vmem_limit_bytes=36 * 2**20),
            cost_estimate=pl.CostEstimate(
                flops=6 * hidden * hidden * tall * cols, bytes_accessed=0, transcendentals=2 * hidden * tall * cols
            ),
        )(fields, *extra)

    left = along(east, "lon", 1, True)
    right = along(west, "lon", -1, True)
    *first_kept, wi, wi_t, wm_t, wo, wo_t = early(0, (w_in, w_mid, w_out.T), prepared)
    up = jnp.concatenate([bottom, left[None, rows - WIDE :], right[None, rows - WIDE :]], 0)
    down = jnp.concatenate([top, left[None, :WIDE], right[None, :WIDE]], 0)
    low = along(up, "lat", 1, False)
    high = along(down, "lat", -1, False)
    done = list(first_kept)
    for k in range(1, EARLY):
        done += early(k, (left, wi_t, wm_t, wo_t), ())

    halves = hidden // LANES
    grain = 8 * lax.axis_size("lat")
    terms_rows = -(-halves * (hidden + 2 * DEEP) // grain) * grain
    field = jax.ShapeDtypeStruct((levels, rows, cols), F32)
    ext_planes = pltpu.VMEM((levels, ext, 2 * LANES), F32)

    def tiles(deep):
        return [pltpu.VMEM((n * deep, LANES), F32) for n in (slots, 16 * packs, 2 * WIDE)]

    kept_halo = pltpu.VMEM((hidden, (8 + packs) * LANES), F32)
    state_mid, state_new, grad_old, grad_now, terms = pl.pallas_call(
        main_kernel,
        out_shape=(field, field, field, field, jax.ShapeDtypeStruct((terms_rows, LANES), F32)),
        in_specs=[vmem] * (11 + 3 * EARLY),
        out_specs=(vmem,) * 5,
        scratch_shapes=[
            pltpu.VMEM((count, ext, 2 * LANES), F32),
            ext_planes,
            ext_planes,
            tiles(DEEP)[0],
            *tiles(DEEP),
            *tiles(SHALLOW),
            *tiles(SHALLOW),
            *tiles(DEEP),
            kept_halo,
            kept_halo,
            pltpu.VMEM((hidden, hidden), F32),
            pltpu.VMEM((DEEP, hidden), F32),
            pltpu.VMEM((DEEP, hidden), F32),
        ],
        compiler_params=pltpu.CompilerParams(vmem_limit_bytes=36 * 2**20),
    )(fields, left, right, low, high, wi, wi_t, wm_t, w_mid, wo, wo_t, *done)

    summed = summed_over(terms, "lat", "lon")
    cells_all = rows * lax.axis_size("lat") * cols * lax.axis_size("lon")
    grad_in, grad_mid, grad_out = pl.pallas_call(
        functools.partial(scale_kernel, GAIN_GRAD / cells_all**0.5),
        out_shape=(
            jax.ShapeDtypeStruct((width_in, hidden), F32),
            jax.ShapeDtypeStruct((hidden, hidden), F32),
            jax.ShapeDtypeStruct((levels, hidden), F32),
        ),
        in_specs=[vmem],
        out_specs=(vmem,) * 3,
        compiler_params=pltpu.CompilerParams(vmem_limit_bytes=8 * 2**20),
    )(summed)
    return state_mid, state_new, grad_old, grad_now, grad_in, grad_mid, grad_out.T


def solution(mesh):
    field = P("grp", "lat", "lon")
    whole = P("grp", None)
    in_specs = (field, field, field, P(("grp", "lat"), "lon"), P(), P(), P(), field, field)
    out_specs = (field, field, field, field, whole, whole, whole)
    return jax.shard_map(body, mesh=mesh, in_specs=in_specs, out_specs=out_specs, check_vma=False)
```

```python
import functools

import jax
import jax.numpy as jnp
from jax import lax
from jax.experimental import pallas as pl
from jax.experimental.pallas import tpu as pltpu
from jax.sharding import PartitionSpec as P

KAPPA = 0.2
DT = 0.1
GAIN_GRAD = 10.0

WIDE = 4
LANES = 128
PART = 8
EARLY = 2
SHARES = 2
DEEP = 16
SHALLOW = 8

F32 = jnp.float32
BF16 = jnp.bfloat16


def dot(left, right):
    return lax.dot_general(left, right, (((1,), (0,)), ((), ())), preferred_element_type=F32)


def dot_nt(left, right):
    return lax.dot_general(left, right, (((1,), (1,)), ((), ())), preferred_element_type=F32)


def pack_kernel(now, old, drift, cnew, cmid, ocean, west, east, top, bottom, fields, wet, sems):
    levels, rows, cols = now.shape
    copies = [
        pltpu.make_async_copy(ref, fields.at[pl.ds(levels * f, levels)], sems.at[f])
        for f, ref in enumerate((now, old, drift, cnew, cmid))
    ]
    copies.append(pltpu.make_async_copy(ocean, wet, sems.at[5]))
    for copy in copies:
        copy.start()
    lane = lax.broadcasted_iota(jnp.int32, (rows, LANES), 1)
    to_west = jnp.zeros((rows, LANES), F32)
    to_east = jnp.zeros((rows, LANES), F32)
    count = fields.shape[0]
    for p in range(count):
        if p % levels == 0:
            copies[p // levels].wait()
        if p == count - 1:
            fields[p] = wet[...].astype(F32)
        plane = fields[p]
        here = (lane >= WIDE * p) & (lane < WIDE * (p + 1))
        to_west = jnp.where(here, pltpu.roll(plane, WIDE * p, 1) if p else plane, to_west)
        to_east = jnp.where(here, pltpu.roll(plane, WIDE * (p + 1), 1), to_east)
        top[p] = plane[:WIDE]
        bottom[p] = plane[rows - WIDE :]
    west[...] = to_west
    east[...] = to_east


def join_kernel(top, bottom, left, right, up, down):
    count = top.shape[0]
    rows = left.shape[0]
    up[pl.ds(0, count)] = bottom[...]
    down[pl.ds(0, count)] = top[...]
    for k, strip in enumerate((left, right)):
        up[count + k] = strip[pl.ds(rows - WIDE, WIDE), :]
        down[count + k] = strip[pl.ds(0, WIDE), :]


def east_of(v):
    return pltpu.roll(v, v.shape[1] - 1, 1)


def west_of(v):
    return pltpu.roll(v, 1, 1)


def north_of(v):
    return pltpu.roll(v, v.shape[0] - 1, 0)


def south_of(v):
    return pltpu.roll(v, 1, 0)


def forward_stages(x, w_first_t, w_second_t):
    z_one = dot(w_first_t[...], x)
    yield
    first = jnp.tanh(z_one)
    low_first = first.astype(BF16)
    yield
    z_two = dot(w_second_t[...], low_first)
    yield
    second = jnp.tanh(z_two)
    return first, second, low_first, second.astype(BF16)


def closure(low_second, w_last_t):
    return dot(w_last_t[...], low_second).astype(BF16).astype(F32)[:SHALLOW]


def staggered(generators):
    live = []
    waiting = list(generators)
    while live or waiting:
        if waiting:
            live.append(waiting.pop(0))
        for part in list(live):
            try:
                next(part)
            except StopIteration:
                live.remove(part)


def lanes_of(ref, deep, base, tiles):
    block = ref[pl.ds(base * deep, tiles * deep), :]
    return jnp.concatenate([block[k * deep : (k + 1) * deep] for k in range(tiles)], 1)


def put_lanes(ref, deep, base, tiles, value):
    for k in range(tiles):
        ref[pl.ds((base + k) * deep, deep), :] = value[:, k * LANES : (k + 1) * LANES]


def early_kernel(start, fields, *refs):
    if start == 0:
        w_in, w_mid, w_out_t, keep1, keep2, cl, wi, wi_t, wm_t, wo, wo_t, ft = refs
        width_in, hidden = w_in.shape
        levels = w_out_t.shape[0]
        spare = jnp.zeros((DEEP - width_in, hidden), F32)
        wide_in = jnp.concatenate([w_in[...].astype(F32), spare], 0)
        wi[...] = wide_in.astype(BF16)
        wi_t[...] = wide_in.T.astype(BF16)
        wm_t[...] = w_mid[...].astype(F32).T.astype(BF16)
        spare = jnp.zeros((DEEP - levels, hidden), F32)
        wide_out = jnp.concatenate([w_out_t[...].astype(F32), spare], 0)
        wo_t[...] = wide_out.astype(BF16)
        wo[...] = wide_out.T.astype(BF16)
    else:
        unused, wi_t, wm_t, wo_t, keep1, keep2, cl, ft = refs
        levels = (fields.shape[0] - 1) // 5
    tall = cl.shape[0] // SHALLOW
    ft[...] = jnp.zeros_like(ft)
    for level in range(levels):
        v = fields[level]
        slope_x = 0.5 * (east_of(v) - west_of(v))
        slope_y = 0.5 * (north_of(v) - south_of(v))
        for f, plane in enumerate((v, slope_x, slope_y)):
            ft[pl.ds(f * levels + level, tall, stride=DEEP), :] = plane[start : start + tall]

    def part(base, kept1, kept2):
        x = lanes_of(ft, DEEP, base, PART).astype(BF16)
        first, second, unused_low, low_second = yield from forward_stages(x, wi_t, wm_t)
        kept1[...] = first
        kept2[...] = second
        yield
        put_lanes(cl, SHALLOW, base, PART, closure(low_second, wo_t))

    staggered(part(k * PART, keep1.at[k], keep2.at[k]) for k in range(tall // PART))


def main_kernel(bands, *refs):
    fields, left, right, low, high, wi, wi_t, wm_t, w_mid, wo, wo_t, *refs = refs
    early, refs = refs[: 3 * EARLY], refs[3 * EARLY :]
    o_mid, o_new, o_old, o_now, o_grad, o_place, planes, mids, olds, *refs = refs
    ft1, ft2, fth, ftx, cl, clh, clx, dc, dch, dcx, df, dfh, dfx, halo1, halo2, acc_mid, acc_in, acc_out = refs
    levels, rows, cols = o_mid.shape
    hidden = w_mid.shape[0]
    count = 5 * levels + 1
    ext = rows + 2 * WIDE
    packs = -(-ext // 16)
    kept1 = [ref.at[k] for ref in early[0::3] for k in range(ref.shape[0])]
    kept2 = [ref.at[k] for ref in early[1::3] for k in range(ref.shape[0])]
    packed = [None] * packs
    rim = [0, rows - 1, rows, ext - 1] + packed + [rows + 1, ext - 2, rows + 2, ext - 3]
    rim_near = 4 + packs
    outer = [rows, ext - 1] + packed + [rows + 1, ext - 2]

    lane = lax.broadcasted_iota(jnp.int32, (ext, LANES), 1)
    band = lax.axis_index("lat")
    o_place[...] = jnp.zeros_like(o_place) + band
    has_low = jnp.where(band > 0, 1.0, 0.0)
    has_high = jnp.where(band < bands - 1, 1.0, 0.0)

    def beyond(p):
        return [high[p] * has_high, low[p] * has_low]

    left_all = jnp.concatenate([left[...]] + beyond(count), 0)
    right_all = jnp.concatenate([right[...]] + beyond(count + 1), 0)
    for p in range(count):
        from_right = pltpu.roll(right_all, LANES - WIDE * p, 1) if p else right_all
        from_left = pltpu.roll(left_all, LANES - WIDE * (p + 1), 1)
        side = jnp.where(lane < WIDE, from_right, jnp.where(lane >= LANES - WIDE, from_left, 0.0))
        planes[p, :, pl.ds(0, LANES)] = jnp.concatenate([fields[p]] + beyond(p), 0)
        planes[p, :, pl.ds(LANES, LANES)] = side

    for ref in (ft1, ft2, fth, ftx, dc, dch, dcx):
        ref[...] = jnp.zeros_like(ref)

    def with_rim(plane):
        body, side = plane[:, :LANES], plane[:, LANES:]
        own = jnp.where(lane == LANES - WIDE, pltpu.roll(body, LANES - WIDE, 1), pltpu.roll(body, WIDE, 1))
        return jnp.where((lane == LANES - WIDE) | (lane == WIDE - 1), own, side)

    def from_rim(body, side):
        own = jnp.where(lane == 0, pltpu.roll(side, WIDE, 1), pltpu.roll(side, LANES - WIDE, 1))
        return jnp.where((lane == 0) | (lane == LANES - 1), own, body)

    def spread(plane, index, deep, main, extra, side, rimmed):
        main[pl.ds(index, rows, stride=deep), :] = plane[:rows, :LANES]
        extra[pl.ds(index, 2 * WIDE, stride=deep), :] = plane[rows:, :LANES]
        side[pl.ds(index, ext, stride=deep), :] = with_rim(plane) if rimmed else plane[:, LANES:]

    def gathered(index, deep, main, extra, side, rimmed):
        body = jnp.concatenate(
            [main[pl.ds(index, rows, stride=deep), :], extra[pl.ds(index, 2 * WIDE, stride=deep), :]], 0
        )
        beside = side[pl.ds(index, ext, stride=deep), :]
        return jnp.concatenate([from_rim(body, beside) if rimmed else body, beside], 1)

    def home(r, deep, main, extra):
        return main.at[pl.ds(r * deep, deep)] if r < rows else extra.at[pl.ds((r - rows) * deep, deep)]

    def pack_halo(order, deep, main, extra, side, rim_too=True):
        where = lax.broadcasted_iota(jnp.int32, (deep, LANES), 1)
        for i, r in enumerate(order):
            if r is not None and (rim_too or r >= rows):
                main[pl.ds((rows + i) * deep, deep), :] = home(r, deep, main, extra)[...]
        first_pack = rows + order.index(None)
        for q in range(packs):
            total = jnp.zeros((deep, LANES), F32)
            for j in range(min(16, ext - 16 * q)):
                moved = pltpu.roll(side[pl.ds((16 * q + j) * deep, deep), :], (2 * WIDE * j + WIDE) % LANES, 1)
                total = jnp.where((where >= 2 * WIDE * j) & (where < 2 * WIDE * (j + 1)), moved, total)
            main[pl.ds((first_pack + q) * deep, deep), :] = total

    def unpack_halo(order, deep, main, extra, side):
        for i, r in enumerate(order):
            if r is not None:
                home(r, deep, main, extra)[...] = main[pl.ds((rows + i) * deep, deep), :]
        first_pack = rows + order.index(None)
        for q in range(packs):
            tile = main[pl.ds((first_pack + q) * deep, deep), :]
            for j in range(min(16, ext - 16 * q)):
                moved = pltpu.roll(tile, LANES - (2 * WIDE * j + WIDE) % LANES, 1)
                side[pl.ds((16 * q + j) * deep, deep), :] = moved

    def inputs_at(ref, base, tiles):
        return lanes_of(ref, DEEP, base, tiles).astype(BF16)

    def cotangents_at(base, tiles):
        part = lanes_of(dc, SHALLOW, base, tiles)
        return jnp.concatenate([part, jnp.zeros_like(part)], 0).astype(BF16)

    def backward_stages(first, second, cot):
        g_two = dot(wo[...], cot)
        yield
        dz_two = (g_two * (1.0 - second * second)).astype(BF16)
        yield
        g_one = dot(w_mid[...], dz_two)
        yield
        dz_one = (g_one * (1.0 - first * first)).astype(BF16)
        yield
        return dz_one, dz_two, dot(wi[...], dz_one).astype(BF16).astype(F32)

    def second_part(base, tiles, sums):
        x = inputs_at(ft2, base, tiles)
        cot = cotangents_at(base, tiles)
        first, second, low_first, low_second = yield from forward_stages(x, wi_t, wm_t)
        yield
        if sums is not None:
            put_lanes(cl, SHALLOW, base, tiles, closure(low_second, wo_t))
        dz_one, dz_two, dfeat = yield from backward_stages(first, second, cot)
        if sums is not None:
            add_terms(sums, (low_first, dz_two), (x, dz_one), (cot, low_second))
        yield
        put_lanes(df, DEEP, base, tiles, dfeat)

    def third_part(base, tiles, held1, held2, counted, sums):
        cot = cotangents_at(base, tiles)
        first = held1[...]
        second = held2[...]
        dz_one, dz_two, dfeat = yield from backward_stages(first, second, cot)
        x = inputs_at(ft1, base, tiles)
        if counted is not None:
            dz_one, dz_two, cot = (jnp.where(counted, v.astype(F32), 0.0).astype(BF16) for v in (dz_one, dz_two, cot))
        add_terms(sums, (first.astype(BF16), dz_two), (x, dz_one), (cot, second.astype(BF16)))
        yield
        put_lanes(df, DEEP, base, tiles, dfeat)

    def add_terms(sums, *pairs):
        for k, pair in enumerate(pairs):
            sums[k] = dot_nt(*pair) if sums[k] is None else sums[k] + dot_nt(*pair)

    def keep_terms(sums, again):
        for acc, total in zip((acc_mid, acc_in, acc_out), sums):
            acc[...] = acc[...] + total if again else total

    def features_of(source, ft, order, rimmed):
        for level in range(levels):
            v = source[level]
            spread(v, level, DEEP, ft, ftx, fth, rimmed)
            spread(0.5 * (east_of(v) - west_of(v)), levels + level, DEEP, ft, ftx, fth, rimmed)
            spread(0.5 * (north_of(v) - south_of(v)), 2 * levels + level, DEEP, ft, ftx, fth, rimmed)
        pack_halo(order, DEEP, ft, ftx, fth)

    def force(v, level, closed):
        eastward, westward, northward, southward = east_of(v), west_of(v), north_of(v), south_of(v)
        laplace = eastward + westward + northward + southward - 4.0 * v
        slope = 0.5 * (eastward - westward)
        return planes[count - 1] * (KAPPA * laplace - planes[2 * levels + level] * slope + closed)

    features_of(planes, ft1, rim, True)
    for k, ref in enumerate(early[2::3]):
        cl[pl.ds(k * ref.shape[0], ref.shape[0]), :] = ref[...]

    def first_part(base, tiles):
        first, second, unused, low_second = yield from forward_stages(inputs_at(ft1, base, tiles), wi_t, wm_t)
        halo1[...] = first
        halo2[...] = second
        yield
        put_lanes(cl, SHALLOW, base, tiles, closure(low_second, wo_t))

    staggered([first_part(rows, len(rim))])
    unpack_halo(rim, SHALLOW, cl, clx, clh)
    for level in range(levels):
        closed = gathered(level, SHALLOW, cl, clx, clh, True)
        mid = planes[levels + level] + 2.0 * DT * force(planes[level], level, closed)
        o_mid[level] = mid[:rows, :LANES]
        mids[level] = mid

    features_of(mids, ft2, outer, False)
    for level in range(levels):
        masked = planes[count - 1] * (2.0 * DT * planes[3 * levels + level])
        spread(masked, level, SHALLOW, dc, dcx, dch, False)
    pack_halo(outer, SHALLOW, dc, dcx, dch)
    sums = [None] * 3
    staggered(
        [second_part(rows, len(outer), None)] + [second_part(k * PART, PART, sums) for k in range(rows // PART)]
    )
    keep_terms(sums, False)
    unpack_halo(outer, DEEP, df, dfx, dfh)

    def adjoint_of(weighted, level, rimmed):
        masked = planes[count - 1] * weighted
        carried = planes[2 * levels + level] * masked
        a0 = gathered(level, DEEP, df, dfx, dfh, rimmed)
        a1 = gathered(levels + level, DEEP, df, dfx, dfh, rimmed)
        a2 = gathered(2 * levels + level, DEEP, df, dfx, dfh, rimmed)
        result = KAPPA * (east_of(masked) + west_of(masked) + north_of(masked) + south_of(masked) - 4.0 * masked)
        result = result + 0.5 * (east_of(carried) - west_of(carried)) + a0
        return result - 0.5 * (east_of(a1) - west_of(a1)) - 0.5 * (north_of(a2) - south_of(a2))

    for level in range(levels):
        closed = jnp.concatenate([cl[pl.ds(level, rows, stride=SHALLOW), :], jnp.zeros((2 * WIDE, LANES), F32)], 0)
        closed = jnp.concatenate([closed, jnp.zeros_like(closed)], 1)
        new = planes[level] + 2.0 * DT * force(mids[level], level, closed)
        o_new[level] = new[:rows, :LANES]
        grad = planes[4 * levels + level] + adjoint_of(2.0 * DT * planes[3 * levels + level], level, False)
        o_old[level] = grad[:rows, :LANES]
        olds[level] = grad

    row = lax.broadcasted_iota(jnp.int32, (ext, LANES), 0)
    inside = (lane > 0) & (lane < LANES - 1) & (row > 0) & (row < rows - 1)
    for level in range(levels):
        masked = planes[count - 1] * (2.0 * DT * olds[level])
        body = masked[:, :LANES]
        dc[pl.ds(level, rows, stride=SHALLOW), :] = jnp.where(inside, body, 0.0)[:rows]
        dcx[pl.ds(level, 2 * WIDE, stride=SHALLOW), :] = body[rows:]
        dch[pl.ds(level, ext, stride=SHALLOW), :] = with_rim(masked)
        for k, r in enumerate(rim[:2]):
            dc[pl.ds((rows + k) * SHALLOW + level, 1), :] = body[r : r + 1]
    pack_halo(rim[:rim_near], SHALLOW, dc, dcx, dch, False)
    at = lax.broadcasted_iota(jnp.int32, (1, rim_near * LANES), 1)
    tile, place = at >> 7, at & (LANES - 1)
    side_row = (tile - 4) * 16 + (place >> 3)
    edge = ((place & 7) == 0) | ((place & 7) == 7)
    counted = (tile < 2) | ((tile >= 4) & edge & (side_row > 0) & (side_row < rows - 1))
    near = pl.ds(0, rim_near * LANES)
    sums = [None] * 3
    staggered(
        [third_part(rows, rim_near, halo1.at[:, near], halo2.at[:, near], counted, sums)]
        + [third_part(k * PART, PART, kept1[k], kept2[k], None, sums) for k in range(rows // PART)]
    )
    keep_terms(sums, True)
    unpack_halo(rim[:rim_near], DEEP, df, dfx, dfh)
    for level in range(levels):
        grad = adjoint_of(2.0 * DT * olds[level], level, True)
        o_now[level] = planes[3 * levels + level, pl.ds(0, rows), pl.ds(0, LANES)] + grad[:rows, :LANES]

    start = 0
    for acc in (acc_mid, acc_in, acc_out):
        deep = acc.shape[0]
        for half in range(hidden // LANES):
            o_grad[pl.ds(start, deep), :] = acc[:, half * LANES : (half + 1) * LANES]
            start += deep
    if start < o_grad.shape[0]:
        o_grad[pl.ds(start, o_grad.shape[0] - start), :] = jnp.zeros((o_grad.shape[0] - start, LANES), F32)


def scale_kernel(factor, *refs):
    terms, (g_in, g_mid, g_out) = refs[:SHARES], refs[SHARES:]
    share = terms[0].shape[0]
    hidden = g_mid.shape[0]
    start = 0
    for ref, deep in ((g_mid, hidden), (g_in, DEEP), (g_out, DEEP)):
        for half in range(hidden // LANES):
            at, end = start, start + ref.shape[0]
            while at < end:
                k, first = divmod(at, share)
                some = min(end - at, share - first)
                piece = terms[k][pl.ds(first, some), :]
                ref[pl.ds(at - start, some), half * LANES : (half + 1) * LANES] = piece * factor
                at += some
            start += deep


def along(value, axis, step):
    count = lax.axis_size(axis)
    return lax.ppermute(value, axis, [(i, (i + step) % count) for i in range(count)])


def swapped(value, axis, bit):
    return lax.ppermute(value, axis, [(i, i ^ bit) for i in range(lax.axis_size(axis))])


def summed_over(values, place, halving, doubling):
    bits = []
    bit = 1
    while bit < lax.axis_size(halving):
        upper = (place & bit) != 0
        half = values[0].shape[0] // 2
        got = [swapped(jnp.where(upper, v[:half], v[half:]), halving, bit) for v in values]
        values = [jnp.where(upper, v[half:], v[:half]) + g for v, g in zip(values, got)]
        bits.append((bit, upper))
        bit *= 2
    bit = 1
    while bit < lax.axis_size(doubling):
        got = [swapped(v, doubling, bit) for v in values]
        values = [v + g for v, g in zip(values, got)]
        bit *= 2
    for bit, upper in reversed(bits):
        got = [swapped(v, halving, bit) for v in values]
        values = [
            jnp.concatenate([jnp.where(upper, g, v), jnp.where(upper, v, g)], 0) for v, g in zip(values, got)
        ]
    return values


def body(state_old, state_now, drift, ocean, w_in, w_mid, w_out, cot_mid, cot_new):
    levels, rows, cols = state_now.shape
    width_in, hidden = w_in.shape
    ext = rows + 2 * WIDE
    count = 5 * levels + 1
    packs = -(-ext // 16)
    slots = rows + 8 + packs
    tall = rows // EARLY
    vmem = pl.BlockSpec(memory_space=pltpu.VMEM)
    strip = jax.ShapeDtypeStruct((rows, LANES), F32)
    edge = jax.ShapeDtypeStruct((count, WIDE, LANES), F32)
    arrays = (state_now, state_old, drift, cot_new, cot_mid, ocean)
    west, east, top, bottom, fields = pl.pallas_call(
        pack_kernel,
        out_shape=(strip, strip, edge, edge, jax.ShapeDtypeStruct((count, rows, cols), F32)),
        in_specs=[pl.BlockSpec(memory_space=pltpu.HBM)] * 6,
        out_specs=(vmem,) * 5,
        scratch_shapes=[pltpu.VMEM((rows, cols), jnp.int32), pltpu.SemaphoreType.DMA((6,))],
        compiler_params=pltpu.CompilerParams(vmem_limit_bytes=8 * 2**20),
    )(*(pltpu.with_memory_space_constraint(a, pltpu.HBM) for a in arrays))

    kept = jax.ShapeDtypeStruct((tall // PART, hidden, PART * LANES), F32)
    closed = jax.ShapeDtypeStruct((tall * SHALLOW, LANES), F32)
    tall_weight = jax.ShapeDtypeStruct((hidden, DEEP), BF16)
    flat_weight = jax.ShapeDtypeStruct((DEEP, hidden), BF16)
    prepared = (flat_weight, tall_weight, jax.ShapeDtypeStruct((hidden, hidden), BF16), tall_weight, flat_weight)

    def early(k, extra, extra_out):
        return pl.pallas_call(
            functools.partial(early_kernel, k * tall),
            out_shape=(kept, kept, closed) + extra_out,
            in_specs=[vmem] * (1 + len(extra)),
            out_specs=(vmem,) * (3 + len(extra_out)),
            scratch_shapes=[pltpu.VMEM((tall * DEEP, LANES), F32)],
            compiler_params=pltpu.CompilerParams(vmem_limit_bytes=12 * 2**20),
            cost_estimate=pl.CostEstimate(
                flops=6 * hidden * hidden * tall * cols, bytes_accessed=0, transcendentals=2 * hidden * tall * cols
            ),
        )(fields, *extra)

    left = along(east, "lon", 1)
    right = along(west, "lon", -1)
    *first_kept, wi, wi_t, wm_t, wo, wo_t = early(0, (w_in, w_mid, w_out.T), prepared)
    message = jax.ShapeDtypeStruct((count + 2, WIDE, LANES), F32)
    up, down = pl.pallas_call(
        join_kernel,
        out_shape=(message, message),
        in_specs=[vmem] * 4,
        out_specs=(vmem,) * 2,
        compiler_params=pltpu.CompilerParams(vmem_limit_bytes=4 * 2**20),
    )(top, bottom, left, right)
    low = along(up, "lat", 1)
    high = along(down, "lat", -1)
    done = list(first_kept)
    for k in range(1, EARLY):
        done += early(k, (left, wi_t, wm_t, wo_t), ())

    halves = hidden // LANES
    grain = 8 * SHARES * lax.axis_size("lat")
    terms_rows = -(-halves * (hidden + 2 * DEEP) // grain) * grain
    field = jax.ShapeDtypeStruct((levels, rows, cols), F32)
    ext_planes = pltpu.VMEM((levels, ext, 2 * LANES), F32)

    def tiles(deep):
        return [pltpu.VMEM((n * deep, LANES), F32) for n in (slots, 16 * packs, 2 * WIDE)]

    kept_halo = pltpu.VMEM((hidden, (8 + packs) * LANES), F32)
    state_mid, state_new, grad_old, grad_now, terms, place = pl.pallas_call(
        functools.partial(main_kernel, lax.axis_size("lat")),
        out_shape=(field, field, field, field, jax.ShapeDtypeStruct((terms_rows, LANES), F32), jax.ShapeDtypeStruct((8, LANES), jnp.int32)),
        in_specs=[vmem] * (11 + 3 * EARLY),
        out_specs=(vmem,) * 6,
        scratch_shapes=[
            pltpu.VMEM((count, ext, 2 * LANES), F32),
            ext_planes,
            ext_planes,
            tiles(DEEP)[0],
            *tiles(DEEP),
            *tiles(SHALLOW),
            *tiles(SHALLOW),
            *tiles(DEEP),
            kept_halo,
            kept_halo,
            pltpu.VMEM((hidden, hidden), F32),
            pltpu.VMEM((DEEP, hidden), F32),
            pltpu.VMEM((DEEP, hidden), F32),
        ],
        compiler_params=pltpu.CompilerParams(vmem_limit_bytes=34 * 2**20),
    )(fields, left, right, low, high, wi, wi_t, wm_t, w_mid, wo, wo_t, *done)

    summed = summed_over(jnp.split(terms, SHARES), place[:1], "lat", "lon")
    cells_all = rows * lax.axis_size("lat") * cols * lax.axis_size("lon")
    grad_in, grad_mid, grad_out = pl.pallas_call(
        functools.partial(scale_kernel, GAIN_GRAD / cells_all**0.5),
        out_shape=(
            jax.ShapeDtypeStruct((width_in, hidden), F32),
            jax.ShapeDtypeStruct((hidden, hidden), F32),
            jax.ShapeDtypeStruct((levels, hidden), F32),
        ),
        in_specs=[vmem] * SHARES,
        out_specs=(vmem,) * 3,
        compiler_params=pltpu.CompilerParams(vmem_limit_bytes=8 * 2**20),
    )(*summed)
    return state_mid, state_new, grad_old, grad_now, grad_in, grad_mid, grad_out.T


def solution(mesh):
    field = P("grp", "lat", "lon")
    whole = P("grp", None)
    in_specs = (field, field, field, P(("grp", "lat"), "lon"), P(), P(), P(), field, field)
    out_specs = (field, field, field, field, whole, whole, whole)
    return jax.shard_map(body, mesh=mesh, in_specs=in_specs, out_specs=out_specs, check_vma=False)
```

```python
import functools

import jax
import jax.numpy as jnp
from jax import lax
from jax.experimental import pallas as pl
from jax.experimental.pallas import tpu as pltpu
from jax.sharding import PartitionSpec as P

KAPPA = 0.2
DT = 0.1
GAIN_GRAD = 10.0

WIDE = 4
LANES = 128
PART = 8
EARLY = 2
SHARES = 1
DEEP = 16
SHALLOW = 8

F32 = jnp.float32
BF16 = jnp.bfloat16


def dot(left, right):
    return lax.dot_general(left, right, (((1,), (0,)), ((), ())), preferred_element_type=F32)


def dot_nt(left, right):
    return lax.dot_general(left, right, (((1,), (1,)), ((), ())), preferred_element_type=F32)


def pack_kernel(now, old, drift, cnew, cmid, ocean, west, east, top, bottom, fields, wet, sems):
    levels, rows, cols = now.shape
    copies = [
        pltpu.make_async_copy(ref, fields.at[pl.ds(levels * f, levels)], sems.at[f])
        for f, ref in enumerate((now, old, drift, cnew, cmid))
    ]
    copies.append(pltpu.make_async_copy(ocean, wet, sems.at[5]))
    for copy in copies:
        copy.start()
    lane = lax.broadcasted_iota(jnp.int32, (rows, LANES), 1)
    to_west = jnp.zeros((rows, LANES), F32)
    to_east = jnp.zeros((rows, LANES), F32)
    count = fields.shape[0]
    for p in range(count):
        if p % levels == 0:
            copies[p // levels].wait()
        if p == count - 1:
            fields[p] = wet[...].astype(F32)
        plane = fields[p]
        here = (lane >= WIDE * p) & (lane < WIDE * (p + 1))
        to_west = jnp.where(here, pltpu.roll(plane, WIDE * p, 1) if p else plane, to_west)
        to_east = jnp.where(here, pltpu.roll(plane, WIDE * (p + 1), 1), to_east)
        top[p] = plane[:WIDE]
        bottom[p] = plane[rows - WIDE :]
    west[...] = to_west
    east[...] = to_east


def join_kernel(top, bottom, left, right, up, down):
    count = top.shape[0]
    rows = left.shape[0]
    up[pl.ds(0, count)] = bottom[...]
    down[pl.ds(0, count)] = top[...]
    for k, strip in enumerate((left, right)):
        up[count + k] = strip[pl.ds(rows - WIDE, WIDE), :]
        down[count + k] = strip[pl.ds(0, WIDE), :]


def east_of(v):
    return pltpu.roll(v, v.shape[1] - 1, 1)


def west_of(v):
    return pltpu.roll(v, 1, 1)


def north_of(v):
    return pltpu.roll(v, v.shape[0] - 1, 0)


def south_of(v):
    return pltpu.roll(v, 1, 0)


def forward_stages(x, w_first_t, w_second_t):
    z_one = dot(w_first_t[...], x)
    yield
    first = jnp.tanh(z_one)
    low_first = first.astype(BF16)
    yield
    z_two = dot(w_second_t[...], low_first)
    yield
    second = jnp.tanh(z_two)
    return first, second, low_first, second.astype(BF16)


def closure(low_second, w_last_t):
    return dot(w_last_t[...], low_second).astype(BF16).astype(F32)[:SHALLOW]


def staggered(generators):
    live = []
    waiting = list(generators)
    while live or waiting:
        if waiting:
            live.append(waiting.pop(0))
        for part in list(live):
            try:
                next(part)
            except StopIteration:
                live.remove(part)


def lanes_of(ref, deep, base, tiles):
    block = ref[pl.ds(base * deep, tiles * deep), :]
    return jnp.concatenate([block[k * deep : (k + 1) * deep] for k in range(tiles)], 1)


def put_lanes(ref, deep, base, tiles, value):
    for k in range(tiles):
        ref[pl.ds((base + k) * deep, deep), :] = value[:, k * LANES : (k + 1) * LANES]


def early_kernel(start, fields, *refs):
    if start == 0:
        w_in, w_mid, w_out_t, keep1, keep2, cl, wi, wi_t, wm_t, wo, wo_t, ft = refs
        width_in, hidden = w_in.shape
        levels = w_out_t.shape[0]
        spare = jnp.zeros((DEEP - width_in, hidden), F32)
        wide_in = jnp.concatenate([w_in[...].astype(F32), spare], 0)
        wi[...] = wide_in.astype(BF16)
        wi_t[...] = wide_in.T.astype(BF16)
        wm_t[...] = w_mid[...].astype(F32).T.astype(BF16)
        spare = jnp.zeros((DEEP - levels, hidden), F32)
        wide_out = jnp.concatenate([w_out_t[...].astype(F32), spare], 0)
        wo_t[...] = wide_out.astype(BF16)
        wo[...] = wide_out.T.astype(BF16)
    else:
        unused, wi_t, wm_t, wo_t, keep1, keep2, cl, ft = refs
        levels = (fields.shape[0] - 1) // 5
    tall = cl.shape[0] // SHALLOW
    ft[...] = jnp.zeros_like(ft)
    for level in range(levels):
        v = fields[level]
        slope_x = 0.5 * (east_of(v) - west_of(v))
        slope_y = 0.5 * (north_of(v) - south_of(v))
        for f, plane in enumerate((v, slope_x, slope_y)):
            ft[pl.ds(f * levels + level, tall, stride=DEEP), :] = plane[start : start + tall]

    def part(base, kept1, kept2):
        x = lanes_of(ft, DEEP, base, PART).astype(BF16)
        first, second, unused_low, low_second = yield from forward_stages(x, wi_t, wm_t)
        kept1[...] = first
        kept2[...] = second
        yield
        put_lanes(cl, SHALLOW, base, PART, closure(low_second, wo_t))

    staggered(part(k * PART, keep1.at[k], keep2.at[k]) for k in range(tall // PART))


def main_kernel(bands, *refs):
    fields, left, right, low, high, wi, wi_t, wm_t, w_mid, wo, wo_t, *refs = refs
    early, refs = refs[: 3 * EARLY], refs[3 * EARLY :]
    o_mid, o_new, o_old, o_now, o_grad, o_place, planes, mids, olds, *refs = refs
    ft1, ft2, fth, ftx, cl, clh, clx, dc, dch, dcx, df, dfh, dfx, halo1, halo2, acc_mid, acc_in, acc_out = refs
    levels, rows, cols = o_mid.shape
    hidden = w_mid.shape[0]
    count = 5 * levels + 1
    ext = rows + 2 * WIDE
    packs = -(-ext // 16)
    kept1 = [ref.at[k] for ref in early[0::3] for k in range(ref.shape[0])]
    kept2 = [ref.at[k] for ref in early[1::3] for k in range(ref.shape[0])]
    packed = [None] * packs
    rim = [0, rows - 1, rows, ext - 1] + packed + [rows + 1, ext - 2, rows + 2, ext - 3]
    rim_near = 4 + packs
    outer = [rows, ext - 1] + packed + [rows + 1, ext - 2]

    lane = lax.broadcasted_iota(jnp.int32, (ext, LANES), 1)
    band = lax.axis_index("lat")
    o_place[...] = jnp.zeros_like(o_place) + band
    has_low = jnp.where(band > 0, 1.0, 0.0)
    has_high = jnp.where(band < bands - 1, 1.0, 0.0)

    def beyond(p):
        return [high[p] * has_high, low[p] * has_low]

    left_all = jnp.concatenate([left[...]] + beyond(count), 0)
    right_all = jnp.concatenate([right[...]] + beyond(count + 1), 0)
    for p in range(count):
        from_right = pltpu.roll(right_all, LANES - WIDE * p, 1) if p else right_all
        from_left = pltpu.roll(left_all, LANES - WIDE * (p + 1), 1)
        side = jnp.where(lane < WIDE, from_right, jnp.where(lane >= LANES - WIDE, from_left, 0.0))
        planes[p, :, pl.ds(0, LANES)] = jnp.concatenate([fields[p]] + beyond(p), 0)
        planes[p, :, pl.ds(LANES, LANES)] = side

    for ref in (ft1, ft2, fth, ftx, dc, dch, dcx):
        ref[...] = jnp.zeros_like(ref)

    def with_rim(plane):
        body, side = plane[:, :LANES], plane[:, LANES:]
        own = jnp.where(lane == LANES - WIDE, pltpu.roll(body, LANES - WIDE, 1), pltpu.roll(body, WIDE, 1))
        return jnp.where((lane == LANES - WIDE) | (lane == WIDE - 1), own, side)

    def from_rim(body, side):
        own = jnp.where(lane == 0, pltpu.roll(side, WIDE, 1), pltpu.roll(side, LANES - WIDE, 1))
        return jnp.where((lane == 0) | (lane == LANES - 1), own, body)

    def spread(plane, index, deep, main, extra, side, rimmed):
        main[pl.ds(index, rows, stride=deep), :] = plane[:rows, :LANES]
        extra[pl.ds(index, 2 * WIDE, stride=deep), :] = plane[rows:, :LANES]
        side[pl.ds(index, ext, stride=deep), :] = with_rim(plane) if rimmed else plane[:, LANES:]

    def gathered(index, deep, main, extra, side, rimmed):
        body = jnp.concatenate(
            [main[pl.ds(index, rows, stride=deep), :], extra[pl.ds(index, 2 * WIDE, stride=deep), :]], 0
        )
        beside = side[pl.ds(index, ext, stride=deep), :]
        return jnp.concatenate([from_rim(body, beside) if rimmed else body, beside], 1)

    def home(r, deep, main, extra):
        return main.at[pl.ds(r * deep, deep)] if r < rows else extra.at[pl.ds((r - rows) * deep, deep)]

    def pack_halo(order, deep, main, extra, side, rim_too=True):
        where = lax.broadcasted_iota(jnp.int32, (deep, LANES), 1)
        for i, r in enumerate(order):
            if r is not None and (rim_too or r >= rows):
                main[pl.ds((rows + i) * deep, deep), :] = home(r, deep, main, extra)[...]
        first_pack = rows + order.index(None)
        for q in range(packs):
            total = jnp.zeros((deep, LANES), F32)
            for j in range(min(16, ext - 16 * q)):
                moved = pltpu.roll(side[pl.ds((16 * q + j) * deep, deep), :], (2 * WIDE * j + WIDE) % LANES, 1)
                total = jnp.where((where >= 2 * WIDE * j) & (where < 2 * WIDE * (j + 1)), moved, total)
            main[pl.ds((first_pack + q) * deep, deep), :] = total

    def unpack_halo(order, deep, main, extra, side):
        for i, r in enumerate(order):
            if r is not None:
                home(r, deep, main, extra)[...] = main[pl.ds((rows + i) * deep, deep), :]
        first_pack = rows + order.index(None)
        for q in range(packs):
            tile = main[pl.ds((first_pack + q) * deep, deep), :]
            for j in range(min(16, ext - 16 * q)):
                moved = pltpu.roll(tile, LANES - (2 * WIDE * j + WIDE) % LANES, 1)
                side[pl.ds((16 * q + j) * deep, deep), :] = moved

    def inputs_at(ref, base, tiles):
        return lanes_of(ref, DEEP, base, tiles).astype(BF16)

    def cotangents_at(base, tiles):
        part = lanes_of(dc, SHALLOW, base, tiles)
        return jnp.concatenate([part, jnp.zeros_like(part)], 0).astype(BF16)

    def backward_stages(first, second, cot):
        g_two = dot(wo[...], cot)
        yield
        dz_two = (g_two * (1.0 - second * second)).astype(BF16)
        yield
        g_one = dot(w_mid[...], dz_two)
        yield
        dz_one = (g_one * (1.0 - first * first)).astype(BF16)
        yield
        return dz_one, dz_two, dot(wi[...], dz_one).astype(BF16).astype(F32)

    def second_part(base, tiles, sums):
        x = inputs_at(ft2, base, tiles)
        cot = cotangents_at(base, tiles)
        first, second, low_first, low_second = yield from forward_stages(x, wi_t, wm_t)
        yield
        if sums is not None:
            put_lanes(cl, SHALLOW, base, tiles, closure(low_second, wo_t))
        dz_one, dz_two, dfeat = yield from backward_stages(first, second, cot)
        if sums is not None:
            add_terms(sums, (low_first, dz_two), (x, dz_one), (low_second, cot))
        yield
        put_lanes(df, DEEP, base, tiles, dfeat)

    def third_part(base, tiles, held1, held2, counted, sums):
        cot = cotangents_at(base, tiles)
        first = held1[...]
        second = held2[...]
        dz_one, dz_two, dfeat = yield from backward_stages(first, second, cot)
        x = inputs_at(ft1, base, tiles)
        if counted is not None:
            dz_one, dz_two, cot = (jnp.where(counted, v.astype(F32), 0.0).astype(BF16) for v in (dz_one, dz_two, cot))
        add_terms(sums, (first.astype(BF16), dz_two), (x, dz_one), (second.astype(BF16), cot))
        yield
        put_lanes(df, DEEP, base, tiles, dfeat)

    def add_terms(sums, *pairs):
        for k, pair in enumerate(pairs):
            sums[k] = dot_nt(*pair) if sums[k] is None else sums[k] + dot_nt(*pair)

    def keep_terms(sums, again):
        for acc, total in zip((acc_mid, acc_in, acc_out), sums):
            acc[...] = acc[...] + total if again else total

    def features_of(source, ft, order, rimmed):
        for level in range(levels):
            v = source[level]
            spread(v, level, DEEP, ft, ftx, fth, rimmed)
            spread(0.5 * (east_of(v) - west_of(v)), levels + level, DEEP, ft, ftx, fth, rimmed)
            spread(0.5 * (north_of(v) - south_of(v)), 2 * levels + level, DEEP, ft, ftx, fth, rimmed)
        pack_halo(order, DEEP, ft, ftx, fth)

    def force(v, level, closed):
        eastward, westward, northward, southward = east_of(v), west_of(v), north_of(v), south_of(v)
        laplace = eastward + westward + northward + southward - 4.0 * v
        slope = 0.5 * (eastward - westward)
        return planes[count - 1] * (KAPPA * laplace - planes[2 * levels + level] * slope + closed)

    features_of(planes, ft1, rim, True)
    for k, ref in enumerate(early[2::3]):
        cl[pl.ds(k * ref.shape[0], ref.shape[0]), :] = ref[...]

    def first_part(base, tiles):
        first, second, unused, low_second = yield from forward_stages(inputs_at(ft1, base, tiles), wi_t, wm_t)
        halo1[...] = first
        halo2[...] = second
        yield
        put_lanes(cl, SHALLOW, base, tiles, closure(low_second, wo_t))

    staggered([first_part(rows, len(rim))])
    unpack_halo(rim, SHALLOW, cl, clx, clh)
    for level in range(levels):
        closed = gathered(level, SHALLOW, cl, clx, clh, True)
        mid = planes[levels + level] + 2.0 * DT * force(planes[level], level, closed)
        o_mid[level] = mid[:rows, :LANES]
        mids[level] = mid

    features_of(mids, ft2, outer, False)
    for level in range(levels):
        masked = planes[count - 1] * (2.0 * DT * planes[3 * levels + level])
        spread(masked, level, SHALLOW, dc, dcx, dch, False)
    pack_halo(outer, SHALLOW, dc, dcx, dch)
    sums = [None] * 3
    staggered(
        [second_part(rows, len(outer), None)] + [second_part(k * PART, PART, sums) for k in range(rows // PART)]
    )
    keep_terms(sums, False)
    unpack_halo(outer, DEEP, df, dfx, dfh)

    def adjoint_of(weighted, level, rimmed):
        masked = planes[count - 1] * weighted
        carried = planes[2 * levels + level] * masked
        a0 = gathered(level, DEEP, df, dfx, dfh, rimmed)
        a1 = gathered(levels + level, DEEP, df, dfx, dfh, rimmed)
        a2 = gathered(2 * levels + level, DEEP, df, dfx, dfh, rimmed)
        result = KAPPA * (east_of(masked) + west_of(masked) + north_of(masked) + south_of(masked) - 4.0 * masked)
        result = result + 0.5 * (east_of(carried) - west_of(carried)) + a0
        return result - 0.5 * (east_of(a1) - west_of(a1)) - 0.5 * (north_of(a2) - south_of(a2))

    for level in range(levels):
        closed = jnp.concatenate([cl[pl.ds(level, rows, stride=SHALLOW), :], jnp.zeros((2 * WIDE, LANES), F32)], 0)
        closed = jnp.concatenate([closed, jnp.zeros_like(closed)], 1)
        new = planes[level] + 2.0 * DT * force(mids[level], level, closed)
        o_new[level] = new[:rows, :LANES]
        grad = planes[4 * levels + level] + adjoint_of(2.0 * DT * planes[3 * levels + level], level, False)
        o_old[level] = grad[:rows, :LANES]
        olds[level] = grad

    row = lax.broadcasted_iota(jnp.int32, (ext, LANES), 0)
    inside = (lane > 0) & (lane < LANES - 1) & (row > 0) & (row < rows - 1)
    for level in range(levels):
        masked = planes[count - 1] * (2.0 * DT * olds[level])
        body = masked[:, :LANES]
        dc[pl.ds(level, rows, stride=SHALLOW), :] = jnp.where(inside, body, 0.0)[:rows]
        dcx[pl.ds(level, 2 * WIDE, stride=SHALLOW), :] = body[rows:]
        dch[pl.ds(level, ext, stride=SHALLOW), :] = with_rim(masked)
        for k, r in enumerate(rim[:2]):
            dc[pl.ds((rows + k) * SHALLOW + level, 1), :] = body[r : r + 1]
    pack_halo(rim[:rim_near], SHALLOW, dc, dcx, dch, False)
    at = lax.broadcasted_iota(jnp.int32, (1, rim_near * LANES), 1)
    tile, place = at >> 7, at & (LANES - 1)
    side_row = (tile - 4) * 16 + (place >> 3)
    edge = ((place & 7) == 0) | ((place & 7) == 7)
    counted = (tile < 2) | ((tile >= 4) & edge & (side_row > 0) & (side_row < rows - 1))
    near = pl.ds(0, rim_near * LANES)
    sums = [None] * 3
    staggered(
        [third_part(rows, rim_near, halo1.at[:, near], halo2.at[:, near], counted, sums)]
        + [third_part(k * PART, PART, kept1[k], kept2[k], None, sums) for k in range(rows // PART)]
    )
    keep_terms(sums, True)
    unpack_halo(rim[:rim_near], DEEP, df, dfx, dfh)
    for level in range(levels):
        grad = adjoint_of(2.0 * DT * olds[level], level, True)
        o_now[level] = planes[3 * levels + level, pl.ds(0, rows), pl.ds(0, LANES)] + grad[:rows, :LANES]

    start = 0
    for total in (acc_mid[...], acc_in[...], acc_out[...].T):
        deep = total.shape[0]
        for half in range(hidden // LANES):
            o_grad[pl.ds(start, deep), :] = total[:, half * LANES : (half + 1) * LANES]
            start += deep
    if start < o_grad.shape[0]:
        o_grad[pl.ds(start, o_grad.shape[0] - start), :] = jnp.zeros((o_grad.shape[0] - start, LANES), F32)


def scale_kernel(factor, *refs):
    terms, (g_in, g_mid, g_out) = refs[:SHARES], refs[SHARES:]
    share = terms[0].shape[0]
    hidden = g_mid.shape[0]
    start = 0
    for ref, deep in ((g_mid, hidden), (g_in, DEEP), (g_out, DEEP)):
        for half in range(hidden // LANES):
            at, end = start, start + ref.shape[0]
            while at < end:
                k, first = divmod(at, share)
                some = min(end - at, share - first)
                piece = terms[k][pl.ds(first, some), :]
                ref[pl.ds(at - start, some), half * LANES : (half + 1) * LANES] = piece * factor
                at += some
            start += deep


def along(value, axis, step):
    count = lax.axis_size(axis)
    return lax.ppermute(value, axis, [(i, (i + step) % count) for i in range(count)])


def swapped(value, axis, bit):
    return lax.ppermute(value, axis, [(i, i ^ bit) for i in range(lax.axis_size(axis))])


def summed_over(values, place, halving, doubling):
    bits = []
    bit = 1
    while bit < lax.axis_size(halving):
        upper = (place & bit) != 0
        half = values[0].shape[0] // 2
        got = [swapped(jnp.where(upper, v[:half], v[half:]), halving, bit) for v in values]
        values = [jnp.where(upper, v[half:], v[:half]) + g for v, g in zip(values, got)]
        bits.append((bit, upper))
        bit *= 2
    bit = 1
    while bit < lax.axis_size(doubling):
        got = [swapped(v, doubling, bit) for v in values]
        values = [v + g for v, g in zip(values, got)]
        bit *= 2
    for bit, upper in reversed(bits):
        got = [swapped(v, halving, bit) for v in values]
        values = [
            jnp.concatenate([jnp.where(upper, g, v), jnp.where(upper, v, g)], 0) for v, g in zip(values, got)
        ]
    return values


def body(state_old, state_now, drift, ocean, w_in, w_mid, w_out, cot_mid, cot_new):
    levels, rows, cols = state_now.shape
    width_in, hidden = w_in.shape
    ext = rows + 2 * WIDE
    count = 5 * levels + 1
    packs = -(-ext // 16)
    slots = rows + 8 + packs
    tall = rows // EARLY
    vmem = pl.BlockSpec(memory_space=pltpu.VMEM)
    strip = jax.ShapeDtypeStruct((rows, LANES), F32)
    edge = jax.ShapeDtypeStruct((count, WIDE, LANES), F32)
    arrays = (state_now, state_old, drift, cot_new, cot_mid, ocean)
    west, east, top, bottom, fields = pl.pallas_call(
        pack_kernel,
        out_shape=(strip, strip, edge, edge, jax.ShapeDtypeStruct((count, rows, cols), F32)),
        in_specs=[pl.BlockSpec(memory_space=pltpu.HBM)] * 6,
        out_specs=(vmem,) * 5,
        scratch_shapes=[pltpu.VMEM((rows, cols), jnp.int32), pltpu.SemaphoreType.DMA((6,))],
        compiler_params=pltpu.CompilerParams(vmem_limit_bytes=8 * 2**20),
    )(*(pltpu.with_memory_space_constraint(a, pltpu.HBM) for a in arrays))

    kept = jax.ShapeDtypeStruct((tall // PART, hidden, PART * LANES), F32)
    closed = jax.ShapeDtypeStruct((tall * SHALLOW, LANES), F32)
    tall_weight = jax.ShapeDtypeStruct((hidden, DEEP), BF16)
    flat_weight = jax.ShapeDtypeStruct((DEEP, hidden), BF16)
    prepared = (flat_weight, tall_weight, jax.ShapeDtypeStruct((hidden, hidden), BF16), tall_weight, flat_weight)

    def early(k, extra, extra_out):
        return pl.pallas_call(
            functools.partial(early_kernel, k * tall),
            out_shape=(kept, kept, closed) + extra_out,
            in_specs=[vmem] * (1 + len(extra)),
            out_specs=(vmem,) * (3 + len(extra_out)),
            scratch_shapes=[pltpu.VMEM((tall * DEEP, LANES), F32)],
            compiler_params=pltpu.CompilerParams(vmem_limit_bytes=12 * 2**20),
            cost_estimate=pl.CostEstimate(
                flops=6 * hidden * hidden * tall * cols, bytes_accessed=0, transcendentals=2 * hidden * tall * cols
            ),
        )(fields, *extra)

    left = along(east, "lon", 1)
    right = along(west, "lon", -1)
    *first_kept, wi, wi_t, wm_t, wo, wo_t = early(0, (w_in, w_mid, w_out.T), prepared)
    message = jax.ShapeDtypeStruct((count + 2, WIDE, LANES), F32)
    up, down = pl.pallas_call(
        join_kernel,
        out_shape=(message, message),
        in_specs=[vmem] * 4,
        out_specs=(vmem,) * 2,
        compiler_params=pltpu.CompilerParams(vmem_limit_bytes=4 * 2**20),
    )(top, bottom, left, right)
    low = along(up, "lat", 1)
    high = along(down, "lat", -1)
    done = list(first_kept)
    for k in range(1, EARLY):
        done += early(k, (left, wi_t, wm_t, wo_t), ())

    halves = hidden // LANES
    grain = 8 * SHARES * lax.axis_size("lat")
    terms_rows = -(-halves * (hidden + 2 * DEEP) // grain) * grain
    field = jax.ShapeDtypeStruct((levels, rows, cols), F32)
    ext_planes = pltpu.VMEM((levels, ext, 2 * LANES), F32)

    def tiles(deep):
        return [pltpu.VMEM((n * deep, LANES), F32) for n in (slots, 16 * packs, 2 * WIDE)]

    kept_halo = pltpu.VMEM((hidden, (8 + packs) * LANES), F32)
    state_mid, state_new, grad_old, grad_now, terms, place = pl.pallas_call(
        functools.partial(main_kernel, lax.axis_size("lat")),
        out_shape=(field, field, field, field, jax.ShapeDtypeStruct((terms_rows, LANES), F32), jax.ShapeDtypeStruct((8, LANES), jnp.int32)),
        in_specs=[vmem] * (11 + 3 * EARLY),
        out_specs=(vmem,) * 6,
        scratch_shapes=[
            pltpu.VMEM((count, ext, 2 * LANES), F32),
            ext_planes,
            ext_planes,
            tiles(DEEP)[0],
            *tiles(DEEP),
            *tiles(SHALLOW),
            *tiles(SHALLOW),
            *tiles(DEEP),
            kept_halo,
            kept_halo,
            pltpu.VMEM((hidden, hidden), F32),
            pltpu.VMEM((DEEP, hidden), F32),
            pltpu.VMEM((hidden, DEEP), F32),
        ],
        compiler_params=pltpu.CompilerParams(vmem_limit_bytes=34 * 2**20),
    )(fields, left, right, low, high, wi, wi_t, wm_t, w_mid, wo, wo_t, *done)

    summed = summed_over(jnp.split(terms, SHARES), place[:1], "lat", "lon")
    cells_all = rows * lax.axis_size("lat") * cols * lax.axis_size("lon")
    grad_in, grad_mid, grad_out = pl.pallas_call(
        functools.partial(scale_kernel, GAIN_GRAD / cells_all**0.5),
        out_shape=(
            jax.ShapeDtypeStruct((width_in, hidden), F32),
            jax.ShapeDtypeStruct((hidden, hidden), F32),
            jax.ShapeDtypeStruct((levels, hidden), F32),
        ),
        in_specs=[vmem] * SHARES,
        out_specs=(vmem,) * 3,
        compiler_params=pltpu.CompilerParams(vmem_limit_bytes=8 * 2**20),
    )(*summed)
    return state_mid, state_new, grad_old, grad_now, grad_in, grad_mid, grad_out.T


def solution(mesh):
    field = P("grp", "lat", "lon")
    whole = P("grp", None)
    in_specs = (field, field, field, P(("grp", "lat"), "lon"), P(), P(), P(), field, field)
    out_specs = (field, field, field, field, whole, whole, whole)
    return jax.shard_map(body, mesh=mesh, in_specs=in_specs, out_specs=out_specs, check_vma=False)
```

```python
import functools

import jax
import jax.numpy as jnp
from jax import lax
from jax.experimental import pallas as pl
from jax.experimental.pallas import tpu as pltpu
from jax.sharding import PartitionSpec as P

KAPPA = 0.2
DT = 0.1
GAIN_GRAD = 10.0

WIDE = 4
LANES = 128
PART = 8
EARLY = 2
SHARES = 1
DEEP = 16
SHALLOW = 8

F32 = jnp.float32
BF16 = jnp.bfloat16


def dot(left, right):
    return lax.dot_general(left, right, (((1,), (0,)), ((), ())), preferred_element_type=F32)


def dot_nt(left, right):
    return lax.dot_general(left, right, (((1,), (1,)), ((), ())), preferred_element_type=F32)


def pack_kernel(
    now, old, drift, cnew, cmid, ocean, w_in, w_mid, w_out,
    west, east, top, bottom, fields, v_in, v_mid, v_out, wet, sems,
):
    levels, rows, cols = now.shape
    copies = [
        pltpu.make_async_copy(ref, fields.at[pl.ds(levels * f, levels)], sems.at[f])
        for f, ref in enumerate((now, old, drift, cnew, cmid))
    ]
    copies.append(pltpu.make_async_copy(ocean, wet, sems.at[5]))
    for k, pair in enumerate(((w_in, v_in), (w_mid, v_mid), (w_out, v_out))):
        copies.append(pltpu.make_async_copy(*pair, sems.at[6 + k]))
    for copy in copies:
        copy.start()
    lane = lax.broadcasted_iota(jnp.int32, (rows, LANES), 1)
    to_west = jnp.zeros((rows, LANES), F32)
    to_east = jnp.zeros((rows, LANES), F32)
    count = fields.shape[0]
    for p in range(count):
        if p % levels == 0:
            copies[p // levels].wait()
        if p == count - 1:
            fields[p] = wet[...].astype(F32)
        plane = fields[p]
        here = (lane >= WIDE * p) & (lane < WIDE * (p + 1))
        to_west = jnp.where(here, pltpu.roll(plane, WIDE * p, 1) if p else plane, to_west)
        to_east = jnp.where(here, pltpu.roll(plane, WIDE * (p + 1), 1), to_east)
        top[p] = plane[:WIDE]
        bottom[p] = plane[rows - WIDE :]
    west[...] = to_west
    east[...] = to_east
    for copy in copies[6:]:
        copy.wait()


def join_kernel(top, bottom, left, right, up, down):
    count = top.shape[0]
    rows = left.shape[0]
    up[pl.ds(0, count)] = bottom[...]
    down[pl.ds(0, count)] = top[...]
    for k, strip in enumerate((left, right)):
        up[count + k] = strip[pl.ds(rows - WIDE, WIDE), :]
        down[count + k] = strip[pl.ds(0, WIDE), :]


def east_of(v):
    return pltpu.roll(v, v.shape[1] - 1, 1)


def west_of(v):
    return pltpu.roll(v, 1, 1)


def north_of(v):
    return pltpu.roll(v, v.shape[0] - 1, 0)


def south_of(v):
    return pltpu.roll(v, 1, 0)


def forward_stages(x, w_first_t, w_second_t):
    z_one = dot(w_first_t[...], x)
    yield
    first = jnp.tanh(z_one)
    low_first = first.astype(BF16)
    yield
    z_two = dot(w_second_t[...], low_first)
    yield
    second = jnp.tanh(z_two)
    return first, second, low_first, second.astype(BF16)


def closure(low_second, w_last_t):
    return dot(w_last_t[...], low_second).astype(BF16).astype(F32)[:SHALLOW]


def staggered(generators):
    live = []
    waiting = list(generators)
    while live or waiting:
        if waiting:
            live.append(waiting.pop(0))
        for part in list(live):
            try:
                next(part)
            except StopIteration:
                live.remove(part)


def lanes_of(ref, deep, base, tiles):
    block = ref[pl.ds(base * deep, tiles * deep), :]
    return jnp.concatenate([block[k * deep : (k + 1) * deep] for k in range(tiles)], 1)


def put_lanes(ref, deep, base, tiles, value):
    for k in range(tiles):
        ref[pl.ds((base + k) * deep, deep), :] = value[:, k * LANES : (k + 1) * LANES]


def early_kernel(start, fields, *refs):
    if start == 0:
        w_in, w_mid, w_out_t, keep1, keep2, cl, wi, wi_t, wm_t, wo, wo_t, ft = refs
        width_in, hidden = w_in.shape
        levels = w_out_t.shape[0]
        spare = jnp.zeros((DEEP - width_in, hidden), F32)
        wide_in = jnp.concatenate([w_in[...].astype(F32), spare], 0)
        wi[...] = wide_in.astype(BF16)
        wi_t[...] = wide_in.T.astype(BF16)
        wm_t[...] = w_mid[...].astype(F32).T.astype(BF16)
        spare = jnp.zeros((DEEP - levels, hidden), F32)
        wide_out = jnp.concatenate([w_out_t[...].astype(F32), spare], 0)
        wo_t[...] = wide_out.astype(BF16)
        wo[...] = wide_out.T.astype(BF16)
    else:
        unused, wi_t, wm_t, wo_t, keep1, keep2, cl, ft = refs
        levels = (fields.shape[0] - 1) // 5
    tall = cl.shape[0] // SHALLOW
    ft[...] = jnp.zeros_like(ft)
    for level in range(levels):
        v = fields[level]
        slope_x = 0.5 * (east_of(v) - west_of(v))
        slope_y = 0.5 * (north_of(v) - south_of(v))
        for f, plane in enumerate((v, slope_x, slope_y)):
            ft[pl.ds(f * levels + level, tall, stride=DEEP), :] = plane[start : start + tall]

    def part(base, kept1, kept2):
        x = lanes_of(ft, DEEP, base, PART).astype(BF16)
        first, second, unused_low, low_second = yield from forward_stages(x, wi_t, wm_t)
        kept1[...] = first
        kept2[...] = second
        yield
        put_lanes(cl, SHALLOW, base, PART, closure(low_second, wo_t))

    staggered(part(k * PART, keep1.at[k], keep2.at[k]) for k in range(tall // PART))


def copied_out(pairs, sems):
    copies = [pltpu.make_async_copy(*pair, sems.at[k]) for k, pair in enumerate(pairs)]
    for copy in copies:
        copy.start()
    return copies


def main_kernel(bands, *refs):
    fields, left, right, low, high, wi, wi_t, wm_t, w_mid, wo, wo_t, *refs = refs
    early, refs = refs[: 3 * EARLY], refs[3 * EARLY :]
    h_mid, h_new, h_old, h_now, o_grad, o_place, o_mid, o_new, o_old, o_now, sems, planes, mids, olds, *refs = refs
    ft1, ft2, fth, ftx, cl, clh, clx, dc, dch, dcx, df, dfh, dfx, halo1, halo2, acc_mid, acc_in, acc_out = refs
    levels, rows, cols = o_mid.shape
    hidden = w_mid.shape[0]
    count = 5 * levels + 1
    ext = rows + 2 * WIDE
    packs = -(-ext // 16)
    kept1 = [ref.at[k] for ref in early[0::3] for k in range(ref.shape[0])]
    kept2 = [ref.at[k] for ref in early[1::3] for k in range(ref.shape[0])]
    packed = [None] * packs
    rim = [0, rows - 1, rows, ext - 1] + packed + [rows + 1, ext - 2, rows + 2, ext - 3]
    rim_near = 4 + packs
    outer = [rows, ext - 1] + packed + [rows + 1, ext - 2]

    lane = lax.broadcasted_iota(jnp.int32, (ext, LANES), 1)
    band = lax.axis_index("lat")
    o_place[...] = jnp.zeros_like(o_place) + band
    has_low = jnp.where(band > 0, 1.0, 0.0)
    has_high = jnp.where(band < bands - 1, 1.0, 0.0)

    def beyond(p):
        return [high[p] * has_high, low[p] * has_low]

    left_all = jnp.concatenate([left[...]] + beyond(count), 0)
    right_all = jnp.concatenate([right[...]] + beyond(count + 1), 0)
    for p in range(count):
        from_right = pltpu.roll(right_all, LANES - WIDE * p, 1) if p else right_all
        from_left = pltpu.roll(left_all, LANES - WIDE * (p + 1), 1)
        side = jnp.where(lane < WIDE, from_right, jnp.where(lane >= LANES - WIDE, from_left, 0.0))
        planes[p, :, pl.ds(0, LANES)] = jnp.concatenate([fields[p]] + beyond(p), 0)
        planes[p, :, pl.ds(LANES, LANES)] = side

    for ref in (ft1, ft2, fth, ftx, dc, dch, dcx):
        ref[...] = jnp.zeros_like(ref)

    def with_rim(plane):
        body, side = plane[:, :LANES], plane[:, LANES:]
        own = jnp.where(lane == LANES - WIDE, pltpu.roll(body, LANES - WIDE, 1), pltpu.roll(body, WIDE, 1))
        return jnp.where((lane == LANES - WIDE) | (lane == WIDE - 1), own, side)

    def from_rim(body, side):
        own = jnp.where(lane == 0, pltpu.roll(side, WIDE, 1), pltpu.roll(side, LANES - WIDE, 1))
        return jnp.where((lane == 0) | (lane == LANES - 1), own, body)

    def spread(plane, index, deep, main, extra, side, rimmed):
        main[pl.ds(index, rows, stride=deep), :] = plane[:rows, :LANES]
        extra[pl.ds(index, 2 * WIDE, stride=deep), :] = plane[rows:, :LANES]
        side[pl.ds(index, ext, stride=deep), :] = with_rim(plane) if rimmed else plane[:, LANES:]

    def gathered(index, deep, main, extra, side, rimmed):
        body = jnp.concatenate(
            [main[pl.ds(index, rows, stride=deep), :], extra[pl.ds(index, 2 * WIDE, stride=deep), :]], 0
        )
        beside = side[pl.ds(index, ext, stride=deep), :]
        return jnp.concatenate([from_rim(body, beside) if rimmed else body, beside], 1)

    def home(r, deep, main, extra):
        return main.at[pl.ds(r * deep, deep)] if r < rows else extra.at[pl.ds((r - rows) * deep, deep)]

    def pack_halo(order, deep, main, extra, side, rim_too=True):
        where = lax.broadcasted_iota(jnp.int32, (deep, LANES), 1)
        for i, r in enumerate(order):
            if r is not None and (rim_too or r >= rows):
                main[pl.ds((rows + i) * deep, deep), :] = home(r, deep, main, extra)[...]
        first_pack = rows + order.index(None)
        for q in range(packs):
            total = jnp.zeros((deep, LANES), F32)
            for j in range(min(16, ext - 16 * q)):
                moved = pltpu.roll(side[pl.ds((16 * q + j) * deep, deep), :], (2 * WIDE * j + WIDE) % LANES, 1)
                total = jnp.where((where >= 2 * WIDE * j) & (where < 2 * WIDE * (j + 1)), moved, total)
            main[pl.ds((first_pack + q) * deep, deep), :] = total

    def unpack_halo(order, deep, main, extra, side):
        for i, r in enumerate(order):
            if r is not None:
                home(r, deep, main, extra)[...] = main[pl.ds((rows + i) * deep, deep), :]
        first_pack = rows + order.index(None)
        for q in range(packs):
            tile = main[pl.ds((first_pack + q) * deep, deep), :]
            for j in range(min(16, ext - 16 * q)):
                moved = pltpu.roll(tile, LANES - (2 * WIDE * j + WIDE) % LANES, 1)
                side[pl.ds((16 * q + j) * deep, deep), :] = moved

    def inputs_at(ref, base, tiles):
        return lanes_of(ref, DEEP, base, tiles).astype(BF16)

    def cotangents_at(base, tiles):
        part = lanes_of(dc, SHALLOW, base, tiles)
        return jnp.concatenate([part, jnp.zeros_like(part)], 0).astype(BF16)

    def backward_stages(first, second, cot):
        g_two = dot(wo[...], cot)
        yield
        dz_two = (g_two * (1.0 - second * second)).astype(BF16)
        yield
        g_one = dot(w_mid[...], dz_two)
        yield
        dz_one = (g_one * (1.0 - first * first)).astype(BF16)
        yield
        return dz_one, dz_two, dot(wi[...], dz_one).astype(BF16).astype(F32)

    def second_part(base, tiles, sums):
        x = inputs_at(ft2, base, tiles)
        cot = cotangents_at(base, tiles)
        first, second, low_first, low_second = yield from forward_stages(x, wi_t, wm_t)
        yield
        if sums is not None:
            put_lanes(cl, SHALLOW, base, tiles, closure(low_second, wo_t))
        dz_one, dz_two, dfeat = yield from backward_stages(first, second, cot)
        if sums is not None:
            add_terms(sums, (low_first, dz_two), (x, dz_one), (low_second, cot))
        yield
        put_lanes(df, DEEP, base, tiles, dfeat)

    def third_part(base, tiles, held1, held2, counted, sums):
        cot = cotangents_at(base, tiles)
        first = held1[...]
        second = held2[...]
        dz_one, dz_two, dfeat = yield from backward_stages(first, second, cot)
        x = inputs_at(ft1, base, tiles)
        if counted is not None:
            dz_one, dz_two, cot = (jnp.where(counted, v.astype(F32), 0.0).astype(BF16) for v in (dz_one, dz_two, cot))
        add_terms(sums, (first.astype(BF16), dz_two), (x, dz_one), (second.astype(BF16), cot))
        yield
        put_lanes(df, DEEP, base, tiles, dfeat)

    def add_terms(sums, *pairs):
        for k, pair in enumerate(pairs):
            sums[k] = dot_nt(*pair) if sums[k] is None else sums[k] + dot_nt(*pair)

    def keep_terms(sums, again):
        for acc, total in zip((acc_mid, acc_in, acc_out), sums):
            acc[...] = acc[...] + total if again else total

    def features_of(source, ft, order, rimmed):
        for level in range(levels):
            v = source[level]
            spread(v, level, DEEP, ft, ftx, fth, rimmed)
            spread(0.5 * (east_of(v) - west_of(v)), levels + level, DEEP, ft, ftx, fth, rimmed)
            spread(0.5 * (north_of(v) - south_of(v)), 2 * levels + level, DEEP, ft, ftx, fth, rimmed)
        pack_halo(order, DEEP, ft, ftx, fth)

    def force(v, level, closed):
        eastward, westward, northward, southward = east_of(v), west_of(v), north_of(v), south_of(v)
        laplace = eastward + westward + northward + southward - 4.0 * v
        slope = 0.5 * (eastward - westward)
        return planes[count - 1] * (KAPPA * laplace - planes[2 * levels + level] * slope + closed)

    features_of(planes, ft1, rim, True)
    for k, ref in enumerate(early[2::3]):
        cl[pl.ds(k * ref.shape[0], ref.shape[0]), :] = ref[...]

    def first_part(base, tiles):
        first, second, unused, low_second = yield from forward_stages(inputs_at(ft1, base, tiles), wi_t, wm_t)
        halo1[...] = first
        halo2[...] = second
        yield
        put_lanes(cl, SHALLOW, base, tiles, closure(low_second, wo_t))

    staggered([first_part(rows, len(rim))])
    unpack_halo(rim, SHALLOW, cl, clx, clh)
    for level in range(levels):
        closed = gathered(level, SHALLOW, cl, clx, clh, True)
        mid = planes[levels + level] + 2.0 * DT * force(planes[level], level, closed)
        o_mid[level] = mid[:rows, :LANES]
        mids[level] = mid
    copies = copied_out([(o_mid, h_mid)], sems.at[pl.ds(0, 1)])

    features_of(mids, ft2, outer, False)
    for level in range(levels):
        masked = planes[count - 1] * (2.0 * DT * planes[3 * levels + level])
        spread(masked, level, SHALLOW, dc, dcx, dch, False)
    pack_halo(outer, SHALLOW, dc, dcx, dch)
    sums = [None] * 3
    staggered(
        [second_part(rows, len(outer), None)] + [second_part(k * PART, PART, sums) for k in range(rows // PART)]
    )
    keep_terms(sums, False)
    unpack_halo(outer, DEEP, df, dfx, dfh)

    def adjoint_of(weighted, level, rimmed):
        masked = planes[count - 1] * weighted
        carried = planes[2 * levels + level] * masked
        a0 = gathered(level, DEEP, df, dfx, dfh, rimmed)
        a1 = gathered(levels + level, DEEP, df, dfx, dfh, rimmed)
        a2 = gathered(2 * levels + level, DEEP, df, dfx, dfh, rimmed)
        result = KAPPA * (east_of(masked) + west_of(masked) + north_of(masked) + south_of(masked) - 4.0 * masked)
        result = result + 0.5 * (east_of(carried) - west_of(carried)) + a0
        return result - 0.5 * (east_of(a1) - west_of(a1)) - 0.5 * (north_of(a2) - south_of(a2))

    for level in range(levels):
        closed = jnp.concatenate([cl[pl.ds(level, rows, stride=SHALLOW), :], jnp.zeros((2 * WIDE, LANES), F32)], 0)
        closed = jnp.concatenate([closed, jnp.zeros_like(closed)], 1)
        new = planes[level] + 2.0 * DT * force(mids[level], level, closed)
        o_new[level] = new[:rows, :LANES]
        grad = planes[4 * levels + level] + adjoint_of(2.0 * DT * planes[3 * levels + level], level, False)
        o_old[level] = grad[:rows, :LANES]
        olds[level] = grad
    copies += copied_out([(o_new, h_new), (o_old, h_old)], sems.at[pl.ds(1, 2)])

    row = lax.broadcasted_iota(jnp.int32, (ext, LANES), 0)
    inside = (lane > 0) & (lane < LANES - 1) & (row > 0) & (row < rows - 1)
    for level in range(levels):
        masked = planes[count - 1] * (2.0 * DT * olds[level])
        body = masked[:, :LANES]
        dc[pl.ds(level, rows, stride=SHALLOW), :] = jnp.where(inside, body, 0.0)[:rows]
        dcx[pl.ds(level, 2 * WIDE, stride=SHALLOW), :] = body[rows:]
        dch[pl.ds(level, ext, stride=SHALLOW), :] = with_rim(masked)
        for k, r in enumerate(rim[:2]):
            dc[pl.ds((rows + k) * SHALLOW + level, 1), :] = body[r : r + 1]
    pack_halo(rim[:rim_near], SHALLOW, dc, dcx, dch, False)
    at = lax.broadcasted_iota(jnp.int32, (1, rim_near * LANES), 1)
    tile, place = at >> 7, at & (LANES - 1)
    side_row = (tile - 4) * 16 + (place >> 3)
    edge = ((place & 7) == 0) | ((place & 7) == 7)
    counted = (tile < 2) | ((tile >= 4) & edge & (side_row > 0) & (side_row < rows - 1))
    near = pl.ds(0, rim_near * LANES)
    sums = [None] * 3
    staggered(
        [third_part(rows, rim_near, halo1.at[:, near], halo2.at[:, near], counted, sums)]
        + [third_part(k * PART, PART, kept1[k], kept2[k], None, sums) for k in range(rows // PART)]
    )
    keep_terms(sums, True)
    unpack_halo(rim[:rim_near], DEEP, df, dfx, dfh)
    for level in range(levels):
        grad = adjoint_of(2.0 * DT * olds[level], level, True)
        o_now[level] = planes[3 * levels + level, pl.ds(0, rows), pl.ds(0, LANES)] + grad[:rows, :LANES]
    copies += copied_out([(o_now, h_now)], sems.at[pl.ds(3, 1)])

    start = 0
    for total in (acc_mid[...], acc_in[...], acc_out[...].T):
        deep = total.shape[0]
        for half in range(hidden // LANES):
            o_grad[pl.ds(start, deep), :] = total[:, half * LANES : (half + 1) * LANES]
            start += deep
    if start < o_grad.shape[0]:
        o_grad[pl.ds(start, o_grad.shape[0] - start), :] = jnp.zeros((o_grad.shape[0] - start, LANES), F32)
    for copy in copies:
        copy.wait()


def scale_kernel(factor, *refs):
    terms, (g_in, g_mid, g_out) = refs[:SHARES], refs[SHARES:]
    share = terms[0].shape[0]
    hidden = g_mid.shape[0]
    start = 0
    for ref, deep in ((g_mid, hidden), (g_in, DEEP), (g_out, DEEP)):
        for half in range(hidden // LANES):
            at, end = start, start + ref.shape[0]
            while at < end:
                k, first = divmod(at, share)
                some = min(end - at, share - first)
                piece = terms[k][pl.ds(first, some), :]
                ref[pl.ds(at - start, some), half * LANES : (half + 1) * LANES] = piece * factor
                at += some
            start += deep


def along(value, axis, step):
    count = lax.axis_size(axis)
    return lax.ppermute(value, axis, [(i, (i + step) % count) for i in range(count)])


def swapped(value, axis, bit):
    return lax.ppermute(value, axis, [(i, i ^ bit) for i in range(lax.axis_size(axis))])


def summed_over(values, place, halving, doubling):
    bits = []
    bit = 1
    while bit < lax.axis_size(halving):
        upper = (place & bit) != 0
        half = values[0].shape[0] // 2
        got = [swapped(jnp.where(upper, v[:half], v[half:]), halving, bit) for v in values]
        values = [jnp.where(upper, v[half:], v[:half]) + g for v, g in zip(values, got)]
        bits.append((bit, upper))
        bit *= 2
    bit = 1
    while bit < lax.axis_size(doubling):
        got = [swapped(v, doubling, bit) for v in values]
        if 2 * bit < lax.axis_size(doubling):
            far = [(swapped(v, doubling, 2 * bit), swapped(v, doubling, 3 * bit)) for v in values]
            values = [(v + g) + (a + b) for v, g, (a, b) in zip(values, got, far)]
            bit *= 4
        else:
            values = [v + g for v, g in zip(values, got)]
            bit *= 2
    for bit, upper in reversed(bits):
        got = [swapped(v, halving, bit) for v in values]
        values = [
            jnp.concatenate([jnp.where(upper, g, v), jnp.where(upper, v, g)], 0) for v, g in zip(values, got)
        ]
    return values


def body(state_old, state_now, drift, ocean, w_in, w_mid, w_out, cot_mid, cot_new):
    levels, rows, cols = state_now.shape
    width_in, hidden = w_in.shape
    ext = rows + 2 * WIDE
    count = 5 * levels + 1
    packs = -(-ext // 16)
    slots = rows + 8 + packs
    tall = rows // EARLY
    vmem = pl.BlockSpec(memory_space=pltpu.VMEM)
    hbm = pl.BlockSpec(memory_space=pltpu.HBM)
    strip = jax.ShapeDtypeStruct((rows, LANES), F32)
    edge = jax.ShapeDtypeStruct((count, WIDE, LANES), F32)
    arrays = (state_now, state_old, drift, cot_new, cot_mid, ocean, w_in, w_mid, w_out.T)
    weights = tuple(jax.ShapeDtypeStruct(a.shape, a.dtype) for a in arrays[6:])
    west, east, top, bottom, fields, *weights = pl.pallas_call(
        pack_kernel,
        out_shape=(strip, strip, edge, edge, jax.ShapeDtypeStruct((count, rows, cols), F32)) + weights,
        in_specs=[hbm] * 9,
        out_specs=(vmem,) * 8,
        scratch_shapes=[pltpu.VMEM((rows, cols), jnp.int32), pltpu.SemaphoreType.DMA((9,))],
        compiler_params=pltpu.CompilerParams(vmem_limit_bytes=8 * 2**20),
    )(*(pltpu.with_memory_space_constraint(a, pltpu.HBM) for a in arrays))

    kept = jax.ShapeDtypeStruct((tall // PART, hidden, PART * LANES), F32)
    closed = jax.ShapeDtypeStruct((tall * SHALLOW, LANES), F32)
    tall_weight = jax.ShapeDtypeStruct((hidden, DEEP), BF16)
    flat_weight = jax.ShapeDtypeStruct((DEEP, hidden), BF16)
    prepared = (flat_weight, tall_weight, jax.ShapeDtypeStruct((hidden, hidden), BF16), tall_weight, flat_weight)

    def early(k, extra, extra_out):
        return pl.pallas_call(
            functools.partial(early_kernel, k * tall),
            out_shape=(kept, kept, closed) + extra_out,
            in_specs=[vmem] * (1 + len(extra)),
            out_specs=(vmem,) * (3 + len(extra_out)),
            scratch_shapes=[pltpu.VMEM((tall * DEEP, LANES), F32)],
            compiler_params=pltpu.CompilerParams(vmem_limit_bytes=12 * 2**20),
            cost_estimate=pl.CostEstimate(
                flops=6 * hidden * hidden * tall * cols, bytes_accessed=0, transcendentals=2 * hidden * tall * cols
            ),
        )(fields, *extra)

    left = along(east, "lon", 1)
    right = along(west, "lon", -1)
    *first_kept, wi, wi_t, wm_t, wo, wo_t = early(0, tuple(weights), prepared)
    message = jax.ShapeDtypeStruct((count + 2, WIDE, LANES), F32)
    up, down = pl.pallas_call(
        join_kernel,
        out_shape=(message, message),
        in_specs=[vmem] * 4,
        out_specs=(vmem,) * 2,
        compiler_params=pltpu.CompilerParams(vmem_limit_bytes=4 * 2**20),
    )(top, bottom, left, right)
    low = along(up, "lat", 1)
    high = along(down, "lat", -1)
    done = list(first_kept)
    for k in range(1, EARLY):
        done += early(k, (left, wi_t, wm_t, wo_t), ())

    halves = hidden // LANES
    grain = 8 * SHARES * lax.axis_size("lat")
    terms_rows = -(-halves * (hidden + 2 * DEEP) // grain) * grain
    field = jax.ShapeDtypeStruct((levels, rows, cols), F32)
    ext_planes = pltpu.VMEM((levels, ext, 2 * LANES), F32)

    def tiles(deep):
        return [pltpu.VMEM((n * deep, LANES), F32) for n in (slots, 16 * packs, 2 * WIDE)]

    kept_halo = pltpu.VMEM((hidden, (8 + packs) * LANES), F32)
    state_mid, state_new, grad_old, grad_now, terms, place = pl.pallas_call(
        functools.partial(main_kernel, lax.axis_size("lat")),
        out_shape=(field, field, field, field, jax.ShapeDtypeStruct((terms_rows, LANES), F32), jax.ShapeDtypeStruct((8, LANES), jnp.int32)),
        in_specs=[vmem] * (11 + 3 * EARLY),
        out_specs=(hbm,) * 4 + (vmem,) * 2,
        scratch_shapes=[
            *[pltpu.VMEM((levels, rows, cols), F32)] * 4,
            pltpu.SemaphoreType.DMA((4,)),
            pltpu.VMEM((count, ext, 2 * LANES), F32),
            ext_planes,
            ext_planes,
            tiles(DEEP)[0],
            *tiles(DEEP),
            *tiles(SHALLOW),
            *tiles(SHALLOW),
            *tiles(DEEP),
            kept_halo,
            kept_halo,
            pltpu.VMEM((hidden, hidden), F32),
            pltpu.VMEM((DEEP, hidden), F32),
            pltpu.VMEM((hidden, DEEP), F32),
        ],
        compiler_params=pltpu.CompilerParams(vmem_limit_bytes=34 * 2**20),
    )(fields, left, right, low, high, wi, wi_t, wm_t, weights[1], wo, wo_t, *done)

    summed = summed_over(jnp.split(terms, SHARES), place[:1], "lat", "lon")
    cells_all = rows * lax.axis_size("lat") * cols * lax.axis_size("lon")
    grad_in, grad_mid, grad_out = pl.pallas_call(
        functools.partial(scale_kernel, GAIN_GRAD / cells_all**0.5),
        out_shape=(
            jax.ShapeDtypeStruct((width_in, hidden), F32),
            jax.ShapeDtypeStruct((hidden, hidden), F32),
            jax.ShapeDtypeStruct((levels, hidden), F32),
        ),
        in_specs=[vmem] * SHARES,
        out_specs=(vmem,) * 3,
        compiler_params=pltpu.CompilerParams(vmem_limit_bytes=8 * 2**20),
    )(*summed)
    return state_mid, state_new, grad_old, grad_now, grad_in, grad_mid, grad_out.T


def solution(mesh):
    field = P("grp", "lat", "lon")
    whole = P("grp", None)
    in_specs = (field, field, field, P(("grp", "lat"), "lon"), P(), P(), P(), field, field)
    out_specs = (field, field, field, field, whole, whole, whole)
    return jax.shard_map(body, mesh=mesh, in_specs=in_specs, out_specs=out_specs, check_vma=False)
```

```python
import functools

import jax
import jax.numpy as jnp
from jax import lax
from jax.experimental import pallas as pl
from jax.experimental.pallas import tpu as pltpu
from jax.sharding import PartitionSpec as P

KAPPA = 0.2
DT = 0.1
GAIN_GRAD = 10.0

WIDE = 4
LANES = 128
PART = 8
EARLY = 2
DEEP = 16
SHALLOW = 8

F32 = jnp.float32
BF16 = jnp.bfloat16


def dot(left, right):
    return lax.dot_general(left, right, (((1,), (0,)), ((), ())), preferred_element_type=F32)


def dot_nt(left, right):
    return lax.dot_general(left, right, (((1,), (1,)), ((), ())), preferred_element_type=F32)


def pack_kernel(
    now, old, drift, cnew, cmid, ocean, w_in, w_mid, w_out,
    west, east, top, bottom, fields, v_in, v_mid, v_out, wet, sems,
):
    levels, rows, cols = now.shape
    copies = [
        pltpu.make_async_copy(ref, fields.at[pl.ds(levels * f, levels)], sems.at[f])
        for f, ref in enumerate((now, old, drift, cnew, cmid))
    ]
    copies.append(pltpu.make_async_copy(ocean, wet, sems.at[5]))
    for k, pair in enumerate(((w_in, v_in), (w_mid, v_mid), (w_out, v_out))):
        copies.append(pltpu.make_async_copy(*pair, sems.at[6 + k]))
    for copy in copies:
        copy.start()
    lane = lax.broadcasted_iota(jnp.int32, (rows, LANES), 1)
    to_west = jnp.zeros((rows, LANES), F32)
    to_east = jnp.zeros((rows, LANES), F32)
    count = fields.shape[0]
    for p in range(count):
        if p % levels == 0:
            copies[p // levels].wait()
        if p == count - 1:
            fields[p] = wet[...].astype(F32)
        plane = fields[p]
        here = (lane >= WIDE * p) & (lane < WIDE * (p + 1))
        to_west = jnp.where(here, pltpu.roll(plane, WIDE * p, 1) if p else plane, to_west)
        to_east = jnp.where(here, pltpu.roll(plane, WIDE * (p + 1), 1), to_east)
        top[p] = plane[:WIDE]
        bottom[p] = plane[rows - WIDE :]
    west[...] = to_west
    east[...] = to_east
    for copy in copies[6:]:
        copy.wait()


def join_kernel(top, bottom, left, right, up, down):
    count = top.shape[0]
    rows = left.shape[0]
    up[pl.ds(0, count)] = bottom[...]
    down[pl.ds(0, count)] = top[...]
    for k, strip in enumerate((left, right)):
        up[count + k] = strip[pl.ds(rows - WIDE, WIDE), :]
        down[count + k] = strip[pl.ds(0, WIDE), :]


def east_of(v):
    return pltpu.roll(v, v.shape[1] - 1, 1)


def west_of(v):
    return pltpu.roll(v, 1, 1)


def north_of(v):
    return pltpu.roll(v, v.shape[0] - 1, 0)


def south_of(v):
    return pltpu.roll(v, 1, 0)


def forward_stages(x, w_first_t, w_second_t):
    z_one = dot(w_first_t[...], x)
    yield
    first = jnp.tanh(z_one)
    low_first = first.astype(BF16)
    yield
    z_two = dot(w_second_t[...], low_first)
    yield
    second = jnp.tanh(z_two)
    return first, second, low_first, second.astype(BF16)


def closure(low_second, w_last_t):
    return dot(w_last_t[...], low_second).astype(BF16).astype(F32)[:SHALLOW]


def staggered(generators):
    live = []
    waiting = list(generators)
    while live or waiting:
        if waiting:
            live.append(waiting.pop(0))
        for part in list(live):
            try:
                next(part)
            except StopIteration:
                live.remove(part)


def lanes_of(ref, deep, base, tiles):
    block = ref[pl.ds(base * deep, tiles * deep), :]
    return jnp.concatenate([block[k * deep : (k + 1) * deep] for k in range(tiles)], 1)


def put_lanes(ref, deep, base, tiles, value):
    for k in range(tiles):
        ref[pl.ds((base + k) * deep, deep), :] = value[:, k * LANES : (k + 1) * LANES]


def early_kernel(start, fields, *refs):
    if start == 0:
        w_in, w_mid, w_out_t, keep1, keep2, cl, wi, wi_t, wm_t, wo, wo_t, ft = refs
        width_in, hidden = w_in.shape
        levels = w_out_t.shape[0]
        spare = jnp.zeros((DEEP - width_in, hidden), F32)
        wide_in = jnp.concatenate([w_in[...].astype(F32), spare], 0)
        wi[...] = wide_in.astype(BF16)
        wi_t[...] = wide_in.T.astype(BF16)
        wm_t[...] = w_mid[...].astype(F32).T.astype(BF16)
        spare = jnp.zeros((DEEP - levels, hidden), F32)
        wide_out = jnp.concatenate([w_out_t[...].astype(F32), spare], 0)
        wo_t[...] = wide_out.astype(BF16)
        wo[...] = wide_out.T.astype(BF16)
    else:
        unused, wi_t, wm_t, wo_t, keep1, keep2, cl, ft = refs
        levels = (fields.shape[0] - 1) // 5
    tall = cl.shape[0] // SHALLOW
    ft[...] = jnp.zeros_like(ft)
    for level in range(levels):
        v = fields[level]
        slope_x = 0.5 * (east_of(v) - west_of(v))
        slope_y = 0.5 * (north_of(v) - south_of(v))
        for f, plane in enumerate((v, slope_x, slope_y)):
            ft[pl.ds(f * levels + level, tall, stride=DEEP), :] = plane[start : start + tall]

    def part(base, kept1, kept2):
        x = lanes_of(ft, DEEP, base, PART).astype(BF16)
        first, second, unused_low, low_second = yield from forward_stages(x, wi_t, wm_t)
        kept1[...] = first
        kept2[...] = second
        yield
        put_lanes(cl, SHALLOW, base, PART, closure(low_second, wo_t))

    staggered(part(k * PART, keep1.at[k], keep2.at[k]) for k in range(tall // PART))


def copied_out(pairs, sems):
    copies = [pltpu.make_async_copy(*pair, sems.at[k]) for k, pair in enumerate(pairs)]
    for copy in copies:
        copy.start()
    return copies


class Block:
    def __init__(self, levels, rows):
        self.levels, self.rows = levels, rows
        self.ext = rows + 2 * WIDE
        self.packs = -(-self.ext // 16)
        self.wet = 5 * levels
        packed = [None] * self.packs
        ext = self.ext
        self.rim = [0, rows - 1, rows, ext - 1] + packed + [rows + 1, ext - 2, rows + 2, ext - 3]
        self.rim_near = self.rim[: 4 + self.packs]
        self.outer = [rows, ext - 1] + packed + [rows + 1, ext - 2]
        self.lane = lax.broadcasted_iota(jnp.int32, (ext, LANES), 1)

    def with_rim(self, plane):
        lane = self.lane
        body, side = plane[:, :LANES], plane[:, LANES:]
        own = jnp.where(lane == LANES - WIDE, pltpu.roll(body, LANES - WIDE, 1), pltpu.roll(body, WIDE, 1))
        return jnp.where((lane == LANES - WIDE) | (lane == WIDE - 1), own, side)

    def from_rim(self, body, side):
        lane = self.lane
        own = jnp.where(lane == 0, pltpu.roll(side, WIDE, 1), pltpu.roll(side, LANES - WIDE, 1))
        return jnp.where((lane == 0) | (lane == LANES - 1), own, body)

    def spread(self, plane, index, deep, main, extra, side, rimmed):
        main[pl.ds(index, self.rows, stride=deep), :] = plane[: self.rows, :LANES]
        extra[pl.ds(index, 2 * WIDE, stride=deep), :] = plane[self.rows :, :LANES]
        side[pl.ds(index, self.ext, stride=deep), :] = self.with_rim(plane) if rimmed else plane[:, LANES:]

    def gathered(self, index, deep, main, extra, side, rimmed):
        body = jnp.concatenate(
            [main[pl.ds(index, self.rows, stride=deep), :], extra[pl.ds(index, 2 * WIDE, stride=deep), :]], 0
        )
        beside = side[pl.ds(index, self.ext, stride=deep), :]
        return jnp.concatenate([self.from_rim(body, beside) if rimmed else body, beside], 1)

    def home(self, r, deep, main, extra):
        return main.at[pl.ds(r * deep, deep)] if r < self.rows else extra.at[pl.ds((r - self.rows) * deep, deep)]

    def pack_halo(self, order, deep, main, extra, side, rim_too=True):
        where = lax.broadcasted_iota(jnp.int32, (deep, LANES), 1)
        for i, r in enumerate(order):
            if r is not None and (rim_too or r >= self.rows):
                main[pl.ds((self.rows + i) * deep, deep), :] = self.home(r, deep, main, extra)[...]
        first_pack = self.rows + order.index(None)
        for q in range(self.packs):
            total = jnp.zeros((deep, LANES), F32)
            for j in range(min(16, self.ext - 16 * q)):
                moved = pltpu.roll(side[pl.ds((16 * q + j) * deep, deep), :], (2 * WIDE * j + WIDE) % LANES, 1)
                total = jnp.where((where >= 2 * WIDE * j) & (where < 2 * WIDE * (j + 1)), moved, total)
            main[pl.ds((first_pack + q) * deep, deep), :] = total

    def unpack_halo(self, order, deep, main, extra, side):
        for i, r in enumerate(order):
            if r is not None:
                self.home(r, deep, main, extra)[...] = main[pl.ds((self.rows + i) * deep, deep), :]
        first_pack = self.rows + order.index(None)
        for q in range(self.packs):
            tile = main[pl.ds((first_pack + q) * deep, deep), :]
            for j in range(min(16, self.ext - 16 * q)):
                moved = pltpu.roll(tile, LANES - (2 * WIDE * j + WIDE) % LANES, 1)
                side[pl.ds((16 * q + j) * deep, deep), :] = moved

    def force(self, planes, v, level, closed):
        eastward, westward, northward, southward = east_of(v), west_of(v), north_of(v), south_of(v)
        laplace = eastward + westward + northward + southward - 4.0 * v
        slope = 0.5 * (eastward - westward)
        return planes[self.wet] * (KAPPA * laplace - planes[2 * self.levels + level] * slope + closed)

    def adjoint(self, planes, weighted, level, tiles, rimmed):
        levels = self.levels
        masked = planes[self.wet] * weighted
        carried = planes[2 * levels + level] * masked
        a0, a1, a2 = (self.gathered(f * levels + level, DEEP, *tiles, rimmed) for f in range(3))
        result = KAPPA * (east_of(masked) + west_of(masked) + north_of(masked) + south_of(masked) - 4.0 * masked)
        result = result + 0.5 * (east_of(carried) - west_of(carried)) + a0
        return result - 0.5 * (east_of(a1) - west_of(a1)) - 0.5 * (north_of(a2) - south_of(a2))


def feature_gradients(dz_one, w_in):
    return dot(w_in[...], dz_one).astype(BF16).astype(F32)


def main_kernel(bands, *refs):
    fields, left, right, low, high, wi, wi_t, wm_t, w_mid, wo, wo_t, *refs = refs
    early, refs = refs[: 3 * EARLY], refs[3 * EARLY :]
    h_mid, h_old, o_sent, o_kept, planes, mids, olds, cl, df, *refs = refs
    o_mid, o_old, sems, ft1, ft2, fth, ftx, clh, clx, dc, dch, dcx, dfh, dfx, halo1, halo2, *refs = refs
    acc_mid, acc_in, acc_out, o_grad = refs
    levels, rows, cols = o_mid.shape
    hidden = w_mid.shape[0]
    block = Block(levels, rows)
    count, ext, lane = block.wet + 1, block.ext, block.lane
    kept1 = [ref.at[k] for ref in early[0::3] for k in range(ref.shape[0])]
    kept2 = [ref.at[k] for ref in early[1::3] for k in range(ref.shape[0])]

    band = lax.axis_index("lat")
    has_low = jnp.where(band > 0, 1.0, 0.0)
    has_high = jnp.where(band < bands - 1, 1.0, 0.0)

    def beyond(p):
        return [high[p] * has_high, low[p] * has_low]

    left_all = jnp.concatenate([left[...]] + beyond(count), 0)
    right_all = jnp.concatenate([right[...]] + beyond(count + 1), 0)
    for p in range(count):
        from_right = pltpu.roll(right_all, LANES - WIDE * p, 1) if p else right_all
        from_left = pltpu.roll(left_all, LANES - WIDE * (p + 1), 1)
        side = jnp.where(lane < WIDE, from_right, jnp.where(lane >= LANES - WIDE, from_left, 0.0))
        planes[p, :, pl.ds(0, LANES)] = jnp.concatenate([fields[p]] + beyond(p), 0)
        planes[p, :, pl.ds(LANES, LANES)] = side

    for ref in (ft1, ft2, fth, ftx, dc, dch, dcx):
        ref[...] = jnp.zeros_like(ref)

    def inputs_at(ref, base, tiles):
        return lanes_of(ref, DEEP, base, tiles).astype(BF16)

    def cotangents_at(base, tiles):
        part = lanes_of(dc, SHALLOW, base, tiles)
        return jnp.concatenate([part, jnp.zeros_like(part)], 0).astype(BF16)

    def backward_stages(first, second, cot):
        g_two = dot(wo[...], cot)
        yield
        dz_two = (g_two * (1.0 - second * second)).astype(BF16)
        yield
        g_one = dot(w_mid[...], dz_two)
        yield
        dz_one = (g_one * (1.0 - first * first)).astype(BF16)
        yield
        return dz_one, dz_two

    def second_part(base, tiles, sums):
        x = inputs_at(ft2, base, tiles)
        cot = cotangents_at(base, tiles)
        first, second, low_first, low_second = yield from forward_stages(x, wi_t, wm_t)
        yield
        if sums is not None:
            put_lanes(cl, SHALLOW, base, tiles, closure(low_second, wo_t))
        dz_one, dz_two = yield from backward_stages(first, second, cot)
        dfeat = feature_gradients(dz_one, wi)
        if sums is not None:
            add_terms(sums, (low_first, dz_two), (x, dz_one), (low_second, cot))
        yield
        put_lanes(df, DEEP, base, tiles, dfeat)

    def third_part(base, tiles, held1, held2, counted, sums):
        cot = cotangents_at(base, tiles)
        first = held1[...]
        second = held2[...]
        dz_one, dz_two = yield from backward_stages(first, second, cot)
        dfeat = feature_gradients(dz_one, wi)
        x = inputs_at(ft1, base, tiles)
        if counted is not None:
            dz_one, dz_two, cot = (jnp.where(counted, v.astype(F32), 0.0).astype(BF16) for v in (dz_one, dz_two, cot))
        add_terms(sums, (first.astype(BF16), dz_two), (x, dz_one), (second.astype(BF16), cot))
        yield
        put_lanes(df, DEEP, base, tiles, dfeat)

    def add_terms(sums, *pairs):
        for k, pair in enumerate(pairs):
            sums[k] = dot_nt(*pair) if sums[k] is None else sums[k] + dot_nt(*pair)

    def features_of(source, ft, order, rimmed):
        for level in range(levels):
            v = source[level]
            for f, plane in enumerate((v, 0.5 * (east_of(v) - west_of(v)), 0.5 * (north_of(v) - south_of(v)))):
                block.spread(plane, f * levels + level, DEEP, ft, ftx, fth, rimmed)
        block.pack_halo(order, DEEP, ft, ftx, fth)

    features_of(planes, ft1, block.rim, True)
    for k, ref in enumerate(early[2::3]):
        cl[pl.ds(k * ref.shape[0], ref.shape[0]), :] = ref[...]

    def first_part(base, tiles):
        first, second, unused, low_second = yield from forward_stages(inputs_at(ft1, base, tiles), wi_t, wm_t)
        halo1[...] = first
        halo2[...] = second
        yield
        put_lanes(cl, SHALLOW, base, tiles, closure(low_second, wo_t))

    staggered([first_part(rows, len(block.rim))])
    block.unpack_halo(block.rim, SHALLOW, cl, clx, clh)
    for level in range(levels):
        closed = block.gathered(level, SHALLOW, cl, clx, clh, True)
        mid = planes[levels + level] + 2.0 * DT * block.force(planes, planes[level], level, closed)
        o_mid[level] = mid[:rows, :LANES]
        mids[level] = mid
    copies = copied_out([(o_mid, h_mid)], sems.at[pl.ds(0, 1)])

    features_of(mids, ft2, block.outer, False)
    for level in range(levels):
        masked = planes[block.wet] * (2.0 * DT * planes[3 * levels + level])
        block.spread(masked, level, SHALLOW, dc, dcx, dch, False)
    block.pack_halo(block.outer, SHALLOW, dc, dcx, dch)
    sums = [None] * 3
    staggered(
        [second_part(rows, len(block.outer), None)]
        + [second_part(k * PART, PART, sums) for k in range(rows // PART)]
    )
    for acc, total in zip((acc_mid, acc_in, acc_out), sums):
        acc[...] = total
    block.unpack_halo(block.outer, DEEP, df, dfx, dfh)
    for level in range(levels):
        weighted = 2.0 * DT * planes[3 * levels + level]
        grad = planes[4 * levels + level] + block.adjoint(planes, weighted, level, (df, dfx, dfh), False)
        o_old[level] = grad[:rows, :LANES]
        olds[level] = grad
    copies += copied_out([(o_old, h_old)], sems.at[pl.ds(1, 1)])

    near = block.rim_near
    row = lax.broadcasted_iota(jnp.int32, (ext, LANES), 0)
    inside = (lane > 0) & (lane < LANES - 1) & (row > 0) & (row < rows - 1)
    for level in range(levels):
        masked = planes[block.wet] * (2.0 * DT * olds[level])
        body = masked[:, :LANES]
        dc[pl.ds(level, rows, stride=SHALLOW), :] = jnp.where(inside, body, 0.0)[:rows]
        dcx[pl.ds(level, 2 * WIDE, stride=SHALLOW), :] = body[rows:]
        dch[pl.ds(level, ext, stride=SHALLOW), :] = block.with_rim(masked)
        for k, r in enumerate(near[:2]):
            dc[pl.ds((rows + k) * SHALLOW + level, 1), :] = body[r : r + 1]
    block.pack_halo(near, SHALLOW, dc, dcx, dch, False)
    at = lax.broadcasted_iota(jnp.int32, (1, len(near) * LANES), 1)
    tile, place = at >> 7, at & (LANES - 1)
    side_row = (tile - 4) * 16 + (place >> 3)
    edge = ((place & 7) == 0) | ((place & 7) == 7)
    counted = (tile < 2) | ((tile >= 4) & edge & (side_row > 0) & (side_row < rows - 1))
    wide = pl.ds(0, len(near) * LANES)
    sums = [None] * 3
    staggered(
        [third_part(rows, len(near), halo1.at[:, wide], halo2.at[:, wide], counted, sums)]
        + [third_part(k * PART, PART, kept1[k], kept2[k], None, sums) for k in range(rows // PART)]
    )

    start = 0
    for total in (acc_mid[...] + sums[0], acc_in[...] + sums[1], (acc_out[...] + sums[2]).T):
        deep = total.shape[0]
        for half in range(hidden // LANES):
            o_grad[pl.ds(start, deep), :] = total[:, half * LANES : (half + 1) * LANES]
            start += deep
    if start < o_grad.shape[0]:
        o_grad[pl.ds(start, o_grad.shape[0] - start), :] = jnp.zeros((o_grad.shape[0] - start, LANES), F32)
    halve(o_grad[...], 1, o_sent, o_kept)
    for copy in copies:
        copy.wait()


def halve(value, bit, sent, kept):
    half = value.shape[0] // 2
    upper = (lax.axis_index("lat") & bit) != 0
    sent[...] = jnp.where(upper, value[:half], value[half:])
    kept[...] = jnp.where(upper, value[half:], value[:half])


def halve_kernel(bit, held, got, sent, kept):
    halve(held[...] + got[...], bit, sent, kept)


def late_kernel(
    fields, planes, mids, olds, cl, gradients, held, h_new, h_now, o_held, o_place, o_new, o_now, sems, df, dfh, dfx
):
    levels, rows, cols = o_new.shape
    block = Block(levels, rows)
    o_held[...] = held[...]
    o_place[...] = jnp.zeros_like(o_place) + lax.axis_index("lat")
    df[...] = gradients[...]
    beside = jnp.zeros((rows, LANES), F32)
    beyond = jnp.zeros((2 * WIDE, 2 * LANES), F32)
    for level in range(levels):
        closed = jnp.concatenate([cl[pl.ds(level, rows, stride=SHALLOW), :], beside], 1)
        closed = jnp.concatenate([closed, beyond], 0)
        new = planes[level] + 2.0 * DT * block.force(planes, mids[level], level, closed)
        o_new[level] = new[:rows, :LANES]
    copies = copied_out([(o_new, h_new)], sems.at[pl.ds(0, 1)])
    block.unpack_halo(block.rim_near, DEEP, df, dfx, dfh)
    for level in range(levels):
        grad = block.adjoint(planes, 2.0 * DT * olds[level], level, (df, dfx, dfh), True)
        o_now[level] = fields[3 * levels + level] + grad[:rows, :LANES]
    copies += copied_out([(o_now, h_now)], sems.at[pl.ds(1, 1)])
    for copy in copies:
        copy.wait()


def scale_kernel(factor, terms, g_in, g_mid, g_out):
    hidden = g_mid.shape[0]
    start = 0
    for ref, deep in ((g_mid, hidden), (g_in, DEEP), (g_out, DEEP)):
        for half in range(hidden // LANES):
            ref[:, half * LANES : (half + 1) * LANES] = terms[pl.ds(start, ref.shape[0]), :] * factor
            start += deep


def along(value, axis, step):
    count = lax.axis_size(axis)
    return lax.ppermute(value, axis, [(i, (i + step) % count) for i in range(count)])


def swapped(value, axis, bit):
    return lax.ppermute(value, axis, [(i, i ^ bit) for i in range(lax.axis_size(axis))])


def added_up(value, axis):
    bit = 1
    while bit < lax.axis_size(axis):
        near = swapped(value, axis, bit)
        if 2 * bit < lax.axis_size(axis):
            value = (value + near) + (swapped(value, axis, 2 * bit) + swapped(value, axis, 3 * bit))
            bit *= 4
        else:
            value = value + near
            bit *= 2
    return value


def put_together(value, place, axis):
    bit = lax.axis_size(axis) // 2
    while bit:
        upper = (place & bit) != 0
        other = swapped(value, axis, bit)
        value = jnp.concatenate([jnp.where(upper, other, value), jnp.where(upper, value, other)], 0)
        bit //= 2
    return value


def body(state_old, state_now, drift, ocean, w_in, w_mid, w_out, cot_mid, cot_new):
    levels, rows, cols = state_now.shape
    width_in, hidden = w_in.shape
    ext = rows + 2 * WIDE
    count = 5 * levels + 1
    packs = -(-ext // 16)
    slots = rows + 8 + packs
    tall = rows // EARLY
    vmem = pl.BlockSpec(memory_space=pltpu.VMEM)
    hbm = pl.BlockSpec(memory_space=pltpu.HBM)
    strip = jax.ShapeDtypeStruct((rows, LANES), F32)
    edge = jax.ShapeDtypeStruct((count, WIDE, LANES), F32)
    arrays = (state_now, state_old, drift, cot_new, cot_mid, ocean, w_in, w_mid, w_out.T)
    weights = tuple(jax.ShapeDtypeStruct(a.shape, a.dtype) for a in arrays[6:])
    west, east, top, bottom, fields, *weights = pl.pallas_call(
        pack_kernel,
        out_shape=(strip, strip, edge, edge, jax.ShapeDtypeStruct((count, rows, cols), F32)) + weights,
        in_specs=[hbm] * 9,
        out_specs=(vmem,) * 8,
        scratch_shapes=[pltpu.VMEM((rows, cols), jnp.int32), pltpu.SemaphoreType.DMA((9,))],
        compiler_params=pltpu.CompilerParams(vmem_limit_bytes=8 * 2**20),
    )(*(pltpu.with_memory_space_constraint(a, pltpu.HBM) for a in arrays))

    kept = jax.ShapeDtypeStruct((tall // PART, hidden, PART * LANES), F32)
    closed = jax.ShapeDtypeStruct((tall * SHALLOW, LANES), F32)
    tall_weight = jax.ShapeDtypeStruct((hidden, DEEP), BF16)
    flat_weight = jax.ShapeDtypeStruct((DEEP, hidden), BF16)
    prepared = (flat_weight, tall_weight, jax.ShapeDtypeStruct((hidden, hidden), BF16), tall_weight, flat_weight)

    def early(k, extra, extra_out):
        return pl.pallas_call(
            functools.partial(early_kernel, k * tall),
            out_shape=(kept, kept, closed) + extra_out,
            in_specs=[vmem] * (1 + len(extra)),
            out_specs=(vmem,) * (3 + len(extra_out)),
            scratch_shapes=[pltpu.VMEM((tall * DEEP, LANES), F32)],
            compiler_params=pltpu.CompilerParams(vmem_limit_bytes=12 * 2**20),
            cost_estimate=pl.CostEstimate(
                flops=6 * hidden * hidden * tall * cols, bytes_accessed=0, transcendentals=2 * hidden * tall * cols
            ),
        )(fields, *extra)

    left = along(east, "lon", 1)
    right = along(west, "lon", -1)
    *first_kept, wi, wi_t, wm_t, wo, wo_t = early(0, tuple(weights), prepared)
    message = jax.ShapeDtypeStruct((count + 2, WIDE, LANES), F32)
    up, down = pl.pallas_call(
        join_kernel,
        out_shape=(message, message),
        in_specs=[vmem] * 4,
        out_specs=(vmem,) * 2,
        compiler_params=pltpu.CompilerParams(vmem_limit_bytes=4 * 2**20),
    )(top, bottom, left, right)
    low = along(up, "lat", 1)
    high = along(down, "lat", -1)
    done = list(first_kept)
    for k in range(1, EARLY):
        done += early(k, (left, wi_t, wm_t, wo_t), ())

    bands = lax.axis_size("lat")
    halves = hidden // LANES
    terms_rows = -(-halves * (hidden + 2 * DEEP) // (8 * bands)) * 8 * bands
    field = jax.ShapeDtypeStruct((levels, rows, cols), F32)
    ext_planes = jax.ShapeDtypeStruct((levels, ext, 2 * LANES), F32)
    staged = pltpu.VMEM((levels, rows, cols), F32)

    def tiles(deep):
        return [pltpu.VMEM((n * deep, LANES), F32) for n in (slots, 16 * packs, 2 * WIDE)]

    def half_terms(parts):
        return (jax.ShapeDtypeStruct((terms_rows // parts, LANES), F32),) * 2

    kept_halo = pltpu.VMEM((hidden, (8 + packs) * LANES), F32)
    state_mid, grad_old, sent, held, planes, mids, olds, closures, gradients = pl.pallas_call(
        functools.partial(main_kernel, bands),
        out_shape=(field, field, *half_terms(2))
        + (jax.ShapeDtypeStruct((count, ext, 2 * LANES), F32), ext_planes, ext_planes)
        + tuple(jax.ShapeDtypeStruct((slots * deep, LANES), F32) for deep in (SHALLOW, DEEP)),
        in_specs=[vmem] * (11 + 3 * EARLY),
        out_specs=(hbm,) * 2 + (vmem,) * 7,
        scratch_shapes=[
            staged,
            staged,
            pltpu.SemaphoreType.DMA((2,)),
            tiles(DEEP)[0],
            *tiles(DEEP),
            *tiles(SHALLOW)[1:],
            *tiles(SHALLOW),
            *tiles(DEEP)[1:],
            kept_halo,
            kept_halo,
            pltpu.VMEM((hidden, hidden), F32),
            pltpu.VMEM((DEEP, hidden), F32),
            pltpu.VMEM((hidden, DEEP), F32),
            pltpu.VMEM((terms_rows, LANES), F32),
        ],
        compiler_params=pltpu.CompilerParams(vmem_limit_bytes=32 * 2**20),
    )(fields, left, right, low, high, wi, wi_t, wm_t, weights[1], wo, wo_t, *done)

    bit = 1
    while 2 * bit < bands:
        got = swapped(sent, "lat", bit)
        bit *= 2
        sent, held = pl.pallas_call(
            functools.partial(halve_kernel, bit),
            out_shape=half_terms(2 * bit),
            in_specs=[vmem] * 2,
            out_specs=(vmem,) * 2,
            compiler_params=pltpu.CompilerParams(vmem_limit_bytes=4 * 2**20),
        )(held, got)
    got = swapped(sent, "lat", bit)
    state_new, grad_now, held, place = pl.pallas_call(
        late_kernel,
        out_shape=(field, field, half_terms(bands)[0], jax.ShapeDtypeStruct((8, LANES), jnp.int32)),
        in_specs=[vmem] * 7,
        out_specs=(hbm,) * 2 + (vmem,) * 2,
        scratch_shapes=[staged, staged, pltpu.SemaphoreType.DMA((2,)), *tiles(DEEP)],
        compiler_params=pltpu.CompilerParams(vmem_limit_bytes=16 * 2**20),
        cost_estimate=pl.CostEstimate(
            flops=2 * hidden * hidden * rows * cols, bytes_accessed=0, transcendentals=0
        ),
    )(fields, planes, mids, olds, closures, gradients, held)
    summed = put_together(added_up(held + got, "lon"), place[:1], "lat")
    cells_all = rows * lax.axis_size("lat") * cols * lax.axis_size("lon")
    grad_in, grad_mid, grad_out = pl.pallas_call(
        functools.partial(scale_kernel, GAIN_GRAD / cells_all**0.5),
        out_shape=(
            jax.ShapeDtypeStruct((width_in, hidden), F32),
            jax.ShapeDtypeStruct((hidden, hidden), F32),
            jax.ShapeDtypeStruct((levels, hidden), F32),
        ),
        in_specs=[vmem],
        out_specs=(vmem,) * 3,
        compiler_params=pltpu.CompilerParams(vmem_limit_bytes=8 * 2**20),
    )(summed)
    return state_mid, state_new, grad_old, grad_now, grad_in, grad_mid, grad_out.T


def solution(mesh):
    field = P("grp", "lat", "lon")
    whole = P("grp", None)
    in_specs = (field, field, field, P(("grp", "lat"), "lon"), P(), P(), P(), field, field)
    out_specs = (field, field, field, field, whole, whole, whole)
    return jax.shard_map(body, mesh=mesh, in_specs=in_specs, out_specs=out_specs, check_vma=False)
```

```python
import functools

import jax
import jax.numpy as jnp
from jax import lax
from jax.experimental import pallas as pl
from jax.experimental.pallas import tpu as pltpu
from jax.sharding import PartitionSpec as P

KAPPA = 0.2
DT = 0.1
GAIN_GRAD = 10.0

WIDE = 4
LANES = 128
PART = 4
EARLY = 2
DEEP = 16
SHALLOW = 8

F32 = jnp.float32
BF16 = jnp.bfloat16


def dot(left, right):
    return lax.dot_general(left, right, (((1,), (0,)), ((), ())), preferred_element_type=F32)


def dot_nt(left, right):
    return lax.dot_general(left, right, (((1,), (1,)), ((), ())), preferred_element_type=F32)


def pack_kernel(
    now, old, drift, cnew, cmid, ocean, w_in, w_mid, w_out,
    west, east, top, bottom, fields, v_in, v_mid, v_out, wet, sems,
):
    levels, rows, cols = now.shape
    copies = [
        pltpu.make_async_copy(ref, fields.at[pl.ds(levels * f, levels)], sems.at[f])
        for f, ref in enumerate((now, old, drift, cnew, cmid))
    ]
    copies.append(pltpu.make_async_copy(ocean, wet, sems.at[5]))
    for k, pair in enumerate(((w_in, v_in), (w_mid, v_mid), (w_out, v_out))):
        copies.append(pltpu.make_async_copy(*pair, sems.at[6 + k]))
    for copy in copies:
        copy.start()
    lane = lax.broadcasted_iota(jnp.int32, (rows, LANES), 1)
    to_west = jnp.zeros((rows, LANES), F32)
    to_east = jnp.zeros((rows, LANES), F32)
    count = fields.shape[0]
    for p in range(count):
        if p % levels == 0:
            copies[p // levels].wait()
        if p == count - 1:
            fields[p] = wet[...].astype(F32)
        plane = fields[p]
        here = (lane >= WIDE * p) & (lane < WIDE * (p + 1))
        to_west = jnp.where(here, pltpu.roll(plane, WIDE * p, 1) if p else plane, to_west)
        to_east = jnp.where(here, pltpu.roll(plane, WIDE * (p + 1), 1), to_east)
        top[p] = plane[:WIDE]
        bottom[p] = plane[rows - WIDE :]
    west[...] = to_west
    east[...] = to_east
    for copy in copies[6:]:
        copy.wait()


def join_kernel(top, bottom, left, right, up, down):
    count = top.shape[0]
    rows = left.shape[0]
    up[pl.ds(0, count)] = bottom[...]
    down[pl.ds(0, count)] = top[...]
    for k, strip in enumerate((left, right)):
        up[count + k] = strip[pl.ds(rows - WIDE, WIDE), :]
        down[count + k] = strip[pl.ds(0, WIDE), :]


def east_of(v):
    return pltpu.roll(v, v.shape[1] - 1, 1)


def west_of(v):
    return pltpu.roll(v, 1, 1)


def north_of(v):
    return pltpu.roll(v, v.shape[0] - 1, 0)


def south_of(v):
    return pltpu.roll(v, 1, 0)


def forward_stages(x, w_first_t, w_second_t):
    z_one = dot(w_first_t[...], x)
    yield
    first = jnp.tanh(z_one)
    low_first = first.astype(BF16)
    yield
    z_two = dot(w_second_t[...], low_first)
    yield
    second = jnp.tanh(z_two)
    return first, second, low_first, second.astype(BF16)


def closure(low_second, w_last_t):
    return dot(w_last_t[...], low_second).astype(BF16).astype(F32)[:SHALLOW]


def staggered(generators):
    live = []
    waiting = list(generators)
    while live or waiting:
        if waiting:
            live.append(waiting.pop(0))
        for part in list(live):
            try:
                next(part)
            except StopIteration:
                live.remove(part)


def lanes_of(ref, deep, base, tiles):
    block = ref[pl.ds(base * deep, tiles * deep), :]
    return jnp.concatenate([block[k * deep : (k + 1) * deep] for k in range(tiles)], 1)


def put_lanes(ref, deep, base, tiles, value):
    for k in range(tiles):
        ref[pl.ds((base + k) * deep, deep), :] = value[:, k * LANES : (k + 1) * LANES]


def early_kernel(start, fields, *refs):
    if start == 0:
        w_in, w_mid, w_out_t, keep1, keep2, cl, wi, wi_t, wm_t, wo, wo_t, ft = refs
        width_in, hidden = w_in.shape
        levels = w_out_t.shape[0]
        spare = jnp.zeros((DEEP - width_in, hidden), F32)
        wide_in = jnp.concatenate([w_in[...].astype(F32), spare], 0)
        wi[...] = wide_in.astype(BF16)
        wi_t[...] = wide_in.T.astype(BF16)
        wm_t[...] = w_mid[...].astype(F32).T.astype(BF16)
        spare = jnp.zeros((DEEP - levels, hidden), F32)
        wide_out = jnp.concatenate([w_out_t[...].astype(F32), spare], 0)
        wo_t[...] = wide_out.astype(BF16)
        wo[...] = wide_out.T.astype(BF16)
    else:
        unused, wi_t, wm_t, wo_t, keep1, keep2, cl, ft = refs
        levels = (fields.shape[0] - 1) // 5
    tall = cl.shape[0] // SHALLOW
    ft[...] = jnp.zeros_like(ft)
    for level in range(levels):
        v = fields[level]
        slope_x = 0.5 * (east_of(v) - west_of(v))
        slope_y = 0.5 * (north_of(v) - south_of(v))
        for f, plane in enumerate((v, slope_x, slope_y)):
            ft[pl.ds(f * levels + level, tall, stride=DEEP), :] = plane[start : start + tall]

    def part(base, kept1, kept2):
        x = lanes_of(ft, DEEP, base, PART).astype(BF16)
        first, second, unused_low, low_second = yield from forward_stages(x, wi_t, wm_t)
        kept1[...] = first
        kept2[...] = second
        yield
        put_lanes(cl, SHALLOW, base, PART, closure(low_second, wo_t))

    staggered(part(k * PART, keep1.at[k], keep2.at[k]) for k in range(tall // PART))


def copied_out(pairs, sems):
    copies = [pltpu.make_async_copy(*pair, sems.at[k]) for k, pair in enumerate(pairs)]
    for copy in copies:
        copy.start()
    return copies


class Block:
    def __init__(self, levels, rows):
        self.levels, self.rows = levels, rows
        self.ext = rows + 2 * WIDE
        self.packs = -(-self.ext // 16)
        self.wet = 5 * levels
        packed = [None] * self.packs
        ext = self.ext
        self.rim = [0, rows - 1, rows, ext - 1] + packed + [rows + 1, ext - 2, rows + 2, ext - 3]
        self.rim_near = self.rim[: 4 + self.packs]
        self.outer = [rows, ext - 1] + packed + [rows + 1, ext - 2]
        self.lane = lax.broadcasted_iota(jnp.int32, (ext, LANES), 1)

    def with_rim(self, plane):
        lane = self.lane
        body, side = plane[:, :LANES], plane[:, LANES:]
        own = jnp.where(lane == LANES - WIDE, pltpu.roll(body, LANES - WIDE, 1), pltpu.roll(body, WIDE, 1))
        return jnp.where((lane == LANES - WIDE) | (lane == WIDE - 1), own, side)

    def from_rim(self, body, side):
        lane = self.lane
        own = jnp.where(lane == 0, pltpu.roll(side, WIDE, 1), pltpu.roll(side, LANES - WIDE, 1))
        return jnp.where((lane == 0) | (lane == LANES - 1), own, body)

    def spread(self, plane, index, deep, main, extra, side, rimmed):
        main[pl.ds(index, self.rows, stride=deep), :] = plane[: self.rows, :LANES]
        extra[pl.ds(index, 2 * WIDE, stride=deep), :] = plane[self.rows :, :LANES]
        side[pl.ds(index, self.ext, stride=deep), :] = self.with_rim(plane) if rimmed else plane[:, LANES:]

    def gathered(self, index, deep, main, extra, side, rimmed):
        body = jnp.concatenate(
            [main[pl.ds(index, self.rows, stride=deep), :], extra[pl.ds(index, 2 * WIDE, stride=deep), :]], 0
        )
        beside = side[pl.ds(index, self.ext, stride=deep), :]
        return jnp.concatenate([self.from_rim(body, beside) if rimmed else body, beside], 1)

    def home(self, r, deep, main, extra):
        return main.at[pl.ds(r * deep, deep)] if r < self.rows else extra.at[pl.ds((r - self.rows) * deep, deep)]

    def pack_halo(self, order, deep, main, extra, side, rim_too=True):
        where = lax.broadcasted_iota(jnp.int32, (deep, LANES), 1)
        for i, r in enumerate(order):
            if r is not None and (rim_too or r >= self.rows):
                main[pl.ds((self.rows + i) * deep, deep), :] = self.home(r, deep, main, extra)[...]
        first_pack = self.rows + order.index(None)
        for q in range(self.packs):
            total = jnp.zeros((deep, LANES), F32)
            for j in range(min(16, self.ext - 16 * q)):
                moved = pltpu.roll(side[pl.ds((16 * q + j) * deep, deep), :], (2 * WIDE * j + WIDE) % LANES, 1)
                total = jnp.where((where >= 2 * WIDE * j) & (where < 2 * WIDE * (j + 1)), moved, total)
            main[pl.ds((first_pack + q) * deep, deep), :] = total

    def unpack_halo(self, order, deep, main, extra, side):
        for i, r in enumerate(order):
            if r is not None:
                self.home(r, deep, main, extra)[...] = main[pl.ds((self.rows + i) * deep, deep), :]
        first_pack = self.rows + order.index(None)
        for q in range(self.packs):
            tile = main[pl.ds((first_pack + q) * deep, deep), :]
            for j in range(min(16, self.ext - 16 * q)):
                moved = pltpu.roll(tile, LANES - (2 * WIDE * j + WIDE) % LANES, 1)
                side[pl.ds((16 * q + j) * deep, deep), :] = moved

    def force(self, planes, v, level, closed):
        eastward, westward, northward, southward = east_of(v), west_of(v), north_of(v), south_of(v)
        laplace = eastward + westward + northward + southward - 4.0 * v
        slope = 0.5 * (eastward - westward)
        return planes[self.wet] * (KAPPA * laplace - planes[2 * self.levels + level] * slope + closed)

    def adjoint(self, planes, weighted, level, tiles, rimmed):
        levels = self.levels
        masked = planes[self.wet] * weighted
        carried = planes[2 * levels + level] * masked
        a0, a1, a2 = (self.gathered(f * levels + level, DEEP, *tiles, rimmed) for f in range(3))
        result = KAPPA * (east_of(masked) + west_of(masked) + north_of(masked) + south_of(masked) - 4.0 * masked)
        result = result + 0.5 * (east_of(carried) - west_of(carried)) + a0
        return result - 0.5 * (east_of(a1) - west_of(a1)) - 0.5 * (north_of(a2) - south_of(a2))


def feature_gradients(dz_one, w_in):
    return dot(w_in[...], dz_one).astype(BF16).astype(F32)


def main_kernel(bands, *refs):
    fields, left, right, low, high, wi, wi_t, wm_t, w_mid, wo, wo_t, *refs = refs
    early, refs = refs[: 3 * EARLY], refs[3 * EARLY :]
    h_mid, h_old, o_sent, o_kept, planes, mids, olds, cl, df, *refs = refs
    o_mid, o_old, sems, ft1, ft2, fth, ftx, clh, clx, dc, dch, dcx, dfh, dfx, halo1, halo2, *refs = refs
    acc_mid, acc_in, acc_out, o_grad = refs
    levels, rows, cols = o_mid.shape
    hidden = w_mid.shape[0]
    block = Block(levels, rows)
    count, ext, lane = block.wet + 1, block.ext, block.lane
    kept1 = [ref.at[k] for ref in early[0::3] for k in range(ref.shape[0])]
    kept2 = [ref.at[k] for ref in early[1::3] for k in range(ref.shape[0])]

    band = lax.axis_index("lat")
    has_low = jnp.where(band > 0, 1.0, 0.0)
    has_high = jnp.where(band < bands - 1, 1.0, 0.0)

    def beyond(p):
        return [high[p] * has_high, low[p] * has_low]

    left_all = jnp.concatenate([left[...]] + beyond(count), 0)
    right_all = jnp.concatenate([right[...]] + beyond(count + 1), 0)
    for p in range(count):
        from_right = pltpu.roll(right_all, LANES - WIDE * p, 1) if p else right_all
        from_left = pltpu.roll(left_all, LANES - WIDE * (p + 1), 1)
        side = jnp.where(lane < WIDE, from_right, jnp.where(lane >= LANES - WIDE, from_left, 0.0))
        planes[p, :, pl.ds(0, LANES)] = jnp.concatenate([fields[p]] + beyond(p), 0)
        planes[p, :, pl.ds(LANES, LANES)] = side

    for ref in (ft1, ft2, fth, ftx, dc, dch, dcx):
        ref[...] = jnp.zeros_like(ref)

    def inputs_at(ref, base, tiles):
        return lanes_of(ref, DEEP, base, tiles).astype(BF16)

    def cotangents_at(base, tiles):
        part = lanes_of(dc, SHALLOW, base, tiles)
        return jnp.concatenate([part, jnp.zeros_like(part)], 0).astype(BF16)

    def backward_stages(first, second, cot):
        g_two = dot(wo[...], cot)
        yield
        dz_two = (g_two * (1.0 - second * second)).astype(BF16)
        yield
        g_one = dot(w_mid[...], dz_two)
        yield
        dz_one = (g_one * (1.0 - first * first)).astype(BF16)
        yield
        return dz_one, dz_two

    def second_part(base, tiles, sums):
        x = inputs_at(ft2, base, tiles)
        cot = cotangents_at(base, tiles)
        first, second, low_first, low_second = yield from forward_stages(x, wi_t, wm_t)
        yield
        if sums is not None:
            put_lanes(cl, SHALLOW, base, tiles, closure(low_second, wo_t))
        dz_one, dz_two = yield from backward_stages(first, second, cot)
        dfeat = feature_gradients(dz_one, wi)
        if sums is not None:
            add_terms(sums, (low_first, dz_two), (x, dz_one), (low_second, cot))
        yield
        put_lanes(df, DEEP, base, tiles, dfeat)

    def third_part(base, tiles, held1, held2, counted, sums):
        cot = cotangents_at(base, tiles)
        first = held1[...]
        second = held2[...]
        dz_one, dz_two = yield from backward_stages(first, second, cot)
        dfeat = feature_gradients(dz_one, wi)
        x = inputs_at(ft1, base, tiles)
        if counted is not None:
            dz_one, dz_two, cot = (jnp.where(counted, v.astype(F32), 0.0).astype(BF16) for v in (dz_one, dz_two, cot))
        add_terms(sums, (first.astype(BF16), dz_two), (x, dz_one), (second.astype(BF16), cot))
        yield
        put_lanes(df, DEEP, base, tiles, dfeat)

    def add_terms(sums, *pairs):
        for k, pair in enumerate(pairs):
            sums[k] = dot_nt(*pair) if sums[k] is None else sums[k] + dot_nt(*pair)

    def features_of(source, ft, order, rimmed):
        for level in range(levels):
            v = source[level]
            for f, plane in enumerate((v, 0.5 * (east_of(v) - west_of(v)), 0.5 * (north_of(v) - south_of(v)))):
                block.spread(plane, f * levels + level, DEEP, ft, ftx, fth, rimmed)
        block.pack_halo(order, DEEP, ft, ftx, fth)

    features_of(planes, ft1, block.rim, True)
    for k, ref in enumerate(early[2::3]):
        cl[pl.ds(k * ref.shape[0], ref.shape[0]), :] = ref[...]

    def first_part(base, tiles):
        first, second, unused, low_second = yield from forward_stages(inputs_at(ft1, base, tiles), wi_t, wm_t)
        halo1[...] = first
        halo2[...] = second
        yield
        put_lanes(cl, SHALLOW, base, tiles, closure(low_second, wo_t))

    staggered([first_part(rows, len(block.rim))])
    block.unpack_halo(block.rim, SHALLOW, cl, clx, clh)
    for level in range(levels):
        closed = block.gathered(level, SHALLOW, cl, clx, clh, True)
        mid = planes[levels + level] + 2.0 * DT * block.force(planes, planes[level], level, closed)
        o_mid[level] = mid[:rows, :LANES]
        mids[level] = mid
    copies = copied_out([(o_mid, h_mid)], sems.at[pl.ds(0, 1)])

    features_of(mids, ft2, block.outer, False)
    for level in range(levels):
        masked = planes[block.wet] * (2.0 * DT * planes[3 * levels + level])
        block.spread(masked, level, SHALLOW, dc, dcx, dch, False)
    block.pack_halo(block.outer, SHALLOW, dc, dcx, dch)
    sums = [None] * 3
    staggered(
        [second_part(rows, len(block.outer), None)]
        + [second_part(k * PART, PART, sums) for k in range(rows // PART)]
    )
    for acc, total in zip((acc_mid, acc_in, acc_out), sums):
        acc[...] = total
    block.unpack_halo(block.outer, DEEP, df, dfx, dfh)
    for level in range(levels):
        weighted = 2.0 * DT * planes[3 * levels + level]
        grad = planes[4 * levels + level] + block.adjoint(planes, weighted, level, (df, dfx, dfh), False)
        o_old[level] = grad[:rows, :LANES]
        olds[level] = grad
    copies += copied_out([(o_old, h_old)], sems.at[pl.ds(1, 1)])

    near = block.rim_near
    row = lax.broadcasted_iota(jnp.int32, (ext, LANES), 0)
    inside = (lane > 0) & (lane < LANES - 1) & (row > 0) & (row < rows - 1)
    for level in range(levels):
        masked = planes[block.wet] * (2.0 * DT * olds[level])
        body = masked[:, :LANES]
        dc[pl.ds(level, rows, stride=SHALLOW), :] = jnp.where(inside, body, 0.0)[:rows]
        dcx[pl.ds(level, 2 * WIDE, stride=SHALLOW), :] = body[rows:]
        dch[pl.ds(level, ext, stride=SHALLOW), :] = block.with_rim(masked)
        for k, r in enumerate(near[:2]):
            dc[pl.ds((rows + k) * SHALLOW + level, 1), :] = body[r : r + 1]
    block.pack_halo(near, SHALLOW, dc, dcx, dch, False)
    at = lax.broadcasted_iota(jnp.int32, (1, len(near) * LANES), 1)
    tile, place = at >> 7, at & (LANES - 1)
    side_row = (tile - 4) * 16 + (place >> 3)
    edge = ((place & 7) == 0) | ((place & 7) == 7)
    counted = (tile < 2) | ((tile >= 4) & edge & (side_row > 0) & (side_row < rows - 1))
    wide = pl.ds(0, len(near) * LANES)
    sums = [None] * 3
    staggered(
        [third_part(rows, len(near), halo1.at[:, wide], halo2.at[:, wide], counted, sums)]
        + [third_part(k * PART, PART, kept1[k], kept2[k], None, sums) for k in range(rows // PART)]
    )

    start = 0
    for total in (acc_mid[...] + sums[0], acc_in[...] + sums[1], (acc_out[...] + sums[2]).T):
        deep = total.shape[0]
        for half in range(hidden // LANES):
            o_grad[pl.ds(start, deep), :] = total[:, half * LANES : (half + 1) * LANES]
            start += deep
    if start < o_grad.shape[0]:
        o_grad[pl.ds(start, o_grad.shape[0] - start), :] = jnp.zeros((o_grad.shape[0] - start, LANES), F32)
    halve(o_grad[...], 1, o_sent, o_kept)
    for copy in copies:
        copy.wait()


def halve(value, bit, sent, kept):
    half = value.shape[0] // 2
    upper = (lax.axis_index("lat") & bit) != 0
    sent[...] = jnp.where(upper, value[:half], value[half:])
    kept[...] = jnp.where(upper, value[half:], value[:half])


def halve_kernel(bit, held, got, sent, kept):
    halve(held[...] + got[...], bit, sent, kept)


def late_kernel(
    fields, planes, mids, olds, cl, gradients, held, h_new, h_now, o_held, o_place, o_new, o_now, sems, df, dfh, dfx
):
    levels, rows, cols = o_new.shape
    block = Block(levels, rows)
    o_held[...] = held[...]
    o_place[...] = jnp.zeros_like(o_place) + lax.axis_index("lat")
    df[...] = gradients[...]
    beside = jnp.zeros((rows, LANES), F32)
    beyond = jnp.zeros((2 * WIDE, 2 * LANES), F32)
    for level in range(levels):
        closed = jnp.concatenate([cl[pl.ds(level, rows, stride=SHALLOW), :], beside], 1)
        closed = jnp.concatenate([closed, beyond], 0)
        new = planes[level] + 2.0 * DT * block.force(planes, mids[level], level, closed)
        o_new[level] = new[:rows, :LANES]
    copies = copied_out([(o_new, h_new)], sems.at[pl.ds(0, 1)])
    block.unpack_halo(block.rim_near, DEEP, df, dfx, dfh)
    for level in range(levels):
        grad = block.adjoint(planes, 2.0 * DT * olds[level], level, (df, dfx, dfh), True)
        o_now[level] = fields[3 * levels + level] + grad[:rows, :LANES]
    copies += copied_out([(o_now, h_now)], sems.at[pl.ds(1, 1)])
    for copy in copies:
        copy.wait()


def scale_kernel(factor, terms, g_in, g_mid, g_out):
    hidden = g_mid.shape[0]
    start = 0
    for ref, deep in ((g_mid, hidden), (g_in, DEEP), (g_out, DEEP)):
        for half in range(hidden // LANES):
            ref[:, half * LANES : (half + 1) * LANES] = terms[pl.ds(start, ref.shape[0]), :] * factor
            start += deep


def along(value, axis, step):
    count = lax.axis_size(axis)
    return lax.ppermute(value, axis, [(i, (i + step) % count) for i in range(count)])


def swapped(value, axis, bit):
    return lax.ppermute(value, axis, [(i, i ^ bit) for i in range(lax.axis_size(axis))])


def added_up(value, axis):
    bit = 1
    while bit < lax.axis_size(axis):
        near = swapped(value, axis, bit)
        if 2 * bit < lax.axis_size(axis):
            value = (value + near) + (swapped(value, axis, 2 * bit) + swapped(value, axis, 3 * bit))
            bit *= 4
        else:
            value = value + near
            bit *= 2
    return value


def put_together(value, place, axis):
    bit = lax.axis_size(axis) // 2
    while bit:
        upper = (place & bit) != 0
        other = swapped(value, axis, bit)
        value = jnp.concatenate([jnp.where(upper, other, value), jnp.where(upper, value, other)], 0)
        bit //= 2
    return value


def body(state_old, state_now, drift, ocean, w_in, w_mid, w_out, cot_mid, cot_new):
    levels, rows, cols = state_now.shape
    width_in, hidden = w_in.shape
    ext = rows + 2 * WIDE
    count = 5 * levels + 1
    packs = -(-ext // 16)
    slots = rows + 8 + packs
    tall = rows // EARLY
    vmem = pl.BlockSpec(memory_space=pltpu.VMEM)
    hbm = pl.BlockSpec(memory_space=pltpu.HBM)
    strip = jax.ShapeDtypeStruct((rows, LANES), F32)
    edge = jax.ShapeDtypeStruct((count, WIDE, LANES), F32)
    arrays = (state_now, state_old, drift, cot_new, cot_mid, ocean, w_in, w_mid, w_out.T)
    weights = tuple(jax.ShapeDtypeStruct(a.shape, a.dtype) for a in arrays[6:])
    west, east, top, bottom, fields, *weights = pl.pallas_call(
        pack_kernel,
        out_shape=(strip, strip, edge, edge, jax.ShapeDtypeStruct((count, rows, cols), F32)) + weights,
        in_specs=[hbm] * 9,
        out_specs=(vmem,) * 8,
        scratch_shapes=[pltpu.VMEM((rows, cols), jnp.int32), pltpu.SemaphoreType.DMA((9,))],
        compiler_params=pltpu.CompilerParams(vmem_limit_bytes=8 * 2**20),
    )(*(pltpu.with_memory_space_constraint(a, pltpu.HBM) for a in arrays))

    kept = jax.ShapeDtypeStruct((tall // PART, hidden, PART * LANES), F32)
    closed = jax.ShapeDtypeStruct((tall * SHALLOW, LANES), F32)
    tall_weight = jax.ShapeDtypeStruct((hidden, DEEP), BF16)
    flat_weight = jax.ShapeDtypeStruct((DEEP, hidden), BF16)
    prepared = (flat_weight, tall_weight, jax.ShapeDtypeStruct((hidden, hidden), BF16), tall_weight, flat_weight)

    def early(k, extra, extra_out):
        return pl.pallas_call(
            functools.partial(early_kernel, k * tall),
            out_shape=(kept, kept, closed) + extra_out,
            in_specs=[vmem] * (1 + len(extra)),
            out_specs=(vmem,) * (3 + len(extra_out)),
            scratch_shapes=[pltpu.VMEM((tall * DEEP, LANES), F32)],
            compiler_params=pltpu.CompilerParams(vmem_limit_bytes=12 * 2**20),
            cost_estimate=pl.CostEstimate(
                flops=6 * hidden * hidden * tall * cols, bytes_accessed=0, transcendentals=2 * hidden * tall * cols
            ),
        )(fields, *extra)

    left = along(east, "lon", 1)
    right = along(west, "lon", -1)
    *first_kept, wi, wi_t, wm_t, wo, wo_t = early(0, tuple(weights), prepared)
    message = jax.ShapeDtypeStruct((count + 2, WIDE, LANES), F32)
    up, down = pl.pallas_call(
        join_kernel,
        out_shape=(message, message),
        in_specs=[vmem] * 4,
        out_specs=(vmem,) * 2,
        compiler_params=pltpu.CompilerParams(vmem_limit_bytes=4 * 2**20),
    )(top, bottom, left, right)
    low = along(up, "lat", 1)
    high = along(down, "lat", -1)
    done = list(first_kept)
    for k in range(1, EARLY):
        done += early(k, (left, wi_t, wm_t, wo_t), ())

    bands = lax.axis_size("lat")
    halves = hidden // LANES
    terms_rows = -(-halves * (hidden + 2 * DEEP) // (8 * bands)) * 8 * bands
    field = jax.ShapeDtypeStruct((levels, rows, cols), F32)
    ext_planes = jax.ShapeDtypeStruct((levels, ext, 2 * LANES), F32)
    staged = pltpu.VMEM((levels, rows, cols), F32)

    def tiles(deep):
        return [pltpu.VMEM((n * deep, LANES), F32) for n in (slots, 16 * packs, 2 * WIDE)]

    def half_terms(parts):
        return (jax.ShapeDtypeStruct((terms_rows // parts, LANES), F32),) * 2

    kept_halo = pltpu.VMEM((hidden, (8 + packs) * LANES), F32)
    state_mid, grad_old, sent, held, planes, mids, olds, closures, gradients = pl.pallas_call(
        functools.partial(main_kernel, bands),
        out_shape=(field, field, *half_terms(2))
        + (jax.ShapeDtypeStruct((count, ext, 2 * LANES), F32), ext_planes, ext_planes)
        + tuple(jax.ShapeDtypeStruct((slots * deep, LANES), F32) for deep in (SHALLOW, DEEP)),
        in_specs=[vmem] * (11 + 3 * EARLY),
        out_specs=(hbm,) * 2 + (vmem,) * 7,
        scratch_shapes=[
            staged,
            staged,
            pltpu.SemaphoreType.DMA((2,)),
            tiles(DEEP)[0],
            *tiles(DEEP),
            *tiles(SHALLOW)[1:],
            *tiles(SHALLOW),
            *tiles(DEEP)[1:],
            kept_halo,
            kept_halo,
            pltpu.VMEM((hidden, hidden), F32),
            pltpu.VMEM((DEEP, hidden), F32),
            pltpu.VMEM((hidden, DEEP), F32),
            pltpu.VMEM((terms_rows, LANES), F32),
        ],
        compiler_params=pltpu.CompilerParams(vmem_limit_bytes=32 * 2**20),
    )(fields, left, right, low, high, wi, wi_t, wm_t, weights[1], wo, wo_t, *done)

    bit = 1
    while 2 * bit < bands:
        got = swapped(sent, "lat", bit)
        bit *= 2
        sent, held = pl.pallas_call(
            functools.partial(halve_kernel, bit),
            out_shape=half_terms(2 * bit),
            in_specs=[vmem] * 2,
            out_specs=(vmem,) * 2,
            compiler_params=pltpu.CompilerParams(vmem_limit_bytes=4 * 2**20),
        )(held, got)
    got = swapped(sent, "lat", bit)
    state_new, grad_now, held, place = pl.pallas_call(
        late_kernel,
        out_shape=(field, field, half_terms(bands)[0], jax.ShapeDtypeStruct((8, LANES), jnp.int32)),
        in_specs=[vmem] * 7,
        out_specs=(hbm,) * 2 + (vmem,) * 2,
        scratch_shapes=[staged, staged, pltpu.SemaphoreType.DMA((2,)), *tiles(DEEP)],
        compiler_params=pltpu.CompilerParams(vmem_limit_bytes=16 * 2**20),
        cost_estimate=pl.CostEstimate(
            flops=2 * hidden * hidden * rows * cols, bytes_accessed=0, transcendentals=0
        ),
    )(fields, planes, mids, olds, closures, gradients, held)
    summed = put_together(added_up(held + got, "lon"), place[:1], "lat")
    cells_all = rows * lax.axis_size("lat") * cols * lax.axis_size("lon")
    grad_in, grad_mid, grad_out = pl.pallas_call(
        functools.partial(scale_kernel, GAIN_GRAD / cells_all**0.5),
        out_shape=(
            jax.ShapeDtypeStruct((width_in, hidden), F32),
            jax.ShapeDtypeStruct((hidden, hidden), F32),
            jax.ShapeDtypeStruct((levels, hidden), F32),
        ),
        in_specs=[vmem],
        out_specs=(vmem,) * 3,
        compiler_params=pltpu.CompilerParams(vmem_limit_bytes=8 * 2**20),
    )(summed)
    return state_mid, state_new, grad_old, grad_now, grad_in, grad_mid, grad_out.T


def solution(mesh):
    field = P("grp", "lat", "lon")
    whole = P("grp", None)
    in_specs = (field, field, field, P(("grp", "lat"), "lon"), P(), P(), P(), field, field)
    out_specs = (field, field, field, field, whole, whole, whole)
    return jax.shard_map(body, mesh=mesh, in_specs=in_specs, out_specs=out_specs, check_vma=False)
```

```python
import functools

import jax
import jax.numpy as jnp
from jax import lax
from jax.experimental import pallas as pl
from jax.experimental.pallas import tpu as pltpu
from jax.sharding import PartitionSpec as P

KAPPA = 0.2
DT = 0.1
GAIN_GRAD = 10.0

WIDE = 4
LANES = 128
PART = 8
EARLY = 2
DEEP = 16
SHALLOW = 8

F32 = jnp.float32
BF16 = jnp.bfloat16


def dot(left, right):
    return lax.dot_general(left, right, (((1,), (0,)), ((), ())), preferred_element_type=F32)


def dot_nt(left, right):
    return lax.dot_general(left, right, (((1,), (1,)), ((), ())), preferred_element_type=F32)


def pack_kernel(
    now, old, drift, cnew, cmid, ocean, w_in, w_mid, w_out,
    west, east, top, bottom, fields, v_in, v_mid, v_out, wet, sems,
):
    levels, rows, cols = now.shape
    copies = [
        pltpu.make_async_copy(ref, fields.at[pl.ds(levels * f, levels)], sems.at[f])
        for f, ref in enumerate((now, old, drift, cnew, cmid))
    ]
    copies.append(pltpu.make_async_copy(ocean, wet, sems.at[5]))
    for k, pair in enumerate(((w_in, v_in), (w_mid, v_mid), (w_out, v_out))):
        copies.append(pltpu.make_async_copy(*pair, sems.at[6 + k]))
    for copy in copies:
        copy.start()
    lane = lax.broadcasted_iota(jnp.int32, (rows, LANES), 1)
    to_west = jnp.zeros((rows, LANES), F32)
    to_east = jnp.zeros((rows, LANES), F32)
    count = fields.shape[0]
    for p in range(count):
        if p % levels == 0:
            copies[p // levels].wait()
        if p == count - 1:
            fields[p] = wet[...].astype(F32)
        plane = fields[p]
        here = (lane >= WIDE * p) & (lane < WIDE * (p + 1))
        to_west = jnp.where(here, pltpu.roll(plane, WIDE * p, 1) if p else plane, to_west)
        to_east = jnp.where(here, pltpu.roll(plane, WIDE * (p + 1), 1), to_east)
        top[p] = plane[:WIDE]
        bottom[p] = plane[rows - WIDE :]
    west[...] = to_west
    east[...] = to_east
    for copy in copies[6:]:
        copy.wait()


def join_kernel(top, bottom, left, right, up, down):
    count = top.shape[0]
    rows = left.shape[0]
    up[pl.ds(0, count)] = bottom[...]
    down[pl.ds(0, count)] = top[...]
    for k, strip in enumerate((left, right)):
        up[count + k] = strip[pl.ds(rows - WIDE, WIDE), :]
        down[count + k] = strip[pl.ds(0, WIDE), :]


def east_of(v):
    return pltpu.roll(v, v.shape[1] - 1, 1)


def west_of(v):
    return pltpu.roll(v, 1, 1)


def north_of(v):
    return pltpu.roll(v, v.shape[0] - 1, 0)


def south_of(v):
    return pltpu.roll(v, 1, 0)


def forward_stages(x, w_first_t, w_second_t):
    z_one = dot(w_first_t[...], x)
    yield
    first = jnp.tanh(z_one)
    low_first = first.astype(BF16)
    yield
    z_two = dot(w_second_t[...], low_first)
    yield
    second = jnp.tanh(z_two)
    return first, second, low_first, second.astype(BF16)


def closure(low_second, w_last_t):
    return dot(w_last_t[...], low_second).astype(BF16).astype(F32)[:SHALLOW]


def staggered(generators):
    live = []
    waiting = list(generators)
    while live or waiting:
        if waiting:
            live.append(waiting.pop(0))
        for part in list(live):
            try:
                next(part)
            except StopIteration:
                live.remove(part)


def lanes_of(ref, deep, base, tiles):
    block = ref[pl.ds(base * deep, tiles * deep), :]
    return jnp.concatenate([block[k * deep : (k + 1) * deep] for k in range(tiles)], 1)


def put_lanes(ref, deep, base, tiles, value):
    for k in range(tiles):
        ref[pl.ds((base + k) * deep, deep), :] = value[:, k * LANES : (k + 1) * LANES]


def early_kernel(start, fields, *refs):
    if start == 0:
        w_in, w_mid, w_out_t, keep1, keep2, cl, wi, wi_t, wm_t, wo, wo_t, ft = refs
        width_in, hidden = w_in.shape
        levels = w_out_t.shape[0]
        spare = jnp.zeros((DEEP - width_in, hidden), F32)
        wide_in = jnp.concatenate([w_in[...].astype(F32), spare], 0)
        wi[...] = wide_in.astype(BF16)
        wi_t[...] = wide_in.T.astype(BF16)
        wm_t[...] = w_mid[...].astype(F32).T.astype(BF16)
        spare = jnp.zeros((DEEP - levels, hidden), F32)
        wide_out = jnp.concatenate([w_out_t[...].astype(F32), spare], 0)
        wo_t[...] = wide_out.astype(BF16)
        wo[...] = wide_out.T.astype(BF16)
    else:
        unused, wi_t, wm_t, wo_t, keep1, keep2, cl, ft = refs
        levels = (fields.shape[0] - 1) // 5
    tall = cl.shape[0] // SHALLOW
    ft[...] = jnp.zeros_like(ft)
    for level in range(levels):
        v = fields[level]
        slope_x = 0.5 * (east_of(v) - west_of(v))
        slope_y = 0.5 * (north_of(v) - south_of(v))
        for f, plane in enumerate((v, slope_x, slope_y)):
            ft[pl.ds(f * levels + level, tall, stride=DEEP), :] = plane[start : start + tall]

    def part(base, kept1, kept2):
        x = lanes_of(ft, DEEP, base, PART).astype(BF16)
        first, second, unused_low, low_second = yield from forward_stages(x, wi_t, wm_t)
        kept1[...] = first
        kept2[...] = second
        yield
        put_lanes(cl, SHALLOW, base, PART, closure(low_second, wo_t))

    staggered(part(k * PART, keep1.at[k], keep2.at[k]) for k in range(tall // PART))


def copied_out(pairs, sems):
    copies = [pltpu.make_async_copy(*pair, sems.at[k]) for k, pair in enumerate(pairs)]
    for copy in copies:
        copy.start()
    return copies


class Block:
    def __init__(self, levels, rows):
        self.levels, self.rows = levels, rows
        self.ext = rows + 2 * WIDE
        self.packs = -(-self.ext // 16)
        self.wet = 5 * levels
        packed = [None] * self.packs
        ext = self.ext
        self.rim = [0, rows - 1, rows, ext - 1] + packed + [rows + 1, ext - 2, rows + 2, ext - 3]
        self.rim_near = self.rim[: 4 + self.packs]
        self.outer = [rows, ext - 1] + packed + [rows + 1, ext - 2]
        self.lane = lax.broadcasted_iota(jnp.int32, (ext, LANES), 1)

    def with_rim(self, plane):
        lane = self.lane
        body, side = plane[:, :LANES], plane[:, LANES:]
        own = jnp.where(lane == LANES - WIDE, pltpu.roll(body, LANES - WIDE, 1), pltpu.roll(body, WIDE, 1))
        return jnp.where((lane == LANES - WIDE) | (lane == WIDE - 1), own, side)

    def from_rim(self, body, side):
        lane = self.lane
        own = jnp.where(lane == 0, pltpu.roll(side, WIDE, 1), pltpu.roll(side, LANES - WIDE, 1))
        return jnp.where((lane == 0) | (lane == LANES - 1), own, body)

    def spread(self, plane, index, deep, main, extra, side, rimmed):
        main[pl.ds(index, self.rows, stride=deep), :] = plane[: self.rows, :LANES]
        extra[pl.ds(index, 2 * WIDE, stride=deep), :] = plane[self.rows :, :LANES]
        side[pl.ds(index, self.ext, stride=deep), :] = self.with_rim(plane) if rimmed else plane[:, LANES:]

    def gathered(self, index, deep, main, extra, side, rimmed):
        body = jnp.concatenate(
            [main[pl.ds(index, self.rows, stride=deep), :], extra[pl.ds(index, 2 * WIDE, stride=deep), :]], 0
        )
        beside = side[pl.ds(index, self.ext, stride=deep), :]
        return jnp.concatenate([self.from_rim(body, beside) if rimmed else body, beside], 1)

    def home(self, r, deep, main, extra):
        return main.at[pl.ds(r * deep, deep)] if r < self.rows else extra.at[pl.ds((r - self.rows) * deep, deep)]

    def pack_halo(self, order, deep, main, extra, side, rim_too=True):
        where = lax.broadcasted_iota(jnp.int32, (deep, LANES), 1)
        for i, r in enumerate(order):
            if r is not None and (rim_too or r >= self.rows):
                main[pl.ds((self.rows + i) * deep, deep), :] = self.home(r, deep, main, extra)[...]
        first_pack = self.rows + order.index(None)
        for q in range(self.packs):
            total = jnp.zeros((deep, LANES), F32)
            for j in range(min(16, self.ext - 16 * q)):
                moved = pltpu.roll(side[pl.ds((16 * q + j) * deep, deep), :], (2 * WIDE * j + WIDE) % LANES, 1)
                total = jnp.where((where >= 2 * WIDE * j) & (where < 2 * WIDE * (j + 1)), moved, total)
            main[pl.ds((first_pack + q) * deep, deep), :] = total

    def unpack_halo(self, order, deep, main, extra, side):
        for i, r in enumerate(order):
            if r is not None:
                self.home(r, deep, main, extra)[...] = main[pl.ds((self.rows + i) * deep, deep), :]
        first_pack = self.rows + order.index(None)
        for q in range(self.packs):
            tile = main[pl.ds((first_pack + q) * deep, deep), :]
            for j in range(min(16, self.ext - 16 * q)):
                moved = pltpu.roll(tile, LANES - (2 * WIDE * j + WIDE) % LANES, 1)
                side[pl.ds((16 * q + j) * deep, deep), :] = moved

    def force(self, planes, v, level, closed):
        eastward, westward, northward, southward = east_of(v), west_of(v), north_of(v), south_of(v)
        laplace = eastward + westward + northward + southward - 4.0 * v
        slope = 0.5 * (eastward - westward)
        return planes[self.wet] * (KAPPA * laplace - planes[2 * self.levels + level] * slope + closed)

    def adjoint(self, planes, weighted, level, tiles, rimmed):
        levels = self.levels
        masked = planes[self.wet] * weighted
        carried = planes[2 * levels + level] * masked
        a0, a1, a2 = (self.gathered(f * levels + level, DEEP, *tiles, rimmed) for f in range(3))
        result = KAPPA * (east_of(masked) + west_of(masked) + north_of(masked) + south_of(masked) - 4.0 * masked)
        result = result + 0.5 * (east_of(carried) - west_of(carried)) + a0
        return result - 0.5 * (east_of(a1) - west_of(a1)) - 0.5 * (north_of(a2) - south_of(a2))


def feature_gradients(dz_one, w_in):
    return dot(w_in[...], dz_one).astype(BF16).astype(F32)


def main_kernel(bands, *refs):
    fields, left, right, low, high, wi, wi_t, wm_t, w_mid, wo, wo_t, *refs = refs
    early, refs = refs[: 3 * EARLY], refs[3 * EARLY :]
    h_mid, h_old, o_sent, o_kept, planes, mids, olds, cl, df, *refs = refs
    o_mid, o_old, sems, ft1, ft2, fth, ftx, clh, clx, dc, dch, dcx, dfh, dfx, halo1, halo2, *refs = refs
    acc_mid, acc_in, acc_out, o_grad = refs
    levels, rows, cols = o_mid.shape
    hidden = w_mid.shape[0]
    block = Block(levels, rows)
    count, ext, lane = block.wet + 1, block.ext, block.lane
    kept1 = [ref.at[k] for ref in early[0::3] for k in range(ref.shape[0])]
    kept2 = [ref.at[k] for ref in early[1::3] for k in range(ref.shape[0])]

    band = lax.axis_index("lat")
    has_low = jnp.where(band > 0, 1.0, 0.0)
    has_high = jnp.where(band < bands - 1, 1.0, 0.0)

    def beyond(p):
        return [high[p] * has_high, low[p] * has_low]

    left_all = jnp.concatenate([left[...]] + beyond(count), 0)
    right_all = jnp.concatenate([right[...]] + beyond(count + 1), 0)
    for p in range(count):
        from_right = pltpu.roll(right_all, LANES - WIDE * p, 1) if p else right_all
        from_left = pltpu.roll(left_all, LANES - WIDE * (p + 1), 1)
        side = jnp.where(lane < WIDE, from_right, jnp.where(lane >= LANES - WIDE, from_left, 0.0))
        planes[p, :, pl.ds(0, LANES)] = jnp.concatenate([fields[p]] + beyond(p), 0)
        planes[p, :, pl.ds(LANES, LANES)] = side

    for ref in (ft1, ft2, fth, ftx, dc, dch, dcx):
        ref[...] = jnp.zeros_like(ref)

    def inputs_at(ref, base, tiles):
        return lanes_of(ref, DEEP, base, tiles).astype(BF16)

    def cotangents_at(base, tiles):
        part = lanes_of(dc, SHALLOW, base, tiles)
        return jnp.concatenate([part, jnp.zeros_like(part)], 0).astype(BF16)

    def backward_stages(first, second, cot):
        g_two = dot(wo[...], cot)
        yield
        dz_two = (g_two * (1.0 - second * second)).astype(BF16)
        yield
        g_one = dot(w_mid[...], dz_two)
        yield
        dz_one = (g_one * (1.0 - first * first)).astype(BF16)
        yield
        return dz_one, dz_two

    def second_part(base, tiles, sums):
        x = inputs_at(ft2, base, tiles)
        cot = cotangents_at(base, tiles)
        first, second, low_first, low_second = yield from forward_stages(x, wi_t, wm_t)
        yield
        if sums is not None:
            put_lanes(cl, SHALLOW, base, tiles, closure(low_second, wo_t))
        dz_one, dz_two = yield from backward_stages(first, second, cot)
        dfeat = feature_gradients(dz_one, wi)
        if sums is not None:
            add_terms(sums, (low_first, dz_two), (x, dz_one), (low_second, cot))
        yield
        put_lanes(df, DEEP, base, tiles, dfeat)

    def third_part(base, tiles, held1, held2, counted, sums):
        cot = cotangents_at(base, tiles)
        first = held1[...]
        second = held2[...]
        dz_one, dz_two = yield from backward_stages(first, second, cot)
        dfeat = feature_gradients(dz_one, wi)
        x = inputs_at(ft1, base, tiles)
        if counted is not None:
            dz_one, dz_two, cot = (jnp.where(counted, v.astype(F32), 0.0).astype(BF16) for v in (dz_one, dz_two, cot))
        add_terms(sums, (first.astype(BF16), dz_two), (x, dz_one), (second.astype(BF16), cot))
        yield
        put_lanes(df, DEEP, base, tiles, dfeat)

    def add_terms(sums, *pairs):
        for k, pair in enumerate(pairs):
            sums[k] = dot_nt(*pair) if sums[k] is None else sums[k] + dot_nt(*pair)

    def features_of(source, ft, order, rimmed):
        for level in range(levels):
            v = source[level]
            for f, plane in enumerate((v, 0.5 * (east_of(v) - west_of(v)), 0.5 * (north_of(v) - south_of(v)))):
                block.spread(plane, f * levels + level, DEEP, ft, ftx, fth, rimmed)
        block.pack_halo(order, DEEP, ft, ftx, fth)

    features_of(planes, ft1, block.rim, True)
    for k, ref in enumerate(early[2::3]):
        cl[pl.ds(k * ref.shape[0], ref.shape[0]), :] = ref[...]

    def first_part(base, tiles):
        first, second, unused, low_second = yield from forward_stages(inputs_at(ft1, base, tiles), wi_t, wm_t)
        halo1[...] = first
        halo2[...] = second
        yield
        put_lanes(cl, SHALLOW, base, tiles, closure(low_second, wo_t))

    staggered([first_part(rows, len(block.rim))])
    block.unpack_halo(block.rim, SHALLOW, cl, clx, clh)
    for level in range(levels):
        closed = block.gathered(level, SHALLOW, cl, clx, clh, True)
        mid = planes[levels + level] + 2.0 * DT * block.force(planes, planes[level], level, closed)
        o_mid[level] = mid[:rows, :LANES]
        mids[level] = mid
    copies = copied_out([(o_mid, h_mid)], sems.at[pl.ds(0, 1)])

    features_of(mids, ft2, block.outer, False)
    for level in range(levels):
        masked = planes[block.wet] * (2.0 * DT * planes[3 * levels + level])
        block.spread(masked, level, SHALLOW, dc, dcx, dch, False)
    block.pack_halo(block.outer, SHALLOW, dc, dcx, dch)
    sums = [None] * 3
    staggered(
        [second_part(rows, len(block.outer), None)]
        + [second_part(k * PART, PART, sums) for k in range(rows // PART)]
    )
    for acc, total in zip((acc_mid, acc_in, acc_out), sums):
        acc[...] = total
    block.unpack_halo(block.outer, DEEP, df, dfx, dfh)
    for level in range(levels):
        weighted = 2.0 * DT * planes[3 * levels + level]
        grad = planes[4 * levels + level] + block.adjoint(planes, weighted, level, (df, dfx, dfh), False)
        o_old[level] = grad[:rows, :LANES]
        olds[level] = grad
    copies += copied_out([(o_old, h_old)], sems.at[pl.ds(1, 1)])

    near = block.rim_near
    row = lax.broadcasted_iota(jnp.int32, (ext, LANES), 0)
    inside = (lane > 0) & (lane < LANES - 1) & (row > 0) & (row < rows - 1)
    for level in range(levels):
        masked = planes[block.wet] * (2.0 * DT * olds[level])
        body = masked[:, :LANES]
        dc[pl.ds(level, rows, stride=SHALLOW), :] = jnp.where(inside, body, 0.0)[:rows]
        dcx[pl.ds(level, 2 * WIDE, stride=SHALLOW), :] = body[rows:]
        dch[pl.ds(level, ext, stride=SHALLOW), :] = block.with_rim(masked)
        for k, r in enumerate(near[:2]):
            dc[pl.ds((rows + k) * SHALLOW + level, 1), :] = body[r : r + 1]
    block.pack_halo(near, SHALLOW, dc, dcx, dch, False)
    at = lax.broadcasted_iota(jnp.int32, (1, len(near) * LANES), 1)
    tile, place = at >> 7, at & (LANES - 1)
    side_row = (tile - 4) * 16 + (place >> 3)
    edge = ((place & 7) == 0) | ((place & 7) == 7)
    counted = (tile < 2) | ((tile >= 4) & edge & (side_row > 0) & (side_row < rows - 1))
    wide = pl.ds(0, len(near) * LANES)
    sums = [None] * 3
    staggered(
        [third_part(rows, len(near), halo1.at[:, wide], halo2.at[:, wide], counted, sums)]
        + [third_part(k * PART, PART, kept1[k], kept2[k], None, sums) for k in range(rows // PART)]
    )

    start = 0
    for total in (acc_mid[...] + sums[0], acc_in[...] + sums[1], (acc_out[...] + sums[2]).T):
        deep = total.shape[0]
        for half in range(hidden // LANES):
            o_grad[pl.ds(start, deep), :] = total[:, half * LANES : (half + 1) * LANES]
            start += deep
    if start < o_grad.shape[0]:
        o_grad[pl.ds(start, o_grad.shape[0] - start), :] = jnp.zeros((o_grad.shape[0] - start, LANES), F32)
    halve(o_grad[...], 1, o_sent, o_kept)
    for copy in copies:
        copy.wait()


def halve(value, bit, sent, kept):
    half = value.shape[0] // 2
    upper = (lax.axis_index("lat") & bit) != 0
    sent[...] = jnp.where(upper, value[:half], value[half:])
    kept[...] = jnp.where(upper, value[half:], value[:half])


def quarter_of(ref, place):
    rows = ref.shape[0] // 4
    return ref.at[pl.ds(pl.multiple_of(place * rows, 8), rows)]


def deal_kernel(held, got, own, *refs):
    sent, total = refs[:-1], refs[-1]
    total[...] = held[...] + got[...]
    place = lax.axis_index("lon") & 3
    own[...] = quarter_of(total, place)[...]
    for k, ref in enumerate(sent):
        ref[...] = quarter_of(total, place ^ (k + 1))[...]


def collect_kernel(own, *refs):
    got, whole = refs[:-1], refs[-1]
    place = lax.axis_index("lon") & 3
    quarter_of(whole, place)[...] = own[...]
    for k, ref in enumerate(got):
        quarter_of(whole, place ^ (k + 1))[...] = ref[...]


def late_kernel(
    fields, planes, mids, olds, cl, gradients, held, h_new, h_now, o_held, o_new, o_now, sems, df, dfh, dfx
):
    levels, rows, cols = o_new.shape
    block = Block(levels, rows)
    o_held[...] = held[...]
    df[...] = gradients[...]
    beside = jnp.zeros((rows, LANES), F32)
    beyond = jnp.zeros((2 * WIDE, 2 * LANES), F32)
    for level in range(levels):
        closed = jnp.concatenate([cl[pl.ds(level, rows, stride=SHALLOW), :], beside], 1)
        closed = jnp.concatenate([closed, beyond], 0)
        new = planes[level] + 2.0 * DT * block.force(planes, mids[level], level, closed)
        o_new[level] = new[:rows, :LANES]
    copies = copied_out([(o_new, h_new)], sems.at[pl.ds(0, 1)])
    block.unpack_halo(block.rim_near, DEEP, df, dfx, dfh)
    for level in range(levels):
        grad = block.adjoint(planes, 2.0 * DT * olds[level], level, (df, dfx, dfh), True)
        o_now[level] = fields[3 * levels + level] + grad[:rows, :LANES]
    copies += copied_out([(o_now, h_now)], sems.at[pl.ds(1, 1)])
    for copy in copies:
        copy.wait()


def scale_kernel(factor, mine, other, g_in, g_mid, g_out, terms):
    half = mine.shape[0]
    upper = (lax.axis_index("lat") & 1) != 0
    terms[pl.ds(0, half), :] = jnp.where(upper, other[...], mine[...]) * factor
    terms[pl.ds(half, half), :] = jnp.where(upper, mine[...], other[...]) * factor
    hidden = g_mid.shape[0]
    start = 0
    for ref, deep in ((g_mid, hidden), (g_in, DEEP), (g_out, DEEP)):
        for half in range(hidden // LANES):
            ref[:, half * LANES : (half + 1) * LANES] = terms[pl.ds(start, ref.shape[0]), :]
            start += deep


def along(value, axis, step):
    count = lax.axis_size(axis)
    return lax.ppermute(value, axis, [(i, (i + step) % count) for i in range(count)])


def swapped(value, axis, bit):
    return lax.ppermute(value, axis, [(i, i ^ bit) for i in range(lax.axis_size(axis))])


def added_up(value, axis, bit):
    while bit < lax.axis_size(axis):
        near = swapped(value, axis, bit)
        if 2 * bit < lax.axis_size(axis):
            value = (value + near) + (swapped(value, axis, 2 * bit) + swapped(value, axis, 3 * bit))
            bit *= 4
        else:
            value = value + near
            bit *= 2
    return value


def body(state_old, state_now, drift, ocean, w_in, w_mid, w_out, cot_mid, cot_new):
    levels, rows, cols = state_now.shape
    width_in, hidden = w_in.shape
    ext = rows + 2 * WIDE
    count = 5 * levels + 1
    packs = -(-ext // 16)
    slots = rows + 8 + packs
    tall = rows // EARLY
    vmem = pl.BlockSpec(memory_space=pltpu.VMEM)
    hbm = pl.BlockSpec(memory_space=pltpu.HBM)
    strip = jax.ShapeDtypeStruct((rows, LANES), F32)
    edge = jax.ShapeDtypeStruct((count, WIDE, LANES), F32)
    arrays = (state_now, state_old, drift, cot_new, cot_mid, ocean, w_in, w_mid, w_out.T)
    weights = tuple(jax.ShapeDtypeStruct(a.shape, a.dtype) for a in arrays[6:])
    west, east, top, bottom, fields, *weights = pl.pallas_call(
        pack_kernel,
        out_shape=(strip, strip, edge, edge, jax.ShapeDtypeStruct((count, rows, cols), F32)) + weights,
        in_specs=[hbm] * 9,
        out_specs=(vmem,) * 8,
        scratch_shapes=[pltpu.VMEM((rows, cols), jnp.int32), pltpu.SemaphoreType.DMA((9,))],
        compiler_params=pltpu.CompilerParams(vmem_limit_bytes=8 * 2**20),
    )(*(pltpu.with_memory_space_constraint(a, pltpu.HBM) for a in arrays))

    kept = jax.ShapeDtypeStruct((tall // PART, hidden, PART * LANES), F32)
    closed = jax.ShapeDtypeStruct((tall * SHALLOW, LANES), F32)
    tall_weight = jax.ShapeDtypeStruct((hidden, DEEP), BF16)
    flat_weight = jax.ShapeDtypeStruct((DEEP, hidden), BF16)
    prepared = (flat_weight, tall_weight, jax.ShapeDtypeStruct((hidden, hidden), BF16), tall_weight, flat_weight)

    def early(k, extra, extra_out):
        return pl.pallas_call(
            functools.partial(early_kernel, k * tall),
            out_shape=(kept, kept, closed) + extra_out,
            in_specs=[vmem] * (1 + len(extra)),
            out_specs=(vmem,) * (3 + len(extra_out)),
            scratch_shapes=[pltpu.VMEM((tall * DEEP, LANES), F32)],
            compiler_params=pltpu.CompilerParams(vmem_limit_bytes=12 * 2**20),
            cost_estimate=pl.CostEstimate(
                flops=6 * hidden * hidden * tall * cols, bytes_accessed=0, transcendentals=2 * hidden * tall * cols
            ),
        )(fields, *extra)

    left = along(east, "lon", 1)
    right = along(west, "lon", -1)
    *first_kept, wi, wi_t, wm_t, wo, wo_t = early(0, tuple(weights), prepared)
    message = jax.ShapeDtypeStruct((count + 2, WIDE, LANES), F32)
    up, down = pl.pallas_call(
        join_kernel,
        out_shape=(message, message),
        in_specs=[vmem] * 4,
        out_specs=(vmem,) * 2,
        compiler_params=pltpu.CompilerParams(vmem_limit_bytes=4 * 2**20),
    )(top, bottom, left, right)
    low = along(up, "lat", 1)
    high = along(down, "lat", -1)
    done = list(first_kept)
    for k in range(1, EARLY):
        done += early(k, (left, wi_t, wm_t, wo_t), ())

    bands = lax.axis_size("lat")
    halves = hidden // LANES
    terms_rows = -(-halves * (hidden + 2 * DEEP) // 64) * 64
    field = jax.ShapeDtypeStruct((levels, rows, cols), F32)
    ext_planes = jax.ShapeDtypeStruct((levels, ext, 2 * LANES), F32)
    staged = pltpu.VMEM((levels, rows, cols), F32)

    def tiles(deep):
        return [pltpu.VMEM((n * deep, LANES), F32) for n in (slots, 16 * packs, 2 * WIDE)]

    half = jax.ShapeDtypeStruct((terms_rows // 2, LANES), F32)
    eighth = jax.ShapeDtypeStruct((terms_rows // 8, LANES), F32)

    kept_halo = pltpu.VMEM((hidden, (8 + packs) * LANES), F32)
    state_mid, grad_old, sent, held, planes, mids, olds, closures, gradients = pl.pallas_call(
        functools.partial(main_kernel, bands),
        out_shape=(field, field, half, half)
        + (jax.ShapeDtypeStruct((count, ext, 2 * LANES), F32), ext_planes, ext_planes)
        + tuple(jax.ShapeDtypeStruct((slots * deep, LANES), F32) for deep in (SHALLOW, DEEP)),
        in_specs=[vmem] * (11 + 3 * EARLY),
        out_specs=(hbm,) * 2 + (vmem,) * 7,
        scratch_shapes=[
            staged,
            staged,
            pltpu.SemaphoreType.DMA((2,)),
            tiles(DEEP)[0],
            *tiles(DEEP),
            *tiles(SHALLOW)[1:],
            *tiles(SHALLOW),
            *tiles(DEEP)[1:],
            kept_halo,
            kept_halo,
            pltpu.VMEM((hidden, hidden), F32),
            pltpu.VMEM((DEEP, hidden), F32),
            pltpu.VMEM((hidden, DEEP), F32),
            pltpu.VMEM((terms_rows, LANES), F32),
        ],
        compiler_params=pltpu.CompilerParams(vmem_limit_bytes=32 * 2**20),
    )(fields, left, right, low, high, wi, wi_t, wm_t, weights[1], wo, wo_t, *done)

    got = swapped(sent, "lat", 1)
    own, *quarters = pl.pallas_call(
        deal_kernel,
        out_shape=(eighth,) * 4,
        in_specs=[vmem] * 2,
        out_specs=(vmem,) * 4,
        scratch_shapes=[pltpu.VMEM(half.shape, F32)],
        compiler_params=pltpu.CompilerParams(vmem_limit_bytes=4 * 2**20),
    )(held, got)
    got = [swapped(quarter, "lon", k + 1) for k, quarter in enumerate(quarters)]
    state_new, grad_now, own = pl.pallas_call(
        late_kernel,
        out_shape=(field, field, eighth),
        in_specs=[vmem] * 7,
        out_specs=(hbm,) * 2 + (vmem,),
        scratch_shapes=[staged, staged, pltpu.SemaphoreType.DMA((2,)), *tiles(DEEP)],
        compiler_params=pltpu.CompilerParams(vmem_limit_bytes=16 * 2**20),
        cost_estimate=pl.CostEstimate(
            flops=2 * hidden * hidden * rows * cols, bytes_accessed=0, transcendentals=0
        ),
    )(fields, planes, mids, olds, closures, gradients, own)
    own = (own + got[0]) + (got[1] + got[2])
    own = added_up(added_up(own, "lat", 2), "lon", 4)
    mine = pl.pallas_call(
        collect_kernel,
        out_shape=half,
        in_specs=[vmem] * 4,
        out_specs=vmem,
        compiler_params=pltpu.CompilerParams(vmem_limit_bytes=4 * 2**20),
    )(own, *(swapped(own, "lon", k) for k in (1, 2, 3)))
    other = swapped(mine, "lat", 1)
    cells_all = rows * lax.axis_size("lat") * cols * lax.axis_size("lon")
    grad_in, grad_mid, grad_out = pl.pallas_call(
        functools.partial(scale_kernel, GAIN_GRAD / cells_all**0.5),
        out_shape=(
            jax.ShapeDtypeStruct((width_in, hidden), F32),
            jax.ShapeDtypeStruct((hidden, hidden), F32),
            jax.ShapeDtypeStruct((levels, hidden), F32),
        ),
        in_specs=[vmem] * 2,
        out_specs=(vmem,) * 3,
        scratch_shapes=[pltpu.VMEM((terms_rows, LANES), F32)],
        compiler_params=pltpu.CompilerParams(vmem_limit_bytes=8 * 2**20),
    )(mine, other)
    return state_mid, state_new, grad_old, grad_now, grad_in, grad_mid, grad_out.T


def solution(mesh):
    field = P("grp", "lat", "lon")
    whole = P("grp", None)
    in_specs = (field, field, field, P(("grp", "lat"), "lon"), P(), P(), P(), field, field)
    out_specs = (field, field, field, field, whole, whole, whole)
    return jax.shard_map(body, mesh=mesh, in_specs=in_specs, out_specs=out_specs, check_vma=False)
```

```python
import functools

import jax
import jax.numpy as jnp
from jax import lax
from jax.experimental import pallas as pl
from jax.experimental.pallas import tpu as pltpu
from jax.sharding import PartitionSpec as P

KAPPA = 0.2
DT = 0.1
GAIN_GRAD = 10.0

WIDE = 4
LANES = 128
PART = 8
DEFERRED = 3
EARLY = 2
DEEP = 16
SHALLOW = 8

F32 = jnp.float32
BF16 = jnp.bfloat16


def dot(left, right):
    return lax.dot_general(left, right, (((1,), (0,)), ((), ())), preferred_element_type=F32)


def dot_nt(left, right):
    return lax.dot_general(left, right, (((1,), (1,)), ((), ())), preferred_element_type=F32)


def pack_kernel(
    now, old, drift, cnew, cmid, ocean, w_in, w_mid, w_out,
    west, east, top, bottom, fields, v_in, v_mid, v_out, wet, sems,
):
    levels, rows, cols = now.shape
    copies = [
        pltpu.make_async_copy(ref, fields.at[pl.ds(levels * f, levels)], sems.at[f])
        for f, ref in enumerate((now, old, drift, cnew, cmid))
    ]
    copies.append(pltpu.make_async_copy(ocean, wet, sems.at[5]))
    for k, pair in enumerate(((w_in, v_in), (w_mid, v_mid), (w_out, v_out))):
        copies.append(pltpu.make_async_copy(*pair, sems.at[6 + k]))
    for copy in copies:
        copy.start()
    lane = lax.broadcasted_iota(jnp.int32, (rows, LANES), 1)
    to_west = jnp.zeros((rows, LANES), F32)
    to_east = jnp.zeros((rows, LANES), F32)
    count = fields.shape[0]
    for p in range(count):
        if p % levels == 0:
            copies[p // levels].wait()
        if p == count - 1:
            fields[p] = wet[...].astype(F32)
        plane = fields[p]
        here = (lane >= WIDE * p) & (lane < WIDE * (p + 1))
        to_west = jnp.where(here, pltpu.roll(plane, WIDE * p, 1) if p else plane, to_west)
        to_east = jnp.where(here, pltpu.roll(plane, WIDE * (p + 1), 1), to_east)
        top[p] = plane[:WIDE]
        bottom[p] = plane[rows - WIDE :]
    west[...] = to_west
    east[...] = to_east
    for copy in copies[6:]:
        copy.wait()


def join_kernel(top, bottom, left, right, up, down):
    count = top.shape[0]
    rows = left.shape[0]
    up[pl.ds(0, count)] = bottom[...]
    down[pl.ds(0, count)] = top[...]
    for k, strip in enumerate((left, right)):
        up[count + k] = strip[pl.ds(rows - WIDE, WIDE), :]
        down[count + k] = strip[pl.ds(0, WIDE), :]


def east_of(v):
    return pltpu.roll(v, v.shape[1] - 1, 1)


def west_of(v):
    return pltpu.roll(v, 1, 1)


def north_of(v):
    return pltpu.roll(v, v.shape[0] - 1, 0)


def south_of(v):
    return pltpu.roll(v, 1, 0)


def forward_stages(x, w_first_t, w_second_t):
    z_one = dot(w_first_t[...], x)
    yield
    first = jnp.tanh(z_one)
    low_first = first.astype(BF16)
    yield
    z_two = dot(w_second_t[...], low_first)
    yield
    second = jnp.tanh(z_two)
    return first, second, low_first, second.astype(BF16)


def closure(low_second, w_last_t):
    return dot(w_last_t[...], low_second).astype(BF16).astype(F32)[:SHALLOW]


def staggered(generators):
    live = []
    waiting = list(generators)
    while live or waiting:
        if waiting:
            live.append(waiting.pop(0))
        for part in list(live):
            try:
                next(part)
            except StopIteration:
                live.remove(part)


def lanes_of(ref, deep, base, tiles):
    block = ref[pl.ds(base * deep, tiles * deep), :]
    return jnp.concatenate([block[k * deep : (k + 1) * deep] for k in range(tiles)], 1)


def put_lanes(ref, deep, base, tiles, value):
    for k in range(tiles):
        ref[pl.ds((base + k) * deep, deep), :] = value[:, k * LANES : (k + 1) * LANES]


def early_kernel(start, fields, *refs):
    if start == 0:
        w_in, w_mid, w_out_t, keep1, keep2, cl, wi, wi_t, wm_t, wo, wo_t, ft = refs
        width_in, hidden = w_in.shape
        levels = w_out_t.shape[0]
        spare = jnp.zeros((DEEP - width_in, hidden), F32)
        wide_in = jnp.concatenate([w_in[...].astype(F32), spare], 0)
        wi[...] = wide_in.astype(BF16)
        wi_t[...] = wide_in.T.astype(BF16)
        wm_t[...] = w_mid[...].astype(F32).T.astype(BF16)
        spare = jnp.zeros((DEEP - levels, hidden), F32)
        wide_out = jnp.concatenate([w_out_t[...].astype(F32), spare], 0)
        wo_t[...] = wide_out.astype(BF16)
        wo[...] = wide_out.T.astype(BF16)
    else:
        unused, wi_t, wm_t, wo_t, keep1, keep2, cl, ft = refs
        levels = (fields.shape[0] - 1) // 5
    tall = cl.shape[0] // SHALLOW
    ft[...] = jnp.zeros_like(ft)
    for level in range(levels):
        v = fields[level]
        slope_x = 0.5 * (east_of(v) - west_of(v))
        slope_y = 0.5 * (north_of(v) - south_of(v))
        for f, plane in enumerate((v, slope_x, slope_y)):
            ft[pl.ds(f * levels + level, tall, stride=DEEP), :] = plane[start : start + tall]

    def part(base, kept1, kept2):
        x = lanes_of(ft, DEEP, base, PART).astype(BF16)
        first, second, unused_low, low_second = yield from forward_stages(x, wi_t, wm_t)
        kept1[...] = first
        kept2[...] = second
        yield
        put_lanes(cl, SHALLOW, base, PART, closure(low_second, wo_t))

    staggered(part(k * PART, keep1.at[k], keep2.at[k]) for k in range(tall // PART))


def copied_out(pairs, sems):
    copies = [pltpu.make_async_copy(*pair, sems.at[k]) for k, pair in enumerate(pairs)]
    for copy in copies:
        copy.start()
    return copies


class Block:
    def __init__(self, levels, rows):
        self.levels, self.rows = levels, rows
        self.ext = rows + 2 * WIDE
        self.packs = -(-self.ext // 16)
        self.wet = 5 * levels
        packed = [None] * self.packs
        ext = self.ext
        self.rim = [0, rows - 1, rows, ext - 1] + packed + [rows + 1, ext - 2, rows + 2, ext - 3]
        self.rim_near = self.rim[: 4 + self.packs]
        self.outer = [rows, ext - 1] + packed + [rows + 1, ext - 2]
        self.lane = lax.broadcasted_iota(jnp.int32, (ext, LANES), 1)

    def with_rim(self, plane):
        lane = self.lane
        body, side = plane[:, :LANES], plane[:, LANES:]
        own = jnp.where(lane == LANES - WIDE, pltpu.roll(body, LANES - WIDE, 1), pltpu.roll(body, WIDE, 1))
        return jnp.where((lane == LANES - WIDE) | (lane == WIDE - 1), own, side)

    def from_rim(self, body, side):
        lane = self.lane
        own = jnp.where(lane == 0, pltpu.roll(side, WIDE, 1), pltpu.roll(side, LANES - WIDE, 1))
        return jnp.where((lane == 0) | (lane == LANES - 1), own, body)

    def spread(self, plane, index, deep, main, extra, side, rimmed):
        main[pl.ds(index, self.rows, stride=deep), :] = plane[: self.rows, :LANES]
        extra[pl.ds(index, 2 * WIDE, stride=deep), :] = plane[self.rows :, :LANES]
        side[pl.ds(index, self.ext, stride=deep), :] = self.with_rim(plane) if rimmed else plane[:, LANES:]

    def gathered(self, index, deep, main, extra, side, rimmed):
        body = jnp.concatenate(
            [main[pl.ds(index, self.rows, stride=deep), :], extra[pl.ds(index, 2 * WIDE, stride=deep), :]], 0
        )
        beside = side[pl.ds(index, self.ext, stride=deep), :]
        return jnp.concatenate([self.from_rim(body, beside) if rimmed else body, beside], 1)

    def home(self, r, deep, main, extra):
        return main.at[pl.ds(r * deep, deep)] if r < self.rows else extra.at[pl.ds((r - self.rows) * deep, deep)]

    def pack_halo(self, order, deep, main, extra, side, rim_too=True):
        where = lax.broadcasted_iota(jnp.int32, (deep, LANES), 1)
        for i, r in enumerate(order):
            if r is not None and (rim_too or r >= self.rows):
                main[pl.ds((self.rows + i) * deep, deep), :] = self.home(r, deep, main, extra)[...]
        first_pack = self.rows + order.index(None)
        for q in range(self.packs):
            total = jnp.zeros((deep, LANES), F32)
            for j in range(min(16, self.ext - 16 * q)):
                moved = pltpu.roll(side[pl.ds((16 * q + j) * deep, deep), :], (2 * WIDE * j + WIDE) % LANES, 1)
                total = jnp.where((where >= 2 * WIDE * j) & (where < 2 * WIDE * (j + 1)), moved, total)
            main[pl.ds((first_pack + q) * deep, deep), :] = total

    def unpack_halo(self, order, deep, main, extra, side):
        for i, r in enumerate(order):
            if r is not None:
                self.home(r, deep, main, extra)[...] = main[pl.ds((self.rows + i) * deep, deep), :]
        first_pack = self.rows + order.index(None)
        for q in range(self.packs):
            tile = main[pl.ds((first_pack + q) * deep, deep), :]
            for j in range(min(16, self.ext - 16 * q)):
                moved = pltpu.roll(tile, LANES - (2 * WIDE * j + WIDE) % LANES, 1)
                side[pl.ds((16 * q + j) * deep, deep), :] = moved

    def force(self, planes, v, level, closed):
        eastward, westward, northward, southward = east_of(v), west_of(v), north_of(v), south_of(v)
        laplace = eastward + westward + northward + southward - 4.0 * v
        slope = 0.5 * (eastward - westward)
        return planes[self.wet] * (KAPPA * laplace - planes[2 * self.levels + level] * slope + closed)

    def adjoint(self, planes, weighted, level, tiles, rimmed):
        levels = self.levels
        masked = planes[self.wet] * weighted
        carried = planes[2 * levels + level] * masked
        a0, a1, a2 = (self.gathered(f * levels + level, DEEP, *tiles, rimmed) for f in range(3))
        result = KAPPA * (east_of(masked) + west_of(masked) + north_of(masked) + south_of(masked) - 4.0 * masked)
        result = result + 0.5 * (east_of(carried) - west_of(carried)) + a0
        return result - 0.5 * (east_of(a1) - west_of(a1)) - 0.5 * (north_of(a2) - south_of(a2))


def feature_gradients(dz_one, w_in):
    return dot(w_in[...], dz_one).astype(BF16).astype(F32)


def main_kernel(bands, *refs):
    fields, left, right, low, high, wi, wi_t, wm_t, w_mid, wo, wo_t, *refs = refs
    early, refs = refs[: 3 * EARLY], refs[3 * EARLY :]
    h_mid, h_old, o_sent, o_kept, planes, mids, olds, cl, df, *refs = refs
    o_mid, o_old, sems, ft1, ft2, fth, ftx, clh, clx, dc, dch, dcx, dfh, dfx, halo1, halo2, *refs = refs
    acc_mid, acc_in, acc_out, o_grad = refs
    levels, rows, cols = o_mid.shape
    hidden = w_mid.shape[0]
    block = Block(levels, rows)
    count, ext, lane = block.wet + 1, block.ext, block.lane
    kept1 = [ref.at[k] for ref in early[0::3] for k in range(ref.shape[0])]
    kept2 = [ref.at[k] for ref in early[1::3] for k in range(ref.shape[0])]

    band = lax.axis_index("lat")
    has_low = jnp.where(band > 0, 1.0, 0.0)
    has_high = jnp.where(band < bands - 1, 1.0, 0.0)

    def beyond(p):
        return [high[p] * has_high, low[p] * has_low]

    left_all = jnp.concatenate([left[...]] + beyond(count), 0)
    right_all = jnp.concatenate([right[...]] + beyond(count + 1), 0)
    for p in range(count):
        from_right = pltpu.roll(right_all, LANES - WIDE * p, 1) if p else right_all
        from_left = pltpu.roll(left_all, LANES - WIDE * (p + 1), 1)
        side = jnp.where(lane < WIDE, from_right, jnp.where(lane >= LANES - WIDE, from_left, 0.0))
        planes[p, :, pl.ds(0, LANES)] = jnp.concatenate([fields[p]] + beyond(p), 0)
        planes[p, :, pl.ds(LANES, LANES)] = side

    for ref in (ft1, ft2, fth, ftx, dc, dch, dcx):
        ref[...] = jnp.zeros_like(ref)

    def inputs_at(ref, base, tiles):
        return lanes_of(ref, DEEP, base, tiles).astype(BF16)

    def cotangents_at(base, tiles):
        part = lanes_of(dc, SHALLOW, base, tiles)
        return jnp.concatenate([part, jnp.zeros_like(part)], 0).astype(BF16)

    def backward_stages(first, second, cot):
        g_two = dot(wo[...], cot)
        yield
        dz_two = (g_two * (1.0 - second * second)).astype(BF16)
        yield
        g_one = dot(w_mid[...], dz_two)
        yield
        dz_one = (g_one * (1.0 - first * first)).astype(BF16)
        yield
        return dz_one, dz_two

    def second_part(base, tiles, sums, later):
        x = inputs_at(ft2, base, tiles)
        cot = cotangents_at(base, tiles)
        first, second, low_first, low_second = yield from forward_stages(x, wi_t, wm_t)
        yield
        if sums is not None:
            put_lanes(cl, SHALLOW, base, tiles, closure(low_second, wo_t))
        dz_one, dz_two = yield from backward_stages(first, second, cot)
        dfeat = feature_gradients(dz_one, wi)
        pairs = (low_first, dz_two), (x, dz_one), (low_second, cot)
        if later is not None:
            later.append(pairs)
        elif sums is not None:
            add_terms(sums, *pairs)
        yield
        put_lanes(df, DEEP, base, tiles, dfeat)

    def third_part(base, tiles, held1, held2, counted, sums):
        cot = cotangents_at(base, tiles)
        first = held1[...]
        second = held2[...]
        dz_one, dz_two = yield from backward_stages(first, second, cot)
        dfeat = feature_gradients(dz_one, wi)
        x = inputs_at(ft1, base, tiles)
        if counted is not None:
            dz_one, dz_two, cot = (jnp.where(counted, v.astype(F32), 0.0).astype(BF16) for v in (dz_one, dz_two, cot))
        add_terms(sums, (first.astype(BF16), dz_two), (x, dz_one), (second.astype(BF16), cot))
        yield
        put_lanes(df, DEEP, base, tiles, dfeat)

    def add_terms(sums, *pairs):
        for k, pair in enumerate(pairs):
            sums[k] = dot_nt(*pair) if sums[k] is None else sums[k] + dot_nt(*pair)

    def features_of(source, ft, order, rimmed):
        for level in range(levels):
            v = source[level]
            for f, plane in enumerate((v, 0.5 * (east_of(v) - west_of(v)), 0.5 * (north_of(v) - south_of(v)))):
                block.spread(plane, f * levels + level, DEEP, ft, ftx, fth, rimmed)
        block.pack_halo(order, DEEP, ft, ftx, fth)

    features_of(planes, ft1, block.rim, True)
    for k, ref in enumerate(early[2::3]):
        cl[pl.ds(k * ref.shape[0], ref.shape[0]), :] = ref[...]

    def first_part(base, tiles):
        first, second, unused, low_second = yield from forward_stages(inputs_at(ft1, base, tiles), wi_t, wm_t)
        halo1[...] = first
        halo2[...] = second
        yield
        put_lanes(cl, SHALLOW, base, tiles, closure(low_second, wo_t))

    def second_cotangents():
        for level in range(levels):
            masked = planes[block.wet] * (2.0 * DT * planes[3 * levels + level])
            block.spread(masked, level, SHALLOW, dc, dcx, dch, False)
            yield
        block.pack_halo(block.outer, SHALLOW, dc, dcx, dch)

    staggered([first_part(rows, len(block.rim)), second_cotangents()])
    block.unpack_halo(block.rim, SHALLOW, cl, clx, clh)
    for level in range(levels):
        closed = block.gathered(level, SHALLOW, cl, clx, clh, True)
        mid = planes[levels + level] + 2.0 * DT * block.force(planes, planes[level], level, closed)
        o_mid[level] = mid[:rows, :LANES]
        mids[level] = mid
    copies = copied_out([(o_mid, h_mid)], sems.at[pl.ds(0, 1)])

    features_of(mids, ft2, block.outer, False)
    sums, later = [None] * 3, []
    last = rows // PART - DEFERRED
    staggered(
        [second_part(rows, len(block.outer), None, None)]
        + [second_part(k * PART, PART, sums, None if k < last else later) for k in range(rows // PART)]
    )

    near = block.rim_near
    row = lax.broadcasted_iota(jnp.int32, (ext, LANES), 0)
    inside = (lane > 0) & (lane < LANES - 1) & (row > 0) & (row < rows - 1)

    def second_gradient():
        block.unpack_halo(block.outer, DEEP, df, dfx, dfh)
        for level in range(levels):
            yield
            weighted = 2.0 * DT * planes[3 * levels + level]
            grad = planes[4 * levels + level] + block.adjoint(planes, weighted, level, (df, dfx, dfh), False)
            o_old[level] = grad[:rows, :LANES]
            olds[level] = grad
            masked = planes[block.wet] * (2.0 * DT * grad)
            body = masked[:, :LANES]
            dc[pl.ds(level, rows, stride=SHALLOW), :] = jnp.where(inside, body, 0.0)[:rows]
            dcx[pl.ds(level, 2 * WIDE, stride=SHALLOW), :] = body[rows:]
            dch[pl.ds(level, ext, stride=SHALLOW), :] = block.with_rim(masked)
            for k, r in enumerate(near[:2]):
                dc[pl.ds((rows + k) * SHALLOW + level, 1), :] = body[r : r + 1]
        yield
        block.pack_halo(near, SHALLOW, dc, dcx, dch, False)

    def deferred_terms():
        for pairs in later:
            for k, pair in enumerate(pairs):
                sums[k] = sums[k] + dot_nt(*pair)
                if k == 0:
                    yield
            yield

    staggered([second_gradient(), deferred_terms()])
    for acc, total in zip((acc_mid, acc_in, acc_out), sums):
        acc[...] = total
    copies += copied_out([(o_old, h_old)], sems.at[pl.ds(1, 1)])

    at = lax.broadcasted_iota(jnp.int32, (1, len(near) * LANES), 1)
    tile, place = at >> 7, at & (LANES - 1)
    side_row = (tile - 4) * 16 + (place >> 3)
    edge = ((place & 7) == 0) | ((place & 7) == 7)
    counted = (tile < 2) | ((tile >= 4) & edge & (side_row > 0) & (side_row < rows - 1))
    wide = pl.ds(0, len(near) * LANES)
    sums = [None] * 3
    staggered(
        [third_part(rows, len(near), halo1.at[:, wide], halo2.at[:, wide], counted, sums)]
        + [third_part(k * PART, PART, kept1[k], kept2[k], None, sums) for k in range(rows // PART)]
    )

    start = 0
    for total in (acc_mid[...] + sums[0], acc_in[...] + sums[1], (acc_out[...] + sums[2]).T):
        deep = total.shape[0]
        for half in range(hidden // LANES):
            o_grad[pl.ds(start, deep), :] = total[:, half * LANES : (half + 1) * LANES]
            start += deep
    if start < o_grad.shape[0]:
        o_grad[pl.ds(start, o_grad.shape[0] - start), :] = jnp.zeros((o_grad.shape[0] - start, LANES), F32)
    halve(o_grad[...], 1, o_sent, o_kept)
    for copy in copies:
        copy.wait()


def halve(value, bit, sent, kept):
    half = value.shape[0] // 2
    upper = (lax.axis_index("lat") & bit) != 0
    sent[...] = jnp.where(upper, value[:half], value[half:])
    kept[...] = jnp.where(upper, value[half:], value[:half])


def halve_kernel(bit, held, got, sent, kept):
    halve(held[...] + got[...], bit, sent, kept)


def late_kernel(
    fields, planes, mids, olds, cl, gradients, held, h_new, h_now, o_held, o_place, o_new, o_now, sems, df, dfh, dfx
):
    levels, rows, cols = o_new.shape
    block = Block(levels, rows)
    o_held[...] = held[...]
    o_place[...] = jnp.zeros_like(o_place) + lax.axis_index("lat")
    df[...] = gradients[...]
    beside = jnp.zeros((rows, LANES), F32)
    beyond = jnp.zeros((2 * WIDE, 2 * LANES), F32)
    for level in range(levels):
        closed = jnp.concatenate([cl[pl.ds(level, rows, stride=SHALLOW), :], beside], 1)
        closed = jnp.concatenate([closed, beyond], 0)
        new = planes[level] + 2.0 * DT * block.force(planes, mids[level], level, closed)
        o_new[level] = new[:rows, :LANES]
    copies = copied_out([(o_new, h_new)], sems.at[pl.ds(0, 1)])
    block.unpack_halo(block.rim_near, DEEP, df, dfx, dfh)
    for level in range(levels):
        grad = block.adjoint(planes, 2.0 * DT * olds[level], level, (df, dfx, dfh), True)
        o_now[level] = fields[3 * levels + level] + grad[:rows, :LANES]
    copies += copied_out([(o_now, h_now)], sems.at[pl.ds(1, 1)])
    for copy in copies:
        copy.wait()


def scale_kernel(factor, terms, g_in, g_mid, g_out):
    hidden = g_mid.shape[0]
    start = 0
    for ref, deep in ((g_mid, hidden), (g_in, DEEP), (g_out, DEEP)):
        for half in range(hidden // LANES):
            ref[:, half * LANES : (half + 1) * LANES] = terms[pl.ds(start, ref.shape[0]), :] * factor
            start += deep


def along(value, axis, step):
    count = lax.axis_size(axis)
    return lax.ppermute(value, axis, [(i, (i + step) % count) for i in range(count)])


def swapped(value, axis, bit):
    return lax.ppermute(value, axis, [(i, i ^ bit) for i in range(lax.axis_size(axis))])


def added_up(value, axis):
    bit = 1
    while bit < lax.axis_size(axis):
        near = swapped(value, axis, bit)
        if 2 * bit < lax.axis_size(axis):
            value = (value + near) + (swapped(value, axis, 2 * bit) + swapped(value, axis, 3 * bit))
            bit *= 4
        else:
            value = value + near
            bit *= 2
    return value


def put_together(value, place, axis):
    bit = lax.axis_size(axis) // 2
    while bit:
        upper = (place & bit) != 0
        other = swapped(value, axis, bit)
        value = jnp.concatenate([jnp.where(upper, other, value), jnp.where(upper, value, other)], 0)
        bit //= 2
    return value


def body(state_old, state_now, drift, ocean, w_in, w_mid, w_out, cot_mid, cot_new):
    levels, rows, cols = state_now.shape
    width_in, hidden = w_in.shape
    ext = rows + 2 * WIDE
    count = 5 * levels + 1
    packs = -(-ext // 16)
    slots = rows + 8 + packs
    tall = rows // EARLY
    vmem = pl.BlockSpec(memory_space=pltpu.VMEM)
    hbm = pl.BlockSpec(memory_space=pltpu.HBM)
    strip = jax.ShapeDtypeStruct((rows, LANES), F32)
    edge = jax.ShapeDtypeStruct((count, WIDE, LANES), F32)
    arrays = (state_now, state_old, drift, cot_new, cot_mid, ocean, w_in, w_mid, w_out.T)
    weights = tuple(jax.ShapeDtypeStruct(a.shape, a.dtype) for a in arrays[6:])
    west, east, top, bottom, fields, *weights = pl.pallas_call(
        pack_kernel,
        out_shape=(strip, strip, edge, edge, jax.ShapeDtypeStruct((count, rows, cols), F32)) + weights,
        in_specs=[hbm] * 9,
        out_specs=(vmem,) * 8,
        scratch_shapes=[pltpu.VMEM((rows, cols), jnp.int32), pltpu.SemaphoreType.DMA((9,))],
        compiler_params=pltpu.CompilerParams(vmem_limit_bytes=8 * 2**20),
    )(*(pltpu.with_memory_space_constraint(a, pltpu.HBM) for a in arrays))

    kept = jax.ShapeDtypeStruct((tall // PART, hidden, PART * LANES), F32)
    closed = jax.ShapeDtypeStruct((tall * SHALLOW, LANES), F32)
    tall_weight = jax.ShapeDtypeStruct((hidden, DEEP), BF16)
    flat_weight = jax.ShapeDtypeStruct((DEEP, hidden), BF16)
    prepared = (flat_weight, tall_weight, jax.ShapeDtypeStruct((hidden, hidden), BF16), tall_weight, flat_weight)

    def early(k, extra, extra_out):
        return pl.pallas_call(
            functools.partial(early_kernel, k * tall),
            out_shape=(kept, kept, closed) + extra_out,
            in_specs=[vmem] * (1 + len(extra)),
            out_specs=(vmem,) * (3 + len(extra_out)),
            scratch_shapes=[pltpu.VMEM((tall * DEEP, LANES), F32)],
            compiler_params=pltpu.CompilerParams(vmem_limit_bytes=12 * 2**20),
            cost_estimate=pl.CostEstimate(
                flops=6 * hidden * hidden * tall * cols, bytes_accessed=0, transcendentals=2 * hidden * tall * cols
            ),
        )(fields, *extra)

    left = along(east, "lon", 1)
    right = along(west, "lon", -1)
    *first_kept, wi, wi_t, wm_t, wo, wo_t = early(0, tuple(weights), prepared)
    message = jax.ShapeDtypeStruct((count + 2, WIDE, LANES), F32)
    up, down = pl.pallas_call(
        join_kernel,
        out_shape=(message, message),
        in_specs=[vmem] * 4,
        out_specs=(vmem,) * 2,
        compiler_params=pltpu.CompilerParams(vmem_limit_bytes=4 * 2**20),
    )(top, bottom, left, right)
    low = along(up, "lat", 1)
    high = along(down, "lat", -1)
    done = list(first_kept)
    for k in range(1, EARLY):
        done += early(k, (left, wi_t, wm_t, wo_t), ())

    bands = lax.axis_size("lat")
    halves = hidden // LANES
    terms_rows = -(-halves * (hidden + 2 * DEEP) // (8 * bands)) * 8 * bands
    field = jax.ShapeDtypeStruct((levels, rows, cols), F32)
    ext_planes = jax.ShapeDtypeStruct((levels, ext, 2 * LANES), F32)
    staged = pltpu.VMEM((levels, rows, cols), F32)

    def tiles(deep):
        return [pltpu.VMEM((n * deep, LANES), F32) for n in (slots, 16 * packs, 2 * WIDE)]

    def half_terms(parts):
        return (jax.ShapeDtypeStruct((terms_rows // parts, LANES), F32),) * 2

    kept_halo = pltpu.VMEM((hidden, (8 + packs) * LANES), F32)
    state_mid, grad_old, sent, held, planes, mids, olds, closures, gradients = pl.pallas_call(
        functools.partial(main_kernel, bands),
        out_shape=(field, field, *half_terms(2))
        + (jax.ShapeDtypeStruct((count, ext, 2 * LANES), F32), ext_planes, ext_planes)
        + tuple(jax.ShapeDtypeStruct((slots * deep, LANES), F32) for deep in (SHALLOW, DEEP)),
        in_specs=[vmem] * (11 + 3 * EARLY),
        out_specs=(hbm,) * 2 + (vmem,) * 7,
        scratch_shapes=[
            staged,
            staged,
            pltpu.SemaphoreType.DMA((2,)),
            tiles(DEEP)[0],
            *tiles(DEEP),
            *tiles(SHALLOW)[1:],
            *tiles(SHALLOW),
            *tiles(DEEP)[1:],
            kept_halo,
            kept_halo,
            pltpu.VMEM((hidden, hidden), F32),
            pltpu.VMEM((DEEP, hidden), F32),
            pltpu.VMEM((hidden, DEEP), F32),
            pltpu.VMEM((terms_rows, LANES), F32),
        ],
        compiler_params=pltpu.CompilerParams(vmem_limit_bytes=32 * 2**20),
    )(fields, left, right, low, high, wi, wi_t, wm_t, weights[1], wo, wo_t, *done)

    bit = 1
    while 2 * bit < bands:
        got = swapped(sent, "lat", bit)
        bit *= 2
        sent, held = pl.pallas_call(
            functools.partial(halve_kernel, bit),
            out_shape=half_terms(2 * bit),
            in_specs=[vmem] * 2,
            out_specs=(vmem,) * 2,
            compiler_params=pltpu.CompilerParams(vmem_limit_bytes=4 * 2**20),
        )(held, got)
    got = swapped(sent, "lat", bit)
    state_new, grad_now, held, place = pl.pallas_call(
        late_kernel,
        out_shape=(field, field, half_terms(bands)[0], jax.ShapeDtypeStruct((8, LANES), jnp.int32)),
        in_specs=[vmem] * 7,
        out_specs=(hbm,) * 2 + (vmem,) * 2,
        scratch_shapes=[staged, staged, pltpu.SemaphoreType.DMA((2,)), *tiles(DEEP)],
        compiler_params=pltpu.CompilerParams(vmem_limit_bytes=16 * 2**20),
        cost_estimate=pl.CostEstimate(
            flops=2 * hidden * hidden * rows * cols, bytes_accessed=0, transcendentals=0
        ),
    )(fields, planes, mids, olds, closures, gradients, held)
    summed = put_together(added_up(held + got, "lon"), place[:1], "lat")
    cells_all = rows * lax.axis_size("lat") * cols * lax.axis_size("lon")
    grad_in, grad_mid, grad_out = pl.pallas_call(
        functools.partial(scale_kernel, GAIN_GRAD / cells_all**0.5),
        out_shape=(
            jax.ShapeDtypeStruct((width_in, hidden), F32),
            jax.ShapeDtypeStruct((hidden, hidden), F32),
            jax.ShapeDtypeStruct((levels, hidden), F32),
        ),
        in_specs=[vmem],
        out_specs=(vmem,) * 3,
        compiler_params=pltpu.CompilerParams(vmem_limit_bytes=8 * 2**20),
    )(summed)
    return state_mid, state_new, grad_old, grad_now, grad_in, grad_mid, grad_out.T


def solution(mesh):
    field = P("grp", "lat", "lon")
    whole = P("grp", None)
    in_specs = (field, field, field, P(("grp", "lat"), "lon"), P(), P(), P(), field, field)
    out_specs = (field, field, field, field, whole, whole, whole)
    return jax.shard_map(body, mesh=mesh, in_specs=in_specs, out_specs=out_specs, check_vma=False)
```

```python
import functools

import jax
import jax.numpy as jnp
from jax import lax
from jax.experimental import pallas as pl
from jax.experimental.pallas import tpu as pltpu
from jax.sharding import PartitionSpec as P

KAPPA = 0.2
DT = 0.1
GAIN_GRAD = 10.0

WIDE = 4
LANES = 128
PART = 8
ROUNDS = 2
EARLY = 2
DEEP = 16
SHALLOW = 8

F32 = jnp.float32
BF16 = jnp.bfloat16


def dot(left, right):
    return lax.dot_general(left, right, (((1,), (0,)), ((), ())), preferred_element_type=F32)


def dot_nt(left, right):
    return lax.dot_general(left, right, (((1,), (1,)), ((), ())), preferred_element_type=F32)


def pack_kernel(
    now, old, drift, cnew, cmid, ocean, w_in, w_mid, w_out,
    west, east, top, bottom, fields, v_in, v_mid, v_out, wet, sems,
):
    levels, rows, cols = now.shape
    copies = [
        pltpu.make_async_copy(ref, fields.at[pl.ds(levels * f, levels)], sems.at[f])
        for f, ref in enumerate((now, old, drift, cnew, cmid))
    ]
    copies.append(pltpu.make_async_copy(ocean, wet, sems.at[5]))
    for k, pair in enumerate(((w_in, v_in), (w_mid, v_mid), (w_out, v_out))):
        copies.append(pltpu.make_async_copy(*pair, sems.at[6 + k]))
    for copy in copies:
        copy.start()
    lane = lax.broadcasted_iota(jnp.int32, (rows, LANES), 1)
    to_west = jnp.zeros((rows, LANES), F32)
    to_east = jnp.zeros((rows, LANES), F32)
    count = fields.shape[0]
    for p in range(count):
        if p % levels == 0:
            copies[p // levels].wait()
        if p == count - 1:
            fields[p] = wet[...].astype(F32)
        plane = fields[p]
        here = (lane >= WIDE * p) & (lane < WIDE * (p + 1))
        to_west = jnp.where(here, pltpu.roll(plane, WIDE * p, 1) if p else plane, to_west)
        to_east = jnp.where(here, pltpu.roll(plane, WIDE * (p + 1), 1), to_east)
        top[p] = plane[:WIDE]
        bottom[p] = plane[rows - WIDE :]
    west[...] = to_west
    east[...] = to_east
    for copy in copies[6:]:
        copy.wait()


def join_kernel(top, bottom, left, right, up, down):
    count = top.shape[0]
    rows = left.shape[0]
    up[pl.ds(0, count)] = bottom[...]
    down[pl.ds(0, count)] = top[...]
    for k, strip in enumerate((left, right)):
        up[count + k] = strip[pl.ds(rows - WIDE, WIDE), :]
        down[count + k] = strip[pl.ds(0, WIDE), :]


def east_of(v):
    return pltpu.roll(v, v.shape[1] - 1, 1)


def west_of(v):
    return pltpu.roll(v, 1, 1)


def north_of(v):
    return pltpu.roll(v, v.shape[0] - 1, 0)


def south_of(v):
    return pltpu.roll(v, 1, 0)


def forward_stages(x, w_first_t, w_second_t):
    z_one = dot(w_first_t[...], x)
    yield
    first = jnp.tanh(z_one)
    low_first = first.astype(BF16)
    yield
    z_two = dot(w_second_t[...], low_first)
    yield
    second = jnp.tanh(z_two)
    return first, second, low_first, second.astype(BF16)


def closure(low_second, w_last_t):
    return dot(w_last_t[...], low_second).astype(BF16).astype(F32)[:SHALLOW]


def staggered(generators):
    live = []
    waiting = list(generators)
    while live or waiting:
        if waiting:
            live.append(waiting.pop(0))
        for part in list(live):
            try:
                next(part)
            except StopIteration:
                live.remove(part)


def lanes_of(ref, deep, base, tiles):
    block = ref[pl.ds(base * deep, tiles * deep), :]
    return jnp.concatenate([block[k * deep : (k + 1) * deep] for k in range(tiles)], 1)


def put_lanes(ref, deep, base, tiles, value):
    for k in range(tiles):
        ref[pl.ds((base + k) * deep, deep), :] = value[:, k * LANES : (k + 1) * LANES]


def early_kernel(start, fields, *refs):
    if start == 0:
        w_in, w_mid, w_out_t, keep1, keep2, cl, wi, wi_t, wm_t, wo, wo_t, ft = refs
        width_in, hidden = w_in.shape
        levels = w_out_t.shape[0]
        spare = jnp.zeros((DEEP - width_in, hidden), F32)
        wide_in = jnp.concatenate([w_in[...].astype(F32), spare], 0)
        wi[...] = wide_in.astype(BF16)
        wi_t[...] = wide_in.T.astype(BF16)
        wm_t[...] = w_mid[...].astype(F32).T.astype(BF16)
        spare = jnp.zeros((DEEP - levels, hidden), F32)
        wide_out = jnp.concatenate([w_out_t[...].astype(F32), spare], 0)
        wo_t[...] = wide_out.astype(BF16)
        wo[...] = wide_out.T.astype(BF16)
    else:
        unused, wi_t, wm_t, wo_t, keep1, keep2, cl, ft = refs
        levels = (fields.shape[0] - 1) // 5
    tall = cl.shape[0] // SHALLOW
    ft[...] = jnp.zeros_like(ft)
    for level in range(levels):
        v = fields[level]
        slope_x = 0.5 * (east_of(v) - west_of(v))
        slope_y = 0.5 * (north_of(v) - south_of(v))
        for f, plane in enumerate((v, slope_x, slope_y)):
            ft[pl.ds(f * levels + level, tall, stride=DEEP), :] = plane[start : start + tall]

    def part(base, kept1, kept2):
        x = lanes_of(ft, DEEP, base, PART).astype(BF16)
        first, second, unused_low, low_second = yield from forward_stages(x, wi_t, wm_t)
        kept1[...] = first
        kept2[...] = second
        yield
        put_lanes(cl, SHALLOW, base, PART, closure(low_second, wo_t))

    staggered(part(k * PART, keep1.at[k], keep2.at[k]) for k in range(tall // PART))


def copied_out(pairs, sems):
    copies = [pltpu.make_async_copy(*pair, sems.at[k]) for k, pair in enumerate(pairs)]
    for copy in copies:
        copy.start()
    return copies


class Block:
    def __init__(self, levels, rows):
        self.levels, self.rows = levels, rows
        self.ext = rows + 2 * WIDE
        self.packs = -(-self.ext // 16)
        self.wet = 5 * levels
        packed = [None] * self.packs
        ext = self.ext
        self.rim = [0, rows - 1, rows, ext - 1] + packed + [rows + 1, ext - 2, rows + 2, ext - 3]
        self.rim_near = self.rim[: 4 + self.packs]
        self.outer = [rows, ext - 1] + packed + [rows + 1, ext - 2]
        self.lane = lax.broadcasted_iota(jnp.int32, (ext, LANES), 1)

    def with_rim(self, plane):
        lane = self.lane
        body, side = plane[:, :LANES], plane[:, LANES:]
        own = jnp.where(lane == LANES - WIDE, pltpu.roll(body, LANES - WIDE, 1), pltpu.roll(body, WIDE, 1))
        return jnp.where((lane == LANES - WIDE) | (lane == WIDE - 1), own, side)

    def from_rim(self, body, side):
        lane = self.lane
        own = jnp.where(lane == 0, pltpu.roll(side, WIDE, 1), pltpu.roll(side, LANES - WIDE, 1))
        return jnp.where((lane == 0) | (lane == LANES - 1), own, body)

    def spread(self, plane, index, deep, main, extra, side, rimmed):
        main[pl.ds(index, self.rows, stride=deep), :] = plane[: self.rows, :LANES]
        extra[pl.ds(index, 2 * WIDE, stride=deep), :] = plane[self.rows :, :LANES]
        side[pl.ds(index, self.ext, stride=deep), :] = self.with_rim(plane) if rimmed else plane[:, LANES:]

    def gathered(self, index, deep, main, extra, side, rimmed):
        body = jnp.concatenate(
            [main[pl.ds(index, self.rows, stride=deep), :], extra[pl.ds(index, 2 * WIDE, stride=deep), :]], 0
        )
        beside = side[pl.ds(index, self.ext, stride=deep), :]
        return jnp.concatenate([self.from_rim(body, beside) if rimmed else body, beside], 1)

    def home(self, r, deep, main, extra):
        return main.at[pl.ds(r * deep, deep)] if r < self.rows else extra.at[pl.ds((r - self.rows) * deep, deep)]

    def pack_halo(self, order, deep, main, extra, side, rim_too=True):
        where = lax.broadcasted_iota(jnp.int32, (deep, LANES), 1)
        for i, r in enumerate(order):
            if r is not None and (rim_too or r >= self.rows):
                main[pl.ds((self.rows + i) * deep, deep), :] = self.home(r, deep, main, extra)[...]
        first_pack = self.rows + order.index(None)
        for q in range(self.packs):
            total = jnp.zeros((deep, LANES), F32)
            for j in range(min(16, self.ext - 16 * q)):
                moved = pltpu.roll(side[pl.ds((16 * q + j) * deep, deep), :], (2 * WIDE * j + WIDE) % LANES, 1)
                total = jnp.where((where >= 2 * WIDE * j) & (where < 2 * WIDE * (j + 1)), moved, total)
            main[pl.ds((first_pack + q) * deep, deep), :] = total

    def unpack_halo(self, order, deep, main, extra, side):
        for i, r in enumerate(order):
            if r is not None:
                self.home(r, deep, main, extra)[...] = main[pl.ds((self.rows + i) * deep, deep), :]
        first_pack = self.rows + order.index(None)
        for q in range(self.packs):
            tile = main[pl.ds((first_pack + q) * deep, deep), :]
            for j in range(min(16, self.ext - 16 * q)):
                moved = pltpu.roll(tile, LANES - (2 * WIDE * j + WIDE) % LANES, 1)
                side[pl.ds((16 * q + j) * deep, deep), :] = moved

    def force(self, planes, v, level, closed):
        eastward, westward, northward, southward = east_of(v), west_of(v), north_of(v), south_of(v)
        laplace = eastward + westward + northward + southward - 4.0 * v
        slope = 0.5 * (eastward - westward)
        return planes[self.wet] * (KAPPA * laplace - planes[2 * self.levels + level] * slope + closed)

    def adjoint(self, planes, weighted, level, tiles, rimmed):
        levels = self.levels
        masked = planes[self.wet] * weighted
        carried = planes[2 * levels + level] * masked
        a0, a1, a2 = (self.gathered(f * levels + level, DEEP, *tiles, rimmed) for f in range(3))
        result = KAPPA * (east_of(masked) + west_of(masked) + north_of(masked) + south_of(masked) - 4.0 * masked)
        result = result + 0.5 * (east_of(carried) - west_of(carried)) + a0
        return result - 0.5 * (east_of(a1) - west_of(a1)) - 0.5 * (north_of(a2) - south_of(a2))


def feature_gradients(dz_one, w_in):
    return dot(w_in[...], dz_one).astype(BF16).astype(F32)


def main_kernel(bands, *refs):
    fields, left, right, low, high, wi, wi_t, wm_t, w_mid, wo, wo_t, *refs = refs
    early, refs = refs[: 3 * EARLY], refs[3 * EARLY :]
    h_mid, h_old, o_sent, o_kept, planes, mids, olds, cl, df, *refs = refs
    o_mid, o_old, sems, ft1, ft2, fth, ftx, clh, clx, dc, dch, dcx, dfh, dfx, halo1, halo2, *refs = refs
    acc_mid, acc_in, acc_out, o_grad = refs
    levels, rows, cols = o_mid.shape
    hidden = w_mid.shape[0]
    block = Block(levels, rows)
    count, ext, lane = block.wet + 1, block.ext, block.lane

    band = lax.axis_index("lat")
    has_low = jnp.where(band > 0, 1.0, 0.0)
    has_high = jnp.where(band < bands - 1, 1.0, 0.0)

    def beyond(p):
        return [high[p] * has_high, low[p] * has_low]

    left_all = jnp.concatenate([left[...]] + beyond(count), 0)
    right_all = jnp.concatenate([right[...]] + beyond(count + 1), 0)
    for p in range(count):
        from_right = pltpu.roll(right_all, LANES - WIDE * p, 1) if p else right_all
        from_left = pltpu.roll(left_all, LANES - WIDE * (p + 1), 1)
        side = jnp.where(lane < WIDE, from_right, jnp.where(lane >= LANES - WIDE, from_left, 0.0))
        planes[p, :, pl.ds(0, LANES)] = jnp.concatenate([fields[p]] + beyond(p), 0)
        planes[p, :, pl.ds(LANES, LANES)] = side

    for ref in (ft1, ft2, fth, ftx, dc, dch, dcx):
        ref[...] = jnp.zeros_like(ref)

    def inputs_at(ref, base, tiles):
        return lanes_of(ref, DEEP, base, tiles).astype(BF16)

    def cotangents_at(base, tiles):
        part = lanes_of(dc, SHALLOW, base, tiles)
        return jnp.concatenate([part, jnp.zeros_like(part)], 0).astype(BF16)

    def backward_stages(first, second, cot):
        g_two = dot(wo[...], cot)
        yield
        dz_two = (g_two * (1.0 - second * second)).astype(BF16)
        yield
        g_one = dot(w_mid[...], dz_two)
        yield
        dz_one = (g_one * (1.0 - first * first)).astype(BF16)
        yield
        return dz_one, dz_two

    def second_part(base, tiles, sums):
        x = inputs_at(ft2, base, tiles)
        cot = cotangents_at(base, tiles)
        first, second, low_first, low_second = yield from forward_stages(x, wi_t, wm_t)
        yield
        if sums is not None:
            put_lanes(cl, SHALLOW, base, tiles, closure(low_second, wo_t))
        dz_one, dz_two = yield from backward_stages(first, second, cot)
        dfeat = feature_gradients(dz_one, wi)
        if sums is not None:
            add_terms(sums, (low_first, dz_two), (x, dz_one), (low_second, cot))
        yield
        put_lanes(df, DEEP, base, tiles, dfeat)

    def third_part(base, tiles, held1, held2, counted, sums):
        cot = cotangents_at(base, tiles)
        first = held1[...]
        second = held2[...]
        dz_one, dz_two = yield from backward_stages(first, second, cot)
        dfeat = feature_gradients(dz_one, wi)
        x = inputs_at(ft1, base, tiles)
        if counted is not None:
            dz_one, dz_two, cot = (jnp.where(counted, v.astype(F32), 0.0).astype(BF16) for v in (dz_one, dz_two, cot))
        add_terms(sums, (first.astype(BF16), dz_two), (x, dz_one), (second.astype(BF16), cot))
        yield
        put_lanes(df, DEEP, base, tiles, dfeat)

    def add_terms(sums, *pairs):
        for k, pair in enumerate(pairs):
            sums[k] = dot_nt(*pair) if sums[k] is None else sums[k] + dot_nt(*pair)

    def features_of(source, ft, order, rimmed):
        for level in range(levels):
            v = source[level]
            for f, plane in enumerate((v, 0.5 * (east_of(v) - west_of(v)), 0.5 * (north_of(v) - south_of(v)))):
                block.spread(plane, f * levels + level, DEEP, ft, ftx, fth, rimmed)
        block.pack_halo(order, DEEP, ft, ftx, fth)

    features_of(planes, ft1, block.rim, True)
    for k, ref in enumerate(early[2::3]):
        cl[pl.ds(k * ref.shape[0], ref.shape[0]), :] = ref[...]

    def first_part(base, tiles):
        first, second, unused, low_second = yield from forward_stages(inputs_at(ft1, base, tiles), wi_t, wm_t)
        halo1[...] = first
        halo2[...] = second
        yield
        put_lanes(cl, SHALLOW, base, tiles, closure(low_second, wo_t))

    def second_cotangents():
        for level in range(levels):
            masked = planes[block.wet] * (2.0 * DT * planes[3 * levels + level])
            block.spread(masked, level, SHALLOW, dc, dcx, dch, False)
            yield
        block.pack_halo(block.outer, SHALLOW, dc, dcx, dch)

    staggered([first_part(rows, len(block.rim)), second_cotangents()])
    block.unpack_halo(block.rim, SHALLOW, cl, clx, clh)
    for level in range(levels):
        closed = block.gathered(level, SHALLOW, cl, clx, clh, True)
        mid = planes[levels + level] + 2.0 * DT * block.force(planes, planes[level], level, closed)
        o_mid[level] = mid[:rows, :LANES]
        mids[level] = mid
    copies = copied_out([(o_mid, h_mid)], sems.at[pl.ds(0, 1)])

    features_of(mids, ft2, block.outer, False)
    for acc in (acc_mid, acc_in, acc_out):
        acc[...] = jnp.zeros_like(acc)

    def keep_terms(sums):
        for acc, total in zip((acc_mid, acc_in, acc_out), sums):
            acc[...] += total

    halo_tiles = -(-len(block.outer) // ROUNDS)

    def second_round(c, carry):
        sums = [None] * 3
        parts = [c * (rows // PART // ROUNDS) + k for k in range(rows // PART // ROUNDS)]
        staggered(
            [second_part(rows + c * halo_tiles, halo_tiles, None)]
            + [second_part(pl.multiple_of(k * PART, PART), PART, sums) for k in parts]
        )
        keep_terms(sums)
        return carry

    lax.fori_loop(0, ROUNDS, second_round, 0)

    near = block.rim_near
    row = lax.broadcasted_iota(jnp.int32, (ext, LANES), 0)
    inside = (lane > 0) & (lane < LANES - 1) & (row > 0) & (row < rows - 1)

    block.unpack_halo(block.outer, DEEP, df, dfx, dfh)
    for level in range(levels):
        weighted = 2.0 * DT * planes[3 * levels + level]
        grad = planes[4 * levels + level] + block.adjoint(planes, weighted, level, (df, dfx, dfh), False)
        o_old[level] = grad[:rows, :LANES]
        olds[level] = grad
        masked = planes[block.wet] * (2.0 * DT * grad)
        body = masked[:, :LANES]
        dc[pl.ds(level, rows, stride=SHALLOW), :] = jnp.where(inside, body, 0.0)[:rows]
        dcx[pl.ds(level, 2 * WIDE, stride=SHALLOW), :] = body[rows:]
        dch[pl.ds(level, ext, stride=SHALLOW), :] = block.with_rim(masked)
        for k, r in enumerate(near[:2]):
            dc[pl.ds((rows + k) * SHALLOW + level, 1), :] = body[r : r + 1]
    block.pack_halo(near, SHALLOW, dc, dcx, dch, False)
    copies += copied_out([(o_old, h_old)], sems.at[pl.ds(1, 1)])

    at = lax.broadcasted_iota(jnp.int32, (1, halo_tiles * LANES), 1)
    place = at & (LANES - 1)
    edge = ((place & 7) == 0) | ((place & 7) == 7)

    def third_round(c, carry):
        tile = (at >> 7) + c * halo_tiles
        side_row = (tile - 4) * 16 + (place >> 3)
        counted = (tile < 2) | ((tile >= 4) & edge & (side_row > 0) & (side_row < rows - 1))
        wide = pl.ds(pl.multiple_of(c * halo_tiles * LANES, LANES), halo_tiles * LANES)
        sums = [None] * 3
        parts = [third_part(rows + c * halo_tiles, halo_tiles, halo1.at[:, wide], halo2.at[:, wide], counted, sums)]
        for e in range(EARLY):
            held1, held2 = early[3 * e], early[3 * e + 1]
            share = held1.shape[0]
            for k in range(share // ROUNDS):
                own = c * (share // ROUNDS) + k
                base = pl.multiple_of((e * share + own) * PART, PART)
                parts.append(third_part(base, PART, held1.at[own], held2.at[own], None, sums))
        staggered(parts)
        keep_terms(sums)
        return carry

    lax.fori_loop(0, ROUNDS, third_round, 0)

    start = 0
    for total in (acc_mid[...], acc_in[...], acc_out[...].T):
        deep = total.shape[0]
        for half in range(hidden // LANES):
            o_grad[pl.ds(start, deep), :] = total[:, half * LANES : (half + 1) * LANES]
            start += deep
    if start < o_grad.shape[0]:
        o_grad[pl.ds(start, o_grad.shape[0] - start), :] = jnp.zeros((o_grad.shape[0] - start, LANES), F32)
    halve(o_grad[...], 1, o_sent, o_kept)
    for copy in copies:
        copy.wait()


def halve(value, bit, sent, kept):
    half = value.shape[0] // 2
    upper = (lax.axis_index("lat") & bit) != 0
    sent[...] = jnp.where(upper, value[:half], value[half:])
    kept[...] = jnp.where(upper, value[half:], value[:half])


def halve_kernel(bit, held, got, sent, kept):
    halve(held[...] + got[...], bit, sent, kept)


def late_kernel(
    fields, planes, mids, olds, cl, gradients, held, h_new, h_now, o_held, o_place, o_new, o_now, sems, df, dfh, dfx
):
    levels, rows, cols = o_new.shape
    block = Block(levels, rows)
    o_held[...] = held[...]
    o_place[...] = jnp.zeros_like(o_place) + lax.axis_index("lat")
    df[...] = gradients[...]
    beside = jnp.zeros((rows, LANES), F32)
    beyond = jnp.zeros((2 * WIDE, 2 * LANES), F32)
    for level in range(levels):
        closed = jnp.concatenate([cl[pl.ds(level, rows, stride=SHALLOW), :], beside], 1)
        closed = jnp.concatenate([closed, beyond], 0)
        new = planes[level] + 2.0 * DT * block.force(planes, mids[level], level, closed)
        o_new[level] = new[:rows, :LANES]
    copies = copied_out([(o_new, h_new)], sems.at[pl.ds(0, 1)])
    block.unpack_halo(block.rim_near, DEEP, df, dfx, dfh)
    for level in range(levels):
        grad = block.adjoint(planes, 2.0 * DT * olds[level], level, (df, dfx, dfh), True)
        o_now[level] = fields[3 * levels + level] + grad[:rows, :LANES]
    copies += copied_out([(o_now, h_now)], sems.at[pl.ds(1, 1)])
    for copy in copies:
        copy.wait()


def scale_kernel(factor, terms, g_in, g_mid, g_out):
    hidden = g_mid.shape[0]
    start = 0
    for ref, deep in ((g_mid, hidden), (g_in, DEEP), (g_out, DEEP)):
        for half in range(hidden // LANES):
            ref[:, half * LANES : (half + 1) * LANES] = terms[pl.ds(start, ref.shape[0]), :] * factor
            start += deep


def along(value, axis, step):
    count = lax.axis_size(axis)
    return lax.ppermute(value, axis, [(i, (i + step) % count) for i in range(count)])


def swapped(value, axis, bit):
    return lax.ppermute(value, axis, [(i, i ^ bit) for i in range(lax.axis_size(axis))])


def added_up(value, axis):
    bit = 1
    while bit < lax.axis_size(axis):
        near = swapped(value, axis, bit)
        if 2 * bit < lax.axis_size(axis):
            value = (value + near) + (swapped(value, axis, 2 * bit) + swapped(value, axis, 3 * bit))
            bit *= 4
        else:
            value = value + near
            bit *= 2
    return value


def put_together(value, place, axis):
    bit = lax.axis_size(axis) // 2
    while bit:
        upper = (place & bit) != 0
        other = swapped(value, axis, bit)
        value = jnp.concatenate([jnp.where(upper, other, value), jnp.where(upper, value, other)], 0)
        bit //= 2
    return value


def body(state_old, state_now, drift, ocean, w_in, w_mid, w_out, cot_mid, cot_new):
    levels, rows, cols = state_now.shape
    width_in, hidden = w_in.shape
    ext = rows + 2 * WIDE
    count = 5 * levels + 1
    packs = -(-ext // 16)
    slots = rows + 8 + packs
    tall = rows // EARLY
    vmem = pl.BlockSpec(memory_space=pltpu.VMEM)
    hbm = pl.BlockSpec(memory_space=pltpu.HBM)
    strip = jax.ShapeDtypeStruct((rows, LANES), F32)
    edge = jax.ShapeDtypeStruct((count, WIDE, LANES), F32)
    arrays = (state_now, state_old, drift, cot_new, cot_mid, ocean, w_in, w_mid, w_out.T)
    weights = tuple(jax.ShapeDtypeStruct(a.shape, a.dtype) for a in arrays[6:])
    west, east, top, bottom, fields, *weights = pl.pallas_call(
        pack_kernel,
        out_shape=(strip, strip, edge, edge, jax.ShapeDtypeStruct((count, rows, cols), F32)) + weights,
        in_specs=[hbm] * 9,
        out_specs=(vmem,) * 8,
        scratch_shapes=[pltpu.VMEM((rows, cols), jnp.int32), pltpu.SemaphoreType.DMA((9,))],
        compiler_params=pltpu.CompilerParams(vmem_limit_bytes=8 * 2**20),
    )(*(pltpu.with_memory_space_constraint(a, pltpu.HBM) for a in arrays))

    kept = jax.ShapeDtypeStruct((tall // PART, hidden, PART * LANES), F32)
    closed = jax.ShapeDtypeStruct((tall * SHALLOW, LANES), F32)
    tall_weight = jax.ShapeDtypeStruct((hidden, DEEP), BF16)
    flat_weight = jax.ShapeDtypeStruct((DEEP, hidden), BF16)
    prepared = (flat_weight, tall_weight, jax.ShapeDtypeStruct((hidden, hidden), BF16), tall_weight, flat_weight)

    def early(k, extra, extra_out):
        return pl.pallas_call(
            functools.partial(early_kernel, k * tall),
            out_shape=(kept, kept, closed) + extra_out,
            in_specs=[vmem] * (1 + len(extra)),
            out_specs=(vmem,) * (3 + len(extra_out)),
            scratch_shapes=[pltpu.VMEM((tall * DEEP, LANES), F32)],
            compiler_params=pltpu.CompilerParams(vmem_limit_bytes=12 * 2**20),
            cost_estimate=pl.CostEstimate(
                flops=6 * hidden * hidden * tall * cols, bytes_accessed=0, transcendentals=2 * hidden * tall * cols
            ),
        )(fields, *extra)

    left = along(east, "lon", 1)
    right = along(west, "lon", -1)
    *first_kept, wi, wi_t, wm_t, wo, wo_t = early(0, tuple(weights), prepared)
    message = jax.ShapeDtypeStruct((count + 2, WIDE, LANES), F32)
    up, down = pl.pallas_call(
        join_kernel,
        out_shape=(message, message),
        in_specs=[vmem] * 4,
        out_specs=(vmem,) * 2,
        compiler_params=pltpu.CompilerParams(vmem_limit_bytes=4 * 2**20),
    )(top, bottom, left, right)
    low = along(up, "lat", 1)
    high = along(down, "lat", -1)
    done = list(first_kept)
    for k in range(1, EARLY):
        done += early(k, (left, wi_t, wm_t, wo_t), ())

    bands = lax.axis_size("lat")
    halves = hidden // LANES
    terms_rows = -(-halves * (hidden + 2 * DEEP) // (8 * bands)) * 8 * bands
    field = jax.ShapeDtypeStruct((levels, rows, cols), F32)
    ext_planes = jax.ShapeDtypeStruct((levels, ext, 2 * LANES), F32)
    staged = pltpu.VMEM((levels, rows, cols), F32)

    def tiles(deep):
        return [pltpu.VMEM((n * deep, LANES), F32) for n in (slots, 16 * packs, 2 * WIDE)]

    def half_terms(parts):
        return (jax.ShapeDtypeStruct((terms_rows // parts, LANES), F32),) * 2

    kept_halo = pltpu.VMEM((hidden, (8 + packs) * LANES), F32)
    state_mid, grad_old, sent, held, planes, mids, olds, closures, gradients = pl.pallas_call(
        functools.partial(main_kernel, bands),
        out_shape=(field, field, *half_terms(2))
        + (jax.ShapeDtypeStruct((count, ext, 2 * LANES), F32), ext_planes, ext_planes)
        + tuple(jax.ShapeDtypeStruct((slots * deep, LANES), F32) for deep in (SHALLOW, DEEP)),
        in_specs=[vmem] * (11 + 3 * EARLY),
        out_specs=(hbm,) * 2 + (vmem,) * 7,
        scratch_shapes=[
            staged,
            staged,
            pltpu.SemaphoreType.DMA((2,)),
            tiles(DEEP)[0],
            *tiles(DEEP),
            *tiles(SHALLOW)[1:],
            *tiles(SHALLOW),
            *tiles(DEEP)[1:],
            kept_halo,
            kept_halo,
            pltpu.VMEM((hidden, hidden), F32),
            pltpu.VMEM((DEEP, hidden), F32),
            pltpu.VMEM((hidden, DEEP), F32),
            pltpu.VMEM((terms_rows, LANES), F32),
        ],
        compiler_params=pltpu.CompilerParams(vmem_limit_bytes=32 * 2**20),
    )(fields, left, right, low, high, wi, wi_t, wm_t, weights[1], wo, wo_t, *done)

    bit = 1
    while 2 * bit < bands:
        got = swapped(sent, "lat", bit)
        bit *= 2
        sent, held = pl.pallas_call(
            functools.partial(halve_kernel, bit),
            out_shape=half_terms(2 * bit),
            in_specs=[vmem] * 2,
            out_specs=(vmem,) * 2,
            compiler_params=pltpu.CompilerParams(vmem_limit_bytes=4 * 2**20),
        )(held, got)
    got = swapped(sent, "lat", bit)
    state_new, grad_now, held, place = pl.pallas_call(
        late_kernel,
        out_shape=(field, field, half_terms(bands)[0], jax.ShapeDtypeStruct((8, LANES), jnp.int32)),
        in_specs=[vmem] * 7,
        out_specs=(hbm,) * 2 + (vmem,) * 2,
        scratch_shapes=[staged, staged, pltpu.SemaphoreType.DMA((2,)), *tiles(DEEP)],
        compiler_params=pltpu.CompilerParams(vmem_limit_bytes=16 * 2**20),
        cost_estimate=pl.CostEstimate(
            flops=2 * hidden * hidden * rows * cols, bytes_accessed=0, transcendentals=0
        ),
    )(fields, planes, mids, olds, closures, gradients, held)
    summed = put_together(added_up(held + got, "lon"), place[:1], "lat")
    cells_all = rows * lax.axis_size("lat") * cols * lax.axis_size("lon")
    grad_in, grad_mid, grad_out = pl.pallas_call(
        functools.partial(scale_kernel, GAIN_GRAD / cells_all**0.5),
        out_shape=(
            jax.ShapeDtypeStruct((width_in, hidden), F32),
            jax.ShapeDtypeStruct((hidden, hidden), F32),
            jax.ShapeDtypeStruct((levels, hidden), F32),
        ),
        in_specs=[vmem],
        out_specs=(vmem,) * 3,
        compiler_params=pltpu.CompilerParams(vmem_limit_bytes=8 * 2**20),
    )(summed)
    return state_mid, state_new, grad_old, grad_now, grad_in, grad_mid, grad_out.T


def solution(mesh):
    field = P("grp", "lat", "lon")
    whole = P("grp", None)
    in_specs = (field, field, field, P(("grp", "lat"), "lon"), P(), P(), P(), field, field)
    out_specs = (field, field, field, field, whole, whole, whole)
    return jax.shard_map(body, mesh=mesh, in_specs=in_specs, out_specs=out_specs, check_vma=False)
```

```python
import functools

import jax
import jax.numpy as jnp
from jax import lax
from jax.experimental import pallas as pl
from jax.experimental.pallas import tpu as pltpu
from jax.sharding import PartitionSpec as P

KAPPA = 0.2
DT = 0.1
GAIN_GRAD = 10.0

WIDE = 4
LANES = 128
PART = 8
DEFERRED = 3
EARLY = 2
DEEP = 16
SHALLOW = 8

F32 = jnp.float32
BF16 = jnp.bfloat16


def dot(left, right):
    return lax.dot_general(left, right, (((1,), (0,)), ((), ())), preferred_element_type=F32)


def dot_nt(left, right):
    return lax.dot_general(left, right, (((1,), (1,)), ((), ())), preferred_element_type=F32)


def pack_kernel(
    now, old, drift, cnew, cmid, ocean, w_in, w_mid, w_out,
    west, east, top, bottom, fields, v_in, v_mid, v_out, wet, sems,
):
    levels, rows, cols = now.shape
    copies = [
        pltpu.make_async_copy(ref, fields.at[pl.ds(levels * f, levels)], sems.at[f])
        for f, ref in enumerate((now, old, drift, cnew, cmid))
    ]
    copies.append(pltpu.make_async_copy(ocean, wet, sems.at[5]))
    for k, pair in enumerate(((w_in, v_in), (w_mid, v_mid), (w_out, v_out))):
        copies.append(pltpu.make_async_copy(*pair, sems.at[6 + k]))
    for copy in copies:
        copy.start()
    lane = lax.broadcasted_iota(jnp.int32, (rows, LANES), 1)
    to_west = jnp.zeros((rows, LANES), F32)
    to_east = jnp.zeros((rows, LANES), F32)
    count = fields.shape[0]
    for p in range(count):
        if p % levels == 0:
            copies[p // levels].wait()
        if p == count - 1:
            fields[p] = wet[...].astype(F32)
        plane = fields[p]
        here = (lane >= WIDE * p) & (lane < WIDE * (p + 1))
        to_west = jnp.where(here, pltpu.roll(plane, WIDE * p, 1) if p else plane, to_west)
        to_east = jnp.where(here, pltpu.roll(plane, WIDE * (p + 1), 1), to_east)
        top[p] = plane[:WIDE]
        bottom[p] = plane[rows - WIDE :]
    west[...] = to_west
    east[...] = to_east
    for copy in copies[6:]:
        copy.wait()


def join_kernel(top, bottom, left, right, up, down):
    count = top.shape[0]
    rows = left.shape[0]
    up[pl.ds(0, count)] = bottom[...]
    down[pl.ds(0, count)] = top[...]
    for k, strip in enumerate((left, right)):
        up[count + k] = strip[pl.ds(rows - WIDE, WIDE), :]
        down[count + k] = strip[pl.ds(0, WIDE), :]


def east_of(v):
    return pltpu.roll(v, v.shape[1] - 1, 1)


def west_of(v):
    return pltpu.roll(v, 1, 1)


def north_of(v):
    return pltpu.roll(v, v.shape[0] - 1, 0)


def south_of(v):
    return pltpu.roll(v, 1, 0)


def forward_stages(x, w_first_t, w_second_t):
    z_one = dot(w_first_t[...], x)
    yield
    first = jnp.tanh(z_one)
    low_first = first.astype(BF16)
    yield
    z_two = dot(w_second_t[...], low_first)
    yield
    second = jnp.tanh(z_two)
    return first, second, low_first, second.astype(BF16)


def closure(low_second, w_last_t):
    return dot(w_last_t[...], low_second).astype(BF16).astype(F32)[:SHALLOW]


def staggered(generators):
    live = []
    waiting = list(generators)
    while live or waiting:
        if waiting:
            live.append(waiting.pop(0))
        for part in list(live):
            try:
                next(part)
            except StopIteration:
                live.remove(part)


def lanes_of(ref, deep, base, tiles):
    block = ref[pl.ds(base * deep, tiles * deep), :]
    return jnp.concatenate([block[k * deep : (k + 1) * deep] for k in range(tiles)], 1)


def put_lanes(ref, deep, base, tiles, value):
    for k in range(tiles):
        ref[pl.ds((base + k) * deep, deep), :] = value[:, k * LANES : (k + 1) * LANES]


def early_kernel(start, fields, *refs):
    if start == 0:
        w_in, w_mid, w_out_t, keep1, keep2, cl, wi, wi_t, wm_t, wo, wo_t, ft = refs
        width_in, hidden = w_in.shape
        levels = w_out_t.shape[0]
        spare = jnp.zeros((DEEP - width_in, hidden), F32)
        wide_in = jnp.concatenate([w_in[...].astype(F32), spare], 0)
        wi[...] = wide_in.astype(BF16)
        wi_t[...] = wide_in.T.astype(BF16)
        wm_t[...] = w_mid[...].astype(F32).T.astype(BF16)
        spare = jnp.zeros((DEEP - levels, hidden), F32)
        wide_out = jnp.concatenate([w_out_t[...].astype(F32), spare], 0)
        wo_t[...] = wide_out.astype(BF16)
        wo[...] = wide_out.T.astype(BF16)
    else:
        unused, wi_t, wm_t, wo_t, keep1, keep2, cl, ft = refs
        levels = (fields.shape[0] - 1) // 5
    tall = cl.shape[0] // SHALLOW
    ft[...] = jnp.zeros_like(ft)
    for level in range(levels):
        v = fields[level]
        slope_x = 0.5 * (east_of(v) - west_of(v))
        slope_y = 0.5 * (north_of(v) - south_of(v))
        for f, plane in enumerate((v, slope_x, slope_y)):
            ft[pl.ds(f * levels + level, tall, stride=DEEP), :] = plane[start : start + tall]

    def part(base, kept1, kept2):
        x = lanes_of(ft, DEEP, base, PART).astype(BF16)
        first, second, unused_low, low_second = yield from forward_stages(x, wi_t, wm_t)
        kept1[...] = first
        kept2[...] = second
        yield
        put_lanes(cl, SHALLOW, base, PART, closure(low_second, wo_t))

    staggered(part(k * PART, keep1.at[k], keep2.at[k]) for k in range(tall // PART))


def copied_out(pairs, sems):
    copies = [pltpu.make_async_copy(*pair, sems.at[k]) for k, pair in enumerate(pairs)]
    for copy in copies:
        copy.start()
    return copies


class Block:
    def __init__(self, levels, rows):
        self.levels, self.rows = levels, rows
        self.ext = rows + 2 * WIDE
        self.packs = -(-self.ext // 16)
        self.wet = 5 * levels
        packed = [None] * self.packs
        ext = self.ext
        self.rim = [0, rows - 1, rows, ext - 1] + packed + [rows + 1, ext - 2, rows + 2, ext - 3]
        self.rim_near = self.rim[: 4 + self.packs]
        self.outer = [rows, ext - 1] + packed + [rows + 1, ext - 2]
        self.lane = lax.broadcasted_iota(jnp.int32, (ext, LANES), 1)

    def with_rim(self, plane):
        lane = self.lane
        body, side = plane[:, :LANES], plane[:, LANES:]
        own = jnp.where(lane == LANES - WIDE, pltpu.roll(body, LANES - WIDE, 1), pltpu.roll(body, WIDE, 1))
        return jnp.where((lane == LANES - WIDE) | (lane == WIDE - 1), own, side)

    def from_rim(self, body, side):
        lane = self.lane
        own = jnp.where(lane == 0, pltpu.roll(side, WIDE, 1), pltpu.roll(side, LANES - WIDE, 1))
        return jnp.where((lane == 0) | (lane == LANES - 1), own, body)

    def spread(self, plane, index, deep, main, extra, side, rimmed):
        main[pl.ds(index, self.rows, stride=deep), :] = plane[: self.rows, :LANES]
        extra[pl.ds(index, 2 * WIDE, stride=deep), :] = plane[self.rows :, :LANES]
        side[pl.ds(index, self.ext, stride=deep), :] = self.with_rim(plane) if rimmed else plane[:, LANES:]

    def gathered(self, index, deep, main, extra, side, rimmed):
        body = jnp.concatenate(
            [main[pl.ds(index, self.rows, stride=deep), :], extra[pl.ds(index, 2 * WIDE, stride=deep), :]], 0
        )
        beside = side[pl.ds(index, self.ext, stride=deep), :]
        return jnp.concatenate([self.from_rim(body, beside) if rimmed else body, beside], 1)

    def home(self, r, deep, main, extra):
        return main.at[pl.ds(r * deep, deep)] if r < self.rows else extra.at[pl.ds((r - self.rows) * deep, deep)]

    def pack_halo(self, order, deep, main, extra, side, rim_too=True):
        where = lax.broadcasted_iota(jnp.int32, (deep, LANES), 1)
        for i, r in enumerate(order):
            if r is not None and (rim_too or r >= self.rows):
                main[pl.ds((self.rows + i) * deep, deep), :] = self.home(r, deep, main, extra)[...]
        first_pack = self.rows + order.index(None)
        for q in range(self.packs):
            total = jnp.zeros((deep, LANES), F32)
            for j in range(min(16, self.ext - 16 * q)):
                moved = pltpu.roll(side[pl.ds((16 * q + j) * deep, deep), :], (2 * WIDE * j + WIDE) % LANES, 1)
                total = jnp.where((where >= 2 * WIDE * j) & (where < 2 * WIDE * (j + 1)), moved, total)
            main[pl.ds((first_pack + q) * deep, deep), :] = total

    def unpack_halo(self, order, deep, main, extra, side):
        for i, r in enumerate(order):
            if r is not None:
                self.home(r, deep, main, extra)[...] = main[pl.ds((self.rows + i) * deep, deep), :]
        first_pack = self.rows + order.index(None)
        for q in range(self.packs):
            tile = main[pl.ds((first_pack + q) * deep, deep), :]
            for j in range(min(16, self.ext - 16 * q)):
                moved = pltpu.roll(tile, LANES - (2 * WIDE * j + WIDE) % LANES, 1)
                side[pl.ds((16 * q + j) * deep, deep), :] = moved

    def force(self, planes, v, level, closed):
        eastward, westward, northward, southward = east_of(v), west_of(v), north_of(v), south_of(v)
        laplace = eastward + westward + northward + southward - 4.0 * v
        slope = 0.5 * (eastward - westward)
        return planes[self.wet] * (KAPPA * laplace - planes[2 * self.levels + level] * slope + closed)

    def adjoint(self, planes, weighted, level, tiles, rimmed):
        levels = self.levels
        masked = planes[self.wet] * weighted
        carried = planes[2 * levels + level] * masked
        a0, a1, a2 = (self.gathered(f * levels + level, DEEP, *tiles, rimmed) for f in range(3))
        result = KAPPA * (east_of(masked) + west_of(masked) + north_of(masked) + south_of(masked) - 4.0 * masked)
        result = result + 0.5 * (east_of(carried) - west_of(carried)) + a0
        return result - 0.5 * (east_of(a1) - west_of(a1)) - 0.5 * (north_of(a2) - south_of(a2))


def feature_gradients(dz_one, w_in):
    return dot(w_in[...], dz_one).astype(BF16).astype(F32)


def main_kernel(bands, *refs):
    fields, left, right, low, high, wi, wi_t, wm_t, w_mid, wo, wo_t, *refs = refs
    early, refs = refs[: 3 * EARLY], refs[3 * EARLY :]
    h_mid, h_old, o_sent, o_kept, planes, mids, olds, cl, df, *refs = refs
    o_mid, o_old, sems, ft1, ft2, fth, ftx, clh, clx, dc, dch, dcx, dfh, dfx, halo1, halo2, *refs = refs
    acc_mid, acc_in, acc_out, o_grad, columns = refs
    levels, rows, cols = o_mid.shape
    hidden = w_mid.shape[0]
    block = Block(levels, rows)
    count, ext, lane = block.wet + 1, block.ext, block.lane
    kept1 = [ref.at[k] for ref in early[0::3] for k in range(ref.shape[0])]
    kept2 = [ref.at[k] for ref in early[1::3] for k in range(ref.shape[0])]

    band = lax.axis_index("lat")
    has_low = jnp.where(band > 0, 1.0, 0.0)
    has_high = jnp.where(band < bands - 1, 1.0, 0.0)

    def beyond(p):
        return [high[p] * has_high, low[p] * has_low]

    left_all = jnp.concatenate([left[...]] + beyond(count), 0)
    right_all = jnp.concatenate([right[...]] + beyond(count + 1), 0)
    for p in range(count):
        from_right = pltpu.roll(right_all, LANES - WIDE * p, 1) if p else right_all
        from_left = pltpu.roll(left_all, LANES - WIDE * (p + 1), 1)
        side = jnp.where(lane < WIDE, from_right, jnp.where(lane >= LANES - WIDE, from_left, 0.0))
        planes[p, :, pl.ds(0, LANES)] = jnp.concatenate([fields[p]] + beyond(p), 0)
        planes[p, :, pl.ds(LANES, LANES)] = side

    for ref in (ft1, ft2, fth, ftx, dc, dch, dcx):
        ref[...] = jnp.zeros_like(ref)

    def inputs_at(ref, base, tiles):
        return lanes_of(ref, DEEP, base, tiles).astype(BF16)

    def cotangents_at(base, tiles):
        part = lanes_of(dc, SHALLOW, base, tiles)
        return jnp.concatenate([part, jnp.zeros_like(part)], 0).astype(BF16)

    for level in range(levels):
        columns[level] = jnp.broadcast_to(wo[...].astype(F32)[:, level : level + 1], (hidden, LANES))

    def spread_out(cot):
        rows_of = cot.astype(F32)
        pieces = []
        for at in range(0, cot.shape[1], LANES):
            terms = [columns[level] * rows_of[level : level + 1, at : at + LANES] for level in range(levels)]
            pieces.append(functools.reduce(jnp.add, terms))
        return jnp.concatenate(pieces, 1)

    def backward_stages(first, second, cot):
        g_two = spread_out(cot)
        yield
        dz_two = (g_two * (1.0 - second * second)).astype(BF16)
        yield
        g_one = dot(w_mid[...], dz_two)
        yield
        dz_one = (g_one * (1.0 - first * first)).astype(BF16)
        yield
        return dz_one, dz_two

    def second_part(base, tiles, sums, later):
        x = inputs_at(ft2, base, tiles)
        cot = cotangents_at(base, tiles)
        first, second, low_first, low_second = yield from forward_stages(x, wi_t, wm_t)
        yield
        if sums is not None:
            put_lanes(cl, SHALLOW, base, tiles, closure(low_second, wo_t))
        dz_one, dz_two = yield from backward_stages(first, second, cot)
        dfeat = feature_gradients(dz_one, wi)
        pairs = (low_first, dz_two), (x, dz_one), (low_second, cot)
        if later is not None:
            later.append(pairs)
        elif sums is not None:
            add_terms(sums, *pairs)
        yield
        put_lanes(df, DEEP, base, tiles, dfeat)

    def third_part(base, tiles, held1, held2, counted, sums):
        cot = cotangents_at(base, tiles)
        first = held1[...]
        second = held2[...]
        dz_one, dz_two = yield from backward_stages(first, second, cot)
        dfeat = feature_gradients(dz_one, wi)
        x = inputs_at(ft1, base, tiles)
        if counted is not None:
            dz_one, dz_two, cot = (jnp.where(counted, v.astype(F32), 0.0).astype(BF16) for v in (dz_one, dz_two, cot))
        add_terms(sums, (first.astype(BF16), dz_two), (x, dz_one), (second.astype(BF16), cot))
        yield
        put_lanes(df, DEEP, base, tiles, dfeat)

    def add_terms(sums, *pairs):
        for k, pair in enumerate(pairs):
            sums[k] = dot_nt(*pair) if sums[k] is None else sums[k] + dot_nt(*pair)

    def features_of(source, ft, order, rimmed):
        for level in range(levels):
            v = source[level]
            for f, plane in enumerate((v, 0.5 * (east_of(v) - west_of(v)), 0.5 * (north_of(v) - south_of(v)))):
                block.spread(plane, f * levels + level, DEEP, ft, ftx, fth, rimmed)
        block.pack_halo(order, DEEP, ft, ftx, fth)

    features_of(planes, ft1, block.rim, True)
    for k, ref in enumerate(early[2::3]):
        cl[pl.ds(k * ref.shape[0], ref.shape[0]), :] = ref[...]

    def first_part(base, tiles):
        first, second, unused, low_second = yield from forward_stages(inputs_at(ft1, base, tiles), wi_t, wm_t)
        halo1[...] = first
        halo2[...] = second
        yield
        put_lanes(cl, SHALLOW, base, tiles, closure(low_second, wo_t))

    def second_cotangents():
        for level in range(levels):
            masked = planes[block.wet] * (2.0 * DT * planes[3 * levels + level])
            block.spread(masked, level, SHALLOW, dc, dcx, dch, False)
            yield
        block.pack_halo(block.outer, SHALLOW, dc, dcx, dch)

    staggered([first_part(rows, len(block.rim)), second_cotangents()])
    block.unpack_halo(block.rim, SHALLOW, cl, clx, clh)
    for level in range(levels):
        closed = block.gathered(level, SHALLOW, cl, clx, clh, True)
        mid = planes[levels + level] + 2.0 * DT * block.force(planes, planes[level], level, closed)
        o_mid[level] = mid[:rows, :LANES]
        mids[level] = mid
    copies = copied_out([(o_mid, h_mid)], sems.at[pl.ds(0, 1)])

    features_of(mids, ft2, block.outer, False)
    sums, later = [None] * 3, []
    last = rows // PART - DEFERRED
    staggered(
        [second_part(rows, len(block.outer), None, None)]
        + [second_part(k * PART, PART, sums, None if k < last else later) for k in range(rows // PART)]
    )

    near = block.rim_near
    row = lax.broadcasted_iota(jnp.int32, (ext, LANES), 0)
    inside = (lane > 0) & (lane < LANES - 1) & (row > 0) & (row < rows - 1)

    def second_gradient():
        block.unpack_halo(block.outer, DEEP, df, dfx, dfh)
        for level in range(levels):
            yield
            weighted = 2.0 * DT * planes[3 * levels + level]
            grad = planes[4 * levels + level] + block.adjoint(planes, weighted, level, (df, dfx, dfh), False)
            o_old[level] = grad[:rows, :LANES]
            olds[level] = grad
            masked = planes[block.wet] * (2.0 * DT * grad)
            body = masked[:, :LANES]
            dc[pl.ds(level, rows, stride=SHALLOW), :] = jnp.where(inside, body, 0.0)[:rows]
            dcx[pl.ds(level, 2 * WIDE, stride=SHALLOW), :] = body[rows:]
            dch[pl.ds(level, ext, stride=SHALLOW), :] = block.with_rim(masked)
            for k, r in enumerate(near[:2]):
                dc[pl.ds((rows + k) * SHALLOW + level, 1), :] = body[r : r + 1]
        yield
        block.pack_halo(near, SHALLOW, dc, dcx, dch, False)

    def deferred_terms():
        for pairs in later:
            for k, pair in enumerate(pairs):
                sums[k] = sums[k] + dot_nt(*pair)
                if k == 0:
                    yield
            yield

    staggered([second_gradient(), deferred_terms()])
    for acc, total in zip((acc_mid, acc_in, acc_out), sums):
        acc[...] = total
    copies += copied_out([(o_old, h_old)], sems.at[pl.ds(1, 1)])

    at = lax.broadcasted_iota(jnp.int32, (1, len(near) * LANES), 1)
    tile, place = at >> 7, at & (LANES - 1)
    side_row = (tile - 4) * 16 + (place >> 3)
    edge = ((place & 7) == 0) | ((place & 7) == 7)
    counted = (tile < 2) | ((tile >= 4) & edge & (side_row > 0) & (side_row < rows - 1))
    wide = pl.ds(0, len(near) * LANES)
    sums = [None] * 3
    staggered(
        [third_part(rows, len(near), halo1.at[:, wide], halo2.at[:, wide], counted, sums)]
        + [third_part(k * PART, PART, kept1[k], kept2[k], None, sums) for k in range(rows // PART)]
    )

    start = 0
    for total in (acc_mid[...] + sums[0], acc_in[...] + sums[1], (acc_out[...] + sums[2]).T):
        deep = total.shape[0]
        for half in range(hidden // LANES):
            o_grad[pl.ds(start, deep), :] = total[:, half * LANES : (half + 1) * LANES]
            start += deep
    if start < o_grad.shape[0]:
        o_grad[pl.ds(start, o_grad.shape[0] - start), :] = jnp.zeros((o_grad.shape[0] - start, LANES), F32)
    halve(o_grad[...], 1, o_sent, o_kept)
    for copy in copies:
        copy.wait()


def halve(value, bit, sent, kept):
    half = value.shape[0] // 2
    upper = (lax.axis_index("lat") & bit) != 0
    sent[...] = jnp.where(upper, value[:half], value[half:])
    kept[...] = jnp.where(upper, value[half:], value[:half])


def halve_kernel(bit, held, got, sent, kept):
    halve(held[...] + got[...], bit, sent, kept)


def late_kernel(
    fields, planes, mids, olds, cl, gradients, held, h_new, h_now, o_held, o_place, o_new, o_now, sems, df, dfh, dfx
):
    levels, rows, cols = o_new.shape
    block = Block(levels, rows)
    o_held[...] = held[...]
    o_place[...] = jnp.zeros_like(o_place) + lax.axis_index("lat")
    df[...] = gradients[...]
    beside = jnp.zeros((rows, LANES), F32)
    beyond = jnp.zeros((2 * WIDE, 2 * LANES), F32)
    for level in range(levels):
        closed = jnp.concatenate([cl[pl.ds(level, rows, stride=SHALLOW), :], beside], 1)
        closed = jnp.concatenate([closed, beyond], 0)
        new = planes[level] + 2.0 * DT * block.force(planes, mids[level], level, closed)
        o_new[level] = new[:rows, :LANES]
    copies = copied_out([(o_new, h_new)], sems.at[pl.ds(0, 1)])
    block.unpack_halo(block.rim_near, DEEP, df, dfx, dfh)
    for level in range(levels):
        grad = block.adjoint(planes, 2.0 * DT * olds[level], level, (df, dfx, dfh), True)
        o_now[level] = fields[3 * levels + level] + grad[:rows, :LANES]
    copies += copied_out([(o_now, h_now)], sems.at[pl.ds(1, 1)])
    for copy in copies:
        copy.wait()


def scale_kernel(factor, terms, g_in, g_mid, g_out):
    hidden = g_mid.shape[0]
    start = 0
    for ref, deep in ((g_mid, hidden), (g_in, DEEP), (g_out, DEEP)):
        for half in range(hidden // LANES):
            ref[:, half * LANES : (half + 1) * LANES] = terms[pl.ds(start, ref.shape[0]), :] * factor
            start += deep


def along(value, axis, step):
    count = lax.axis_size(axis)
    return lax.ppermute(value, axis, [(i, (i + step) % count) for i in range(count)])


def swapped(value, axis, bit):
    return lax.ppermute(value, axis, [(i, i ^ bit) for i in range(lax.axis_size(axis))])


def added_up(value, axis):
    bit = 1
    while bit < lax.axis_size(axis):
        near = swapped(value, axis, bit)
        if 2 * bit < lax.axis_size(axis):
            value = (value + near) + (swapped(value, axis, 2 * bit) + swapped(value, axis, 3 * bit))
            bit *= 4
        else:
            value = value + near
            bit *= 2
    return value


def put_together(value, place, axis):
    bit = lax.axis_size(axis) // 2
    while bit:
        upper = (place & bit) != 0
        other = swapped(value, axis, bit)
        value = jnp.concatenate([jnp.where(upper, other, value), jnp.where(upper, value, other)], 0)
        bit //= 2
    return value


def body(state_old, state_now, drift, ocean, w_in, w_mid, w_out, cot_mid, cot_new):
    levels, rows, cols = state_now.shape
    width_in, hidden = w_in.shape
    ext = rows + 2 * WIDE
    count = 5 * levels + 1
    packs = -(-ext // 16)
    slots = rows + 8 + packs
    tall = rows // EARLY
    vmem = pl.BlockSpec(memory_space=pltpu.VMEM)
    hbm = pl.BlockSpec(memory_space=pltpu.HBM)
    strip = jax.ShapeDtypeStruct((rows, LANES), F32)
    edge = jax.ShapeDtypeStruct((count, WIDE, LANES), F32)
    arrays = (state_now, state_old, drift, cot_new, cot_mid, ocean, w_in, w_mid, w_out.T)
    weights = tuple(jax.ShapeDtypeStruct(a.shape, a.dtype) for a in arrays[6:])
    west, east, top, bottom, fields, *weights = pl.pallas_call(
        pack_kernel,
        out_shape=(strip, strip, edge, edge, jax.ShapeDtypeStruct((count, rows, cols), F32)) + weights,
        in_specs=[hbm] * 9,
        out_specs=(vmem,) * 8,
        scratch_shapes=[pltpu.VMEM((rows, cols), jnp.int32), pltpu.SemaphoreType.DMA((9,))],
        compiler_params=pltpu.CompilerParams(vmem_limit_bytes=8 * 2**20),
    )(*(pltpu.with_memory_space_constraint(a, pltpu.HBM) for a in arrays))

    kept = jax.ShapeDtypeStruct((tall // PART, hidden, PART * LANES), F32)
    closed = jax.ShapeDtypeStruct((tall * SHALLOW, LANES), F32)
    tall_weight = jax.ShapeDtypeStruct((hidden, DEEP), BF16)
    flat_weight = jax.ShapeDtypeStruct((DEEP, hidden), BF16)
    prepared = (flat_weight, tall_weight, jax.ShapeDtypeStruct((hidden, hidden), BF16), tall_weight, flat_weight)

    def early(k, extra, extra_out):
        return pl.pallas_call(
            functools.partial(early_kernel, k * tall),
            out_shape=(kept, kept, closed) + extra_out,
            in_specs=[vmem] * (1 + len(extra)),
            out_specs=(vmem,) * (3 + len(extra_out)),
            scratch_shapes=[pltpu.VMEM((tall * DEEP, LANES), F32)],
            compiler_params=pltpu.CompilerParams(vmem_limit_bytes=12 * 2**20),
            cost_estimate=pl.CostEstimate(
                flops=6 * hidden * hidden * tall * cols, bytes_accessed=0, transcendentals=2 * hidden * tall * cols
            ),
        )(fields, *extra)

    left = along(east, "lon", 1)
    right = along(west, "lon", -1)
    *first_kept, wi, wi_t, wm_t, wo, wo_t = early(0, tuple(weights), prepared)
    message = jax.ShapeDtypeStruct((count + 2, WIDE, LANES), F32)
    up, down = pl.pallas_call(
        join_kernel,
        out_shape=(message, message),
        in_specs=[vmem] * 4,
        out_specs=(vmem,) * 2,
        compiler_params=pltpu.CompilerParams(vmem_limit_bytes=4 * 2**20),
    )(top, bottom, left, right)
    low = along(up, "lat", 1)
    high = along(down, "lat", -1)
    done = list(first_kept)
    for k in range(1, EARLY):
        done += early(k, (left, wi_t, wm_t, wo_t), ())

    bands = lax.axis_size("lat")
    halves = hidden // LANES
    terms_rows = -(-halves * (hidden + 2 * DEEP) // (8 * bands)) * 8 * bands
    field = jax.ShapeDtypeStruct((levels, rows, cols), F32)
    ext_planes = jax.ShapeDtypeStruct((levels, ext, 2 * LANES), F32)
    staged = pltpu.VMEM((levels, rows, cols), F32)

    def tiles(deep):
        return [pltpu.VMEM((n * deep, LANES), F32) for n in (slots, 16 * packs, 2 * WIDE)]

    def half_terms(parts):
        return (jax.ShapeDtypeStruct((terms_rows // parts, LANES), F32),) * 2

    kept_halo = pltpu.VMEM((hidden, (8 + packs) * LANES), F32)
    state_mid, grad_old, sent, held, planes, mids, olds, closures, gradients = pl.pallas_call(
        functools.partial(main_kernel, bands),
        out_shape=(field, field, *half_terms(2))
        + (jax.ShapeDtypeStruct((count, ext, 2 * LANES), F32), ext_planes, ext_planes)
        + tuple(jax.ShapeDtypeStruct((slots * deep, LANES), F32) for deep in (SHALLOW, DEEP)),
        in_specs=[vmem] * (11 + 3 * EARLY),
        out_specs=(hbm,) * 2 + (vmem,) * 7,
        scratch_shapes=[
            staged,
            staged,
            pltpu.SemaphoreType.DMA((2,)),
            tiles(DEEP)[0],
            *tiles(DEEP),
            *tiles(SHALLOW)[1:],
            *tiles(SHALLOW),
            *tiles(DEEP)[1:],
            kept_halo,
            kept_halo,
            pltpu.VMEM((hidden, hidden), F32),
            pltpu.VMEM((DEEP, hidden), F32),
            pltpu.VMEM((hidden, DEEP), F32),
            pltpu.VMEM((terms_rows, LANES), F32),
            pltpu.VMEM((levels, hidden, LANES), F32),
        ],
        compiler_params=pltpu.CompilerParams(vmem_limit_bytes=32 * 2**20),
    )(fields, left, right, low, high, wi, wi_t, wm_t, weights[1], wo, wo_t, *done)

    bit = 1
    while 2 * bit < bands:
        got = swapped(sent, "lat", bit)
        bit *= 2
        sent, held = pl.pallas_call(
            functools.partial(halve_kernel, bit),
            out_shape=half_terms(2 * bit),
            in_specs=[vmem] * 2,
            out_specs=(vmem,) * 2,
            compiler_params=pltpu.CompilerParams(vmem_limit_bytes=4 * 2**20),
        )(held, got)
    got = swapped(sent, "lat", bit)
    state_new, grad_now, held, place = pl.pallas_call(
        late_kernel,
        out_shape=(field, field, half_terms(bands)[0], jax.ShapeDtypeStruct((8, LANES), jnp.int32)),
        in_specs=[vmem] * 7,
        out_specs=(hbm,) * 2 + (vmem,) * 2,
        scratch_shapes=[staged, staged, pltpu.SemaphoreType.DMA((2,)), *tiles(DEEP)],
        compiler_params=pltpu.CompilerParams(vmem_limit_bytes=16 * 2**20),
        cost_estimate=pl.CostEstimate(
            flops=2 * hidden * hidden * rows * cols, bytes_accessed=0, transcendentals=0
        ),
    )(fields, planes, mids, olds, closures, gradients, held)
    summed = put_together(added_up(held + got, "lon"), place[:1], "lat")
    cells_all = rows * lax.axis_size("lat") * cols * lax.axis_size("lon")
    grad_in, grad_mid, grad_out = pl.pallas_call(
        functools.partial(scale_kernel, GAIN_GRAD / cells_all**0.5),
        out_shape=(
            jax.ShapeDtypeStruct((width_in, hidden), F32),
            jax.ShapeDtypeStruct((hidden, hidden), F32),
            jax.ShapeDtypeStruct((levels, hidden), F32),
        ),
        in_specs=[vmem],
        out_specs=(vmem,) * 3,
        compiler_params=pltpu.CompilerParams(vmem_limit_bytes=8 * 2**20),
    )(summed)
    return state_mid, state_new, grad_old, grad_now, grad_in, grad_mid, grad_out.T


def solution(mesh):
    field = P("grp", "lat", "lon")
    whole = P("grp", None)
    in_specs = (field, field, field, P(("grp", "lat"), "lon"), P(), P(), P(), field, field)
    out_specs = (field, field, field, field, whole, whole, whole)
    return jax.shard_map(body, mesh=mesh, in_specs=in_specs, out_specs=out_specs, check_vma=False)
```

```python
import functools

import jax
import jax.numpy as jnp
from jax import lax
from jax.experimental import pallas as pl
from jax.experimental.pallas import tpu as pltpu
from jax.sharding import PartitionSpec as P

KAPPA = 0.2
DT = 0.1
GAIN_GRAD = 10.0

WIDE = 4
LANES = 128
PART = 8
FINE = 4
EARLY = 2
DEEP = 16
SHALLOW = 8

F32 = jnp.float32
BF16 = jnp.bfloat16


def dot(left, right):
    return lax.dot_general(left, right, (((1,), (0,)), ((), ())), preferred_element_type=F32)


def dot_nt(left, right):
    return lax.dot_general(left, right, (((1,), (1,)), ((), ())), preferred_element_type=F32)


def pack_kernel(
    now, old, drift, cnew, cmid, ocean, w_in, w_mid, w_out,
    west, east, top, bottom, fields, v_in, v_mid, v_out, wet, sems,
):
    levels, rows, cols = now.shape
    copies = [
        pltpu.make_async_copy(ref, fields.at[pl.ds(levels * f, levels)], sems.at[f])
        for f, ref in enumerate((now, old, drift, cnew, cmid))
    ]
    copies.append(pltpu.make_async_copy(ocean, wet, sems.at[5]))
    for k, pair in enumerate(((w_in, v_in), (w_mid, v_mid), (w_out, v_out))):
        copies.append(pltpu.make_async_copy(*pair, sems.at[6 + k]))
    for copy in copies:
        copy.start()
    lane = lax.broadcasted_iota(jnp.int32, (rows, LANES), 1)
    to_west = jnp.zeros((rows, LANES), F32)
    to_east = jnp.zeros((rows, LANES), F32)
    count = fields.shape[0]
    for p in range(count):
        if p % levels == 0:
            copies[p // levels].wait()
        if p == count - 1:
            fields[p] = wet[...].astype(F32)
        plane = fields[p]
        here = (lane >= WIDE * p) & (lane < WIDE * (p + 1))
        to_west = jnp.where(here, pltpu.roll(plane, WIDE * p, 1) if p else plane, to_west)
        to_east = jnp.where(here, pltpu.roll(plane, WIDE * (p + 1), 1), to_east)
        top[p] = plane[:WIDE]
        bottom[p] = plane[rows - WIDE :]
    west[...] = to_west
    east[...] = to_east
    for copy in copies[6:]:
        copy.wait()


def join_kernel(top, bottom, left, right, up, down):
    count = top.shape[0]
    rows = left.shape[0]
    up[pl.ds(0, count)] = bottom[...]
    down[pl.ds(0, count)] = top[...]
    for k, strip in enumerate((left, right)):
        up[count + k] = strip[pl.ds(rows - WIDE, WIDE), :]
        down[count + k] = strip[pl.ds(0, WIDE), :]


def east_of(v):
    return pltpu.roll(v, v.shape[1] - 1, 1)


def west_of(v):
    return pltpu.roll(v, 1, 1)


def north_of(v):
    return pltpu.roll(v, v.shape[0] - 1, 0)


def south_of(v):
    return pltpu.roll(v, 1, 0)


def forward_stages(x, w_first_t, w_second_t):
    z_one = dot(w_first_t[...], x)
    yield
    first = jnp.tanh(z_one)
    low_first = first.astype(BF16)
    yield
    z_two = dot(w_second_t[...], low_first)
    yield
    second = jnp.tanh(z_two)
    return first, second, low_first, second.astype(BF16)


def closure(low_second, w_last_t):
    return dot(w_last_t[...], low_second).astype(BF16).astype(F32)[:SHALLOW]


def staggered(generators):
    live = []
    waiting = list(generators)
    while live or waiting:
        if waiting:
            live.append(waiting.pop(0))
        for part in list(live):
            try:
                next(part)
            except StopIteration:
                live.remove(part)


def lanes_of(ref, deep, base, tiles):
    block = ref[pl.ds(base * deep, tiles * deep), :]
    return jnp.concatenate([block[k * deep : (k + 1) * deep] for k in range(tiles)], 1)


def put_lanes(ref, deep, base, tiles, value):
    for k in range(tiles):
        ref[pl.ds((base + k) * deep, deep), :] = value[:, k * LANES : (k + 1) * LANES]


def early_kernel(start, fields, *refs):
    if start == 0:
        w_in, w_mid, w_out_t, keep1, keep2, cl, wi, wi_t, wm_t, wo, wo_t, ft = refs
        width_in, hidden = w_in.shape
        levels = w_out_t.shape[0]
        spare = jnp.zeros((DEEP - width_in, hidden), F32)
        wide_in = jnp.concatenate([w_in[...].astype(F32), spare], 0)
        wi[...] = wide_in.astype(BF16)
        wi_t[...] = wide_in.T.astype(BF16)
        wm_t[...] = w_mid[...].astype(F32).T.astype(BF16)
        spare = jnp.zeros((DEEP - levels, hidden), F32)
        wide_out = jnp.concatenate([w_out_t[...].astype(F32), spare], 0)
        wo_t[...] = wide_out.astype(BF16)
        wo[...] = wide_out.T.astype(BF16)
    else:
        unused, wi_t, wm_t, wo_t, keep1, keep2, cl, ft = refs
        levels = (fields.shape[0] - 1) // 5
    tall = cl.shape[0] // SHALLOW
    ft[...] = jnp.zeros_like(ft)
    for level in range(levels):
        v = fields[level]
        slope_x = 0.5 * (east_of(v) - west_of(v))
        slope_y = 0.5 * (north_of(v) - south_of(v))
        for f, plane in enumerate((v, slope_x, slope_y)):
            ft[pl.ds(f * levels + level, tall, stride=DEEP), :] = plane[start : start + tall]

    def part(base, kept1, kept2):
        x = lanes_of(ft, DEEP, base, PART).astype(BF16)
        first, second, unused_low, low_second = yield from forward_stages(x, wi_t, wm_t)
        kept1[...] = first
        kept2[...] = second
        yield
        put_lanes(cl, SHALLOW, base, PART, closure(low_second, wo_t))

    staggered(part(k * PART, keep1.at[k], keep2.at[k]) for k in range(tall // PART))


def copied_out(pairs, sems):
    copies = [pltpu.make_async_copy(*pair, sems.at[k]) for k, pair in enumerate(pairs)]
    for copy in copies:
        copy.start()
    return copies


class Block:
    def __init__(self, levels, rows):
        self.levels, self.rows = levels, rows
        self.ext = rows + 2 * WIDE
        self.packs = -(-self.ext // 16)
        self.wet = 5 * levels
        packed = [None] * self.packs
        ext = self.ext
        self.rim = [0, rows - 1, rows, ext - 1] + packed + [rows + 1, ext - 2, rows + 2, ext - 3]
        self.rim_near = self.rim[: 4 + self.packs]
        self.outer = [rows, ext - 1] + packed + [rows + 1, ext - 2]
        self.lane = lax.broadcasted_iota(jnp.int32, (ext, LANES), 1)

    def with_rim(self, plane):
        lane = self.lane
        body, side = plane[:, :LANES], plane[:, LANES:]
        own = jnp.where(lane == LANES - WIDE, pltpu.roll(body, LANES - WIDE, 1), pltpu.roll(body, WIDE, 1))
        return jnp.where((lane == LANES - WIDE) | (lane == WIDE - 1), own, side)

    def from_rim(self, body, side):
        lane = self.lane
        own = jnp.where(lane == 0, pltpu.roll(side, WIDE, 1), pltpu.roll(side, LANES - WIDE, 1))
        return jnp.where((lane == 0) | (lane == LANES - 1), own, body)

    def spread(self, plane, index, deep, main, extra, side, rimmed):
        main[pl.ds(index, self.rows, stride=deep), :] = plane[: self.rows, :LANES]
        extra[pl.ds(index, 2 * WIDE, stride=deep), :] = plane[self.rows :, :LANES]
        side[pl.ds(index, self.ext, stride=deep), :] = self.with_rim(plane) if rimmed else plane[:, LANES:]

    def gathered(self, index, deep, main, extra, side, rimmed):
        body = jnp.concatenate(
            [main[pl.ds(index, self.rows, stride=deep), :], extra[pl.ds(index, 2 * WIDE, stride=deep), :]], 0
        )
        beside = side[pl.ds(index, self.ext, stride=deep), :]
        return jnp.concatenate([self.from_rim(body, beside) if rimmed else body, beside], 1)

    def home(self, r, deep, main, extra):
        return main.at[pl.ds(r * deep, deep)] if r < self.rows else extra.at[pl.ds((r - self.rows) * deep, deep)]

    def pack_halo(self, order, deep, main, extra, side, rim_too=True):
        where = lax.broadcasted_iota(jnp.int32, (deep, LANES), 1)
        for i, r in enumerate(order):
            if r is not None and (rim_too or r >= self.rows):
                main[pl.ds((self.rows + i) * deep, deep), :] = self.home(r, deep, main, extra)[...]
        first_pack = self.rows + order.index(None)
        for q in range(self.packs):
            total = jnp.zeros((deep, LANES), F32)
            for j in range(min(16, self.ext - 16 * q)):
                moved = pltpu.roll(side[pl.ds((16 * q + j) * deep, deep), :], (2 * WIDE * j + WIDE) % LANES, 1)
                total = jnp.where((where >= 2 * WIDE * j) & (where < 2 * WIDE * (j + 1)), moved, total)
            main[pl.ds((first_pack + q) * deep, deep), :] = total

    def unpack_halo(self, order, deep, main, extra, side):
        for i, r in enumerate(order):
            if r is not None:
                self.home(r, deep, main, extra)[...] = main[pl.ds((self.rows + i) * deep, deep), :]
        first_pack = self.rows + order.index(None)
        for q in range(self.packs):
            tile = main[pl.ds((first_pack + q) * deep, deep), :]
            for j in range(min(16, self.ext - 16 * q)):
                moved = pltpu.roll(tile, LANES - (2 * WIDE * j + WIDE) % LANES, 1)
                side[pl.ds((16 * q + j) * deep, deep), :] = moved

    def force(self, planes, v, level, closed):
        eastward, westward, northward, southward = east_of(v), west_of(v), north_of(v), south_of(v)
        laplace = eastward + westward + northward + southward - 4.0 * v
        slope = 0.5 * (eastward - westward)
        return planes[self.wet] * (KAPPA * laplace - planes[2 * self.levels + level] * slope + closed)

    def adjoint(self, planes, weighted, level, tiles, rimmed):
        levels = self.levels
        masked = planes[self.wet] * weighted
        carried = planes[2 * levels + level] * masked
        a0, a1, a2 = (self.gathered(f * levels + level, DEEP, *tiles, rimmed) for f in range(3))
        result = KAPPA * (east_of(masked) + west_of(masked) + north_of(masked) + south_of(masked) - 4.0 * masked)
        result = result + 0.5 * (east_of(carried) - west_of(carried)) + a0
        return result - 0.5 * (east_of(a1) - west_of(a1)) - 0.5 * (north_of(a2) - south_of(a2))


def feature_gradients(dz_one, w_in):
    return dot(w_in[...], dz_one).astype(BF16).astype(F32)


def main_kernel(bands, *refs):
    fields, left, right, low, high, wi, wi_t, wm_t, w_mid, wo, wo_t, *refs = refs
    early, refs = refs[: 3 * EARLY], refs[3 * EARLY :]
    h_mid, h_old, o_sent, o_kept, planes, mids, olds, seconds, dz_ones, dz_halo, *refs = refs
    o_mid, o_old, sems, ft1, ft2, fth, ftx, cl, clh, clx, dc, dch, dcx, df, dfh, dfx, halo1, halo2, *refs = refs
    acc_mid, acc_in, acc_out, o_grad = refs
    levels, rows, cols = o_mid.shape
    hidden = w_mid.shape[0]
    block = Block(levels, rows)
    count, ext, lane = block.wet + 1, block.ext, block.lane
    span = FINE * LANES
    cuts = [pl.ds(at, span) for at in range(0, PART * LANES, span)]
    kept1 = [ref.at[k, :, cut] for ref in early[0::3] for k in range(ref.shape[0]) for cut in cuts]
    kept2 = [ref.at[k, :, cut] for ref in early[1::3] for k in range(ref.shape[0]) for cut in cuts]

    band = lax.axis_index("lat")
    has_low = jnp.where(band > 0, 1.0, 0.0)
    has_high = jnp.where(band < bands - 1, 1.0, 0.0)

    def beyond(p):
        return [high[p] * has_high, low[p] * has_low]

    left_all = jnp.concatenate([left[...]] + beyond(count), 0)
    right_all = jnp.concatenate([right[...]] + beyond(count + 1), 0)
    for p in range(count):
        from_right = pltpu.roll(right_all, LANES - WIDE * p, 1) if p else right_all
        from_left = pltpu.roll(left_all, LANES - WIDE * (p + 1), 1)
        side = jnp.where(lane < WIDE, from_right, jnp.where(lane >= LANES - WIDE, from_left, 0.0))
        planes[p, :, pl.ds(0, LANES)] = jnp.concatenate([fields[p]] + beyond(p), 0)
        planes[p, :, pl.ds(LANES, LANES)] = side

    for ref in (ft1, ft2, fth, ftx, dc, dch, dcx):
        ref[...] = jnp.zeros_like(ref)

    def inputs_at(ref, base, tiles):
        return lanes_of(ref, DEEP, base, tiles).astype(BF16)

    def cotangents_at(base, tiles):
        part = lanes_of(dc, SHALLOW, base, tiles)
        return jnp.concatenate([part, jnp.zeros_like(part)], 0).astype(BF16)

    def backward_stages(first, second, cot):
        g_two = dot(wo[...], cot)
        yield
        dz_two = (g_two * (1.0 - second * second)).astype(BF16)
        yield
        g_one = dot(w_mid[...], dz_two)
        yield
        dz_one = (g_one * (1.0 - first * first)).astype(BF16)
        yield
        return dz_one, dz_two

    def second_part(base, tiles, held, sums):
        x = inputs_at(ft2, base, tiles)
        cot = cotangents_at(base, tiles)
        first, second, low_first, low_second = yield from forward_stages(x, wi_t, wm_t)
        if held is not None:
            held[...] = low_second
        yield
        dz_one, dz_two = yield from backward_stages(first, second, cot)
        dfeat = feature_gradients(dz_one, wi)
        if sums is not None:
            add_terms(sums, (low_first, dz_two), (x, dz_one), (low_second, cot))
        yield
        put_lanes(df, DEEP, base, tiles, dfeat)

    def third_part(base, tiles, held1, held2, held, counted, sums):
        cot = cotangents_at(base, tiles)
        first = held1[...]
        second = held2[...]
        dz_one, dz_two = yield from backward_stages(first, second, cot)
        held[...] = dz_one
        yield
        x = inputs_at(ft1, base, tiles)
        if counted is not None:
            dz_one, dz_two, cot = (jnp.where(counted, v.astype(F32), 0.0).astype(BF16) for v in (dz_one, dz_two, cot))
        add_terms(sums, (first.astype(BF16), dz_two), (x, dz_one), (second.astype(BF16), cot))

    def add_terms(sums, *pairs):
        for k, pair in enumerate(pairs):
            sums[k] = dot_nt(*pair) if sums[k] is None else sums[k] + dot_nt(*pair)

    def features_of(source, ft, order, rimmed):
        for level in range(levels):
            v = source[level]
            for f, plane in enumerate((v, 0.5 * (east_of(v) - west_of(v)), 0.5 * (north_of(v) - south_of(v)))):
                block.spread(plane, f * levels + level, DEEP, ft, ftx, fth, rimmed)
        block.pack_halo(order, DEEP, ft, ftx, fth)

    features_of(planes, ft1, block.rim, True)
    for k, ref in enumerate(early[2::3]):
        cl[pl.ds(k * ref.shape[0], ref.shape[0]), :] = ref[...]

    def first_part(base, tiles):
        first, second, unused, low_second = yield from forward_stages(inputs_at(ft1, base, tiles), wi_t, wm_t)
        halo1[...] = first
        halo2[...] = second
        yield
        put_lanes(cl, SHALLOW, base, tiles, closure(low_second, wo_t))

    staggered([first_part(rows, len(block.rim))])
    block.unpack_halo(block.rim, SHALLOW, cl, clx, clh)
    for level in range(levels):
        closed = block.gathered(level, SHALLOW, cl, clx, clh, True)
        mid = planes[levels + level] + 2.0 * DT * block.force(planes, planes[level], level, closed)
        o_mid[level] = mid[:rows, :LANES]
        mids[level] = mid
    copies = copied_out([(o_mid, h_mid)], sems.at[pl.ds(0, 1)])

    features_of(mids, ft2, block.outer, False)
    for level in range(levels):
        masked = planes[block.wet] * (2.0 * DT * planes[3 * levels + level])
        block.spread(masked, level, SHALLOW, dc, dcx, dch, False)
    block.pack_halo(block.outer, SHALLOW, dc, dcx, dch)
    sums = [None] * 3
    staggered(
        [second_part(rows, len(block.outer), None, None)]
        + [second_part(k * FINE, FINE, seconds.at[k], sums) for k in range(rows // FINE)]
    )
    for acc, total in zip((acc_mid, acc_in, acc_out), sums):
        acc[...] = total
    block.unpack_halo(block.outer, DEEP, df, dfx, dfh)
    for level in range(levels):
        weighted = 2.0 * DT * planes[3 * levels + level]
        grad = planes[4 * levels + level] + block.adjoint(planes, weighted, level, (df, dfx, dfh), False)
        o_old[level] = grad[:rows, :LANES]
        olds[level] = grad
    copies += copied_out([(o_old, h_old)], sems.at[pl.ds(1, 1)])

    near = block.rim_near
    row = lax.broadcasted_iota(jnp.int32, (ext, LANES), 0)
    inside = (lane > 0) & (lane < LANES - 1) & (row > 0) & (row < rows - 1)
    for level in range(levels):
        masked = planes[block.wet] * (2.0 * DT * olds[level])
        body = masked[:, :LANES]
        dc[pl.ds(level, rows, stride=SHALLOW), :] = jnp.where(inside, body, 0.0)[:rows]
        dcx[pl.ds(level, 2 * WIDE, stride=SHALLOW), :] = body[rows:]
        dch[pl.ds(level, ext, stride=SHALLOW), :] = block.with_rim(masked)
        for k, r in enumerate(near[:2]):
            dc[pl.ds((rows + k) * SHALLOW + level, 1), :] = body[r : r + 1]
    block.pack_halo(near, SHALLOW, dc, dcx, dch, False)
    at = lax.broadcasted_iota(jnp.int32, (1, len(near) * LANES), 1)
    tile, place = at >> 7, at & (LANES - 1)
    side_row = (tile - 4) * 16 + (place >> 3)
    edge = ((place & 7) == 0) | ((place & 7) == 7)
    counted = (tile < 2) | ((tile >= 4) & edge & (side_row > 0) & (side_row < rows - 1))
    wide = pl.ds(0, len(near) * LANES)
    sums = [None] * 3
    staggered(
        [third_part(rows, len(near), halo1.at[:, wide], halo2.at[:, wide], dz_halo, counted, sums)]
        + [third_part(k * FINE, FINE, kept1[k], kept2[k], dz_ones.at[k], None, sums) for k in range(rows // FINE)]
    )

    start = 0
    for total in (acc_mid[...] + sums[0], acc_in[...] + sums[1], (acc_out[...] + sums[2]).T):
        deep = total.shape[0]
        for half in range(hidden // LANES):
            o_grad[pl.ds(start, deep), :] = total[:, half * LANES : (half + 1) * LANES]
            start += deep
    if start < o_grad.shape[0]:
        o_grad[pl.ds(start, o_grad.shape[0] - start), :] = jnp.zeros((o_grad.shape[0] - start, LANES), F32)
    halve(o_grad[...], 1, o_sent, o_kept)
    for copy in copies:
        copy.wait()


def halve(value, bit, sent, kept):
    half = value.shape[0] // 2
    upper = (lax.axis_index("lat") & bit) != 0
    sent[...] = jnp.where(upper, value[:half], value[half:])
    kept[...] = jnp.where(upper, value[half:], value[:half])


def halve_kernel(bit, held, got, sent, kept):
    halve(held[...] + got[...], bit, sent, kept)


def late_kernel(fields, planes, mids, olds, seconds, dz_ones, dz_halo, wi, wo_t, held, *refs):
    h_new, h_now, o_held, o_place, o_new, o_now, sems, cl, df, dfh, dfx = refs
    levels, rows, cols = o_new.shape
    block = Block(levels, rows)
    o_held[...] = held[...]
    o_place[...] = jnp.zeros_like(o_place) + lax.axis_index("lat")
    put_lanes(df, DEEP, rows, len(block.rim_near), feature_gradients(dz_halo[...], wi))
    for k in range(0, rows // FINE, 2):
        for ref, put, deep, kind in ((dz_ones, df, DEEP, 0), (seconds, cl, SHALLOW, 1)):
            both = jnp.concatenate([ref[k], ref[k + 1]], 1)
            value = closure(both, wo_t) if kind else feature_gradients(both, wi)
            put_lanes(put, deep, k * FINE, 2 * FINE, value)
    beside = jnp.zeros((rows, LANES), F32)
    beyond = jnp.zeros((2 * WIDE, 2 * LANES), F32)
    for level in range(levels):
        closed = jnp.concatenate([cl[pl.ds(level, rows, stride=SHALLOW), :], beside], 1)
        closed = jnp.concatenate([closed, beyond], 0)
        new = planes[level] + 2.0 * DT * block.force(planes, mids[level], level, closed)
        o_new[level] = new[:rows, :LANES]
    copies = copied_out([(o_new, h_new)], sems.at[pl.ds(0, 1)])
    block.unpack_halo(block.rim_near, DEEP, df, dfx, dfh)
    for level in range(levels):
        grad = block.adjoint(planes, 2.0 * DT * olds[level], level, (df, dfx, dfh), True)
        o_now[level] = fields[3 * levels + level] + grad[:rows, :LANES]
    copies += copied_out([(o_now, h_now)], sems.at[pl.ds(1, 1)])
    for copy in copies:
        copy.wait()


def scale_kernel(factor, terms, g_in, g_mid, g_out):
    hidden = g_mid.shape[0]
    start = 0
    for ref, deep in ((g_mid, hidden), (g_in, DEEP), (g_out, DEEP)):
        for half in range(hidden // LANES):
            ref[:, half * LANES : (half + 1) * LANES] = terms[pl.ds(start, ref.shape[0]), :] * factor
            start += deep


def along(value, axis, step):
    count = lax.axis_size(axis)
    return lax.ppermute(value, axis, [(i, (i + step) % count) for i in range(count)])


def swapped(value, axis, bit):
    return lax.ppermute(value, axis, [(i, i ^ bit) for i in range(lax.axis_size(axis))])


def added_up(value, axis):
    bit = 1
    while bit < lax.axis_size(axis):
        near = swapped(value, axis, bit)
        if 2 * bit < lax.axis_size(axis):
            value = (value + near) + (swapped(value, axis, 2 * bit) + swapped(value, axis, 3 * bit))
            bit *= 4
        else:
            value = value + near
            bit *= 2
    return value


def put_together(value, place, axis):
    bit = lax.axis_size(axis) // 2
    while bit:
        upper = (place & bit) != 0
        other = swapped(value, axis, bit)
        value = jnp.concatenate([jnp.where(upper, other, value), jnp.where(upper, value, other)], 0)
        bit //= 2
    return value


def body(state_old, state_now, drift, ocean, w_in, w_mid, w_out, cot_mid, cot_new):
    levels, rows, cols = state_now.shape
    width_in, hidden = w_in.shape
    ext = rows + 2 * WIDE
    count = 5 * levels + 1
    packs = -(-ext // 16)
    slots = rows + 8 + packs
    tall = rows // EARLY
    vmem = pl.BlockSpec(memory_space=pltpu.VMEM)
    hbm = pl.BlockSpec(memory_space=pltpu.HBM)
    strip = jax.ShapeDtypeStruct((rows, LANES), F32)
    edge = jax.ShapeDtypeStruct((count, WIDE, LANES), F32)
    arrays = (state_now, state_old, drift, cot_new, cot_mid, ocean, w_in, w_mid, w_out.T)
    weights = tuple(jax.ShapeDtypeStruct(a.shape, a.dtype) for a in arrays[6:])
    west, east, top, bottom, fields, *weights = pl.pallas_call(
        pack_kernel,
        out_shape=(strip, strip, edge, edge, jax.ShapeDtypeStruct((count, rows, cols), F32)) + weights,
        in_specs=[hbm] * 9,
        out_specs=(vmem,) * 8,
        scratch_shapes=[pltpu.VMEM((rows, cols), jnp.int32), pltpu.SemaphoreType.DMA((9,))],
        compiler_params=pltpu.CompilerParams(vmem_limit_bytes=8 * 2**20),
    )(*(pltpu.with_memory_space_constraint(a, pltpu.HBM) for a in arrays))

    kept = jax.ShapeDtypeStruct((tall // PART, hidden, PART * LANES), F32)
    closed = jax.ShapeDtypeStruct((tall * SHALLOW, LANES), F32)
    tall_weight = jax.ShapeDtypeStruct((hidden, DEEP), BF16)
    flat_weight = jax.ShapeDtypeStruct((DEEP, hidden), BF16)
    prepared = (flat_weight, tall_weight, jax.ShapeDtypeStruct((hidden, hidden), BF16), tall_weight, flat_weight)

    def early(k, extra, extra_out):
        return pl.pallas_call(
            functools.partial(early_kernel, k * tall),
            out_shape=(kept, kept, closed) + extra_out,
            in_specs=[vmem] * (1 + len(extra)),
            out_specs=(vmem,) * (3 + len(extra_out)),
            scratch_shapes=[pltpu.VMEM((tall * DEEP, LANES), F32)],
            compiler_params=pltpu.CompilerParams(vmem_limit_bytes=12 * 2**20),
            cost_estimate=pl.CostEstimate(
                flops=6 * hidden * hidden * tall * cols, bytes_accessed=0, transcendentals=2 * hidden * tall * cols
            ),
        )(fields, *extra)

    left = along(east, "lon", 1)
    right = along(west, "lon", -1)
    *first_kept, wi, wi_t, wm_t, wo, wo_t = early(0, tuple(weights), prepared)
    message = jax.ShapeDtypeStruct((count + 2, WIDE, LANES), F32)
    up, down = pl.pallas_call(
        join_kernel,
        out_shape=(message, message),
        in_specs=[vmem] * 4,
        out_specs=(vmem,) * 2,
        compiler_params=pltpu.CompilerParams(vmem_limit_bytes=4 * 2**20),
    )(top, bottom, left, right)
    low = along(up, "lat", 1)
    high = along(down, "lat", -1)
    done = list(first_kept)
    for k in range(1, EARLY):
        done += early(k, (left, wi_t, wm_t, wo_t), ())

    bands = lax.axis_size("lat")
    halves = hidden // LANES
    terms_rows = -(-halves * (hidden + 2 * DEEP) // (8 * bands)) * 8 * bands
    field = jax.ShapeDtypeStruct((levels, rows, cols), F32)
    ext_planes = jax.ShapeDtypeStruct((levels, ext, 2 * LANES), F32)
    low_kept = jax.ShapeDtypeStruct((rows // FINE, hidden, FINE * LANES), BF16)
    near = (4 + packs) * LANES
    staged = pltpu.VMEM((levels, rows, cols), F32)

    def tiles(deep):
        return [pltpu.VMEM((n * deep, LANES), F32) for n in (slots, 16 * packs, 2 * WIDE)]

    def half_terms(parts):
        return (jax.ShapeDtypeStruct((terms_rows // parts, LANES), F32),) * 2

    kept_halo = pltpu.VMEM((hidden, (8 + packs) * LANES), F32)
    state_mid, grad_old, sent, held, planes, mids, olds, seconds, dz_ones, dz_halo = pl.pallas_call(
        functools.partial(main_kernel, bands),
        out_shape=(field, field, *half_terms(2))
        + (jax.ShapeDtypeStruct((count, ext, 2 * LANES), F32), ext_planes, ext_planes)
        + (low_kept, low_kept, jax.ShapeDtypeStruct((hidden, near), BF16)),
        in_specs=[vmem] * (11 + 3 * EARLY),
        out_specs=(hbm,) * 2 + (vmem,) * 8,
        scratch_shapes=[
            staged,
            staged,
            pltpu.SemaphoreType.DMA((2,)),
            tiles(DEEP)[0],
            *tiles(DEEP),
            *tiles(SHALLOW),
            *tiles(SHALLOW),
            *tiles(DEEP),
            kept_halo,
            kept_halo,
            pltpu.VMEM((hidden, hidden), F32),
            pltpu.VMEM((DEEP, hidden), F32),
            pltpu.VMEM((hidden, DEEP), F32),
            pltpu.VMEM((terms_rows, LANES), F32),
        ],
        compiler_params=pltpu.CompilerParams(vmem_limit_bytes=24 * 2**20),
    )(fields, left, right, low, high, wi, wi_t, wm_t, weights[1], wo, wo_t, *done)

    bit = 1
    while 2 * bit < bands:
        got = swapped(sent, "lat", bit)
        bit *= 2
        sent, held = pl.pallas_call(
            functools.partial(halve_kernel, bit),
            out_shape=half_terms(2 * bit),
            in_specs=[vmem] * 2,
            out_specs=(vmem,) * 2,
            compiler_params=pltpu.CompilerParams(vmem_limit_bytes=4 * 2**20),
        )(held, got)
    got = swapped(sent, "lat", bit)
    state_new, grad_now, held, place = pl.pallas_call(
        late_kernel,
        out_shape=(field, field, half_terms(bands)[0], jax.ShapeDtypeStruct((8, LANES), jnp.int32)),
        in_specs=[vmem] * 10,
        out_specs=(hbm,) * 2 + (vmem,) * 2,
        scratch_shapes=[
            staged,
            staged,
            pltpu.SemaphoreType.DMA((2,)),
            tiles(SHALLOW)[0],
            *tiles(DEEP),
        ],
        compiler_params=pltpu.CompilerParams(vmem_limit_bytes=16 * 2**20),
        cost_estimate=pl.CostEstimate(
            flops=4 * DEEP * hidden * rows * cols, bytes_accessed=0, transcendentals=0
        ),
    )(fields, planes, mids, olds, seconds, dz_ones, dz_halo, wi, wo_t, held)
    summed = put_together(added_up(held + got, "lon"), place[:1], "lat")
    cells_all = rows * lax.axis_size("lat") * cols * lax.axis_size("lon")
    grad_in, grad_mid, grad_out = pl.pallas_call(
        functools.partial(scale_kernel, GAIN_GRAD / cells_all**0.5),
        out_shape=(
            jax.ShapeDtypeStruct((width_in, hidden), F32),
            jax.ShapeDtypeStruct((hidden, hidden), F32),
            jax.ShapeDtypeStruct((levels, hidden), F32),
        ),
        in_specs=[vmem],
        out_specs=(vmem,) * 3,
        compiler_params=pltpu.CompilerParams(vmem_limit_bytes=8 * 2**20),
    )(summed)
    return state_mid, state_new, grad_old, grad_now, grad_in, grad_mid, grad_out.T


def solution(mesh):
    field = P("grp", "lat", "lon")
    whole = P("grp", None)
    in_specs = (field, field, field, P(("grp", "lat"), "lon"), P(), P(), P(), field, field)
    out_specs = (field, field, field, field, whole, whole, whole)
    return jax.shard_map(body, mesh=mesh, in_specs=in_specs, out_specs=out_specs, check_vma=False)
```

```python
import functools

import jax
import jax.numpy as jnp
from jax import lax
from jax.experimental import pallas as pl
from jax.experimental.pallas import tpu as pltpu
from jax.sharding import PartitionSpec as P

KAPPA = 0.2
DT = 0.1
GAIN_GRAD = 10.0

WIDE = 4
LANES = 128
PART = 8
FINE = 4
EARLY = 2
DEEP = 16
SHALLOW = 8

F32 = jnp.float32
BF16 = jnp.bfloat16


def dot(left, right):
    return lax.dot_general(left, right, (((1,), (0,)), ((), ())), preferred_element_type=F32)


def dot_nt(left, right):
    return lax.dot_general(left, right, (((1,), (1,)), ((), ())), preferred_element_type=F32)


def pack_kernel(
    now, old, drift, cnew, cmid, ocean, w_in, w_mid, w_out,
    west, east, top, bottom, fields, v_in, v_mid, v_out, wet, sems,
):
    levels, rows, cols = now.shape
    copies = [
        pltpu.make_async_copy(ref, fields.at[pl.ds(levels * f, levels)], sems.at[f])
        for f, ref in enumerate((now, old, drift, cnew, cmid))
    ]
    copies.append(pltpu.make_async_copy(ocean, wet, sems.at[5]))
    for k, pair in enumerate(((w_in, v_in), (w_mid, v_mid), (w_out, v_out))):
        copies.append(pltpu.make_async_copy(*pair, sems.at[6 + k]))
    for copy in copies:
        copy.start()
    lane = lax.broadcasted_iota(jnp.int32, (rows, LANES), 1)
    to_west = jnp.zeros((rows, LANES), F32)
    to_east = jnp.zeros((rows, LANES), F32)
    count = fields.shape[0]
    for p in range(count):
        if p % levels == 0:
            copies[p // levels].wait()
        if p == count - 1:
            fields[p] = wet[...].astype(F32)
        plane = fields[p]
        here = (lane >= WIDE * p) & (lane < WIDE * (p + 1))
        to_west = jnp.where(here, pltpu.roll(plane, WIDE * p, 1) if p else plane, to_west)
        to_east = jnp.where(here, pltpu.roll(plane, WIDE * (p + 1), 1), to_east)
        top[p] = plane[:WIDE]
        bottom[p] = plane[rows - WIDE :]
    west[...] = to_west
    east[...] = to_east
    for copy in copies[6:]:
        copy.wait()


def join_kernel(top, bottom, left, right, up, down):
    count = top.shape[0]
    rows = left.shape[0]
    up[pl.ds(0, count)] = bottom[...]
    down[pl.ds(0, count)] = top[...]
    for k, strip in enumerate((left, right)):
        up[count + k] = strip[pl.ds(rows - WIDE, WIDE), :]
        down[count + k] = strip[pl.ds(0, WIDE), :]


def east_of(v):
    return pltpu.roll(v, v.shape[1] - 1, 1)


def west_of(v):
    return pltpu.roll(v, 1, 1)


def north_of(v):
    return pltpu.roll(v, v.shape[0] - 1, 0)


def south_of(v):
    return pltpu.roll(v, 1, 0)


def forward_stages(x, w_first_t, w_second_t):
    z_one = dot(w_first_t[...], x)
    yield
    first = jnp.tanh(z_one)
    low_first = first.astype(BF16)
    yield
    z_two = dot(w_second_t[...], low_first)
    yield
    second = jnp.tanh(z_two)
    return first, second, low_first, second.astype(BF16)


def closure(low_second, w_last_t):
    return dot(w_last_t[...], low_second).astype(BF16).astype(F32)[:SHALLOW]


def staggered(generators):
    live = []
    waiting = list(generators)
    while live or waiting:
        if waiting:
            live.append(waiting.pop(0))
        for part in list(live):
            try:
                next(part)
            except StopIteration:
                live.remove(part)


def lanes_of(ref, deep, base, tiles):
    block = ref[pl.ds(base * deep, tiles * deep), :]
    return jnp.concatenate([block[k * deep : (k + 1) * deep] for k in range(tiles)], 1)


def put_lanes(ref, deep, base, tiles, value):
    for k in range(tiles):
        ref[pl.ds((base + k) * deep, deep), :] = value[:, k * LANES : (k + 1) * LANES]


def early_kernel(start, fields, *refs):
    if start == 0:
        w_in, w_mid, w_out_t, keep1, keep2, cl, wi, wi_t, wm_t, wo, wo_t, ft = refs
        width_in, hidden = w_in.shape
        levels = w_out_t.shape[0]
        spare = jnp.zeros((DEEP - width_in, hidden), F32)
        wide_in = jnp.concatenate([w_in[...].astype(F32), spare], 0)
        wi[...] = wide_in.astype(BF16)
        wi_t[...] = wide_in.T.astype(BF16)
        wm_t[...] = w_mid[...].astype(F32).T.astype(BF16)
        spare = jnp.zeros((DEEP - levels, hidden), F32)
        wide_out = jnp.concatenate([w_out_t[...].astype(F32), spare], 0)
        wo_t[...] = wide_out.astype(BF16)
        wo[...] = wide_out.T.astype(BF16)
    else:
        unused, wi_t, wm_t, wo_t, keep1, keep2, cl, ft = refs
        levels = (fields.shape[0] - 1) // 5
    tall = cl.shape[0] // SHALLOW
    ft[...] = jnp.zeros_like(ft)
    for level in range(levels):
        v = fields[level]
        slope_x = 0.5 * (east_of(v) - west_of(v))
        slope_y = 0.5 * (north_of(v) - south_of(v))
        for f, plane in enumerate((v, slope_x, slope_y)):
            ft[pl.ds(f * levels + level, tall, stride=DEEP), :] = plane[start : start + tall]

    def part(base, kept1, kept2):
        x = lanes_of(ft, DEEP, base, PART).astype(BF16)
        first, second, unused_low, low_second = yield from forward_stages(x, wi_t, wm_t)
        kept1[...] = first
        kept2[...] = second
        yield
        put_lanes(cl, SHALLOW, base, PART, closure(low_second, wo_t))

    staggered(part(k * PART, keep1.at[k], keep2.at[k]) for k in range(tall // PART))


def copied_out(pairs, sems):
    copies = [pltpu.make_async_copy(*pair, sems.at[k]) for k, pair in enumerate(pairs)]
    for copy in copies:
        copy.start()
    return copies


class Block:
    def __init__(self, levels, rows):
        self.levels, self.rows = levels, rows
        self.ext = rows + 2 * WIDE
        self.packs = -(-self.ext // 16)
        self.wet = 5 * levels
        packed = [None] * self.packs
        ext = self.ext
        self.rim = [0, rows - 1, rows, ext - 1] + packed + [rows + 1, ext - 2, rows + 2, ext - 3]
        self.rim_near = self.rim[: 4 + self.packs]
        self.outer = [rows, ext - 1] + packed + [rows + 1, ext - 2]
        self.lane = lax.broadcasted_iota(jnp.int32, (ext, LANES), 1)

    def with_rim(self, plane):
        lane = self.lane
        body, side = plane[:, :LANES], plane[:, LANES:]
        own = jnp.where(lane == LANES - WIDE, pltpu.roll(body, LANES - WIDE, 1), pltpu.roll(body, WIDE, 1))
        return jnp.where((lane == LANES - WIDE) | (lane == WIDE - 1), own, side)

    def from_rim(self, body, side):
        lane = self.lane
        own = jnp.where(lane == 0, pltpu.roll(side, WIDE, 1), pltpu.roll(side, LANES - WIDE, 1))
        return jnp.where((lane == 0) | (lane == LANES - 1), own, body)

    def spread(self, plane, index, deep, main, extra, side, rimmed):
        main[pl.ds(index, self.rows, stride=deep), :] = plane[: self.rows, :LANES]
        extra[pl.ds(index, 2 * WIDE, stride=deep), :] = plane[self.rows :, :LANES]
        side[pl.ds(index, self.ext, stride=deep), :] = self.with_rim(plane) if rimmed else plane[:, LANES:]

    def gathered(self, index, deep, main, extra, side, rimmed):
        body = jnp.concatenate(
            [main[pl.ds(index, self.rows, stride=deep), :], extra[pl.ds(index, 2 * WIDE, stride=deep), :]], 0
        )
        beside = side[pl.ds(index, self.ext, stride=deep), :]
        return jnp.concatenate([self.from_rim(body, beside) if rimmed else body, beside], 1)

    def home(self, r, deep, main, extra):
        return main.at[pl.ds(r * deep, deep)] if r < self.rows else extra.at[pl.ds((r - self.rows) * deep, deep)]

    def pack_halo(self, order, deep, main, extra, side, rim_too=True):
        where = lax.broadcasted_iota(jnp.int32, (deep, LANES), 1)
        for i, r in enumerate(order):
            if r is not None and (rim_too or r >= self.rows):
                main[pl.ds((self.rows + i) * deep, deep), :] = self.home(r, deep, main, extra)[...]
        first_pack = self.rows + order.index(None)
        for q in range(self.packs):
            total = jnp.zeros((deep, LANES), F32)
            for j in range(min(16, self.ext - 16 * q)):
                moved = pltpu.roll(side[pl.ds((16 * q + j) * deep, deep), :], (2 * WIDE * j + WIDE) % LANES, 1)
                total = jnp.where((where >= 2 * WIDE * j) & (where < 2 * WIDE * (j + 1)), moved, total)
            main[pl.ds((first_pack + q) * deep, deep), :] = total

    def unpack_halo(self, order, deep, main, extra, side):
        for i, r in enumerate(order):
            if r is not None:
                self.home(r, deep, main, extra)[...] = main[pl.ds((self.rows + i) * deep, deep), :]
        first_pack = self.rows + order.index(None)
        for q in range(self.packs):
            tile = main[pl.ds((first_pack + q) * deep, deep), :]
            for j in range(min(16, self.ext - 16 * q)):
                moved = pltpu.roll(tile, LANES - (2 * WIDE * j + WIDE) % LANES, 1)
                side[pl.ds((16 * q + j) * deep, deep), :] = moved

    def force(self, planes, v, level, closed):
        eastward, westward, northward, southward = east_of(v), west_of(v), north_of(v), south_of(v)
        laplace = eastward + westward + northward + southward - 4.0 * v
        slope = 0.5 * (eastward - westward)
        return planes[self.wet] * (KAPPA * laplace - planes[2 * self.levels + level] * slope + closed)

    def adjoint(self, planes, weighted, level, tiles, rimmed):
        levels = self.levels
        masked = planes[self.wet] * weighted
        carried = planes[2 * levels + level] * masked
        a0, a1, a2 = (self.gathered(f * levels + level, DEEP, *tiles, rimmed) for f in range(3))
        result = KAPPA * (east_of(masked) + west_of(masked) + north_of(masked) + south_of(masked) - 4.0 * masked)
        result = result + 0.5 * (east_of(carried) - west_of(carried)) + a0
        return result - 0.5 * (east_of(a1) - west_of(a1)) - 0.5 * (north_of(a2) - south_of(a2))


def feature_gradients(dz_one, w_in):
    return dot(w_in[...], dz_one).astype(BF16).astype(F32)


def main_kernel(bands, *refs):
    fields, left, right, low, high, wi, wi_t, wm_t, w_mid, wo, wo_t, *refs = refs
    early, refs = refs[: 3 * EARLY], refs[3 * EARLY :]
    h_mid, h_old, o_sent, o_kept, planes, mids, olds, seconds, dz_ones, dz_halo, *refs = refs
    o_mid, o_old, sems, ft1, ft2, fth, ftx, cl, clh, clx, dc, dch, dcx, df, dfh, dfx, halo1, halo2, *refs = refs
    acc_mid, acc_in, acc_out, o_grad = refs
    levels, rows, cols = o_mid.shape
    hidden = w_mid.shape[0]
    block = Block(levels, rows)
    count, ext, lane = block.wet + 1, block.ext, block.lane
    span = FINE * LANES
    cuts = [pl.ds(at, span) for at in range(0, PART * LANES, span)]
    kept1 = [ref.at[k, :, cut] for ref in early[0::3] for k in range(ref.shape[0]) for cut in cuts]
    kept2 = [ref.at[k, :, cut] for ref in early[1::3] for k in range(ref.shape[0]) for cut in cuts]

    band = lax.axis_index("lat")
    has_low = jnp.where(band > 0, 1.0, 0.0)
    has_high = jnp.where(band < bands - 1, 1.0, 0.0)

    def beyond(p):
        return [high[p] * has_high, low[p] * has_low]

    left_all = jnp.concatenate([left[...]] + beyond(count), 0)
    right_all = jnp.concatenate([right[...]] + beyond(count + 1), 0)
    for p in range(count):
        from_right = pltpu.roll(right_all, LANES - WIDE * p, 1) if p else right_all
        from_left = pltpu.roll(left_all, LANES - WIDE * (p + 1), 1)
        side = jnp.where(lane < WIDE, from_right, jnp.where(lane >= LANES - WIDE, from_left, 0.0))
        planes[p, :, pl.ds(0, LANES)] = jnp.concatenate([fields[p]] + beyond(p), 0)
        planes[p, :, pl.ds(LANES, LANES)] = side

    for ref in (ft1, ft2, fth, ftx, dc, dch, dcx):
        ref[...] = jnp.zeros_like(ref)

    def inputs_at(ref, base, tiles):
        return lanes_of(ref, DEEP, base, tiles).astype(BF16)

    def cotangents_at(base, tiles):
        part = lanes_of(dc, SHALLOW, base, tiles)
        return jnp.concatenate([part, jnp.zeros_like(part)], 0).astype(BF16)

    def backward_stages(first, second, cot):
        g_two = dot(wo[...], cot)
        yield
        dz_two = (g_two * (1.0 - second * second)).astype(BF16)
        yield
        g_one = dot(w_mid[...], dz_two)
        yield
        dz_one = (g_one * (1.0 - first * first)).astype(BF16)
        yield
        return dz_one, dz_two

    def second_part(base, tiles, held, sums):
        x = inputs_at(ft2, base, tiles)
        cot = cotangents_at(base, tiles)
        first, second, low_first, low_second = yield from forward_stages(x, wi_t, wm_t)
        if held is not None:
            held[...] = low_second
        yield
        dz_one, dz_two = yield from backward_stages(first, second, cot)
        dfeat = feature_gradients(dz_one, wi)
        if sums is not None:
            add_terms(sums, (low_first, dz_two), (x, dz_one), (low_second, cot))
        yield
        put_lanes(df, DEEP, base, tiles, dfeat)

    def third_part(base, tiles, held1, held2, held, counted, sums):
        cot = cotangents_at(base, tiles)
        first = held1[...]
        second = held2[...]
        dz_one, dz_two = yield from backward_stages(first, second, cot)
        held[...] = dz_one
        yield
        x = inputs_at(ft1, base, tiles)
        if counted is not None:
            dz_one, dz_two, cot = (jnp.where(counted, v.astype(F32), 0.0).astype(BF16) for v in (dz_one, dz_two, cot))
        add_terms(sums, (first.astype(BF16), dz_two), (x, dz_one), (second.astype(BF16), cot))

    def add_terms(sums, *pairs):
        for k, pair in enumerate(pairs):
            sums[k] = dot_nt(*pair) if sums[k] is None else sums[k] + dot_nt(*pair)

    def features_of(source, ft, order, rimmed):
        for level in range(levels):
            v = source[level]
            for f, plane in enumerate((v, 0.5 * (east_of(v) - west_of(v)), 0.5 * (north_of(v) - south_of(v)))):
                block.spread(plane, f * levels + level, DEEP, ft, ftx, fth, rimmed)
        block.pack_halo(order, DEEP, ft, ftx, fth)

    features_of(planes, ft1, block.rim, True)
    for k, ref in enumerate(early[2::3]):
        cl[pl.ds(k * ref.shape[0], ref.shape[0]), :] = ref[...]

    def first_part(at, tiles):
        base = rows + at
        first, second, unused, low_second = yield from forward_stages(inputs_at(ft1, base, tiles), wi_t, wm_t)
        halo1[:, pl.ds(at * LANES, tiles * LANES)] = first
        halo2[:, pl.ds(at * LANES, tiles * LANES)] = second
        yield
        put_lanes(cl, SHALLOW, base, tiles, closure(low_second, wo_t))

    def second_cotangents():
        for level in range(levels):
            masked = planes[block.wet] * (2.0 * DT * planes[3 * levels + level])
            block.spread(masked, level, SHALLOW, dc, dcx, dch, False)
            yield
        block.pack_halo(block.outer, SHALLOW, dc, dcx, dch)

    half = len(block.rim) // 2
    staggered([first_part(0, half), first_part(half, len(block.rim) - half), second_cotangents()])
    block.unpack_halo(block.rim, SHALLOW, cl, clx, clh)
    for level in range(levels):
        closed = block.gathered(level, SHALLOW, cl, clx, clh, True)
        mid = planes[levels + level] + 2.0 * DT * block.force(planes, planes[level], level, closed)
        o_mid[level] = mid[:rows, :LANES]
        mids[level] = mid
    copies = copied_out([(o_mid, h_mid)], sems.at[pl.ds(0, 1)])

    features_of(mids, ft2, block.outer, False)
    sums = [None] * 3
    staggered(
        [second_part(rows, len(block.outer), None, None)]
        + [second_part(k * FINE, FINE, seconds.at[k], sums) for k in range(rows // FINE)]
    )
    for acc, total in zip((acc_mid, acc_in, acc_out), sums):
        acc[...] = total
    block.unpack_halo(block.outer, DEEP, df, dfx, dfh)
    for level in range(levels):
        weighted = 2.0 * DT * planes[3 * levels + level]
        grad = planes[4 * levels + level] + block.adjoint(planes, weighted, level, (df, dfx, dfh), False)
        o_old[level] = grad[:rows, :LANES]
        olds[level] = grad
    copies += copied_out([(o_old, h_old)], sems.at[pl.ds(1, 1)])

    near = block.rim_near
    row = lax.broadcasted_iota(jnp.int32, (ext, LANES), 0)
    inside = (lane > 0) & (lane < LANES - 1) & (row > 0) & (row < rows - 1)
    for level in range(levels):
        masked = planes[block.wet] * (2.0 * DT * olds[level])
        body = masked[:, :LANES]
        dc[pl.ds(level, rows, stride=SHALLOW), :] = jnp.where(inside, body, 0.0)[:rows]
        dcx[pl.ds(level, 2 * WIDE, stride=SHALLOW), :] = body[rows:]
        dch[pl.ds(level, ext, stride=SHALLOW), :] = block.with_rim(masked)
        for k, r in enumerate(near[:2]):
            dc[pl.ds((rows + k) * SHALLOW + level, 1), :] = body[r : r + 1]
    block.pack_halo(near, SHALLOW, dc, dcx, dch, False)
    at = lax.broadcasted_iota(jnp.int32, (1, len(near) * LANES), 1)
    tile, place = at >> 7, at & (LANES - 1)
    side_row = (tile - 4) * 16 + (place >> 3)
    edge = ((place & 7) == 0) | ((place & 7) == 7)
    counted = (tile < 2) | ((tile >= 4) & edge & (side_row > 0) & (side_row < rows - 1))
    wide = pl.ds(0, len(near) * LANES)
    sums = [None] * 3
    staggered(
        [third_part(rows, len(near), halo1.at[:, wide], halo2.at[:, wide], dz_halo, counted, sums)]
        + [third_part(k * FINE, FINE, kept1[k], kept2[k], dz_ones.at[k], None, sums) for k in range(rows // FINE)]
    )

    start = 0
    for total in (acc_mid[...] + sums[0], acc_in[...] + sums[1], (acc_out[...] + sums[2]).T):
        deep = total.shape[0]
        for half in range(hidden // LANES):
            o_grad[pl.ds(start, deep), :] = total[:, half * LANES : (half + 1) * LANES]
            start += deep
    if start < o_grad.shape[0]:
        o_grad[pl.ds(start, o_grad.shape[0] - start), :] = jnp.zeros((o_grad.shape[0] - start, LANES), F32)
    halve(o_grad[...], 1, o_sent, o_kept)
    for copy in copies:
        copy.wait()


def halve(value, bit, sent, kept):
    half = value.shape[0] // 2
    upper = (lax.axis_index("lat") & bit) != 0
    sent[...] = jnp.where(upper, value[:half], value[half:])
    kept[...] = jnp.where(upper, value[half:], value[:half])


def halve_kernel(bit, held, got, sent, kept):
    halve(held[...] + got[...], bit, sent, kept)


def late_kernel(fields, planes, mids, olds, seconds, dz_ones, dz_halo, wi, wo_t, held, *refs):
    h_new, h_now, o_held, o_place, o_new, o_now, sems, cl, df, dfh, dfx = refs
    levels, rows, cols = o_new.shape
    block = Block(levels, rows)
    o_held[...] = held[...]
    o_place[...] = jnp.zeros_like(o_place) + lax.axis_index("lat")
    put_lanes(df, DEEP, rows, len(block.rim_near), feature_gradients(dz_halo[...], wi))
    for k in range(0, rows // FINE, 2):
        for ref, put, deep, kind in ((dz_ones, df, DEEP, 0), (seconds, cl, SHALLOW, 1)):
            both = jnp.concatenate([ref[k], ref[k + 1]], 1)
            value = closure(both, wo_t) if kind else feature_gradients(both, wi)
            put_lanes(put, deep, k * FINE, 2 * FINE, value)
    beside = jnp.zeros((rows, LANES), F32)
    beyond = jnp.zeros((2 * WIDE, 2 * LANES), F32)
    for level in range(levels):
        closed = jnp.concatenate([cl[pl.ds(level, rows, stride=SHALLOW), :], beside], 1)
        closed = jnp.concatenate([closed, beyond], 0)
        new = planes[level] + 2.0 * DT * block.force(planes, mids[level], level, closed)
        o_new[level] = new[:rows, :LANES]
    copies = copied_out([(o_new, h_new)], sems.at[pl.ds(0, 1)])
    block.unpack_halo(block.rim_near, DEEP, df, dfx, dfh)
    for level in range(levels):
        grad = block.adjoint(planes, 2.0 * DT * olds[level], level, (df, dfx, dfh), True)
        o_now[level] = fields[3 * levels + level] + grad[:rows, :LANES]
    copies += copied_out([(o_now, h_now)], sems.at[pl.ds(1, 1)])
    for copy in copies:
        copy.wait()


def scale_kernel(factor, terms, g_in, g_mid, g_out):
    hidden = g_mid.shape[0]
    start = 0
    for ref, deep in ((g_mid, hidden), (g_in, DEEP), (g_out, DEEP)):
        for half in range(hidden // LANES):
            ref[:, half * LANES : (half + 1) * LANES] = terms[pl.ds(start, ref.shape[0]), :] * factor
            start += deep


def along(value, axis, step):
    count = lax.axis_size(axis)
    return lax.ppermute(value, axis, [(i, (i + step) % count) for i in range(count)])


def swapped(value, axis, bit):
    return lax.ppermute(value, axis, [(i, i ^ bit) for i in range(lax.axis_size(axis))])


def added_up(value, axis):
    bit = 1
    while bit < lax.axis_size(axis):
        near = swapped(value, axis, bit)
        if 2 * bit < lax.axis_size(axis):
            value = (value + near) + (swapped(value, axis, 2 * bit) + swapped(value, axis, 3 * bit))
            bit *= 4
        else:
            value = value + near
            bit *= 2
    return value


def put_together(value, place, axis):
    bit = lax.axis_size(axis) // 2
    while bit:
        upper = (place & bit) != 0
        other = swapped(value, axis, bit)
        value = jnp.concatenate([jnp.where(upper, other, value), jnp.where(upper, value, other)], 0)
        bit //= 2
    return value


def body(state_old, state_now, drift, ocean, w_in, w_mid, w_out, cot_mid, cot_new):
    levels, rows, cols = state_now.shape
    width_in, hidden = w_in.shape
    ext = rows + 2 * WIDE
    count = 5 * levels + 1
    packs = -(-ext // 16)
    slots = rows + 8 + packs
    tall = rows // EARLY
    vmem = pl.BlockSpec(memory_space=pltpu.VMEM)
    hbm = pl.BlockSpec(memory_space=pltpu.HBM)
    strip = jax.ShapeDtypeStruct((rows, LANES), F32)
    edge = jax.ShapeDtypeStruct((count, WIDE, LANES), F32)
    arrays = (state_now, state_old, drift, cot_new, cot_mid, ocean, w_in, w_mid, w_out.T)
    weights = tuple(jax.ShapeDtypeStruct(a.shape, a.dtype) for a in arrays[6:])
    west, east, top, bottom, fields, *weights = pl.pallas_call(
        pack_kernel,
        out_shape=(strip, strip, edge, edge, jax.ShapeDtypeStruct((count, rows, cols), F32)) + weights,
        in_specs=[hbm] * 9,
        out_specs=(vmem,) * 8,
        scratch_shapes=[pltpu.VMEM((rows, cols), jnp.int32), pltpu.SemaphoreType.DMA((9,))],
        compiler_params=pltpu.CompilerParams(vmem_limit_bytes=8 * 2**20),
    )(*(pltpu.with_memory_space_constraint(a, pltpu.HBM) for a in arrays))

    kept = jax.ShapeDtypeStruct((tall // PART, hidden, PART * LANES), F32)
    closed = jax.ShapeDtypeStruct((tall * SHALLOW, LANES), F32)
    tall_weight = jax.ShapeDtypeStruct((hidden, DEEP), BF16)
    flat_weight = jax.ShapeDtypeStruct((DEEP, hidden), BF16)
    prepared = (flat_weight, tall_weight, jax.ShapeDtypeStruct((hidden, hidden), BF16), tall_weight, flat_weight)

    def early(k, extra, extra_out):
        return pl.pallas_call(
            functools.partial(early_kernel, k * tall),
            out_shape=(kept, kept, closed) + extra_out,
            in_specs=[vmem] * (1 + len(extra)),
            out_specs=(vmem,) * (3 + len(extra_out)),
            scratch_shapes=[pltpu.VMEM((tall * DEEP, LANES), F32)],
            compiler_params=pltpu.CompilerParams(vmem_limit_bytes=12 * 2**20),
            cost_estimate=pl.CostEstimate(
                flops=6 * hidden * hidden * tall * cols, bytes_accessed=0, transcendentals=2 * hidden * tall * cols
            ),
        )(fields, *extra)

    left = along(east, "lon", 1)
    right = along(west, "lon", -1)
    *first_kept, wi, wi_t, wm_t, wo, wo_t = early(0, tuple(weights), prepared)
    message = jax.ShapeDtypeStruct((count + 2, WIDE, LANES), F32)
    up, down = pl.pallas_call(
        join_kernel,
        out_shape=(message, message),
        in_specs=[vmem] * 4,
        out_specs=(vmem,) * 2,
        compiler_params=pltpu.CompilerParams(vmem_limit_bytes=4 * 2**20),
    )(top, bottom, left, right)
    low = along(up, "lat", 1)
    high = along(down, "lat", -1)
    done = list(first_kept)
    for k in range(1, EARLY):
        done += early(k, (left, wi_t, wm_t, wo_t), ())

    bands = lax.axis_size("lat")
    halves = hidden // LANES
    terms_rows = -(-halves * (hidden + 2 * DEEP) // (8 * bands)) * 8 * bands
    field = jax.ShapeDtypeStruct((levels, rows, cols), F32)
    ext_planes = jax.ShapeDtypeStruct((levels, ext, 2 * LANES), F32)
    low_kept = jax.ShapeDtypeStruct((rows // FINE, hidden, FINE * LANES), BF16)
    near = (4 + packs) * LANES
    staged = pltpu.VMEM((levels, rows, cols), F32)

    def tiles(deep):
        return [pltpu.VMEM((n * deep, LANES), F32) for n in (slots, 16 * packs, 2 * WIDE)]

    def half_terms(parts):
        return (jax.ShapeDtypeStruct((terms_rows // parts, LANES), F32),) * 2

    kept_halo = pltpu.VMEM((hidden, (8 + packs) * LANES), F32)
    state_mid, grad_old, sent, held, planes, mids, olds, seconds, dz_ones, dz_halo = pl.pallas_call(
        functools.partial(main_kernel, bands),
        out_shape=(field, field, *half_terms(2))
        + (jax.ShapeDtypeStruct((count, ext, 2 * LANES), F32), ext_planes, ext_planes)
        + (low_kept, low_kept, jax.ShapeDtypeStruct((hidden, near), BF16)),
        in_specs=[vmem] * (11 + 3 * EARLY),
        out_specs=(hbm,) * 2 + (vmem,) * 8,
        scratch_shapes=[
            staged,
            staged,
            pltpu.SemaphoreType.DMA((2,)),
            tiles(DEEP)[0],
            *tiles(DEEP),
            *tiles(SHALLOW),
            *tiles(SHALLOW),
            *tiles(DEEP),
            kept_halo,
            kept_halo,
            pltpu.VMEM((hidden, hidden), F32),
            pltpu.VMEM((DEEP, hidden), F32),
            pltpu.VMEM((hidden, DEEP), F32),
            pltpu.VMEM((terms_rows, LANES), F32),
        ],
        compiler_params=pltpu.CompilerParams(vmem_limit_bytes=24 * 2**20),
    )(fields, left, right, low, high, wi, wi_t, wm_t, weights[1], wo, wo_t, *done)

    bit = 1
    while 2 * bit < bands:
        got = swapped(sent, "lat", bit)
        bit *= 2
        sent, held = pl.pallas_call(
            functools.partial(halve_kernel, bit),
            out_shape=half_terms(2 * bit),
            in_specs=[vmem] * 2,
            out_specs=(vmem,) * 2,
            compiler_params=pltpu.CompilerParams(vmem_limit_bytes=4 * 2**20),
        )(held, got)
    got = swapped(sent, "lat", bit)
    state_new, grad_now, held, place = pl.pallas_call(
        late_kernel,
        out_shape=(field, field, half_terms(bands)[0], jax.ShapeDtypeStruct((8, LANES), jnp.int32)),
        in_specs=[vmem] * 10,
        out_specs=(hbm,) * 2 + (vmem,) * 2,
        scratch_shapes=[
            staged,
            staged,
            pltpu.SemaphoreType.DMA((2,)),
            tiles(SHALLOW)[0],
            *tiles(DEEP),
        ],
        compiler_params=pltpu.CompilerParams(vmem_limit_bytes=16 * 2**20),
        cost_estimate=pl.CostEstimate(
            flops=4 * DEEP * hidden * rows * cols, bytes_accessed=0, transcendentals=0
        ),
    )(fields, planes, mids, olds, seconds, dz_ones, dz_halo, wi, wo_t, held)
    summed = put_together(added_up(held + got, "lon"), place[:1], "lat")
    cells_all = rows * lax.axis_size("lat") * cols * lax.axis_size("lon")
    grad_in, grad_mid, grad_out = pl.pallas_call(
        functools.partial(scale_kernel, GAIN_GRAD / cells_all**0.5),
        out_shape=(
            jax.ShapeDtypeStruct((width_in, hidden), F32),
            jax.ShapeDtypeStruct((hidden, hidden), F32),
            jax.ShapeDtypeStruct((levels, hidden), F32),
        ),
        in_specs=[vmem],
        out_specs=(vmem,) * 3,
        compiler_params=pltpu.CompilerParams(vmem_limit_bytes=8 * 2**20),
    )(summed)
    return state_mid, state_new, grad_old, grad_now, grad_in, grad_mid, grad_out.T


def solution(mesh):
    field = P("grp", "lat", "lon")
    whole = P("grp", None)
    in_specs = (field, field, field, P(("grp", "lat"), "lon"), P(), P(), P(), field, field)
    out_specs = (field, field, field, field, whole, whole, whole)
    return jax.shard_map(body, mesh=mesh, in_specs=in_specs, out_specs=out_specs, check_vma=False)
```
